128 devices in a mesh: scene: 8 (over y_hi, x), row: 16 (over z, y_lo, core).
Axes of the slice: x: 4, y: 4 (y_hi: 2, y_lo: 2; y = y_hi * 2 + y_lo), z: 4, core: 2. Of those that a mesh axis runs over, the one named last changes fastest.
Arguments:
- tokens: bfloat16 [8, 224, 14, 1024], P('scene', 'row'), may hold values from -6 to 6
- qkv_weight: bfloat16 [1024, 3072], replicated, may hold values from -0.1875 to 0.1875
- out_weight: bfloat16 [1024, 1024], replicated, may hold values from -0.1875 to 0.1875
- position_bias: float32 [32, 169], replicated, may hold values from -260 to 260
- window_shift: int32 [2], replicated, may hold values from 1 to 6, as said below
- expert_up: bfloat16 [32, 1024, 4096], P('scene', None, 'row'), may hold values from -0.1875 to 0.1875
- expert_down: bfloat16 [32, 4096, 1024], P('scene', 'row'), may hold values from -0.09375 to 0.09375
- expert_choice: int32 [8, 224, 14, 1], P('scene', 'row'), may hold values from 0 to 31; in each aligned block of 196 rows (0 to 195, 196 to 391, ..., all dimensions but the last counted through in order) at most 7 rows name the same one
- combine_weight: float32 [8, 224, 14], P('scene', 'row'), may hold values from 0.2 to 1
- reduce_weight: bfloat16 [4096, 2048], P(None, 'scene'), may hold values from -0.09375 to 0.09375
- merged_grad: bfloat16 [8, 112, 7, 2048], P(None, 'row', None, 'scene'), may hold values from -6 to 6
Outputs:
- merged: bfloat16 [8, 112, 7, 2048], P(None, 'row', None, 'scene')
- tokens_grad: bfloat16 [8, 224, 14, 1024], P('scene', 'row')
- up_grad: float32 [32, 1024, 4096], P('scene', None, 'row')
- down_grad: float32 [32, 4096, 1024], P('scene', 'row')
The draws below stay inside these ranges and needn't reach their ends.
Inputs may be any that keep to these rules, and one draw needn't show every extreme that they name: `expert_choice`: within the tokens of one device no expert is named by more than 7 tokens, and in every draw some expert is named by exactly 7 tokens of some device. `window_shift`: both shifts lie between 1 and 6, and one of them equals 6.
All inputs are finite; a program needn't handle non-finite values.
Results may differ from the reference program's by a relative error of at most 0.024.
Values may be sent and summed in bfloat16 or wider, within the bound.
A program may use at most 192 MiB of HBM per device.

```python
import math
import jax
import jax.numpy as jnp
import numpy as np
from jax import lax

C = 1024
HEADS = 32
HID = 4096
WIN = 7
WIDTH = 14
TOK_DEV = 196
EXPERTS = 32
CAP = 7
SCENES = 8
HEIGHT = 224
N_SCENE = 8
N_ROW = 16


def draw_window_shift(key, part):
    key = jax.random.fold_in(key, 11)
    which_one = jax.random.randint(jax.random.fold_in(key, 1), (), 0, 2)
    other_shift = jax.random.randint(jax.random.fold_in(key, 2), (), 1, WIN)
    return jnp.where(jnp.arange(2) == which_one, WIN - 1, other_shift).astype(jnp.int32)


def draw_position_bias(key, part):
    key = jax.random.fold_in(key, 23)
    span_area = (2 * WIN - 1) ** 2
    values = jnp.clip(2.0 * jax.random.normal(jax.random.fold_in(key, 1), (HEADS, span_area), jnp.float32), -12.0, 12.0)
    return values.astype(jnp.float32)


def raised(values, own_key, source, target, shards_of, factor):
    def block_of(dim):
        return (jnp.arange(values.shape[dim]) // (values.shape[dim] // shards_of)).reshape((-1,) + (1,) * (values.ndim - 1 - dim))

    one_side = jax.random.permutation(own_key, shards_of)[block_of(target)]
    other_side = (block_of(target) + shards_of // 2) % shards_of
    return jnp.where((block_of(source) == one_side) | (block_of(source) == other_side), factor * values, values)


def block_scale(rng, shape, shards, least, high):
    gain, own = 1.0, jax.random.fold_in(rng, 6)
    for axis_at, shards_of in shards:
        heights = jnp.exp(jax.random.uniform(jax.random.fold_in(own, axis_at), (shards_of,), jnp.float32, least / len(shards), high / len(shards)))
        gain = gain * jnp.repeat(heights, shape[axis_at] // shards_of).reshape([-1 if axis == axis_at else 1 for axis in range(len(shape))])
    return gain


def deal_out(key, own, number, rows, number_of, top, reach, skew):
    order = jax.random.permutation(key, number_of)
    crowded, usual = shares(number_of, rows * top, reach, skew, True), shares(number_of, rows * top, reach, skew, False)
    places = jnp.arange(number_of)

    def named(sizes, turn):
        used = int((sizes > 0).sum())
        fixed = max(1, used // 4)
        moved = fixed + (places - fixed + turn * (used - fixed)) % max(1, number_of - fixed)
        return jnp.zeros((number_of,), jnp.int32).at[order[jnp.where(places < fixed, places, moved)]].set(jnp.asarray(sizes, jnp.int32))

    sizes = jnp.where(number % 4 == 0, named(crowded, number // 4), named(usual, number - number // 4 - 1))
    mixed = jax.random.permutation(jax.random.fold_in(own, 3), number_of)
    giver, receiver = mixed[0:number_of // 2 * 2:2], mixed[1:number_of // 2 * 2:2]
    margin = jnp.minimum(sizes[giver] - 1, reach - sizes[receiver]) // 2
    margin = jnp.where((giver == order[0]) | (receiver == order[0]) | (sizes[receiver] == 0), 0, jnp.maximum(margin, 0))
    moved = jax.random.randint(jax.random.fold_in(own, 4), (number_of // 2,), 0, 1 << 20) % (margin + 1)
    sizes = sizes.at[giver].add(-moved).at[receiver].add(moved)
    items = jnp.searchsorted(jnp.cumsum(sizes), jnp.arange(rows * top), side="right").astype(jnp.int32)
    table = items.reshape(top, rows).T
    table = table[jax.random.permutation(jax.random.fold_in(own, 1), rows)]
    turn = jax.random.randint(jax.random.fold_in(own, 2), (rows, 1), 0, top)
    return jnp.take_along_axis(table, (jnp.arange(top)[None, :] + turn) % top, axis=1)


def shares(count, total, most, skew, full):
    portions = [(1 << 20) // math.isqrt(standing ** skew) + 1 for standing in range(1, count + 1)]
    largest = most if full else min(most, max(-(-total // count), total * portions[0] // sum(portions)))
    least = 1 if total - largest >= count - 1 else 0
    given, surplus = [largest] + [least] * (count - 1), total - largest - least * (count - 1)
    while surplus > 0:
        free = [i for i in range(1, count) if given[i] < largest] or [i for i in range(1, count) if given[i] < most]
        pool, left = sum([portions[i] for i in free]), surplus
        for i in free:
            more = min(most - given[i], max(1, left * portions[i] // pool), surplus)
            given[i] = given[i] + more
            surplus = surplus - more
    return np.array(given)


def gaussian(stream_key, shape, deviation, most, pieces=(), kind=jnp.bfloat16):
    values = jax.random.normal(stream_key, shape, jnp.float32) * deviation
    if len(pieces) > 0:
        values = block_scale(stream_key, shape, pieces, -0.22, 0.18) * values
    return jnp.clip(values, min=-most, max=most).astype(kind)


def noise_with(stream_key, extent, scale, limit, shards, heavy, kind=jnp.bfloat16):
    array = scale * jax.random.normal(stream_key, extent, jnp.float32)
    if shards:
        array = array * block_scale(stream_key, extent, shards, -0.22, 0.18)
    return jnp.clip(raised(array, jax.random.fold_in(stream_key, 3), *heavy), -limit, limit).astype(kind)


def setup_inputs(seed: int = 0) -> dict:
    streams_of = jax.random.split(jax.random.key(seed), 12)
    tokens = gaussian(streams_of[0], (SCENES, HEIGHT, WIDTH, C), 1.0, 6.0, ((0, 8), (1, 16)))
    qkv_weight = gaussian(streams_of[1], (C, 3 * C), C ** -0.5, 0.1875)
    out_weight = gaussian(streams_of[2], (C, C), C ** -0.5, 0.1875)
    position_bias = draw_position_bias(jax.random.fold_in(streams_of[11], 71), 0)
    window_shift = draw_window_shift(jax.random.fold_in(streams_of[11], 71), 0)
    expert_up = gaussian(streams_of[5], (EXPERTS, C, HID), C ** -0.5, 0.1875, ((0, 8), (2, 16)))
    expert_down = gaussian(streams_of[6], (EXPERTS, HID, C), HID ** -0.5, 0.09375, ((0, 8), (1, 16)))
    expert_choice_keys = jax.random.split(jax.random.fold_in(streams_of[7], 1), SCENES * HEIGHT * WIDTH // TOK_DEV)
    expert_choice_turns = jax.random.permutation(jax.random.fold_in(streams_of[7], 3), SCENES * HEIGHT * WIDTH // TOK_DEV)
    expert_choice = jax.vmap(lambda own, number: deal_out(jax.random.fold_in(streams_of[7], 2), own, number, TOK_DEV, EXPERTS, 1, CAP, 2))(expert_choice_keys, expert_choice_turns).reshape((SCENES, HEIGHT, WIDTH, 1))
    combine_weight = jnp.clip(jnp.exp(math.log(1.0) - 1.609438 * jax.random.uniform(streams_of[8], (SCENES, HEIGHT, WIDTH), jnp.float32) ** block_scale(streams_of[8], (SCENES, HEIGHT, WIDTH), ((0, 8), (1, 16)), -0.2, 0.2)), 0.2, 1.0)
    reduce_weight = gaussian(streams_of[9], (4 * C, 2 * C), (4 * C) ** -0.5, 0.09375, ((1, 8),))
    merged_grad = noise_with(streams_of[10], (SCENES, HEIGHT // 2, WIDTH // 2, 2 * C), 1.0, 6.0, ((1, 16), (3, 8)), (3, 0, 8, 2.0))
    return {"tokens": tokens, "qkv_weight": qkv_weight, "out_weight": out_weight, "position_bias": position_bias, "window_shift": window_shift, "expert_up": expert_up, "expert_down": expert_down, "expert_choice": expert_choice, "combine_weight": combine_weight, "reduce_weight": reduce_weight, "merged_grad": merged_grad}


EPSILON = 1e-05

def layer_norm(values):
    centre = lax.optimization_barrier(jnp.mean(values, axis=-1, keepdims=True))
    centred = values - centre
    spread = lax.optimization_barrier(jnp.mean(centred * centred, axis=-1, keepdims=True))
    return centred * lax.rsqrt(spread + EPSILON)

def norm_grad(values, cotangent):
    _, pullback = jax.vjp(layer_norm, values)
    return pullback(cotangent)[0]

def gelu_exact(values):
    return jax.nn.gelu(values, approximate=False)

def bias_pairs():
    rel_span = 2 * WIN - 1
    window_area = WIN * WIN
    positions = np.arange(window_area)
    pos_y = positions // WIN
    pos_x = positions % WIN
    relative = (pos_y[:, None] - pos_y[None, :] + WIN - 1) * rel_span + (pos_x[:, None] - pos_x[None, :] + WIN - 1)
    return (relative.reshape(-1)[:, None] == np.arange(rel_span * rel_span)[None, :]).astype(np.float32)

def region(first_row, row_count, total_rows, shift_amount):
    position = first_row + jnp.arange(row_count, dtype=jnp.int32)
    return jnp.where(position < total_rows - WIN, 0, jnp.where(position < total_rows - shift_amount, 1, 2))

def window_attention(field, qkv_weight, out_weight, position_bias, row_start, total_rows, shift_row, shift_col):
    scene_count, row_count, col_count, features = field.shape
    head_count = position_bias.shape[0]
    head_dim = features // head_count
    window_area = WIN * WIN
    win_rows = row_count // WIN
    win_cols = col_count // WIN
    qkv = jnp.dot(field.reshape(-1, features), qkv_weight, preferred_element_type=jnp.float32).astype(jnp.bfloat16)
    qkv = qkv.reshape(scene_count, win_rows, WIN, win_cols, WIN, 3, head_count, head_dim)
    qkv = qkv.transpose(0, 1, 3, 2, 4, 5, 6, 7).reshape(scene_count, win_rows * win_cols, window_area, 3, head_count, head_dim)
    queries = qkv[:, :, :, 0]
    key_rows = qkv[:, :, :, 1]
    value_rows = qkv[:, :, :, 2]
    pairs = jnp.asarray(bias_pairs().T)
    bias_table = jnp.dot(position_bias, pairs, precision=lax.Precision.HIGHEST).reshape(head_count, window_area, window_area)
    row_labels = region(row_start, row_count, total_rows, shift_row)
    col_labels = region(0, col_count, col_count, shift_col)
    labels = row_labels[:, None] * 3 + col_labels[None, :]
    labels = labels.reshape(win_rows, WIN, win_cols, WIN).transpose(0, 2, 1, 3).reshape(win_rows * win_cols, window_area)
    region_mask = jnp.where(labels[:, :, None] == labels[:, None, :], 0.0, -100.0).astype(jnp.float32)
    scores = jnp.einsum('snqhd,snkhd->snhqk', queries, key_rows, preferred_element_type=jnp.float32)
    scores = scores * head_dim ** (-0.5) + bias_table[None, None] + region_mask[None, :, None]
    attn_probs = jax.nn.softmax(scores, axis=-1).astype(jnp.bfloat16)
    mixed_heads = jnp.einsum('snhqk,snkhd->snqhd', attn_probs, value_rows, preferred_element_type=jnp.float32).astype(jnp.bfloat16)
    mixed_heads = mixed_heads.reshape(scene_count, win_rows, win_cols, WIN, WIN, features)
    mixed_heads = mixed_heads.transpose(0, 1, 3, 2, 4, 5).reshape(-1, features)
    projected = jnp.dot(mixed_heads, out_weight, preferred_element_type=jnp.float32).astype(jnp.bfloat16)
    return projected.reshape(scene_count, row_count, col_count, features)

def route_table(choices, expert_total, capacity):
    onehot = (choices[..., None] == jnp.arange(expert_total, dtype=jnp.int32)).astype(jnp.int32)
    rank_in = jnp.cumsum(onehot, axis=-2) - onehot
    slot_index = lax.optimization_barrier(jnp.sum(rank_in * onehot, axis=-1))
    position = choices * capacity + slot_index
    return (position[..., None] == jnp.arange(expert_total * capacity, dtype=jnp.int32)).astype(jnp.bfloat16)

def fold_quads(field):
    return jnp.concatenate([field[:, 0::2, 0::2], field[:, 1::2, 0::2], field[:, 0::2, 1::2], field[:, 1::2, 1::2]], axis=-1)

def unfold_quads(grads):
    quarters = jnp.split(grads, 4, axis=-1)
    even_rows = jnp.stack([quarters[0], quarters[2]], 3)
    odd_rows = jnp.stack([quarters[1], quarters[3]], 3)
    rebuilt = jnp.stack([even_rows, odd_rows], 2)
    shape_now = rebuilt.shape
    return rebuilt.reshape(shape_now[0], shape_now[1] * 2, shape_now[3] * 2, shape_now[5])

def reference(tokens, qkv_weight, out_weight, position_bias, window_shift, expert_up, expert_down, expert_choice, combine_weight, reduce_weight, merged_grad):
    shift_row = window_shift[0]
    shift_col = window_shift[1]
    height = tokens.shape[1]
    tokens_f32 = tokens.astype(jnp.float32)
    normed = layer_norm(tokens_f32).astype(jnp.bfloat16)
    shifted = jnp.roll(normed, (-shift_row, -shift_col), axis=(1, 2))

    def attend(field):
        return window_attention(field, qkv_weight, out_weight, position_bias, 0, height, shift_row, shift_col)
    attended, attend_pull = jax.vjp(attend, shifted)
    restored = jnp.roll(attended, (shift_row, shift_col), axis=(1, 2))
    after_attn = (tokens_f32 + restored.astype(jnp.float32)).astype(jnp.bfloat16)
    second_norm = layer_norm(after_attn.astype(jnp.float32)).astype(jnp.bfloat16)
    blocks = SCENES * N_ROW
    routing = route_table(expert_choice.reshape(blocks, TOK_DEV), EXPERTS, CAP)
    slot_rows = jnp.einsum('btk,btc->bkc', routing, second_norm.reshape(blocks, TOK_DEV, C), preferred_element_type=jnp.float32).astype(jnp.bfloat16)
    expert_in = slot_rows.reshape(blocks, EXPERTS, CAP, C).transpose(1, 0, 2, 3).reshape(EXPERTS, blocks * CAP, C)
    hidden_share = HID // N_ROW

    def expert_forward(operands):
        inputs, up_proj, down_proj = operands
        slot_total = inputs.shape[0]
        pre_act = jnp.dot(inputs, up_proj, preferred_element_type=jnp.float32)
        activated = gelu_exact(pre_act).astype(jnp.bfloat16)
        partials = jnp.einsum('mgh,ghc->gmc', activated.reshape(slot_total, N_ROW, hidden_share), down_proj.reshape(N_ROW, hidden_share, C), preferred_element_type=jnp.float32).astype(jnp.bfloat16)
        return lax.optimization_barrier(jnp.sum(partials.astype(jnp.float32), axis=0)).astype(jnp.bfloat16)
    expert_out = lax.map(expert_forward, (expert_in, expert_up, expert_down))
    returned = expert_out.reshape(EXPERTS, blocks, CAP, C).transpose(1, 0, 2, 3).reshape(blocks, EXPERTS * CAP, C)
    expert_tok = jnp.einsum('btk,bkc->btc', routing, returned, preferred_element_type=jnp.float32)
    gate_scale = combine_weight.reshape(blocks, TOK_DEV, 1)
    block_out = (after_attn.astype(jnp.float32).reshape(blocks, TOK_DEV, C) + gate_scale * expert_tok).astype(jnp.bfloat16).reshape(tokens.shape)
    quartets = fold_quads(block_out)
    merge_norm = layer_norm(quartets.astype(jnp.float32)).astype(jnp.bfloat16)
    merged = jnp.dot(merge_norm.reshape(-1, 4 * C), reduce_weight, preferred_element_type=jnp.float32).astype(jnp.bfloat16)
    merged = merged.reshape(SCENES, height // 2, WIDTH // 2, 2 * C)
    column_group = 2 * C // N_SCENE
    d_merge_norm = jnp.zeros(quartets.shape, jnp.float32)
    for group_index in range(N_SCENE):
        grad_cols = merged_grad[..., group_index * column_group:(group_index + 1) * column_group]
        weight_cols = reduce_weight[:, group_index * column_group:(group_index + 1) * column_group]
        partial_grad = jnp.einsum('sabd,cd->sabc', grad_cols, weight_cols, preferred_element_type=jnp.float32).astype(jnp.bfloat16)
        d_merge_norm = d_merge_norm + partial_grad.astype(jnp.float32)
    d_block = unfold_quads(norm_grad(quartets.astype(jnp.float32), d_merge_norm))
    d_expert_tok = gate_scale * d_block.reshape(blocks, TOK_DEV, C)
    d_slot = jnp.einsum('btk,btc->bkc', routing.astype(jnp.float32), d_expert_tok, precision=lax.Precision.HIGHEST).astype(jnp.bfloat16)
    d_slot = d_slot.reshape(blocks, EXPERTS, CAP, C).transpose(1, 0, 2, 3).reshape(EXPERTS, blocks * CAP, C)

    def expert_backward(operands):
        inputs, slot_grads, up_proj, down_proj = operands
        slot_total = inputs.shape[0]
        pre_act = jnp.dot(inputs, up_proj, preferred_element_type=jnp.float32)
        activated = gelu_exact(pre_act).astype(jnp.bfloat16)
        d_full = jnp.dot(slot_grads, down_proj.T, preferred_element_type=jnp.float32)
        _, gelu_pull = jax.vjp(gelu_exact, pre_act)
        d_pre = gelu_pull(d_full)[0].astype(jnp.bfloat16)
        down_part = jnp.dot(activated.T, slot_grads, preferred_element_type=jnp.float32)
        up_part = jnp.dot(inputs.T, d_pre, preferred_element_type=jnp.float32)
        partials = jnp.einsum('mgh,gch->gmc', d_pre.reshape(slot_total, N_ROW, hidden_share), up_proj.reshape(C, N_ROW, hidden_share).transpose(1, 0, 2), preferred_element_type=jnp.float32).astype(jnp.bfloat16)
        d_inputs = lax.optimization_barrier(jnp.sum(partials.astype(jnp.float32), axis=0)).astype(jnp.bfloat16)
        return (up_part, down_part, d_inputs)
    up_grad, down_grad, d_slot_in = lax.map(expert_backward, (expert_in, d_slot, expert_up, expert_down))
    d_home = d_slot_in.reshape(EXPERTS, blocks, CAP, C).transpose(1, 0, 2, 3).reshape(blocks, EXPERTS * CAP, C)
    d_second = jnp.einsum('btk,bkc->btc', routing, d_home, preferred_element_type=jnp.float32).reshape(tokens.shape)
    d_after = d_block + norm_grad(after_attn.astype(jnp.float32), d_second)
    d_attended = jnp.roll(d_after.astype(jnp.bfloat16), (-shift_row, -shift_col), axis=(1, 2))
    d_shifted = attend_pull(d_attended)[0]
    d_normed = jnp.roll(d_shifted, (shift_row, shift_col), axis=(1, 2))
    tokens_grad = (d_after + norm_grad(tokens_f32, d_normed.astype(jnp.float32))).astype(jnp.bfloat16)
    return (merged, tokens_grad, up_grad, down_grad)
```

```python
import functools

import jax
import jax.numpy as jnp
import numpy as np
from jax import lax
from jax.experimental import pallas as pl
from jax.experimental.pallas import tpu as pltpu
from jax.sharding import PartitionSpec as P

MESH = pl.DeviceIdType.MESH
F32 = jnp.float32
BF = jnp.bfloat16
EPS = 1e-5
C = 1024
HC = C // 2
TOK = 196
TP = 208
HALO = 96
GRP = 256
NEG = -1e30
VMEM_BIG = 56 * 1024 * 1024
VM = pl.BlockSpec(memory_space=pltpu.VMEM)
SM = pl.BlockSpec(memory_space=pltpu.SMEM)
HB = pl.BlockSpec(memory_space=pl.ANY)


def sds(shape, dtype):
    return jax.ShapeDtypeStruct(shape, dtype)


def params(**kw):
    return pltpu.CompilerParams(vmem_limit_bytes=VMEM_BIG, **kw)


def cost(flops, nbytes):
    return pl.CostEstimate(flops=flops, bytes_accessed=nbytes, transcendentals=0)


def dot(a, b, da=1, db=0):
    return lax.dot_general(a, b, (((da,), (db,)), ((), ())), preferred_element_type=F32)


def iota(shape, dim):
    return lax.broadcasted_iota(jnp.int32, shape, dim)


def norm_parts(values):
    centre = jnp.mean(values, axis=-1, keepdims=True)
    centred = values - centre
    spread = jnp.mean(centred * centred, axis=-1, keepdims=True)
    scale = lax.rsqrt(spread + EPS)
    return centred * scale, scale


def norm_back(values, cot):
    unit, scale = norm_parts(values)
    mean_cot = jnp.mean(cot, axis=-1, keepdims=True)
    mean_dot = jnp.mean(cot * unit, axis=-1, keepdims=True)
    return scale * (cot - mean_cot - unit * mean_dot)


def split3(values):
    high = values.astype(BF)
    rest = values - high.astype(F32)
    mid = rest.astype(BF)
    low = (rest - mid.astype(F32)).astype(BF)
    return high, mid, low


def place_of(tok, r, c):
    rho = (tok * 4682) >> 16
    gam = tok - 14 * rho
    i = rho - r
    i = jnp.where(i < 0, i + 14, i)
    j = gam - c
    j = jnp.where(j < 0, j + 14, j)
    a = jnp.where(i >= 7, 1, 0)
    b = jnp.where(j >= 7, 1, 0)
    return i, j, a, b


def pos_of(tok, r, c):
    i, j, a, b = place_of(tok, r, c)
    return (i - 7 * a) * 7 + (j - 7 * b)


def group_of(tok, r, c, last):
    i, j, a, b = place_of(tok, r, c)
    la = jnp.where(i >= 7, jnp.where(i < 14 - r, 1, 2), 0) * last
    lb = jnp.where(j >= 7, jnp.where(j < 14 - c, 1, 2), 0)
    return a * 2 + b, la * 3 + lb


def pack_rows(low, high, blocks):
    return jnp.concatenate([low.reshape(blocks, 8, HC), high.reshape(blocks, 8, HC)], axis=1).astype(BF)


def unpack_rows(packed, blocks):
    wide = packed.astype(F32)
    low = wide[:, :8, :].reshape(blocks * 8, HC)
    high = wide[:, 8:, :].reshape(blocks * 8, HC)
    return low, high


def attn_fwd(scal, x, halo, wq, wk, wv, wo, bias, att, q_out, k_out, v_out, p_out, normed, mask, ecol, erow, acc):
    g = pl.program_id(0)

    @pl.when(g == 0)
    def _():
        r, c, last = scal[0], scal[1], scal[2]
        own = x[:HALO, :].astype(F32)
        top = jnp.where(iota((HALO, C), 0) < 14 * r, halo[...].astype(F32), own)
        normed[:HALO, :] = norm_parts(top)[0].astype(BF)
        normed[HALO:, :] = norm_parts(x[HALO:, :].astype(F32))[0].astype(BF)
        tq, tk = iota((TP, TP), 0), iota((TP, TP), 1)
        wq_, lq = group_of(tq, r, c, last)
        wk_, lk = group_of(tk, r, c, last)
        open_ = jnp.where(lq == lk, 0.0, -100.0)
        seen = jnp.where(wq_ == wk_, open_, NEG)
        mask[...] = jnp.where(tk < TOK, seen, NEG)
        row_pos = pos_of(iota((TP, 192), 0), r, c)
        erow[...] = jnp.where(row_pos == (iota((TP, 192), 1) & 63), 1.0, 0.0).astype(BF)
        col_pos = pos_of(iota((192, TP), 1), r, c)
        ecol[...] = jnp.where(col_pos == (iota((192, TP), 0) & 63), 1.0, 0.0).astype(BF)
        acc[...] = jnp.zeros_like(acc)

    n = normed[...]
    q = dot(n, wq[...]).astype(BF)
    k = dot(n, wk[...]).astype(BF)
    v = dot(n, wv[...]).astype(BF)
    q_out[...] = q
    k_out[...] = k
    v_out[...] = v
    wide = dot(jnp.concatenate(split3(bias[...].reshape(8 * 64, 64)), axis=1), ecol[...])
    w_hi, w_mid, w_lo = split3(wide)
    lane_head = iota((TP, GRP), 1) >> 5
    mixed = jnp.zeros((TP, GRP), F32)
    q32 = q.astype(F32)
    for h in range(8):
        mine = lane_head == h
        qm = jnp.where(mine, q32, 0.0).astype(BF)
        s = dot(qm, k, 1, 1) * (32.0 ** -0.5)
        part = slice(h * 64, h * 64 + 64)
        s = s + dot(erow[...], jnp.concatenate([w_hi[part], w_mid[part], w_lo[part]], axis=0)) + mask[...]
        e = jnp.exp(s - jnp.max(s, axis=-1, keepdims=True))
        p = (e / jnp.sum(e, axis=-1, keepdims=True)).astype(BF)
        p_out[h * TP:(h + 1) * TP, :] = p
        mixed = jnp.where(mine, dot(p, v), mixed)
    acc[...] += dot(mixed.astype(BF), wo[...])

    @pl.when(g == 3)
    def _():
        att[...] = acc[...].astype(BF)


def attn_bwd(scal, own, halo, wq, wk, wv, wo, q_in, k_in, v_in, p_in, d_shift, d_att, acc):
    g = pl.program_id(0)

    @pl.when(g == 0)
    def _():
        top = jnp.where(iota((HALO, C), 0) < 14 * scal[0], halo[...].astype(F32), own[:HALO, :].astype(F32))
        d_att[:HALO, :] = top.astype(BF)
        d_att[HALO:, :] = own[HALO:, :]
        acc[...] = jnp.zeros_like(acc)

    q, k, v = q_in[...], k_in[...], v_in[...]
    d_mixed = dot(d_att[...], wo[...], 1, 1).astype(BF).astype(F32)
    q32 = q.astype(F32)
    lane_head = iota((TP, GRP), 1) >> 5
    dq = jnp.zeros((TP, GRP), F32)
    dk = jnp.zeros((TP, GRP), F32)
    dv = jnp.zeros((TP, GRP), F32)
    for h in range(8):
        mine = lane_head == h
        dm = jnp.where(mine, d_mixed, 0.0).astype(BF)
        qm = jnp.where(mine, q32, 0.0).astype(BF)
        p = p_in[h * TP:(h + 1) * TP, :]
        p32 = p.astype(F32)
        dp = dot(dm, v, 1, 1).astype(BF).astype(F32)
        ds = p32 * (dp - jnp.sum(dp * p32, axis=-1, keepdims=True)) * (32.0 ** -0.5)
        ds = ds.astype(BF)
        dq = jnp.where(mine, dot(ds, k), dq)
        dk = dk + dot(ds, qm, 0, 0)
        dv = dv + dot(p, dm, 0, 0)
    acc[...] += dot(dq.astype(BF), wq[...], 1, 1) + dot(dk.astype(BF), wk[...], 1, 1) + dot(dv.astype(BF), wv[...], 1, 1)

    @pl.when(g == 3)
    def _():
        d_shift[...] = acc[...].astype(BF)


def route(scal, x, att, halo, choice_col, choice_row, after_out, slots, table_out):
    r = scal[0]
    top = jnp.where(iota((HALO, C), 0) < 14 * r, halo[...].astype(F32), att[:HALO, :].astype(F32))
    after_out[:HALO, :] = (x[:HALO, :].astype(F32) + top).astype(BF)
    after_out[HALO:, :] = (x[HALO:, :].astype(F32) + att[HALO:, :].astype(F32)).astype(BF)
    after = after_out[...].astype(F32)
    n2 = norm_parts(after)[0].astype(BF)
    col = choice_col[...]
    same = jnp.where(col == choice_row[...], 1.0, 0.0)
    same = jnp.where(iota((TP, TP), 1) < iota((TP, TP), 0), same, 0.0)
    rank = jnp.sum(same, axis=1, keepdims=True).astype(jnp.int32)
    table = jnp.where(col * 8 + rank == iota((TP, 256), 1), 1.0, 0.0).astype(BF)
    table_out[...] = table
    slots[...] = pack_rows(dot(table, n2[:, :HC], 0, 0), dot(table, n2[:, HC:], 0, 0), 32)


def quad_table():
    row = iota((256, TP), 0)
    tok = iota((256, TP), 1)
    q = row >> 6
    n = row & 63
    a = (n * 9363) >> 16
    b = n - 7 * a
    want = (2 * a + (q & 1)) * 14 + 2 * b + (q >> 1)
    hit = jnp.where(want == tok, 1.0, 0.0)
    return jnp.where(n < 49, hit, 0.0).astype(BF)


def gathered(ret, table):
    low, high = unpack_rows(ret[0].astype(F32) + ret[1].astype(F32), 32)
    return jnp.concatenate([dot(table, low.astype(BF)), dot(table, high.astype(BF))], axis=1)


def merge_mid(after, ret, table_in, gate_in, parts, mn_out, d_block_out, slots, spread):
    table = table_in[...]
    gate = gate_in[...]
    block = (after[...].astype(F32) + gate * gathered(ret, table)).astype(BF)
    perm = quad_table()
    quads = dot(perm, block)
    vals = [quads[64 * q:64 * q + 49, :] for q in range(4)]
    inv = 1.0 / (4 * C)
    centre = sum(jnp.sum(v, axis=-1, keepdims=True) for v in vals) * inv
    cent = [v - centre for v in vals]
    var = sum(jnp.sum(v * v, axis=-1, keepdims=True) for v in cent) * inv
    scale = lax.rsqrt(var + EPS)
    unit = [v * scale for v in cent]
    for q in range(4):
        mn_out[:, q * C:(q + 1) * C] = unit[q].astype(BF)
    cots = []
    for q in range(4):
        tot = parts[0, :, q * C:(q + 1) * C].astype(F32)
        for s in range(1, 8):
            tot = tot + parts[s, :, q * C:(q + 1) * C].astype(F32)
        cots.append(tot)
    mean_cot = sum(jnp.sum(v, axis=-1, keepdims=True) for v in cots) * inv
    mean_dot = sum(jnp.sum(v * u, axis=-1, keepdims=True) for v, u in zip(cots, unit)) * inv
    spread[...] = jnp.zeros_like(spread)
    for q in range(4):
        spread[64 * q:64 * q + 49, :] = scale * (cots[q] - mean_cot - unit[q] * mean_dot)
    high, mid, low = split3(spread[...])
    d_block = dot(perm, high, 0, 0) + dot(perm, mid, 0, 0) + dot(perm, low, 0, 0)
    d_block_out[...] = d_block
    scaled = (gate * d_block).astype(BF)
    slots[...] = pack_rows(dot(table, scaled[:, :HC], 0, 0), dot(table, scaled[:, HC:], 0, 0), 32)


def after_back(after, ret, table, d_block, d_after_out, d_att_out):
    d_second = gathered(ret, table[...])
    d_after = d_block[...] + norm_back(after[...].astype(F32), d_second)
    d_after_out[...] = d_after
    d_att_out[...] = d_after.astype(BF)


def finish(scal, x, d_after, own, halo, out):
    r = scal[0]
    top = jnp.where(iota((HALO, C), 0) < 14 * r, halo[...].astype(F32), own[:HALO, :].astype(F32))
    out[:HALO, :] = (d_after[:HALO, :] + norm_back(x[:HALO, :].astype(F32), top)).astype(BF)
    out[HALO:, :] = (
        d_after[HALO:, :] + norm_back(x[HALO:, :].astype(F32), own[HALO:, :].astype(F32))
    ).astype(BF)


def expert_fwd(slots, *refs):
    ups, downs = refs[:4], refs[4:8]
    flat, act_out, slope_out, packed = refs[8:]
    low, high = unpack_rows(slots[...], 32)
    rows = jnp.concatenate([low, high], axis=1).astype(BF)
    flat[...] = rows
    total = jnp.zeros((256, C), F32)
    for k in range(4):
        pre = dot(rows, ups[k][...])
        cdf = 0.5 * (1.0 + lax.erf(pre * np.float32(2.0 ** -0.5)))
        act = (pre * cdf).astype(BF)
        slope = cdf + pre * jnp.exp(-0.5 * pre * pre) * np.float32((2.0 * np.pi) ** -0.5)
        act_out[:, k * 256:(k + 1) * 256] = act
        slope_out[:, k * 256:(k + 1) * 256] = slope.astype(BF)
        total = total + dot(act, downs[k][...])
    packed[...] = pack_rows(total[:, :HC], total[:, HC:], 32)


def expert_bwd(slots, slope, *refs):
    ups, downs = refs[:4], refs[4:8]
    flat, d_pre_out, packed = refs[8:]
    low, high = unpack_rows(slots[...], 32)
    rows = jnp.concatenate([low, high], axis=1).astype(BF)
    flat[...] = rows
    total = jnp.zeros((256, C), F32)
    for k in range(4):
        cols = slice(k * 256, (k + 1) * 256)
        d_pre = (slope[:, cols].astype(F32) * dot(rows, downs[k][...], 1, 1)).astype(BF)
        d_pre_out[:, cols] = d_pre
        total = total + dot(d_pre, ups[k][...], 1, 1)
    packed[...] = pack_rows(total[:, :HC], total[:, HC:], 32)


def expert_grads(act, d_rows, rows, d_pre, down_out, up_out):
    down_out[0] = dot(act[...], d_rows[...], 0, 0).astype(BF)
    up_out[0] = dot(rows[...], d_pre[...], 0, 0).astype(BF)


def place_grads(turn, *refs):
    ins, (up_out, down_out) = refs[:8], refs[8:]
    for k in range(4):
        @pl.when(pl.program_id(0) == k)
        def _():
            up_out[0] = ins[k][...].astype(F32)
            down_out[0] = ins[4 + k][...].astype(F32)


def coords():
    s = lax.axis_index("scene")
    row = lax.axis_index("row")
    z, m = row // 4, row % 4
    return s, z, m // 2, m % 2


def at(s, z, y, c):
    return (s, z * 4 + y * 2 + c)


def greet(s, z, y, c):
    barrier = pltpu.get_barrier_semaphore()
    mine = s * 4 + z

    def hail(k, carry):
        peer = (mine + k) % 32
        pl.semaphore_signal(barrier, inc=1, device_id=at(peer // 4, peer % 4, y, c), device_id_type=MESH)
        pl.semaphore_signal(barrier, inc=1, device_id=at(peer // 4, peer % 4, 1 - y, c), device_id_type=MESH)
        return carry

    lax.fori_loop(1, 32, hail, 0)
    pl.semaphore_signal(barrier, inc=1, device_id=at(s, z, 1 - y, c), device_id_type=MESH)
    pl.semaphore_signal(barrier, inc=1, device_id=at(s, z, y, 1 - c), device_id_type=MESH)
    pl.semaphore_wait(barrier, 64)


def dispatch_kernel(src, out, send_sem, recv_sem, pair_send, pair_recv):
    s, z, y, c = coords()
    mine = s * 4 + z
    greet(s, z, y, c)

    def push(k, carry):
        peer = (mine + k) % 32
        for yy in range(2):
            pltpu.make_async_remote_copy(
                src_ref=src.at[peer], dst_ref=out.at[y * 2 + c, mine], send_sem=send_sem, recv_sem=recv_sem.at[y],
                device_id=at(peer // 4, peer % 4, (y + yy) % 2, c), device_id_type=MESH,
            ).start()
        return carry

    pltpu.make_async_copy(src.at[mine], out.at[y * 2 + c, mine], recv_sem.at[y]).start()
    pltpu.make_async_remote_copy(
        src_ref=src.at[mine], dst_ref=out.at[y * 2 + c, mine], send_sem=send_sem, recv_sem=recv_sem.at[y],
        device_id=at(s, z, 1 - y, c), device_id_type=MESH,
    ).start()
    lax.fori_loop(1, 32, push, 0)
    pairs = []
    for yy in range(2):
        block = out.at[yy * 2 + c]
        pltpu.make_async_copy(block, block, recv_sem.at[yy]).wait()
        copy = pltpu.make_async_remote_copy(
            src_ref=block, dst_ref=block, send_sem=pair_send.at[yy], recv_sem=pair_recv.at[yy],
            device_id=at(s, z, y, 1 - c), device_id_type=MESH,
        )
        copy.start()
        pairs.append(copy)
    for copy in pairs:
        copy.wait()
    pltpu.make_async_copy(src, src, send_sem).wait()
    pltpu.make_async_copy(src.at[pl.ds(0, 31)], src.at[pl.ds(0, 31)], send_sem).wait()


def dispatch(slots):
    return pl.pallas_call(
        dispatch_kernel,
        out_shape=sds((4, 32, 16, HC), BF),
        in_specs=[VM],
        out_specs=VM,
        scratch_shapes=[
            pltpu.SemaphoreType.DMA,
            pltpu.SemaphoreType.DMA((2,)),
            pltpu.SemaphoreType.DMA((2,)),
            pltpu.SemaphoreType.DMA((2,)),
        ],
        compiler_params=params(collective_id=0, has_side_effects=True),
        cost_estimate=cost(0, 40 << 20),
        name="dispatch",
    )(slots)


def combine_kernel(part, out, other, total, send_sem, recv_sem, pair_send, pair_recv):
    s, z, y, c = coords()
    mine = s * 4 + z
    greet(s, z, y, c)
    pairs = []
    for yy in range(2):
        copy = pltpu.make_async_remote_copy(
            src_ref=part.at[yy * 2 + (1 - c)], dst_ref=other.at[yy], send_sem=pair_send.at[yy],
            recv_sem=pair_recv.at[yy], device_id=at(s, z, y, 1 - c), device_id_type=MESH,
        )
        copy.start()
        pairs.append(copy)

    def add(yy, peer):
        summed = part[yy * 2 + c, peer].astype(F32) + other[yy, peer].astype(F32)
        total[yy, peer] = summed.astype(BF)

    def ship(yy, peer):
        pltpu.make_async_remote_copy(
            src_ref=total.at[yy, peer], dst_ref=out.at[y, mine], send_sem=send_sem, recv_sem=recv_sem,
            device_id=at(peer // 4, peer % 4, yy, c), device_id_type=MESH,
        ).start()

    for copy in pairs:
        copy.wait_recv()

    def push(k, carry):
        peer = (mine + k) % 32
        add(1 - y, peer)
        ship(1 - y, peer)
        add(y, peer)
        ship(y, peer)
        return carry

    lax.fori_loop(1, 32, push, 0)
    add(1 - y, mine)
    ship(1 - y, mine)
    add(y, mine)
    pltpu.make_async_copy(total.at[y, mine], out.at[y, mine], recv_sem).start()
    for copy in pairs:
        copy.wait_send()
    pltpu.make_async_copy(total, total, recv_sem).wait()
    pltpu.make_async_copy(total.at[0], total.at[0], send_sem).wait()
    pltpu.make_async_copy(total.at[0, pl.ds(0, 31)], total.at[0, pl.ds(0, 31)], send_sem).wait()


def combine(part):
    return pl.pallas_call(
        combine_kernel,
        out_shape=sds((2, 32, 16, HC), BF),
        in_specs=[VM],
        out_specs=VM,
        scratch_shapes=[
            pltpu.VMEM((2, 32, 16, HC), BF),
            pltpu.VMEM((2, 32, 16, HC), BF),
            pltpu.SemaphoreType.DMA,
            pltpu.SemaphoreType.DMA,
            pltpu.SemaphoreType.DMA((2,)),
            pltpu.SemaphoreType.DMA((2,)),
        ],
        compiler_params=params(collective_id=1, has_side_effects=True),
        cost_estimate=cost(0, 40 << 20),
        name="combine",
    )(part)


def row_shift(value, steps):
    pairs = [(source, (source + steps) % 16) for source in range(16)]
    return lax.ppermute(value, "row", pairs)


def z_shift(value, steps):
    pairs = [(z * 4 + m, ((z + steps) % 4) * 4 + m) for z in range(4) for m in range(4)]
    return lax.ppermute(value, "row", pairs)


def bias_pairs():
    spot = np.arange(49)
    py, px = spot // 7, spot % 7
    relative = (py[:, None] - py[None, :] + 6) * 13 + (px[:, None] - px[None, :] + 6)
    table = np.zeros((169, 64, 64), np.float32)
    a, b = np.meshgrid(spot, spot, indexing="ij")
    table[relative.reshape(-1), a.reshape(-1), b.reshape(-1)] = 1.0
    return table.reshape(169, 4096)


def whole(kernel, out_shape, args, specs, scratch=(), flops=0, nbytes=0):
    return pl.pallas_call(
        kernel,
        out_shape=out_shape,
        in_specs=specs,
        out_specs=[VM] * len(out_shape),
        scratch_shapes=list(scratch),
        compiler_params=params(),
        cost_estimate=cost(flops, nbytes),
        name=kernel.__name__,
    )(*args)


def local(
    tokens,
    qkv_weight,
    out_weight,
    position_bias,
    window_shift,
    expert_up,
    expert_down,
    expert_choice,
    combine_weight,
    reduce_weight,
    merged_grad,
):
    row = lax.axis_index("row")
    z = row // 4
    x = jnp.pad(tokens.reshape(TOK, C), ((0, TP - TOK), (0, 0)))
    scal = jnp.stack([window_shift[0], window_shift[1], (row == 15).astype(jnp.int32), z.astype(jnp.int32)])
    choice = jnp.pad(expert_choice.reshape(TOK), (0, TP - TOK), constant_values=-1000)
    gate = jnp.pad(combine_weight.reshape(TOK, 1), ((0, TP - TOK), (0, 0)))

    below = row_shift(x[:HALO], -1)
    ups, downs = [], []
    for k in range(4):
        expert = (z + k) % 4
        up_k = lax.dynamic_index_in_dim(expert_up, expert, 0, keepdims=False)
        down_k = lax.dynamic_index_in_dim(expert_down, expert, 0, keepdims=False)
        ups.append(z_shift(up_k, k) if k else up_k)
        downs.append(z_shift(down_k, k) if k else down_k)

    d_parts = jnp.einsum(
        "nkd,cd->nkc", merged_grad.reshape(8, 49, -1), reduce_weight, preferred_element_type=F32
    ).astype(BF)
    d_parts = lax.all_to_all(d_parts, "scene", split_axis=0, concat_axis=0, tiled=True)

    bias = jnp.dot(position_bias, jnp.asarray(bias_pairs()), precision=lax.Precision.HIGHEST).reshape(32, 64, 64)

    full = lambda shape: pl.BlockSpec(shape, lambda g: (0,) * len(shape))
    w_spec = lambda which: pl.BlockSpec((C, GRP), lambda g: (0, 4 * which + g))
    wo_spec = pl.BlockSpec((GRP, C), lambda g: (g, 0))
    head_spec = pl.BlockSpec((TP, GRP), lambda g: (0, g))
    prob_spec = pl.BlockSpec((8 * TP, TP), lambda g: (g, 0))
    att, q, k, v, probs = pl.pallas_call(
        attn_fwd,
        grid=(4,),
        out_shape=[sds((TP, C), BF)] * 4 + [sds((32 * TP, TP), BF)],
        in_specs=[SM, full((TP, C)), full((HALO, C)), w_spec(0), w_spec(1), w_spec(2), wo_spec,
                  pl.BlockSpec((8, 64, 64), lambda g: (g, 0, 0))],
        out_specs=[full((TP, C)), head_spec, head_spec, head_spec, prob_spec],
        scratch_shapes=[pltpu.VMEM((TP, C), BF), pltpu.VMEM((TP, TP), F32), pltpu.VMEM((192, TP), BF),
                        pltpu.VMEM((TP, 192), BF), pltpu.VMEM((TP, C), F32)],
        compiler_params=params(),
        cost_estimate=cost(6 << 30, 14 << 20),
        name="attn_fwd",
    )(scal, x, below, qkv_weight, qkv_weight, qkv_weight, out_weight, bias)

    above = row_shift(att[:HALO], 1)
    after, slots, table = whole(
        route,
        [sds((TP, C), BF), sds((32, 16, HC), BF), sds((TP, 256), BF)],
        (scal, x, att, above, choice.reshape(TP, 1), choice.reshape(1, TP)),
        [SM] + [VM] * 5, flops=1 << 30, nbytes=4 << 20,
    )
    slot_in = dispatch(slots).reshape(128, 16, HC)

    slot_spec = pl.BlockSpec((32, 16, HC), lambda g: (g, 0, 0))
    row_spec = pl.BlockSpec((256, C), lambda g: (g, 0))
    weight_specs = [full((C, 256))] * 4 + [full((256, C))] * 4
    flat_in, act, slope, part = pl.pallas_call(
        expert_fwd,
        grid=(4,),
        out_shape=[sds((C, C), BF)] * 3 + [sds((128, 16, HC), BF)],
        in_specs=[slot_spec] + weight_specs,
        out_specs=[row_spec] * 3 + [slot_spec],
        compiler_params=params(),
        cost_estimate=cost(4 << 30, 14 << 20),
        name="expert_fwd",
    )(slot_in, *ups, *downs)
    ret = combine(part.reshape(4, 32, 16, HC))

    merge_norm, d_block, d_slots = whole(
        merge_mid,
        [sds((49, 4 * C), BF), sds((TP, C), F32), sds((32, 16, HC), BF)],
        (after, ret, table, gate, d_parts),
        [VM] * 5, scratch=[pltpu.VMEM((256, C), F32)], flops=2 << 30, nbytes=8 << 20,
    )
    d_slot_in = dispatch(d_slots).reshape(128, 16, HC)
    flat_d, d_pre, d_part = pl.pallas_call(
        expert_bwd,
        grid=(4,),
        out_shape=[sds((C, C), BF)] * 2 + [sds((128, 16, HC), BF)],
        in_specs=[slot_spec, row_spec] + weight_specs,
        out_specs=[row_spec] * 2 + [slot_spec],
        compiler_params=params(),
        cost_estimate=cost(4 << 30, 14 << 20),
        name="expert_bwd",
    )(d_slot_in, slope, *ups, *downs)
    d_ret = combine(d_part.reshape(4, 32, 16, HC))

    col_spec = pl.BlockSpec((C, 256), lambda g: (0, g))
    down_parts, up_parts = pl.pallas_call(
        expert_grads,
        grid=(4,),
        out_shape=[sds((4, 256, C), BF), sds((4, C, 256), BF)],
        in_specs=[col_spec, full((C, C)), full((C, C)), col_spec],
        out_specs=[pl.BlockSpec((1, 256, C), lambda g: (g, 0, 0)), pl.BlockSpec((1, C, 256), lambda g: (g, 0, 0))],
        compiler_params=params(),
        cost_estimate=cost(4 << 30, 14 << 20),
        name="expert_grads",
    )(act, flat_d, flat_in, d_pre)
    up_back = [up_parts[0]] + [z_shift(up_parts[k], -k) for k in range(1, 4)]
    down_back = [down_parts[0]] + [z_shift(down_parts[k], -k) for k in range(1, 4)]

    d_after, d_att = whole(
        after_back, [sds((TP, C), F32), sds((TP, C), BF)], (after, d_ret, table, d_block), [VM] * 4,
        flops=1 << 30, nbytes=4 << 20,
    )
    d_below = row_shift(d_att[:HALO], -1)
    d_shift = pl.pallas_call(
        attn_bwd,
        grid=(4,),
        out_shape=sds((TP, C), BF),
        in_specs=[SM, full((TP, C)), full((HALO, C)), w_spec(0), w_spec(1), w_spec(2), wo_spec,
                  head_spec, head_spec, head_spec, prob_spec],
        out_specs=full((TP, C)),
        scratch_shapes=[pltpu.VMEM((TP, C), BF), pltpu.VMEM((TP, C), F32)],
        compiler_params=params(),
        cost_estimate=cost(8 << 30, 14 << 20),
        name="attn_bwd",
    )(scal, d_att, d_below, qkv_weight, qkv_weight, qkv_weight, out_weight, q, k, v, probs)
    d_above = row_shift(d_shift[:HALO], 1)
    (grad,) = whole(
        finish, [sds((TP, C), BF)], (scal, x, d_after, d_shift, d_above), [SM] + [VM] * 4,
        flops=1 << 28, nbytes=3 << 20,
    )
    tokens_grad = grad[:TOK].reshape(tokens.shape)

    merged = jnp.einsum(
        "nkc,cd->nkd", lax.all_gather(merge_norm[None], "scene", axis=0, tiled=True), reduce_weight,
        preferred_element_type=F32,
    ).astype(BF).reshape(merged_grad.shape)

    up_grad, down_grad = pl.pallas_call(
        place_grads,
        grid_spec=pltpu.PrefetchScalarGridSpec(
            num_scalar_prefetch=1,
            grid=(4,),
            in_specs=[pl.BlockSpec((C, 256), lambda g, t: (0, 0))] * 4 + [pl.BlockSpec((256, C), lambda g, t: (0, 0))] * 4,
            out_specs=[pl.BlockSpec((1, C, 256), lambda g, t: ((t[0] + g) % 4, 0, 0)),
                       pl.BlockSpec((1, 256, C), lambda g, t: ((t[0] + g) % 4, 0, 0))],
        ),
        out_shape=[sds((4, C, 256), F32), sds((4, 256, C), F32)],
        compiler_params=params(),
        cost_estimate=cost(0, 12 << 20),
        name="place_grads",
    )(z.reshape(1).astype(jnp.int32), *up_back, *down_back)
    return (merged, tokens_grad, up_grad, down_grad)


def solution(mesh):
    placed = (
        P("scene", "row", None, None),
        P(),
        P(),
        P(),
        P(),
        P("scene", None, "row"),
        P("scene", "row", None),
        P("scene", "row", None, None),
        P("scene", "row", None),
        P(None, "scene"),
        P(None, "row", None, "scene"),
    )
    return jax.shard_map(
        local,
        mesh=mesh,
        in_specs=placed,
        out_specs=(
            P(None, "row", None, "scene"),
            P("scene", "row", None, None),
            P("scene", None, "row"),
            P("scene", "row", None),
        ),
        check_vma=False,
    )
```

```python
import functools

import jax
import jax.numpy as jnp
import numpy as np
from jax import lax
from jax.experimental import pallas as pl
from jax.experimental.pallas import tpu as pltpu
from jax.sharding import PartitionSpec as P

MESH = pl.DeviceIdType.MESH
F32 = jnp.float32
BF = jnp.bfloat16
EPS = 1e-5
C = 1024
HC = C // 2
TOK = 196
TP = 208
HALO = 96
GRP = 256
NEG = -1e30
VMEM_BIG = 56 * 1024 * 1024
VM = pl.BlockSpec(memory_space=pltpu.VMEM)
SM = pl.BlockSpec(memory_space=pltpu.SMEM)
HB = pl.BlockSpec(memory_space=pl.ANY)


def sds(shape, dtype):
    return jax.ShapeDtypeStruct(shape, dtype)


def params(**kw):
    return pltpu.CompilerParams(vmem_limit_bytes=VMEM_BIG, **kw)


def cost(flops, nbytes):
    return pl.CostEstimate(flops=flops, bytes_accessed=nbytes, transcendentals=0)


def dot(a, b, da=1, db=0):
    return lax.dot_general(a, b, (((da,), (db,)), ((), ())), preferred_element_type=F32)


def iota(shape, dim):
    return lax.broadcasted_iota(jnp.int32, shape, dim)


def norm_parts(values):
    centre = jnp.mean(values, axis=-1, keepdims=True)
    centred = values - centre
    spread = jnp.mean(centred * centred, axis=-1, keepdims=True)
    scale = lax.rsqrt(spread + EPS)
    return centred * scale, scale


def norm_back(values, cot):
    unit, scale = norm_parts(values)
    mean_cot = jnp.mean(cot, axis=-1, keepdims=True)
    mean_dot = jnp.mean(cot * unit, axis=-1, keepdims=True)
    return scale * (cot - mean_cot - unit * mean_dot)


def split3(values):
    high = values.astype(BF)
    rest = values - high.astype(F32)
    mid = rest.astype(BF)
    low = (rest - mid.astype(F32)).astype(BF)
    return high, mid, low


def place_of(tok, r, c):
    rho = (tok * 4682) >> 16
    gam = tok - 14 * rho
    i = rho - r
    i = jnp.where(i < 0, i + 14, i)
    j = gam - c
    j = jnp.where(j < 0, j + 14, j)
    a = jnp.where(i >= 7, 1, 0)
    b = jnp.where(j >= 7, 1, 0)
    return i, j, a, b


def pos_of(tok, r, c):
    i, j, a, b = place_of(tok, r, c)
    return (i - 7 * a) * 7 + (j - 7 * b)


def group_of(tok, r, c, last):
    i, j, a, b = place_of(tok, r, c)
    la = jnp.where(i >= 7, jnp.where(i < 14 - r, 1, 2), 0) * last
    lb = jnp.where(j >= 7, jnp.where(j < 14 - c, 1, 2), 0)
    return a * 2 + b, la * 3 + lb


def pack_rows(low, high, blocks):
    return jnp.concatenate([low.reshape(blocks, 8, HC), high.reshape(blocks, 8, HC)], axis=1).astype(BF)


def unpack_rows(packed, blocks):
    wide = packed.astype(F32)
    low = wide[:, :8, :].reshape(blocks * 8, HC)
    high = wide[:, 8:, :].reshape(blocks * 8, HC)
    return low, high


def attn_masks(r, c, last, mask, ecol, erow):
    tq, tk = iota((TP, TP), 0), iota((TP, TP), 1)
    wq_, lq = group_of(tq, r, c, last)
    wk_, lk = group_of(tk, r, c, last)
    seen = jnp.where(wq_ == wk_, jnp.where(lq == lk, 0.0, -100.0), NEG)
    mask[...] = jnp.where(tk < TOK, seen, NEG)
    row_pos = pos_of(iota((TP, 192), 0), r, c)
    erow[...] = jnp.where(row_pos == (iota((TP, 192), 1) & 63), 1.0, 0.0).astype(BF)
    col_pos = pos_of(iota((192, TP), 1), r, c)
    ecol[...] = jnp.where(col_pos == (iota((192, TP), 0) & 63), 1.0, 0.0).astype(BF)


def cols(start):
    return pl.ds(pl.multiple_of(start, GRP), GRP)


def attn_group(g, normed, wqkv, wo, bias, mask, ecol, erow, qkv, probs, acc):
    n = normed[...]
    q = dot(n, wqkv[:, cols(g * GRP)]).astype(BF)
    k = dot(n, wqkv[:, cols(C + g * GRP)]).astype(BF)
    v = dot(n, wqkv[:, cols(2 * C + g * GRP)]).astype(BF)
    qkv[0, g] = q
    qkv[1, g] = k
    qkv[2, g] = v
    wide = dot(jnp.concatenate(split3(bias[pl.ds(g * 8, 8)].reshape(8 * 64, 64)), axis=1), ecol[...])
    w_hi, w_mid, w_lo = split3(wide)
    lane_head = iota((TP, GRP), 1) >> 5
    mixed = jnp.zeros((TP, GRP), F32)
    q32 = q.astype(F32)
    for h in range(8):
        mine = lane_head == h
        qm = jnp.where(mine, q32, 0.0).astype(BF)
        s = dot(qm, k, 1, 1) * (32.0 ** -0.5)
        part = slice(h * 64, h * 64 + 64)
        s = s + dot(erow[...], jnp.concatenate([w_hi[part], w_mid[part], w_lo[part]], axis=0)) + mask[...]
        e = jnp.exp(s - jnp.max(s, axis=-1, keepdims=True))
        p = (e / jnp.sum(e, axis=-1, keepdims=True)).astype(BF)
        probs[pl.ds(pl.multiple_of((g * 8 + h) * TP, 16), TP), :] = p
        mixed = jnp.where(mine, dot(p, v), mixed)
    acc[...] += dot(mixed.astype(BF), wo[pl.ds(pl.multiple_of(g * GRP, GRP), GRP), :])


def attn_bwd(scal, own, halo, wq, wk, wv, wo, q_in, k_in, v_in, p_in, d_shift, d_att, acc):
    g = pl.program_id(0)

    @pl.when(g == 0)
    def _():
        top = jnp.where(iota((HALO, C), 0) < 14 * scal[0], halo[...].astype(F32), own[:HALO, :].astype(F32))
        d_att[:HALO, :] = top.astype(BF)
        d_att[HALO:, :] = own[HALO:, :]
        acc[...] = jnp.zeros_like(acc)

    q, k, v = q_in[0, 0], k_in[0, 0], v_in[0, 0]
    d_mixed = dot(d_att[...], wo[...], 1, 1).astype(BF).astype(F32)
    q32 = q.astype(F32)
    lane_head = iota((TP, GRP), 1) >> 5
    dq = jnp.zeros((TP, GRP), F32)
    dk = jnp.zeros((TP, GRP), F32)
    dv = jnp.zeros((TP, GRP), F32)
    for h in range(8):
        mine = lane_head == h
        dm = jnp.where(mine, d_mixed, 0.0).astype(BF)
        qm = jnp.where(mine, q32, 0.0).astype(BF)
        p = p_in[h * TP:(h + 1) * TP, :]
        p32 = p.astype(F32)
        dp = dot(dm, v, 1, 1).astype(BF).astype(F32)
        ds = p32 * (dp - jnp.sum(dp * p32, axis=-1, keepdims=True)) * (32.0 ** -0.5)
        ds = ds.astype(BF)
        dq = jnp.where(mine, dot(ds, k), dq)
        dk = dk + dot(ds, qm, 0, 0)
        dv = dv + dot(p, dm, 0, 0)
    acc[...] += dot(dq.astype(BF), wq[...], 1, 1) + dot(dk.astype(BF), wk[...], 1, 1) + dot(dv.astype(BF), wv[...], 1, 1)

    @pl.when(g == 3)
    def _():
        d_shift[...] = acc[...].astype(BF)


def route(r, x, att, halo, choice_col, choice_row, after_out, slots, table_out):
    top = jnp.where(iota((HALO, C), 0) < 14 * r, halo[...].astype(F32), att[:HALO, :].astype(F32))
    after_out[:HALO, :] = (x[:HALO, :].astype(F32) + top).astype(BF)
    after_out[HALO:, :] = (x[HALO:, :].astype(F32) + att[HALO:, :].astype(F32)).astype(BF)
    after = after_out[...].astype(F32)
    n2 = norm_parts(after)[0].astype(BF)
    col = choice_col[...]
    same = jnp.where(col == choice_row[...], 1.0, 0.0)
    same = jnp.where(iota((TP, TP), 1) < iota((TP, TP), 0), same, 0.0)
    rank = jnp.sum(same, axis=1, keepdims=True).astype(jnp.int32)
    table = jnp.where(col * 8 + rank == iota((TP, 256), 1), 1.0, 0.0).astype(BF)
    table_out[...] = table
    slots[...] = pack_rows(dot(table, n2[:, :HC], 0, 0), dot(table, n2[:, HC:], 0, 0), 32)


def quad_table():
    row = iota((256, TP), 0)
    tok = iota((256, TP), 1)
    q = row >> 6
    n = row & 63
    a = (n * 9363) >> 16
    b = n - 7 * a
    want = (2 * a + (q & 1)) * 14 + 2 * b + (q >> 1)
    hit = jnp.where(want == tok, 1.0, 0.0)
    return jnp.where(n < 49, hit, 0.0).astype(BF)


def gathered(ret, table):
    low, high = unpack_rows(ret[0].astype(F32) + ret[1].astype(F32), 32)
    return jnp.concatenate([dot(table, low.astype(BF)), dot(table, high.astype(BF))], axis=1)


def merge_mid(after, ret, table_in, gate_in, parts, tail, mn_out, d_block_out, slots, spread):
    table = table_in[...]
    gate = gate_in[...]
    block = (after[...].astype(F32) + gate * gathered(ret, table)).astype(BF)
    perm = quad_table()
    quads = dot(perm, block)
    vals = [quads[64 * q:64 * q + 49, :] for q in range(4)]
    inv = 1.0 / (4 * C)
    centre = sum(jnp.sum(v, axis=-1, keepdims=True) for v in vals) * inv
    cent = [v - centre for v in vals]
    var = sum(jnp.sum(v * v, axis=-1, keepdims=True) for v in cent) * inv
    scale = lax.rsqrt(var + EPS)
    unit = [v * scale for v in cent]
    for q in range(4):
        mn_out[:, q * C:(q + 1) * C] = unit[q].astype(BF)
    tails = jnp.sum(tail[...].astype(F32), axis=0)
    cots = []
    for q in range(4):
        tot = parts[0, :, q * C:(q + 1) * C].astype(F32)
        for s in range(1, 8):
            tot = tot + parts[s, :, q * C:(q + 1) * C].astype(F32)
        last = jnp.concatenate([tails[4 * q + i:4 * q + i + 1, :] for i in range(4)], axis=1)
        cots.append(jnp.concatenate([tot, last], axis=0))
    mean_cot = sum(jnp.sum(v, axis=-1, keepdims=True) for v in cots) * inv
    mean_dot = sum(jnp.sum(v * u, axis=-1, keepdims=True) for v, u in zip(cots, unit)) * inv
    spread[...] = jnp.zeros_like(spread)
    for q in range(4):
        spread[64 * q:64 * q + 49, :] = scale * (cots[q] - mean_cot - unit[q] * mean_dot)
    high, mid, low = split3(spread[...])
    d_block = dot(perm, high, 0, 0) + dot(perm, mid, 0, 0) + dot(perm, low, 0, 0)
    d_block_out[...] = d_block
    scaled = (gate * d_block).astype(BF)
    slots[...] = pack_rows(dot(table, scaled[:, :HC], 0, 0), dot(table, scaled[:, HC:], 0, 0), 32)


def after_back(after, ret, table, d_block, d_after_out, d_att_out):
    d_second = gathered(ret, table[...])
    d_after = d_block[...] + norm_back(after[...].astype(F32), d_second)
    d_after_out[...] = d_after
    d_att_out[...] = d_after.astype(BF)


def finish(scal, x, d_after, own, halo, out):
    r = scal[0]
    top = jnp.where(iota((HALO, C), 0) < 14 * r, halo[...].astype(F32), own[:HALO, :].astype(F32))
    out[:HALO, :] = (d_after[:HALO, :] + norm_back(x[:HALO, :].astype(F32), top)).astype(BF)
    out[HALO:, :] = (
        d_after[HALO:, :] + norm_back(x[HALO:, :].astype(F32), own[HALO:, :].astype(F32))
    ).astype(BF)


def expert_chunk(j, recv, part, ups, downs, flat, act_out, slope_out):
    here = pl.ds(8 * j, 8)
    rows_here = pl.ds(256 * j, 256)
    low, high = unpack_rows(recv[:, here].reshape(32, 16, HC), 32)
    rows = jnp.concatenate([low, high], axis=1).astype(BF)
    flat[rows_here, :] = rows
    total = jnp.zeros((256, C), F32)
    for k in range(4):
        pre = dot(rows, ups[k])
        cdf = 0.5 * (1.0 + lax.erf(pre * np.float32(2.0 ** -0.5)))
        act = (pre * cdf).astype(BF)
        slope = cdf + pre * jnp.exp(-0.5 * pre * pre) * np.float32((2.0 * np.pi) ** -0.5)
        act_out[rows_here, k * 256:(k + 1) * 256] = act
        slope_out[rows_here, k * 256:(k + 1) * 256] = slope.astype(BF)
        total = total + dot(act, downs[k])
    part[:, here] = pack_rows(total[:, :HC], total[:, HC:], 32).reshape(4, 8, 16, HC)


def expert_bwd(slots, slope, ups, downs, flat, d_pre_out, packed):
    low, high = unpack_rows(slots[...].reshape(32, 16, HC), 32)
    rows = jnp.concatenate([low, high], axis=1).astype(BF)
    flat[...] = rows
    total = jnp.zeros((256, C), F32)
    for k in range(4):
        span = slice(k * 256, (k + 1) * 256)
        d_pre = (slope[:, span].astype(F32) * dot(rows, downs[k], 1, 1)).astype(BF)
        d_pre_out[:, span] = d_pre
        total = total + dot(d_pre, ups[k], 1, 1)
    packed[...] = pack_rows(total[:, :HC], total[:, HC:], 32).reshape(4, 8, 16, HC)


def expert_grads(act, d_rows, rows, d_pre, down_out, up_out):
    down_out[0] = dot(act[...], d_rows[...], 0, 0).astype(BF)
    up_out[0] = dot(rows[...], d_pre[...], 0, 0).astype(BF)


def place_grads(turn, *refs):
    ins, (up_out, down_out) = refs[:8], refs[8:]
    for k in range(4):
        @pl.when(pl.program_id(0) == k)
        def _():
            up_out[0] = ins[k][...].astype(F32)
            down_out[0] = ins[4 + k][...].astype(F32)


def coords():
    s = lax.axis_index("scene")
    row = lax.axis_index("row")
    z, m = row // 4, row % 4
    return s, z, m // 2, m % 2


def at(s, z, y, c):
    return (s, z * 4 + y * 2 + c)


def greet(s, z, y, c, total=64):
    barrier = pltpu.get_barrier_semaphore()
    mine = s * 4 + z

    def hail(k, carry):
        peer = (mine + k) % 32
        pl.semaphore_signal(barrier, inc=1, device_id=at(peer // 4, peer % 4, y, c), device_id_type=MESH)
        pl.semaphore_signal(barrier, inc=1, device_id=at(peer // 4, peer % 4, 1 - y, c), device_id_type=MESH)
        return carry

    lax.fori_loop(1, 32, hail, 0)
    pl.semaphore_signal(barrier, inc=1, device_id=at(s, z, 1 - y, c), device_id_type=MESH)
    pl.semaphore_signal(barrier, inc=1, device_id=at(s, z, y, 1 - c), device_id_type=MESH)
    pl.semaphore_wait(barrier, total)


def remote(src, dst, send, recv, device):
    return pltpu.make_async_remote_copy(
        src_ref=src, dst_ref=dst, send_sem=send, recv_sem=recv, device_id=device, device_id_type=MESH
    )


def await_bytes(ref, sem):
    pltpu.make_async_copy(ref, ref, sem).wait()


SLOT_SEMS = [
    pltpu.SemaphoreType.DMA,
    pltpu.SemaphoreType.DMA((2, 4)),
    pltpu.SemaphoreType.DMA((2, 4)),
    pltpu.SemaphoreType.DMA((2, 4)),
    pltpu.SemaphoreType.DMA((2, 4)),
    pltpu.SemaphoreType.DMA((2, 4)),
    pltpu.SemaphoreType.DMA,
    pltpu.SemaphoreType.DMA,
]


def slots_through(place, slots, recv, part, other, total, ret, sems, compute):
    s, z, y, c = place
    mine = s * 4 + z
    send, arrive, f_send, f_recv, p_send, p_recv, r_send, r_recv = sems
    pair = at(s, z, y, 1 - c)

    def to_peer(k, peer, yy):
        remote(slots.at[peer], recv.at[y * 2 + c, k], send, arrive.at[y, k // 8], at(peer // 4, peer % 4, yy, c)).start()

    def push(k, carry):
        peer = (mine + k) % 32
        to_peer(k, peer, y)
        to_peer(k, peer, 1 - y)
        return carry

    pltpu.make_async_copy(slots.at[mine], recv.at[y * 2 + c, 0], arrive.at[y, 0]).start()
    to_peer(0, mine, 1 - y)
    lax.fori_loop(1, 32, push, 0)
    forwards, partials = {}, {}

    def forward(j):
        for yy in range(2):
            block = recv.at[yy * 2 + c, pl.ds(8 * j, 8)]
            await_bytes(block, arrive.at[yy, j])
            forwards[yy, j] = remote(block, block, f_send.at[yy, j], f_recv.at[yy, j], pair)
            forwards[yy, j].start()

    def work(j):
        for yy in range(2):
            forwards[yy, j].wait_recv()
        compute(j)
        for yy in range(2):
            here = pl.ds(8 * j, 8)
            partials[yy, j] = remote(
                part.at[yy * 2 + (1 - c), here], other.at[yy, here], p_send.at[yy, j], p_recv.at[yy, j], pair
            )
            partials[yy, j].start()

    def give(k, yy):
        peer = (mine - k + 32) % 32
        remote(total.at[yy, k], ret.at[y, mine], r_send, r_recv, at(peer // 4, peer % 4, yy, c)).start()

    def give_both(k, carry):
        give(k, 1 - y)
        give(k, y)
        return carry

    def back(j):
        here = pl.ds(8 * j, 8)
        for yy in range(2):
            partials[yy, j].wait_recv()
            total[yy, here] = (part[yy * 2 + c, here].astype(F32) + other[yy, here].astype(F32)).astype(BF)
        if j == 0:
            give(0, 1 - y)
            pltpu.make_async_copy(total.at[y, 0], ret.at[y, mine], r_recv).start()
        lax.fori_loop(max(1, 8 * j), 8 * j + 8, give_both, 0)

    forward(0)
    forward(1)
    work(0)
    forward(2)
    work(1)
    back(0)
    forward(3)
    work(2)
    back(1)
    work(3)
    back(2)
    back(3)

    def finish_sends():
        for copy in list(forwards.values()) + list(partials.values()):
            copy.wait_send()
        for sem in (send, r_send):
            await_bytes(total.at[0], sem)
            await_bytes(total.at[0, pl.ds(0, 31)], sem)

    await_bytes(ret, r_recv)
    return finish_sends


def front(
    scal, x, bias, choice_col, choice_row, gate, grad48, grad_tail, qkv_weight, out_weight, expert_up, expert_down, reduce_weight,
    after, table, merge_norm, d_block, d_slots, qkv_out, probs_out, flat_out, act_out, slope_out, up_out, down_out,
    halo, halo2, normed, mask, ecol, erow, acc, att, wqkv, wo, wred, qkv, probs,
    d_send, d_recv, t_wide, t_send, t_recv, ups, downs, relay_up, relay_down,
    slots, recv, part, other, total, ret, flat, act, slope, spread,
    io_sem, halo_sem, w_send, w_recv, d_sem, *slot_sems,
):
    place = coords()
    s, z, y, c = place
    row = z * 4 + y * 2 + c
    r, cc, last = scal[0], scal[1], scal[2]
    ins = [
        pltpu.make_async_copy(reduce_weight, wred, io_sem.at[0]),
        pltpu.make_async_copy(qkv_weight, wqkv, io_sem.at[1]),
        pltpu.make_async_copy(out_weight, wo, io_sem.at[2]),
        pltpu.make_async_copy(expert_up.at[z], ups.at[0], io_sem.at[3]),
        pltpu.make_async_copy(expert_down.at[z], downs.at[0], io_sem.at[4]),
    ]
    for copy in ins:
        copy.start()
    greet_all(place)

    nxt = (s, (row + 1) % 16)
    prv = (s, (row + 15) % 16)
    z_up, z_down = at(s, (z + 1) % 4, y, c), at(s, (z + 3) % 4, y, c)
    halo_copy = remote(x.at[pl.ds(0, HALO)], halo, halo_sem.at[0], halo_sem.at[1], prv)
    halo_copy.start()
    weights = [
        remote(expert_up.at[(z + 2) % 4], relay_up, w_send.at[0], w_recv.at[0], z_up),
        remote(expert_down.at[(z + 2) % 4], relay_down, w_send.at[1], w_recv.at[1], z_down),
        remote(expert_up.at[(z + 1) % 4], ups.at[1], w_send.at[2], w_recv.at[2], z_up),
        remote(expert_up.at[(z + 3) % 4], ups.at[3], w_send.at[3], w_recv.at[3], z_down),
        remote(expert_down.at[(z + 1) % 4], downs.at[1], w_send.at[4], w_recv.at[4], z_up),
        remote(expert_down.at[(z + 3) % 4], downs.at[3], w_send.at[5], w_recv.at[5], z_down),
    ]
    for copy in weights:
        copy.start()
    relayed = [
        remote(relay_up, ups.at[2], w_send.at[6], w_recv.at[6], z_up),
        remote(relay_down, downs.at[2], w_send.at[7], w_recv.at[7], z_down),
    ]

    ins[0].wait()
    for half in range(4):
        span = pl.ds(half * C, C)
        d_send[:, :, span] = dot(grad48[...], wred[span, :], 1, 1).astype(BF).reshape(8, 48, C)
        tail = dot(grad_tail[...], wred[span, :], 1, 1)
        for i in range(4):
            t_wide[:, 4 * half + i, :] = tail[:8, i * 256:(i + 1) * 256]
    t_send[...] = t_wide[...].astype(BF)
    gifts = []
    for k in range(1, 8):
        peer = (s + k) % 8
        gifts.append(remote(d_send.at[peer], d_recv.at[s], d_sem.at[0, k], d_sem.at[1, k], at(peer, z, y, c)))
        gifts.append(remote(t_send.at[peer], t_recv.at[s], d_sem.at[2, k], d_sem.at[3, k], at(peer, z, y, c)))
    for copy in gifts:
        copy.start()
    own = [
        pltpu.make_async_copy(d_send.at[s], d_recv.at[s], io_sem.at[5]),
        pltpu.make_async_copy(t_send.at[s], t_recv.at[s], io_sem.at[6]),
    ]
    for copy in own:
        copy.start()

    attn_masks(r, cc, last, mask, ecol, erow)
    normed[HALO:, :] = norm_parts(x[HALO:, :].astype(F32))[0].astype(BF)
    acc[...] = jnp.zeros_like(acc)
    halo_copy.wait_recv()
    top = jnp.where(iota((HALO, C), 0) < 14 * r, halo[...].astype(F32), x[:HALO, :].astype(F32))
    normed[:HALO, :] = norm_parts(top)[0].astype(BF)
    ins[1].wait()
    ins[2].wait()

    def group(g, carry):
        attn_group(g, normed, wqkv, wo, bias, mask, ecol, erow, qkv, probs, acc)
        return carry

    lax.fori_loop(0, 3, group, 0)
    for arrived, onward in zip(weights, relayed):
        arrived.wait_recv()
        onward.start()
    lax.fori_loop(3, 4, group, 0)
    att[...] = acc[...].astype(BF)
    halo2_copy = remote(att.at[pl.ds(0, HALO)], halo2, halo_sem.at[2], halo_sem.at[3], nxt)
    halo2_copy.start()
    outs = [
        pltpu.make_async_copy(qkv, qkv_out, io_sem.at[7]),
        pltpu.make_async_copy(probs, probs_out, io_sem.at[8]),
    ]
    for copy in outs:
        copy.start()
    halo2_copy.wait_recv()
    route(r, x, att, halo2, choice_col, choice_row, after, slots, table)

    def compute(j):
        if j == 0:
            for copy in weights[2:] + relayed:
                copy.wait_recv()
            ins[3].wait()
            ins[4].wait()
        expert_chunk(j, recv, part, ups, downs, flat, act, slope)

    finish_sends = slots_through(place, slots, recv, part, other, total, ret, slot_sems, compute)
    more = [
        pltpu.make_async_copy(flat, flat_out, io_sem.at[9]),
        pltpu.make_async_copy(act, act_out, io_sem.at[10]),
        pltpu.make_async_copy(slope, slope_out, io_sem.at[11]),
        pltpu.make_async_copy(ups, up_out, io_sem.at[12]),
        pltpu.make_async_copy(downs, down_out, io_sem.at[13]),
    ]
    for copy in more:
        copy.start()
    for k in range(1, 8):
        gifts[2 * k - 2].wait_recv()
        gifts[2 * k - 1].wait_recv()
    for copy in own:
        copy.wait()
    merge_mid(after, ret, table, gate, d_recv, t_recv, merge_norm, d_block, d_slots, spread)
    for copy in outs + more:
        copy.wait()
    finish_sends()
    for copy in weights + relayed + gifts + [halo_copy, halo2_copy]:
        copy.wait_send()


def greet_all(place):
    s, z, y, c = place
    barrier = pltpu.get_barrier_semaphore()
    row = z * 4 + y * 2 + c
    pl.semaphore_signal(barrier, inc=1, device_id=(s, (row + 1) % 16), device_id_type=MESH)
    pl.semaphore_signal(barrier, inc=1, device_id=(s, (row + 15) % 16), device_id_type=MESH)
    greet(s, z, y, c, 66)


def dispatch_kernel(src, out, send_sem, recv_sem, pair_send, pair_recv):
    s, z, y, c = coords()
    mine = s * 4 + z
    greet(s, z, y, c)

    def push(k, carry):
        peer = (mine + k) % 32
        for yy in range(2):
            pltpu.make_async_remote_copy(
                src_ref=src.at[peer], dst_ref=out.at[y * 2 + c, k], send_sem=send_sem, recv_sem=recv_sem.at[y],
                device_id=at(peer // 4, peer % 4, (y + yy) % 2, c), device_id_type=MESH,
            ).start()
        return carry

    pltpu.make_async_copy(src.at[mine], out.at[y * 2 + c, 0], recv_sem.at[y]).start()
    pltpu.make_async_remote_copy(
        src_ref=src.at[mine], dst_ref=out.at[y * 2 + c, 0], send_sem=send_sem, recv_sem=recv_sem.at[y],
        device_id=at(s, z, 1 - y, c), device_id_type=MESH,
    ).start()
    lax.fori_loop(1, 32, push, 0)
    pairs = []
    for yy in range(2):
        block = out.at[yy * 2 + c]
        pltpu.make_async_copy(block, block, recv_sem.at[yy]).wait()
        copy = pltpu.make_async_remote_copy(
            src_ref=block, dst_ref=block, send_sem=pair_send.at[yy], recv_sem=pair_recv.at[yy],
            device_id=at(s, z, y, 1 - c), device_id_type=MESH,
        )
        copy.start()
        pairs.append(copy)
    for copy in pairs:
        copy.wait()
    pltpu.make_async_copy(src, src, send_sem).wait()
    pltpu.make_async_copy(src.at[pl.ds(0, 31)], src.at[pl.ds(0, 31)], send_sem).wait()


def dispatch(slots):
    return pl.pallas_call(
        dispatch_kernel,
        out_shape=sds((4, 32, 16, HC), BF),
        in_specs=[VM],
        out_specs=VM,
        scratch_shapes=[
            pltpu.SemaphoreType.DMA,
            pltpu.SemaphoreType.DMA((2,)),
            pltpu.SemaphoreType.DMA((2,)),
            pltpu.SemaphoreType.DMA((2,)),
        ],
        compiler_params=params(collective_id=0, has_side_effects=True),
        cost_estimate=cost(0, 40 << 20),
        name="dispatch",
    )(slots)


def combine_kernel(part, out, other, total, send_sem, recv_sem, pair_send, pair_recv):
    s, z, y, c = coords()
    mine = s * 4 + z
    greet(s, z, y, c)
    pairs = []
    for yy in range(2):
        copy = pltpu.make_async_remote_copy(
            src_ref=part.at[yy * 2 + (1 - c)], dst_ref=other.at[yy], send_sem=pair_send.at[yy],
            recv_sem=pair_recv.at[yy], device_id=at(s, z, y, 1 - c), device_id_type=MESH,
        )
        copy.start()
        pairs.append(copy)

    def add(yy, k):
        summed = part[yy * 2 + c, k].astype(F32) + other[yy, k].astype(F32)
        total[yy, k] = summed.astype(BF)

    def ship(yy, k):
        peer = (mine - k + 32) % 32
        pltpu.make_async_remote_copy(
            src_ref=total.at[yy, k], dst_ref=out.at[y, mine], send_sem=send_sem, recv_sem=recv_sem,
            device_id=at(peer // 4, peer % 4, yy, c), device_id_type=MESH,
        ).start()

    for copy in pairs:
        copy.wait_recv()

    def push(k, carry):
        add(1 - y, k)
        ship(1 - y, k)
        add(y, k)
        ship(y, k)
        return carry

    lax.fori_loop(1, 32, push, 0)
    add(1 - y, 0)
    ship(1 - y, 0)
    add(y, 0)
    pltpu.make_async_copy(total.at[y, 0], out.at[y, mine], recv_sem).start()
    for copy in pairs:
        copy.wait_send()
    pltpu.make_async_copy(total, total, recv_sem).wait()
    pltpu.make_async_copy(total.at[0], total.at[0], send_sem).wait()
    pltpu.make_async_copy(total.at[0, pl.ds(0, 31)], total.at[0, pl.ds(0, 31)], send_sem).wait()


def combine(part):
    return pl.pallas_call(
        combine_kernel,
        out_shape=sds((2, 32, 16, HC), BF),
        in_specs=[VM],
        out_specs=VM,
        scratch_shapes=[
            pltpu.VMEM((2, 32, 16, HC), BF),
            pltpu.VMEM((2, 32, 16, HC), BF),
            pltpu.SemaphoreType.DMA,
            pltpu.SemaphoreType.DMA,
            pltpu.SemaphoreType.DMA((2,)),
            pltpu.SemaphoreType.DMA((2,)),
        ],
        compiler_params=params(collective_id=1, has_side_effects=True),
        cost_estimate=cost(0, 40 << 20),
        name="combine",
    )(part)


def row_shift(value, steps):
    pairs = [(source, (source + steps) % 16) for source in range(16)]
    return lax.ppermute(value, "row", pairs)


def z_shift(value, steps):
    pairs = [(z * 4 + m, ((z + steps) % 4) * 4 + m) for z in range(4) for m in range(4)]
    return lax.ppermute(value, "row", pairs)


def bias_pairs():
    spot = np.arange(49)
    py, px = spot // 7, spot % 7
    relative = (py[:, None] - py[None, :] + 6) * 13 + (px[:, None] - px[None, :] + 6)
    table = np.zeros((169, 64, 64), np.float32)
    a, b = np.meshgrid(spot, spot, indexing="ij")
    table[relative.reshape(-1), a.reshape(-1), b.reshape(-1)] = 1.0
    return table.reshape(169, 4096)


def whole(kernel, out_shape, args, specs, scratch=(), flops=0, nbytes=0):
    return pl.pallas_call(
        kernel,
        out_shape=out_shape,
        in_specs=specs,
        out_specs=[VM] * len(out_shape),
        scratch_shapes=list(scratch),
        compiler_params=params(),
        cost_estimate=cost(flops, nbytes),
        name=kernel.__name__,
    )(*args)


def local(
    tokens,
    qkv_weight,
    out_weight,
    position_bias,
    window_shift,
    expert_up,
    expert_down,
    expert_choice,
    combine_weight,
    reduce_weight,
    merged_grad,
):
    row = lax.axis_index("row")
    z = row // 4
    x = jnp.pad(tokens.reshape(TOK, C), ((0, TP - TOK), (0, 0)))
    scal = jnp.stack([window_shift[0], window_shift[1], (row == 15).astype(jnp.int32), z.astype(jnp.int32)])
    choice = jnp.pad(expert_choice.reshape(TOK), (0, TP - TOK), constant_values=-1000)
    gate = jnp.pad(combine_weight.reshape(TOK, 1), ((0, TP - TOK), (0, 0)))

    grads49 = merged_grad.reshape(8, 49, -1)
    grad48 = grads49[:, :48].reshape(8 * 48, -1)
    grad_tail = jnp.pad(grads49[:, 48], ((0, 8), (0, 0)))
    bias = jnp.dot(position_bias, jnp.asarray(bias_pairs()), precision=lax.Precision.HIGHEST).reshape(32, 64, 64)

    full = lambda shape: pl.BlockSpec(shape, lambda g: (0,) * len(shape))
    w_spec = lambda which: pl.BlockSpec((C, GRP), lambda g: (0, 4 * which + g))
    wo_spec = pl.BlockSpec((GRP, C), lambda g: (g, 0))
    head_spec = pl.BlockSpec((TP, GRP), lambda g: (0, g))
    prob_spec = pl.BlockSpec((8 * TP, TP), lambda g: (g, 0))
    after, table, merge_norm, d_block, d_slots, qkv, probs, flat_in, act, slope, ups, downs = pl.pallas_call(
        front,
        out_shape=[
            sds((TP, C), BF), sds((TP, 256), BF), sds((49, 4 * C), BF), sds((TP, C), F32), sds((32, 16, HC), BF),
            sds((3, 4, TP, GRP), BF), sds((32 * TP, TP), BF), sds((C, C), BF), sds((C, C), BF), sds((C, C), BF),
            sds((4, C, 256), BF), sds((4, 256, C), BF),
        ],
        in_specs=[SM] + [VM] * 7 + [HB] * 5,
        out_specs=[VM] * 5 + [HB] * 7,
        scratch_shapes=[
            pltpu.VMEM((HALO, C), BF), pltpu.VMEM((HALO, C), BF), pltpu.VMEM((TP, C), BF), pltpu.VMEM((TP, TP), F32),
            pltpu.VMEM((192, TP), BF), pltpu.VMEM((TP, 192), BF), pltpu.VMEM((TP, C), F32), pltpu.VMEM((TP, C), BF),
            pltpu.VMEM((C, 3 * C), BF), pltpu.VMEM((C, C), BF), pltpu.VMEM((4 * C, 256), BF),
            pltpu.VMEM((3, 4, TP, GRP), BF), pltpu.VMEM((32 * TP, TP), BF),
            pltpu.VMEM((8, 48, 4 * C), BF), pltpu.VMEM((8, 48, 4 * C), BF), pltpu.VMEM((8, 16, 256), F32),
            pltpu.VMEM((8, 16, 256), BF), pltpu.VMEM((8, 16, 256), BF),
            pltpu.VMEM((4, C, 256), BF), pltpu.VMEM((4, 256, C), BF), pltpu.VMEM((C, 256), BF), pltpu.VMEM((256, C), BF),
            pltpu.VMEM((32, 16, HC), BF), pltpu.VMEM((4, 32, 16, HC), BF), pltpu.VMEM((4, 32, 16, HC), BF),
            pltpu.VMEM((2, 32, 16, HC), BF), pltpu.VMEM((2, 32, 16, HC), BF), pltpu.VMEM((2, 32, 16, HC), BF),
            pltpu.VMEM((C, C), BF), pltpu.VMEM((C, C), BF), pltpu.VMEM((C, C), BF), pltpu.VMEM((256, C), F32),
            pltpu.SemaphoreType.DMA((14,)), pltpu.SemaphoreType.DMA((4,)), pltpu.SemaphoreType.DMA((8,)),
            pltpu.SemaphoreType.DMA((8,)), pltpu.SemaphoreType.DMA((4, 8)), *SLOT_SEMS,
        ],
        compiler_params=params(collective_id=2, has_side_effects=True),
        cost_estimate=cost(12 << 30, 60 << 20),
        name="front",
    )(scal, x, bias, choice.reshape(TP, 1), choice.reshape(1, TP), gate, grad48, grad_tail, qkv_weight, out_weight,
      expert_up, expert_down, reduce_weight)

    full = lambda shape: pl.BlockSpec(shape, lambda g: (0,) * len(shape))
    w_spec = lambda which: pl.BlockSpec((C, GRP), lambda g: (0, 4 * which + g))
    wo_spec = pl.BlockSpec((GRP, C), lambda g: (g, 0))
    head_spec = lambda which: pl.BlockSpec((1, 1, TP, GRP), lambda g: (which, g, 0, 0))
    prob_spec = pl.BlockSpec((8 * TP, TP), lambda g: (g, 0))
    slot_spec = pl.BlockSpec((4, 8, 16, HC), lambda g: (0, g, 0, 0))
    row_spec = pl.BlockSpec((256, C), lambda g: (g, 0))
    weight_specs = [full((4, C, 256)), full((4, 256, C))]

    d_slot_in = dispatch(d_slots)
    flat_d, d_pre, d_part = pl.pallas_call(
        expert_bwd,
        grid=(4,),
        out_shape=[sds((C, C), BF)] * 2 + [sds((4, 32, 16, HC), BF)],
        in_specs=[slot_spec, row_spec] + weight_specs,
        out_specs=[row_spec] * 2 + [slot_spec],
        compiler_params=params(),
        cost_estimate=cost(4 << 30, 14 << 20),
        name="expert_bwd",
    )(d_slot_in, slope, ups, downs)
    d_ret = combine(d_part)

    col_spec = pl.BlockSpec((C, 256), lambda g: (0, g))
    down_parts, up_parts = pl.pallas_call(
        expert_grads,
        grid=(4,),
        out_shape=[sds((4, 256, C), BF), sds((4, C, 256), BF)],
        in_specs=[col_spec, full((C, C)), full((C, C)), col_spec],
        out_specs=[pl.BlockSpec((1, 256, C), lambda g: (g, 0, 0)), pl.BlockSpec((1, C, 256), lambda g: (g, 0, 0))],
        compiler_params=params(),
        cost_estimate=cost(4 << 30, 14 << 20),
        name="expert_grads",
    )(act, flat_d, flat_in, d_pre)
    up_back = [up_parts[0]] + [z_shift(up_parts[k], -k) for k in range(1, 4)]
    down_back = [down_parts[0]] + [z_shift(down_parts[k], -k) for k in range(1, 4)]

    d_after, d_att = whole(
        after_back, [sds((TP, C), F32), sds((TP, C), BF)], (after, d_ret, table, d_block), [VM] * 4,
        flops=1 << 30, nbytes=4 << 20,
    )
    d_below = row_shift(d_att[:HALO], -1)
    d_shift = pl.pallas_call(
        attn_bwd,
        grid=(4,),
        out_shape=sds((TP, C), BF),
        in_specs=[SM, full((TP, C)), full((HALO, C)), w_spec(0), w_spec(1), w_spec(2), wo_spec,
                  head_spec(0), head_spec(1), head_spec(2), prob_spec],
        out_specs=full((TP, C)),
        scratch_shapes=[pltpu.VMEM((TP, C), BF), pltpu.VMEM((TP, C), F32)],
        compiler_params=params(),
        cost_estimate=cost(8 << 30, 14 << 20),
        name="attn_bwd",
    )(scal, d_att, d_below, qkv_weight, qkv_weight, qkv_weight, out_weight, qkv, qkv, qkv, probs)
    d_above = row_shift(d_shift[:HALO], 1)
    (grad,) = whole(
        finish, [sds((TP, C), BF)], (scal, x, d_after, d_shift, d_above), [SM] + [VM] * 4,
        flops=1 << 28, nbytes=3 << 20,
    )
    tokens_grad = grad[:TOK].reshape(tokens.shape)

    merged = jnp.einsum(
        "nkc,cd->nkd", lax.all_gather(merge_norm[None], "scene", axis=0, tiled=True), reduce_weight,
        preferred_element_type=F32,
    ).astype(BF).reshape(merged_grad.shape)

    up_grad, down_grad = pl.pallas_call(
        place_grads,
        grid_spec=pltpu.PrefetchScalarGridSpec(
            num_scalar_prefetch=1,
            grid=(4,),
            in_specs=[pl.BlockSpec((C, 256), lambda g, t: (0, 0))] * 4 + [pl.BlockSpec((256, C), lambda g, t: (0, 0))] * 4,
            out_specs=[pl.BlockSpec((1, C, 256), lambda g, t: ((t[0] + g) % 4, 0, 0)),
                       pl.BlockSpec((1, 256, C), lambda g, t: ((t[0] + g) % 4, 0, 0))],
        ),
        out_shape=[sds((4, C, 256), F32), sds((4, 256, C), F32)],
        compiler_params=params(),
        cost_estimate=cost(0, 12 << 20),
        name="place_grads",
    )(z.reshape(1).astype(jnp.int32), *up_back, *down_back)
    return (merged, tokens_grad, up_grad, down_grad)


def solution(mesh):
    placed = (
        P("scene", "row", None, None),
        P(),
        P(),
        P(),
        P(),
        P("scene", None, "row"),
        P("scene", "row", None),
        P("scene", "row", None, None),
        P("scene", "row", None),
        P(None, "scene"),
        P(None, "row", None, "scene"),
    )
    return jax.shard_map(
        local,
        mesh=mesh,
        in_specs=placed,
        out_specs=(
            P(None, "row", None, "scene"),
            P("scene", "row", None, None),
            P("scene", None, "row"),
            P("scene", "row", None),
        ),
        check_vma=False,
    )
```

```python
import functools

import jax
import jax.numpy as jnp
import numpy as np
from jax import lax
from jax.experimental import pallas as pl
from jax.experimental.pallas import tpu as pltpu
from jax.sharding import PartitionSpec as P

MESH = pl.DeviceIdType.MESH
F32 = jnp.float32
BF = jnp.bfloat16
EPS = 1e-5
C = 1024
HC = C // 2
TOK = 196
TP = 208
HALO = 96
GRP = 256
NEG = -1e30
VMEM_BIG = 56 * 1024 * 1024
VM = pl.BlockSpec(memory_space=pltpu.VMEM)
SM = pl.BlockSpec(memory_space=pltpu.SMEM)
HB = pl.BlockSpec(memory_space=pl.ANY)


def sds(shape, dtype):
    return jax.ShapeDtypeStruct(shape, dtype)


def params(**kw):
    return pltpu.CompilerParams(vmem_limit_bytes=VMEM_BIG, **kw)


def cost(flops, nbytes):
    return pl.CostEstimate(flops=flops, bytes_accessed=nbytes, transcendentals=0)


def dot(a, b, da=1, db=0):
    return lax.dot_general(a, b, (((da,), (db,)), ((), ())), preferred_element_type=F32)


def iota(shape, dim):
    return lax.broadcasted_iota(jnp.int32, shape, dim)


def norm_parts(values):
    centre = jnp.mean(values, axis=-1, keepdims=True)
    centred = values - centre
    spread = jnp.mean(centred * centred, axis=-1, keepdims=True)
    scale = lax.rsqrt(spread + EPS)
    return centred * scale, scale


def norm_back(values, cot):
    unit, scale = norm_parts(values)
    mean_cot = jnp.mean(cot, axis=-1, keepdims=True)
    mean_dot = jnp.mean(cot * unit, axis=-1, keepdims=True)
    return scale * (cot - mean_cot - unit * mean_dot)


def split3(values):
    high = values.astype(BF)
    rest = values - high.astype(F32)
    mid = rest.astype(BF)
    low = (rest - mid.astype(F32)).astype(BF)
    return high, mid, low


def place_of(tok, r, c):
    rho = (tok * 4682) >> 16
    gam = tok - 14 * rho
    i = rho - r
    i = jnp.where(i < 0, i + 14, i)
    j = gam - c
    j = jnp.where(j < 0, j + 14, j)
    a = jnp.where(i >= 7, 1, 0)
    b = jnp.where(j >= 7, 1, 0)
    return i, j, a, b


def pos_of(tok, r, c):
    i, j, a, b = place_of(tok, r, c)
    return (i - 7 * a) * 7 + (j - 7 * b)


def group_of(tok, r, c, last):
    i, j, a, b = place_of(tok, r, c)
    la = jnp.where(i >= 7, jnp.where(i < 14 - r, 1, 2), 0) * last
    lb = jnp.where(j >= 7, jnp.where(j < 14 - c, 1, 2), 0)
    return a * 2 + b, la * 3 + lb


def pack_rows(low, high, blocks):
    return jnp.concatenate([low.reshape(blocks, 8, HC), high.reshape(blocks, 8, HC)], axis=1).astype(BF)


def unpack_rows(packed, blocks):
    wide = packed.astype(F32)
    low = wide[:, :8, :].reshape(blocks * 8, HC)
    high = wide[:, 8:, :].reshape(blocks * 8, HC)
    return low, high


def attn_masks(r, c, last, mask, ecol, erow):
    tq, tk = iota((TP, TP), 0), iota((TP, TP), 1)
    wq_, lq = group_of(tq, r, c, last)
    wk_, lk = group_of(tk, r, c, last)
    seen = jnp.where(wq_ == wk_, jnp.where(lq == lk, 0.0, -100.0), NEG)
    mask[...] = jnp.where(tk < TOK, seen, NEG)
    row_pos = pos_of(iota((TP, 192), 0), r, c)
    erow[...] = jnp.where(row_pos == (iota((TP, 192), 1) & 63), 1.0, 0.0).astype(BF)
    col_pos = pos_of(iota((192, TP), 1), r, c)
    ecol[...] = jnp.where(col_pos == (iota((192, TP), 0) & 63), 1.0, 0.0).astype(BF)


def cols(start):
    return pl.ds(pl.multiple_of(start, GRP), GRP)


def attn_group(g, normed, wqkv, wo, bias, mask, ecol, erow, qkv, probs, acc):
    n = normed[...]
    q = dot(n, wqkv[:, cols(g * GRP)]).astype(BF)
    k = dot(n, wqkv[:, cols(C + g * GRP)]).astype(BF)
    v = dot(n, wqkv[:, cols(2 * C + g * GRP)]).astype(BF)
    qkv[0, g] = q
    qkv[1, g] = k
    qkv[2, g] = v
    wide = dot(jnp.concatenate(split3(bias[pl.ds(g * 8, 8)][:, :, :64].reshape(8 * 64, 64)), axis=1), ecol[...])
    w_hi, w_mid, w_lo = split3(wide)
    lane_head = iota((TP, GRP), 1) >> 5
    mixed = jnp.zeros((TP, GRP), F32)
    q32 = q.astype(F32)
    for h in range(8):
        mine = lane_head == h
        qm = jnp.where(mine, q32, 0.0).astype(BF)
        s = dot(qm, k, 1, 1) * (32.0 ** -0.5)
        part = slice(h * 64, h * 64 + 64)
        s = s + dot(erow[...], jnp.concatenate([w_hi[part], w_mid[part], w_lo[part]], axis=0)) + mask[...]
        e = jnp.exp(s - jnp.max(s, axis=-1, keepdims=True))
        p = (e / jnp.sum(e, axis=-1, keepdims=True)).astype(BF)
        probs[pl.ds(pl.multiple_of((g * 8 + h) * TP, 16), TP), :] = p
        mixed = jnp.where(mine, dot(p, v), mixed)
    acc[...] += dot(mixed.astype(BF), wo[pl.ds(pl.multiple_of(g * GRP, GRP), GRP), :])


def attn_group_back(g, d_att, wqkv, wo, qkv, probs, acc):
    q, k, v = qkv[0, g], qkv[1, g], qkv[2, g]
    d_mixed = dot(d_att[...], wo[pl.ds(pl.multiple_of(g * GRP, GRP), GRP), :], 1, 1).astype(BF).astype(F32)
    q32 = q.astype(F32)
    lane_head = iota((TP, GRP), 1) >> 5
    dq = jnp.zeros((TP, GRP), F32)
    dk = jnp.zeros((TP, GRP), F32)
    dv = jnp.zeros((TP, GRP), F32)
    for h in range(8):
        mine = lane_head == h
        dm = jnp.where(mine, d_mixed, 0.0).astype(BF)
        qm = jnp.where(mine, q32, 0.0).astype(BF)
        p = probs[pl.ds(pl.multiple_of((g * 8 + h) * TP, 16), TP), :]
        p32 = p.astype(F32)
        dp = dot(dm, v, 1, 1).astype(BF).astype(F32)
        ds = p32 * (dp - jnp.sum(dp * p32, axis=-1, keepdims=True)) * (32.0 ** -0.5)
        ds = ds.astype(BF)
        dq = jnp.where(mine, dot(ds, k), dq)
        dk = dk + dot(ds, qm, 0, 0)
        dv = dv + dot(p, dm, 0, 0)
    acc[...] += (
        dot(dq.astype(BF), wqkv[:, cols(g * GRP)], 1, 1)
        + dot(dk.astype(BF), wqkv[:, cols(C + g * GRP)], 1, 1)
        + dot(dv.astype(BF), wqkv[:, cols(2 * C + g * GRP)], 1, 1)
    )


def route(r, x, att, halo, meta, after_out, slots, table_out):
    top = jnp.where(iota((HALO, C), 0) < 14 * r, halo[...].astype(F32), att[:HALO, :].astype(F32))
    after_out[:HALO, :] = (x[:HALO, :].astype(F32) + top).astype(BF)
    after_out[HALO:, :] = (x[HALO:, :].astype(F32) + att[HALO:, :].astype(F32)).astype(BF)
    after = after_out[...].astype(F32)
    n2 = norm_parts(after)[0].astype(BF)
    tok, other = iota((TP, TP), 0), iota((TP, TP), 1)
    col = jnp.where(iota((TP, 1), 0) < TOK, meta[:, 0:1], -1000.0)
    line = jnp.sum(jnp.where(tok == other, col, 0.0), axis=0, keepdims=True)
    same = jnp.where(col == line, 1.0, 0.0)
    same = jnp.where(other < tok, same, 0.0)
    rank = jnp.sum(same, axis=1, keepdims=True).astype(jnp.int32)
    table = jnp.where(col.astype(jnp.int32) * 8 + rank == iota((TP, 256), 1), 1.0, 0.0).astype(BF)
    table_out[...] = table
    slots[...] = pack_rows(dot(table, n2[:, :HC], 0, 0), dot(table, n2[:, HC:], 0, 0), 32)


def quad_table():
    row = iota((256, TP), 0)
    tok = iota((256, TP), 1)
    q = row >> 6
    n = row & 63
    a = (n * 9363) >> 16
    b = n - 7 * a
    want = (2 * a + (q & 1)) * 14 + 2 * b + (q >> 1)
    hit = jnp.where(want == tok, 1.0, 0.0)
    return jnp.where(n < 49, hit, 0.0).astype(BF)


def gathered(ret, table):
    low, high = unpack_rows(ret[0].astype(F32) + ret[1].astype(F32), 32)
    return jnp.concatenate([dot(table, low.astype(BF)), dot(table, high.astype(BF))], axis=1)


def merge_mid(after, ret, table_in, meta, parts, tail, mn_out, mn_tail, d_block_out, slots, spread, t_wide):
    table = table_in[...]
    gate = meta[:, 1:2]
    block = (after[...].astype(F32) + gate * gathered(ret, table)).astype(BF)
    perm = quad_table()
    quads = dot(perm, block)
    vals = [quads[64 * q:64 * q + 49, :] for q in range(4)]
    inv = 1.0 / (4 * C)
    centre = sum(jnp.sum(v, axis=-1, keepdims=True) for v in vals) * inv
    cent = [v - centre for v in vals]
    var = sum(jnp.sum(v * v, axis=-1, keepdims=True) for v in cent) * inv
    scale = lax.rsqrt(var + EPS)
    unit = [v * scale for v in cent]
    for q in range(4):
        mn_out[:, q * C:(q + 1) * C] = unit[q][:48].astype(BF)
        for i in range(4):
            t_wide[0, 4 * q + i:4 * q + i + 1, :] = unit[q][48:49, i * 256:(i + 1) * 256]
    mn_tail[...] = t_wide[0].astype(BF)
    tails = jnp.sum(tail[...].astype(F32), axis=0)
    cots = []
    for q in range(4):
        tot = parts[0, :, q * C:(q + 1) * C].astype(F32)
        for s in range(1, 8):
            tot = tot + parts[s, :, q * C:(q + 1) * C].astype(F32)
        last = jnp.concatenate([tails[4 * q + i:4 * q + i + 1, :] for i in range(4)], axis=1)
        cots.append(jnp.concatenate([tot, last], axis=0))
    mean_cot = sum(jnp.sum(v, axis=-1, keepdims=True) for v in cots) * inv
    mean_dot = sum(jnp.sum(v * u, axis=-1, keepdims=True) for v, u in zip(cots, unit)) * inv
    spread[...] = jnp.zeros_like(spread)
    for q in range(4):
        spread[64 * q:64 * q + 49, :] = scale * (cots[q] - mean_cot - unit[q] * mean_dot)
    high, mid, low = split3(spread[...])
    d_block = dot(perm, high, 0, 0) + dot(perm, mid, 0, 0) + dot(perm, low, 0, 0)
    d_block_out[...] = d_block
    scaled = (gate * d_block).astype(BF)
    slots[...] = pack_rows(dot(table, scaled[:, :HC], 0, 0), dot(table, scaled[:, HC:], 0, 0), 32)


def after_back(after, ret, table, d_block, d_after_out, d_att_out):
    d_second = gathered(ret, table[...])
    d_after = d_block[...] + norm_back(after[...].astype(F32), d_second)
    d_after_out[...] = d_after
    d_att_out[...] = d_after.astype(BF)


def lay_rows(tokens, wide, x):
    wide[TOK - 4:, :] = jnp.zeros((TP - TOK + 4, C), F32)
    for i in range(14):
        wide[14 * i:14 * i + 14, :] = tokens[0, i].astype(F32)
    x[...] = wide[...].astype(BF)


def expert_chunk(j, recv, part, ups, downs, flat, act_out, slope_out):
    here = pl.ds(8 * j, 8)
    rows_here = pl.ds(256 * j, 256)
    low, high = unpack_rows(recv[:, here].reshape(32, 16, HC), 32)
    rows = jnp.concatenate([low, high], axis=1).astype(BF)
    flat[rows_here, :] = rows
    total = jnp.zeros((256, C), F32)
    for k in range(4):
        pre = dot(rows, ups[k])
        cdf = 0.5 * (1.0 + lax.erf(pre * np.float32(2.0 ** -0.5)))
        act = (pre * cdf).astype(BF)
        slope = cdf + pre * jnp.exp(-0.5 * pre * pre) * np.float32((2.0 * np.pi) ** -0.5)
        act_out[rows_here, k * 256:(k + 1) * 256] = act
        slope_out[rows_here, k * 256:(k + 1) * 256] = slope.astype(BF)
        total = total + dot(act, downs[k])
    part[:, here] = pack_rows(total[:, :HC], total[:, HC:], 32).reshape(4, 8, 16, HC)


def expert_chunk_back(j, recv, part, ups, downs, flat, slope):
    here = pl.ds(8 * j, 8)
    rows_here = pl.ds(256 * j, 256)
    low, high = unpack_rows(recv[:, here].reshape(32, 16, HC), 32)
    rows = jnp.concatenate([low, high], axis=1).astype(BF)
    flat[rows_here, :] = rows
    total = jnp.zeros((256, C), F32)
    for k in range(4):
        span = slice(k * 256, (k + 1) * 256)
        d_pre = (slope[rows_here, span].astype(F32) * dot(rows, downs[k], 1, 1)).astype(BF)
        slope[rows_here, span] = d_pre
        total = total + dot(d_pre, ups[k], 1, 1)
    part[:, here] = pack_rows(total[:, :HC], total[:, HC:], 32).reshape(4, 8, 16, HC)


def coords():
    s = lax.axis_index("scene")
    row = lax.axis_index("row")
    z, m = row // 4, row % 4
    return s, z, m // 2, m % 2


def at(s, z, y, c):
    return (s, z * 4 + y * 2 + c)


def greet(s, z, y, c, total=64):
    barrier = pltpu.get_barrier_semaphore()
    mine = s * 4 + z

    def hail(k, carry):
        peer = (mine + k) % 32
        pl.semaphore_signal(barrier, inc=1, device_id=at(peer // 4, peer % 4, y, c), device_id_type=MESH)
        pl.semaphore_signal(barrier, inc=1, device_id=at(peer // 4, peer % 4, 1 - y, c), device_id_type=MESH)
        return carry

    lax.fori_loop(1, 32, hail, 0)
    pl.semaphore_signal(barrier, inc=1, device_id=at(s, z, 1 - y, c), device_id_type=MESH)
    pl.semaphore_signal(barrier, inc=1, device_id=at(s, z, y, 1 - c), device_id_type=MESH)
    pl.semaphore_wait(barrier, total)


def remote(src, dst, send, recv, device):
    return pltpu.make_async_remote_copy(
        src_ref=src, dst_ref=dst, send_sem=send, recv_sem=recv, device_id=device, device_id_type=MESH
    )


def await_bytes(ref, sem):
    pltpu.make_async_copy(ref, ref, sem).wait()


SLOT_SEMS = [
    pltpu.SemaphoreType.DMA,
    pltpu.SemaphoreType.DMA((2, 4)),
    pltpu.SemaphoreType.DMA((2, 4)),
    pltpu.SemaphoreType.DMA((2, 4)),
    pltpu.SemaphoreType.DMA((2, 4)),
    pltpu.SemaphoreType.DMA((2, 4)),
    pltpu.SemaphoreType.DMA,
    pltpu.SemaphoreType.DMA,
]


def slots_through(place, slots, recv, part, other, total, ret, sems, compute, meanwhile=None):
    s, z, y, c = place
    mine = s * 4 + z
    send, arrive, f_send, f_recv, p_send, p_recv, r_send, r_recv = sems
    pair = at(s, z, y, 1 - c)

    def to_peer(k, peer, yy):
        remote(slots.at[peer], recv.at[y * 2 + c, k], send, arrive.at[y, k // 8], at(peer // 4, peer % 4, yy, c)).start()

    def push(k, carry):
        peer = (mine + k) % 32
        to_peer(k, peer, y)
        to_peer(k, peer, 1 - y)
        return carry

    pltpu.make_async_copy(slots.at[mine], recv.at[y * 2 + c, 0], arrive.at[y, 0]).start()
    to_peer(0, mine, 1 - y)
    lax.fori_loop(1, 32, push, 0)
    forwards, partials = {}, {}

    def forward(j):
        for yy in range(2):
            block = recv.at[yy * 2 + c, pl.ds(8 * j, 8)]
            await_bytes(block, arrive.at[yy, j])
            forwards[yy, j] = remote(block, block, f_send.at[yy, j], f_recv.at[yy, j], pair)
            forwards[yy, j].start()

    def work(j):
        for yy in range(2):
            forwards[yy, j].wait_recv()
        compute(j)
        for yy in range(2):
            here = pl.ds(8 * j, 8)
            partials[yy, j] = remote(
                part.at[yy * 2 + (1 - c), here], other.at[yy, here], p_send.at[yy, j], p_recv.at[yy, j], pair
            )
            partials[yy, j].start()

    def give(k, yy):
        peer = (mine - k + 32) % 32
        remote(total.at[yy, k], ret.at[y, mine], r_send, r_recv, at(peer // 4, peer % 4, yy, c)).start()

    def give_both(k, carry):
        give(k, 1 - y)
        give(k, y)
        return carry

    def back(j):
        here = pl.ds(8 * j, 8)
        for yy in range(2):
            partials[yy, j].wait_recv()
            total[yy, here] = (part[yy * 2 + c, here].astype(F32) + other[yy, here].astype(F32)).astype(BF)
        if j == 0:
            give(0, 1 - y)
            pltpu.make_async_copy(total.at[y, 0], ret.at[y, mine], r_recv).start()
        lax.fori_loop(max(1, 8 * j), 8 * j + 8, give_both, 0)

    forward(0)
    forward(1)
    work(0)
    forward(2)
    work(1)
    back(0)
    forward(3)
    work(2)
    back(1)
    work(3)
    back(2)
    back(3)

    def finish_sends():
        for copy in list(forwards.values()) + list(partials.values()):
            copy.wait_send()
        for sem in (send, r_send):
            await_bytes(total.at[0], sem)
            await_bytes(total.at[0, pl.ds(0, 31)], sem)

    if meanwhile is not None:
        meanwhile()
    await_bytes(ret, r_recv)
    return finish_sends


def front(
    scal, x, bias, choice_col, choice_row, gate, grad48, grad_tail, qkv_weight, out_weight, expert_up, expert_down, reduce_weight,
    after, table, merge_norm, d_block, d_slots, qkv_out, probs_out, flat_out, act_out, slope_out, up_out, down_out,
    halo, halo2, normed, mask, ecol, erow, acc, att, wqkv, wo, wred, qkv, probs,
    d_send, d_recv, t_wide, t_send, t_recv, ups, downs, relay_up, relay_down,
    slots, recv, part, other, total, ret, flat, act, slope, spread,
    io_sem, halo_sem, w_send, w_recv, d_sem, *slot_sems,
):
    place = coords()
    s, z, y, c = place
    row = z * 4 + y * 2 + c
    r, cc, last = scal[0], scal[1], scal[2]
    ins = [
        pltpu.make_async_copy(reduce_weight, wred, io_sem.at[0]),
        pltpu.make_async_copy(qkv_weight, wqkv, io_sem.at[1]),
        pltpu.make_async_copy(out_weight, wo, io_sem.at[2]),
        pltpu.make_async_copy(expert_up.at[z], ups.at[0], io_sem.at[3]),
        pltpu.make_async_copy(expert_down.at[z], downs.at[0], io_sem.at[4]),
    ]
    for copy in ins:
        copy.start()
    greet_all(place)

    nxt = (s, (row + 1) % 16)
    prv = (s, (row + 15) % 16)
    z_up, z_down = at(s, (z + 1) % 4, y, c), at(s, (z + 3) % 4, y, c)
    halo_copy = remote(x.at[pl.ds(0, HALO)], halo, halo_sem.at[0], halo_sem.at[1], prv)
    halo_copy.start()
    weights = [
        remote(expert_up.at[(z + 2) % 4], relay_up, w_send.at[0], w_recv.at[0], z_up),
        remote(expert_down.at[(z + 2) % 4], relay_down, w_send.at[1], w_recv.at[1], z_down),
        remote(expert_up.at[(z + 1) % 4], ups.at[1], w_send.at[2], w_recv.at[2], z_up),
        remote(expert_up.at[(z + 3) % 4], ups.at[3], w_send.at[3], w_recv.at[3], z_down),
        remote(expert_down.at[(z + 1) % 4], downs.at[1], w_send.at[4], w_recv.at[4], z_up),
        remote(expert_down.at[(z + 3) % 4], downs.at[3], w_send.at[5], w_recv.at[5], z_down),
    ]
    for copy in weights:
        copy.start()
    relayed = [
        remote(relay_up, ups.at[2], w_send.at[6], w_recv.at[6], z_up),
        remote(relay_down, downs.at[2], w_send.at[7], w_recv.at[7], z_down),
    ]

    ins[0].wait()
    for half in range(4):
        span = pl.ds(half * C, C)
        d_send[:, :, span] = dot(grad48[...], wred[span, :], 1, 1).astype(BF).reshape(8, 48, C)
        tail = dot(grad_tail[...], wred[span, :], 1, 1)
        for i in range(4):
            t_wide[:, 4 * half + i, :] = tail[:8, i * 256:(i + 1) * 256]
    t_send[...] = t_wide[...].astype(BF)
    gifts = []
    for k in range(1, 8):
        peer = (s + k) % 8
        gifts.append(remote(d_send.at[peer], d_recv.at[s], d_sem.at[0, k], d_sem.at[1, k], at(peer, z, y, c)))
        gifts.append(remote(t_send.at[peer], t_recv.at[s], d_sem.at[2, k], d_sem.at[3, k], at(peer, z, y, c)))
    for copy in gifts:
        copy.start()
    own = [
        pltpu.make_async_copy(d_send.at[s], d_recv.at[s], io_sem.at[5]),
        pltpu.make_async_copy(t_send.at[s], t_recv.at[s], io_sem.at[6]),
    ]
    for copy in own:
        copy.start()

    attn_masks(r, cc, last, mask, ecol, erow)
    normed[HALO:, :] = norm_parts(x[HALO:, :].astype(F32))[0].astype(BF)
    acc[...] = jnp.zeros_like(acc)
    halo_copy.wait_recv()
    top = jnp.where(iota((HALO, C), 0) < 14 * r, halo[...].astype(F32), x[:HALO, :].astype(F32))
    normed[:HALO, :] = norm_parts(top)[0].astype(BF)
    ins[1].wait()
    ins[2].wait()

    def group(g, carry):
        attn_group(g, normed, wqkv, wo, bias, mask, ecol, erow, qkv, probs, acc)
        return carry

    lax.fori_loop(0, 3, group, 0)
    for arrived, onward in zip(weights, relayed):
        arrived.wait_recv()
        onward.start()
    lax.fori_loop(3, 4, group, 0)
    att[...] = acc[...].astype(BF)
    halo2_copy = remote(att.at[pl.ds(0, HALO)], halo2, halo_sem.at[2], halo_sem.at[3], nxt)
    halo2_copy.start()
    outs = [
        pltpu.make_async_copy(qkv, qkv_out, io_sem.at[7]),
        pltpu.make_async_copy(probs, probs_out, io_sem.at[8]),
    ]
    for copy in outs:
        copy.start()
    halo2_copy.wait_recv()
    route(r, x, att, halo2, choice_col, choice_row, after, slots, table)

    def compute(j):
        if j == 0:
            for copy in weights[2:] + relayed:
                copy.wait_recv()
            ins[3].wait()
            ins[4].wait()
        expert_chunk(j, recv, part, ups, downs, flat, act, slope)

    finish_sends = slots_through(place, slots, recv, part, other, total, ret, slot_sems, compute)
    more = [
        pltpu.make_async_copy(flat, flat_out, io_sem.at[9]),
        pltpu.make_async_copy(act, act_out, io_sem.at[10]),
        pltpu.make_async_copy(slope, slope_out, io_sem.at[11]),
        pltpu.make_async_copy(ups, up_out, io_sem.at[12]),
        pltpu.make_async_copy(downs, down_out, io_sem.at[13]),
    ]
    for copy in more:
        copy.start()
    for k in range(1, 8):
        gifts[2 * k - 2].wait_recv()
        gifts[2 * k - 1].wait_recv()
    for copy in own:
        copy.wait()
    merge_mid(after, ret, table, gate, d_recv, t_recv, merge_norm, d_block, d_slots, spread)
    for copy in outs + more:
        copy.wait()
    finish_sends()
    for copy in weights + relayed + gifts + [halo_copy, halo2_copy]:
        copy.wait_send()


def greet_all(place):
    s, z, y, c = place
    barrier = pltpu.get_barrier_semaphore()
    row = z * 4 + y * 2 + c
    pl.semaphore_signal(barrier, inc=1, device_id=(s, (row + 1) % 16), device_id_type=MESH)
    pl.semaphore_signal(barrier, inc=1, device_id=(s, (row + 15) % 16), device_id_type=MESH)
    greet(s, z, y, c, 66)


def remote(src, dst, send, recv, device):
    return pltpu.make_async_remote_copy(
        src_ref=src, dst_ref=dst, send_sem=send, recv_sem=recv, device_id=device, device_id_type=MESH
    )


def await_bytes(ref, sem):
    pltpu.make_async_copy(ref, ref, sem).wait()


SLOT_SEMS = [
    pltpu.SemaphoreType.DMA,
    pltpu.SemaphoreType.DMA((2, 4)),
    pltpu.SemaphoreType.DMA((2, 4)),
    pltpu.SemaphoreType.DMA((2, 4)),
    pltpu.SemaphoreType.DMA((2, 4)),
    pltpu.SemaphoreType.DMA((2, 4)),
    pltpu.SemaphoreType.DMA,
    pltpu.SemaphoreType.DMA,
]


def slots_through(place, slots, recv, part, other, total, ret, sems, compute, meanwhile=None):
    s, z, y, c = place
    mine = s * 4 + z
    send, arrive, f_send, f_recv, p_send, p_recv, r_send, r_recv = sems
    pair = at(s, z, y, 1 - c)

    def to_peer(k, peer, yy):
        remote(slots.at[peer], recv.at[y * 2 + c, k], send, arrive.at[y, k // 8], at(peer // 4, peer % 4, yy, c)).start()

    def push(k, carry):
        peer = (mine + k) % 32
        to_peer(k, peer, y)
        to_peer(k, peer, 1 - y)
        return carry

    pltpu.make_async_copy(slots.at[mine], recv.at[y * 2 + c, 0], arrive.at[y, 0]).start()
    to_peer(0, mine, 1 - y)
    lax.fori_loop(1, 32, push, 0)
    forwards, partials = {}, {}

    def forward(j):
        for yy in range(2):
            block = recv.at[yy * 2 + c, pl.ds(8 * j, 8)]
            await_bytes(block, arrive.at[yy, j])
            forwards[yy, j] = remote(block, block, f_send.at[yy, j], f_recv.at[yy, j], pair)
            forwards[yy, j].start()

    def work(j):
        for yy in range(2):
            forwards[yy, j].wait_recv()
        compute(j)
        for yy in range(2):
            here = pl.ds(8 * j, 8)
            partials[yy, j] = remote(
                part.at[yy * 2 + (1 - c), here], other.at[yy, here], p_send.at[yy, j], p_recv.at[yy, j], pair
            )
            partials[yy, j].start()

    def give(k, yy):
        peer = (mine - k + 32) % 32
        remote(total.at[yy, k], ret.at[y, mine], r_send, r_recv, at(peer // 4, peer % 4, yy, c)).start()

    def give_both(k, carry):
        give(k, 1 - y)
        give(k, y)
        return carry

    def back(j):
        here = pl.ds(8 * j, 8)
        for yy in range(2):
            partials[yy, j].wait_recv()
            total[yy, here] = (part[yy * 2 + c, here].astype(F32) + other[yy, here].astype(F32)).astype(BF)
        if j == 0:
            give(0, 1 - y)
            pltpu.make_async_copy(total.at[y, 0], ret.at[y, mine], r_recv).start()
        lax.fori_loop(max(1, 8 * j), 8 * j + 8, give_both, 0)

    forward(0)
    forward(1)
    work(0)
    forward(2)
    work(1)
    back(0)
    forward(3)
    work(2)
    back(1)
    work(3)
    back(2)
    back(3)

    def finish_sends():
        for copy in list(forwards.values()) + list(partials.values()):
            copy.wait_send()
        for sem in (send, r_send):
            await_bytes(total.at[0], sem)
            await_bytes(total.at[0, pl.ds(0, 31)], sem)

    if meanwhile is not None:
        meanwhile()
    await_bytes(ret, r_recv)
    return finish_sends


def front(
    shift, tokens, meta, position_bias, pairs, merged_grad, qkv_weight, out_weight, expert_up, expert_down, reduce_weight,
    after, table, merge_norm, mn_tail, d_block, d_slots, qkv_out, probs_out, flat_out, act_out, slope_out, up_out, down_out,
    x, x_wide, bias, table_of, grad_wide, halo, halo2, normed, mask, ecol, erow, acc, att, wqkv, wo, wred, qkv, probs,
    d_send, d_recv, t_wide, t_send, t_recv, ups, downs, relay_up, relay_down,
    slots, recv, part, other, total, ret, flat, act, slope, spread,
    io_sem, halo_sem, w_send, w_recv, d_sem, *slot_sems,
):
    place = coords()
    s, z, y, c = place
    row = z * 4 + y * 2 + c
    r, cc = shift[0], shift[1]
    last = jnp.where(row == 15, 1, 0)
    ins = [
        pltpu.make_async_copy(reduce_weight, wred, io_sem.at[0]),
        pltpu.make_async_copy(qkv_weight, wqkv, io_sem.at[1]),
        pltpu.make_async_copy(out_weight, wo, io_sem.at[2]),
        pltpu.make_async_copy(expert_up.at[z], ups.at[0], io_sem.at[3]),
        pltpu.make_async_copy(expert_down.at[z], downs.at[0], io_sem.at[4]),
        pltpu.make_async_copy(pairs, table_of, io_sem.at[14]),
    ]
    for copy in ins:
        copy.start()
    lay_rows(tokens, x_wide, x)
    greet_all(place)

    nxt = (s, (row + 1) % 16)
    prv = (s, (row + 15) % 16)
    z_up, z_down = at(s, (z + 1) % 4, y, c), at(s, (z + 3) % 4, y, c)
    halo_copy = remote(x.at[pl.ds(0, HALO)], halo, halo_sem.at[0], halo_sem.at[1], prv)
    halo_copy.start()
    weights = [
        remote(expert_up.at[(z + 2) % 4], relay_up, w_send.at[0], w_recv.at[0], z_up),
        remote(expert_down.at[(z + 2) % 4], relay_down, w_send.at[1], w_recv.at[1], z_down),
        remote(expert_up.at[(z + 1) % 4], ups.at[1], w_send.at[2], w_recv.at[2], z_up),
        remote(expert_up.at[(z + 3) % 4], ups.at[3], w_send.at[3], w_recv.at[3], z_down),
        remote(expert_down.at[(z + 1) % 4], downs.at[1], w_send.at[4], w_recv.at[4], z_up),
        remote(expert_down.at[(z + 3) % 4], downs.at[3], w_send.at[5], w_recv.at[5], z_down),
    ]
    for copy in weights:
        copy.start()
    relayed = [
        remote(relay_up, ups.at[2], w_send.at[6], w_recv.at[6], z_up),
        remote(relay_down, downs.at[2], w_send.at[7], w_recv.at[7], z_down),
    ]

    for a in range(7):
        grad_wide[:, 7 * a:7 * a + 7, :] = merged_grad[:, a].astype(F32)
    grad48 = grad_wide[:, :48, :].astype(BF).reshape(8 * 48, 256)
    grad_tail = jnp.concatenate([grad_wide[:, 48, :], jnp.zeros((8, 256), F32)], axis=0).astype(BF)
    ins[0].wait()
    for half in range(4):
        span = pl.ds(half * C, C)
        d_send[:, :, span] = dot(grad48, wred[span, :], 1, 1).astype(BF).reshape(8, 48, C)
        tail = dot(grad_tail, wred[span, :], 1, 1)
        for i in range(4):
            t_wide[:, 4 * half + i, :] = tail[:8, i * 256:(i + 1) * 256]
    t_send[...] = t_wide[...].astype(BF)
    gifts = []
    for k in range(1, 8):
        peer = (s + k) % 8
        gifts.append(remote(d_send.at[peer], d_recv.at[s], d_sem.at[0, k], d_sem.at[1, k], at(peer, z, y, c)))
        gifts.append(remote(t_send.at[peer], t_recv.at[s], d_sem.at[2, k], d_sem.at[3, k], at(peer, z, y, c)))
    for copy in gifts:
        copy.start()
    own = [
        pltpu.make_async_copy(d_send.at[s], d_recv.at[s], io_sem.at[5]),
        pltpu.make_async_copy(t_send.at[s], t_recv.at[s], io_sem.at[6]),
    ]
    for copy in own:
        copy.start()

    attn_masks(r, cc, last, mask, ecol, erow)
    ins[5].wait()
    bias[...] = jnp.zeros_like(bias)
    parts3 = jnp.concatenate(split3(position_bias[...]), axis=0)
    for pair in range(25):
        wide = dot(parts3, table_of[:, pair * 256:(pair + 1) * 256])
        wide = wide[:32] + wide[32:64] + wide[64:]
        for i in range(2):
            if 2 * pair + i < 49:
                bias[:, 2 * pair + i, :] = wide[:, i * 128:(i + 1) * 128]
    normed[HALO:, :] = norm_parts(x[HALO:, :].astype(F32))[0].astype(BF)
    acc[...] = jnp.zeros_like(acc)
    halo_copy.wait_recv()
    top = jnp.where(iota((HALO, C), 0) < 14 * r, halo[...].astype(F32), x[:HALO, :].astype(F32))
    normed[:HALO, :] = norm_parts(top)[0].astype(BF)
    ins[1].wait()
    ins[2].wait()

    def group(g, carry):
        attn_group(g, normed, wqkv, wo, bias, mask, ecol, erow, qkv, probs, acc)
        return carry

    lax.fori_loop(0, 3, group, 0)
    for arrived, onward in zip(weights, relayed):
        arrived.wait_recv()
        onward.start()
    lax.fori_loop(3, 4, group, 0)
    att[...] = acc[...].astype(BF)
    halo2_copy = remote(att.at[pl.ds(0, HALO)], halo2, halo_sem.at[2], halo_sem.at[3], nxt)
    halo2_copy.start()
    outs = [
        pltpu.make_async_copy(qkv, qkv_out, io_sem.at[7]),
        pltpu.make_async_copy(probs, probs_out, io_sem.at[8]),
    ]
    for copy in outs:
        copy.start()
    halo2_copy.wait_recv()
    route(r, x, att, halo2, meta, after, slots, table)

    def compute(j):
        if j == 0:
            for copy in weights[2:] + relayed:
                copy.wait_recv()
            ins[3].wait()
            ins[4].wait()
        expert_chunk(j, recv, part, ups, downs, flat, act, slope)

    finish_sends = slots_through(place, slots, recv, part, other, total, ret, slot_sems, compute)
    more = [
        pltpu.make_async_copy(flat, flat_out, io_sem.at[9]),
        pltpu.make_async_copy(act, act_out, io_sem.at[10]),
        pltpu.make_async_copy(slope, slope_out, io_sem.at[11]),
        pltpu.make_async_copy(ups, up_out, io_sem.at[12]),
        pltpu.make_async_copy(downs, down_out, io_sem.at[13]),
    ]
    for copy in more:
        copy.start()
    for k in range(1, 8):
        gifts[2 * k - 2].wait_recv()
        gifts[2 * k - 1].wait_recv()
    for copy in own:
        copy.wait()
    merge_mid(after, ret, table, meta, d_recv, t_recv, merge_norm, mn_tail, d_block, d_slots, spread, t_wide)
    for copy in outs + more:
        copy.wait()
    finish_sends()
    for copy in weights + relayed + gifts + [halo_copy, halo2_copy]:
        copy.wait_send()


def back(
    shift, tokens, after, table, merge_norm, mn_tail, d_block, d_slots,
    qkv_weight, out_weight, reduce_weight, qkv_in, probs_in, flat_in, act_in, slope_in, up_in, down_in,
    tokens_grad, merged, up_grad, down_grad,
    x, x_wide, halo, halo2, d_att, acc, d_after, d_shift, wqkv, wo, wred, qkv, probs, flat, act, slope, ups, downs,
    recv, part, other, total, ret, flat_d, send_up, send_down, relay_up, relay_down, land_up, land_down, wide_up, wide_down,
    mn_all, mt_all, merged_wide,
    io_sem, halo_sem, g_send, g_recv, m_sem, *slot_sems,
):
    place = coords()
    s, z, y, c = place
    row = z * 4 + y * 2 + c
    r = shift[0]
    loads = [
        (down_in, downs), (slope_in, slope), (up_in, ups), (act_in, act), (flat_in, flat),
        (out_weight, wo), (qkv_in, qkv), (probs_in, probs), (qkv_weight, wqkv), (reduce_weight, wred),
    ]
    ins = [pltpu.make_async_copy(a, b, io_sem.at[i]) for i, (a, b) in enumerate(loads)]
    for copy in ins:
        copy.start()
    greet_all(place)
    nxt = (s, (row + 1) % 16)
    prv = (s, (row + 15) % 16)
    z_up, z_down = at(s, (z + 1) % 4, y, c), at(s, (z + 3) % 4, y, c)

    def compute(j):
        if j == 0:
            for copy in ins[:3]:
                copy.wait()
        expert_chunk_back(j, recv, part, ups, downs, flat_d, slope)

    returns = [
        remote(send_up.at[1], relay_up, g_send.at[0], g_recv.at[0], z_up),
        remote(send_down.at[1], relay_down, g_send.at[1], g_recv.at[1], z_down),
        remote(send_up.at[0], land_up.at[0], g_send.at[2], g_recv.at[2], z_down),
        remote(send_down.at[0], land_down.at[0], g_send.at[3], g_recv.at[3], z_down),
        remote(send_up.at[2], land_up.at[2], g_send.at[4], g_recv.at[4], z_up),
        remote(send_down.at[2], land_down.at[2], g_send.at[5], g_recv.at[5], z_up),
    ]
    relayed = [
        remote(relay_up, land_up.at[1], g_send.at[6], g_recv.at[6], z_up),
        remote(relay_down, land_down.at[1], g_send.at[7], g_recv.at[7], z_down),
    ]
    gifts = []
    for k in range(1, 8):
        peer = (s + k) % 8
        gifts.append(remote(merge_norm, mn_all.at[s], m_sem.at[0, k], m_sem.at[1, k], at(peer, z, y, c)))
        gifts.append(remote(mn_tail, mt_all.at[s], m_sem.at[2, k], m_sem.at[3, k], at(peer, z, y, c)))
    own = [
        pltpu.make_async_copy(merge_norm, mn_all.at[s], io_sem.at[10]),
        pltpu.make_async_copy(mn_tail, mt_all.at[s], io_sem.at[11]),
    ]
    own_out = [
        pltpu.make_async_copy(wide_up.at[0], up_grad.at[z], io_sem.at[12]),
        pltpu.make_async_copy(wide_down.at[0], down_grad.at[z], io_sem.at[13]),
    ]

    def grads():
        for copy in ins[3:5]:
            copy.wait()
        for k in (2, 1, 3, 0):
            span = slice(k * 256, (k + 1) * 256)
            up_part = dot(flat[...], slope[:, span], 0, 0)
            down_part = dot(act[:, span], flat_d[...], 0, 0)
            if k:
                send_up[k - 1] = up_part.astype(BF)
                send_down[k - 1] = down_part.astype(BF)
                first = {2: 0, 1: 2, 3: 4}[k]
                returns[first].start()
                returns[first + 1].start()
            else:
                wide_up[0] = up_part
                wide_down[0] = down_part
                for copy in own_out:
                    copy.start()

    finish_sends = slots_through(place, d_slots, recv, part, other, total, ret, slot_sems, compute, grads)
    for copy in gifts + own:
        copy.start()
    after_back(after, ret, table, d_block, d_after, d_att)
    halo_copy = remote(d_att.at[pl.ds(0, HALO)], halo, halo_sem.at[0], halo_sem.at[1], prv)
    halo_copy.start()
    lay_rows(tokens, x_wide, x)
    acc[...] = jnp.zeros_like(acc)
    for copy in ins[5:9]:
        copy.wait()
    halo_copy.wait_recv()
    halo_copy.wait_send()
    top = jnp.where(iota((HALO, C), 0) < 14 * r, halo[...].astype(F32), d_att[:HALO, :].astype(F32))
    d_att[:HALO, :] = top.astype(BF)

    def group(g, carry):
        attn_group_back(g, d_att, wqkv, wo, qkv, probs, acc)
        return carry

    lax.fori_loop(0, 3, group, 0)
    for arrived, onward in zip(returns, relayed):
        arrived.wait_recv()
        onward.start()
    lax.fori_loop(3, 4, group, 0)
    d_shift[...] = acc[...].astype(BF)
    halo2_copy = remote(d_shift.at[pl.ds(0, HALO)], halo2, halo_sem.at[2], halo_sem.at[3], nxt)
    halo2_copy.start()

    for copy in gifts:
        copy.wait_recv()
    for copy in own + [ins[9]]:
        copy.wait()
    merged_wide[:, :48, :] = dot(mn_all[...].reshape(8 * 48, 4 * C), wred[...]).reshape(8, 48, 256)
    tails = mt_all[...].astype(F32)
    last = jnp.concatenate([tails[:, i, :] for i in range(16)], axis=1)
    last = jnp.concatenate([last, jnp.zeros_like(last)], axis=0).astype(BF)
    merged_wide[:, 48, :] = dot(last, wred[...])[:8]
    for a in range(7):
        merged[:, a] = merged_wide[:, 7 * a:7 * a + 7, :].astype(BF)

    halo2_copy.wait_recv()
    top = jnp.where(iota((HALO, C), 0) < 14 * r, halo2[...].astype(F32), d_shift[:HALO, :].astype(F32))
    x_wide[:HALO, :] = d_after[:HALO, :] + norm_back(x[:HALO, :].astype(F32), top)
    x_wide[HALO:, :] = d_after[HALO:, :] + norm_back(x[HALO:, :].astype(F32), d_shift[HALO:, :].astype(F32))
    for i in range(14):
        tokens_grad[0, i] = x_wide[14 * i:14 * i + 14, :].astype(BF)

    placed = []
    for n, (k, pair) in enumerate(((1, returns[2:4]), (3, returns[4:6]), (2, relayed))):
        expert = (z + k) % 4
        for copy in pair:
            copy.wait_recv()
        turn = (n + 1) % 2
        if turn == 0:
            for copy in own_out:
                copy.wait()
        elif placed:
            for copy in placed[0]:
                copy.wait()
        wide_up[turn] = land_up[k - 1].astype(F32)
        wide_down[turn] = land_down[k - 1].astype(F32)
        out = [
            pltpu.make_async_copy(wide_up.at[turn], up_grad.at[expert], io_sem.at[14 + 2 * n]),
            pltpu.make_async_copy(wide_down.at[turn], down_grad.at[expert], io_sem.at[15 + 2 * n]),
        ]
        for copy in out:
            copy.start()
        placed.append(out)
    for out in placed[1:]:
        for copy in out:
            copy.wait()
    finish_sends()
    for copy in returns + relayed + gifts + [halo2_copy]:
        copy.wait_send()


def bias_pairs():
    spot = np.arange(49)
    py, px = spot // 7, spot % 7
    relative = (py[:, None] - py[None, :] + 6) * 13 + (px[:, None] - px[None, :] + 6)
    table = np.zeros((169, 50, 128), np.float32)
    a, b = np.meshgrid(spot, spot, indexing="ij")
    table[relative.reshape(-1), a.reshape(-1), b.reshape(-1)] = 1.0
    return table.reshape(169, 6400)


def local(
    tokens,
    qkv_weight,
    out_weight,
    position_bias,
    window_shift,
    expert_up,
    expert_down,
    expert_choice,
    combine_weight,
    reduce_weight,
    merged_grad,
):
    meta = jnp.concatenate([expert_choice.reshape(TOK, 1).astype(F32), combine_weight.reshape(TOK, 1)], axis=1)
    meta = jnp.pad(meta, ((0, TP - TOK), (0, 0)))
    pairs = jnp.asarray(bias_pairs(), dtype=BF)
    V = pltpu.VMEM
    D = pltpu.SemaphoreType.DMA

    after, table, merge_norm, mn_tail, d_block, d_slots, qkv, probs, flat_in, act, slope, ups, downs = pl.pallas_call(
        front,
        out_shape=[
            sds((TP, C), BF), sds((TP, 256), BF), sds((48, 4 * C), BF), sds((16, 256), BF), sds((TP, C), F32),
            sds((32, 16, HC), BF), sds((3, 4, TP, GRP), BF), sds((32 * TP, TP), BF), sds((C, C), BF), sds((C, C), BF),
            sds((C, C), BF), sds((4, C, 256), BF), sds((4, 256, C), BF),
        ],
        in_specs=[SM, VM, VM, VM, HB, VM] + [HB] * 5,
        out_specs=[VM] * 6 + [HB] * 7,
        scratch_shapes=[
            V((TP, C), BF), V((TP, C), F32), V((32, 64, 128), F32), V((169, 6400), BF), V((8, 49, 256), F32),
            V((HALO, C), BF), V((HALO, C), BF), V((TP, C), BF), V((TP, TP), F32),
            V((192, TP), BF), V((TP, 192), BF), V((TP, C), F32), V((TP, C), BF),
            V((C, 3 * C), BF), V((C, C), BF), V((4 * C, 256), BF),
            V((3, 4, TP, GRP), BF), V((32 * TP, TP), BF),
            V((8, 48, 4 * C), BF), V((8, 48, 4 * C), BF), V((8, 16, 256), F32),
            V((8, 16, 256), BF), V((8, 16, 256), BF),
            V((4, C, 256), BF), V((4, 256, C), BF), V((C, 256), BF), V((256, C), BF),
            V((32, 16, HC), BF), V((4, 32, 16, HC), BF), V((4, 32, 16, HC), BF),
            V((2, 32, 16, HC), BF), V((2, 32, 16, HC), BF), V((2, 32, 16, HC), BF),
            V((C, C), BF), V((C, C), BF), V((C, C), BF), V((256, C), F32),
            D((15,)), D((4,)), D((8,)), D((8,)), D((4, 8)), *SLOT_SEMS,
        ],
        compiler_params=params(collective_id=0, has_side_effects=True),
        cost_estimate=cost(12 << 30, 60 << 20),
        name="front",
    )(window_shift, tokens, meta, position_bias, pairs, merged_grad, qkv_weight, out_weight,
      expert_up, expert_down, reduce_weight)

    tokens_grad, merged, up_grad, down_grad = pl.pallas_call(
        back,
        out_shape=[
            sds(tokens.shape, BF), sds(merged_grad.shape, BF), sds((4, C, 256), F32), sds((4, 256, C), F32),
        ],
        in_specs=[SM] + [VM] * 7 + [HB] * 10,
        out_specs=[VM] * 2 + [HB] * 2,
        scratch_shapes=[
            V((TP, C), BF), V((TP, C), F32), V((HALO, C), BF), V((HALO, C), BF), V((TP, C), BF), V((TP, C), F32),
            V((TP, C), F32), V((TP, C), BF), V((C, 3 * C), BF), V((C, C), BF), V((4 * C, 256), BF),
            V((3, 4, TP, GRP), BF), V((32 * TP, TP), BF), V((C, C), BF), V((C, C), BF), V((C, C), BF),
            V((4, C, 256), BF), V((4, 256, C), BF),
            V((4, 32, 16, HC), BF), V((4, 32, 16, HC), BF), V((2, 32, 16, HC), BF), V((2, 32, 16, HC), BF),
            V((2, 32, 16, HC), BF), V((C, C), BF), V((3, C, 256), BF), V((3, 256, C), BF), V((C, 256), BF), V((256, C), BF),
            V((3, C, 256), BF), V((3, 256, C), BF), V((2, C, 256), F32), V((2, 256, C), F32),
            V((8, 48, 4 * C), BF), V((8, 16, 256), BF), V((8, 49, 256), F32),
            D((20,)), D((4,)), D((8,)), D((8,)), D((4, 8)), *SLOT_SEMS,
        ],
        compiler_params=pltpu.CompilerParams(
            vmem_limit_bytes=60 * 1024 * 1024, collective_id=1, has_side_effects=True
        ),
        cost_estimate=cost(16 << 30, 60 << 20),
        name="back",
    )(window_shift, tokens, after, table, merge_norm, mn_tail, d_block, d_slots, qkv_weight, out_weight, reduce_weight,
      qkv, probs, flat_in, act, slope, ups, downs)
    return (merged, tokens_grad, up_grad, down_grad)


def solution(mesh):
    placed = (
        P("scene", "row", None, None),
        P(),
        P(),
        P(),
        P(),
        P("scene", None, "row"),
        P("scene", "row", None),
        P("scene", "row", None, None),
        P("scene", "row", None),
        P(None, "scene"),
        P(None, "row", None, "scene"),
    )
    return jax.shard_map(
        local,
        mesh=mesh,
        in_specs=placed,
        out_specs=(
            P(None, "row", None, "scene"),
            P("scene", "row", None, None),
            P("scene", None, "row"),
            P("scene", "row", None),
        ),
        check_vma=False,
    )
```

```python
import functools

import jax
import jax.numpy as jnp
import numpy as np
from jax import lax
from jax.experimental import pallas as pl
from jax.experimental.pallas import tpu as pltpu
from jax.sharding import PartitionSpec as P

MESH = pl.DeviceIdType.MESH
F32 = jnp.float32
BF = jnp.bfloat16
EPS = 1e-5
C = 1024
HC = C // 2
TOK = 196
TP = 208
HALO = 96
GRP = 256
NEG = -1e30
VMEM_BIG = 56 * 1024 * 1024
VM = pl.BlockSpec(memory_space=pltpu.VMEM)
SM = pl.BlockSpec(memory_space=pltpu.SMEM)
HB = pl.BlockSpec(memory_space=pl.ANY)


def sds(shape, dtype):
    return jax.ShapeDtypeStruct(shape, dtype)


def params(**kw):
    return pltpu.CompilerParams(vmem_limit_bytes=VMEM_BIG, **kw)


def cost(flops, nbytes):
    return pl.CostEstimate(flops=flops, bytes_accessed=nbytes, transcendentals=0)


def dot(a, b, da=1, db=0):
    return lax.dot_general(a, b, (((da,), (db,)), ((), ())), preferred_element_type=F32)


def iota(shape, dim):
    return lax.broadcasted_iota(jnp.int32, shape, dim)


def norm_parts(values):
    centre = jnp.mean(values, axis=-1, keepdims=True)
    centred = values - centre
    spread = jnp.mean(centred * centred, axis=-1, keepdims=True)
    scale = lax.rsqrt(spread + EPS)
    return centred * scale, scale


def norm_back(values, cot):
    unit, scale = norm_parts(values)
    mean_cot = jnp.mean(cot, axis=-1, keepdims=True)
    mean_dot = jnp.mean(cot * unit, axis=-1, keepdims=True)
    return scale * (cot - mean_cot - unit * mean_dot)


def split3(values):
    high = values.astype(BF)
    rest = values - high.astype(F32)
    mid = rest.astype(BF)
    low = (rest - mid.astype(F32)).astype(BF)
    return high, mid, low


def place_of(tok, r, c):
    rho = (tok * 4682) >> 16
    gam = tok - 14 * rho
    i = rho - r
    i = jnp.where(i < 0, i + 14, i)
    j = gam - c
    j = jnp.where(j < 0, j + 14, j)
    a = jnp.where(i >= 7, 1, 0)
    b = jnp.where(j >= 7, 1, 0)
    return i, j, a, b


def pos_of(tok, r, c):
    i, j, a, b = place_of(tok, r, c)
    return (i - 7 * a) * 7 + (j - 7 * b)


def group_of(tok, r, c, last):
    i, j, a, b = place_of(tok, r, c)
    la = jnp.where(i >= 7, jnp.where(i < 14 - r, 1, 2), 0) * last
    lb = jnp.where(j >= 7, jnp.where(j < 14 - c, 1, 2), 0)
    return a * 2 + b, la * 3 + lb


def pack_rows(low, high, blocks):
    return jnp.concatenate([low.reshape(blocks, 8, HC), high.reshape(blocks, 8, HC)], axis=1).astype(BF)


def unpack_rows(packed, blocks):
    wide = packed.astype(F32)
    low = wide[:, :8, :].reshape(blocks * 8, HC)
    high = wide[:, 8:, :].reshape(blocks * 8, HC)
    return low, high


def attn_masks(r, c, last, mask, ecol, erow):
    tq, tk = iota((TP, TP), 0), iota((TP, TP), 1)
    wq_, lq = group_of(tq, r, c, last)
    wk_, lk = group_of(tk, r, c, last)
    seen = jnp.where(wq_ == wk_, jnp.where(lq == lk, 0.0, -100.0), NEG)
    mask[...] = jnp.where(tk < TOK, seen, NEG)
    row_pos = pos_of(iota((TP, 192), 0), r, c)
    erow[...] = jnp.where(row_pos == (iota((TP, 192), 1) & 63), 1.0, 0.0).astype(BF)
    col_pos = pos_of(iota((192, TP), 1), r, c)
    ecol[...] = jnp.where(col_pos == (iota((192, TP), 0) & 63), 1.0, 0.0).astype(BF)


def cols(start):
    return pl.ds(pl.multiple_of(start, GRP), GRP)


def attn_group(g, normed, wqkv, wo, bias, mask, ecol, erow, qkv, probs, acc):
    n = normed[...]
    q = dot(n, wqkv[:, cols(g * GRP)]).astype(BF)
    k = dot(n, wqkv[:, cols(C + g * GRP)]).astype(BF)
    v = dot(n, wqkv[:, cols(2 * C + g * GRP)]).astype(BF)
    qkv[0, g] = q
    qkv[1, g] = k
    qkv[2, g] = v
    wide = dot(jnp.concatenate(split3(bias[pl.ds(g * 8, 8)][:, :, :64].reshape(8 * 64, 64)), axis=1), ecol[...])
    w_hi, w_mid, w_lo = split3(wide)
    lane_head = iota((TP, GRP), 1) >> 5
    mixed = jnp.zeros((TP, GRP), F32)
    q32 = q.astype(F32)
    for h in range(8):
        mine = lane_head == h
        qm = jnp.where(mine, q32, 0.0).astype(BF)
        s = dot(qm, k, 1, 1) * (32.0 ** -0.5)
        part = slice(h * 64, h * 64 + 64)
        s = s + dot(erow[...], jnp.concatenate([w_hi[part], w_mid[part], w_lo[part]], axis=0)) + mask[...]
        e = jnp.exp(s - jnp.max(s, axis=-1, keepdims=True))
        p = (e / jnp.sum(e, axis=-1, keepdims=True)).astype(BF)
        probs[pl.ds(pl.multiple_of((g * 8 + h) * TP, 16), TP), :] = p
        mixed = jnp.where(mine, dot(p, v), mixed)
    acc[...] += dot(mixed.astype(BF), wo[pl.ds(pl.multiple_of(g * GRP, GRP), GRP), :])


def attn_group_back(g, d_att, wqkv, wo, qkv, probs, acc):
    q, k, v = qkv[0, g], qkv[1, g], qkv[2, g]
    d_mixed = dot(d_att[...], wo[pl.ds(pl.multiple_of(g * GRP, GRP), GRP), :], 1, 1).astype(BF).astype(F32)
    q32 = q.astype(F32)
    lane_head = iota((TP, GRP), 1) >> 5
    dq = jnp.zeros((TP, GRP), F32)
    dk = jnp.zeros((TP, GRP), F32)
    dv = jnp.zeros((TP, GRP), F32)
    for h in range(8):
        mine = lane_head == h
        dm = jnp.where(mine, d_mixed, 0.0).astype(BF)
        qm = jnp.where(mine, q32, 0.0).astype(BF)
        p = probs[pl.ds(pl.multiple_of((g * 8 + h) * TP, 16), TP), :]
        p32 = p.astype(F32)
        dp = dot(dm, v, 1, 1).astype(BF).astype(F32)
        ds = p32 * (dp - jnp.sum(dp * p32, axis=-1, keepdims=True)) * (32.0 ** -0.5)
        ds = ds.astype(BF)
        dq = jnp.where(mine, dot(ds, k), dq)
        dk = dk + dot(ds, qm, 0, 0)
        dv = dv + dot(p, dm, 0, 0)
    acc[...] += (
        dot(dq.astype(BF), wqkv[:, cols(g * GRP)], 1, 1)
        + dot(dk.astype(BF), wqkv[:, cols(C + g * GRP)], 1, 1)
        + dot(dv.astype(BF), wqkv[:, cols(2 * C + g * GRP)], 1, 1)
    )


def route(r, x, att, halo, choice, after_out, slots, table_out):
    top = jnp.where(iota((HALO, C), 0) < 14 * r, halo[...].astype(F32), att[:HALO, :].astype(F32))
    after_out[:HALO, :] = (x[:HALO, :].astype(F32) + top).astype(BF)
    after_out[HALO:, :] = (x[HALO:, :].astype(F32) + att[HALO:, :].astype(F32)).astype(BF)
    after = after_out[...].astype(F32)
    n2 = norm_parts(after)[0].astype(BF)
    tok, other = iota((TP, TP), 0), iota((TP, TP), 1)
    col = jnp.where(iota((TP, 1), 0) < TOK, choice, -1000.0)
    line = jnp.sum(jnp.where(tok == other, col, 0.0), axis=0, keepdims=True)
    same = jnp.where(col == line, 1.0, 0.0)
    same = jnp.where(other < tok, same, 0.0)
    rank = jnp.sum(same, axis=1, keepdims=True).astype(jnp.int32)
    table = jnp.where(col.astype(jnp.int32) * 8 + rank == iota((TP, 256), 1), 1.0, 0.0).astype(BF)
    table_out[...] = table
    slots[...] = pack_rows(dot(table, n2[:, :HC], 0, 0), dot(table, n2[:, HC:], 0, 0), 32)


def quad_table():
    row = iota((256, TP), 0)
    tok = iota((256, TP), 1)
    q = row >> 6
    n = row & 63
    a = (n * 9363) >> 16
    b = n - 7 * a
    want = (2 * a + (q & 1)) * 14 + 2 * b + (q >> 1)
    hit = jnp.where(want == tok, 1.0, 0.0)
    return jnp.where(n < 49, hit, 0.0).astype(BF)


def gathered(ret, table):
    low, high = unpack_rows(ret[0].astype(F32) + ret[1].astype(F32), 32)
    return jnp.concatenate([dot(table, low.astype(BF)), dot(table, high.astype(BF))], axis=1)


def merge_mid(after, ret, table_in, gate, parts, tail, mn_out, mn_tail, d_block_out, slots, spread, t_wide):
    table = table_in[...]
    block = (after[...].astype(F32) + gate * gathered(ret, table)).astype(BF)
    perm = quad_table()
    quads = dot(perm, block)
    vals = [quads[64 * q:64 * q + 49, :] for q in range(4)]
    inv = 1.0 / (4 * C)
    centre = sum(jnp.sum(v, axis=-1, keepdims=True) for v in vals) * inv
    cent = [v - centre for v in vals]
    var = sum(jnp.sum(v * v, axis=-1, keepdims=True) for v in cent) * inv
    scale = lax.rsqrt(var + EPS)
    unit = [v * scale for v in cent]
    for q in range(4):
        mn_out[:, q * C:(q + 1) * C] = unit[q][:48].astype(BF)
        for i in range(4):
            t_wide[0, 4 * q + i:4 * q + i + 1, :] = unit[q][48:49, i * 256:(i + 1) * 256]
    mn_tail[...] = t_wide[0].astype(BF)
    tails = jnp.sum(tail[...].astype(F32), axis=0)
    cots = []
    for q in range(4):
        tot = sum(part[:, q * C:(q + 1) * C].astype(F32) for part in parts)
        last = jnp.concatenate([tails[4 * q + i:4 * q + i + 1, :] for i in range(4)], axis=1)
        cots.append(jnp.concatenate([tot, last], axis=0))
    mean_cot = sum(jnp.sum(v, axis=-1, keepdims=True) for v in cots) * inv
    mean_dot = sum(jnp.sum(v * u, axis=-1, keepdims=True) for v, u in zip(cots, unit)) * inv
    spread[...] = jnp.zeros_like(spread)
    for q in range(4):
        spread[64 * q:64 * q + 49, :] = scale * (cots[q] - mean_cot - unit[q] * mean_dot)
    high, mid, low = split3(spread[...])
    d_block = dot(perm, high, 0, 0) + dot(perm, mid, 0, 0) + dot(perm, low, 0, 0)
    d_block_out[...] = d_block
    scaled = (gate * d_block).astype(BF)
    slots[...] = pack_rows(dot(table, scaled[:, :HC], 0, 0), dot(table, scaled[:, HC:], 0, 0), 32)


def after_back(after, ret, table, d_block, d_after_out, d_att_out):
    d_second = gathered(ret, table[...])
    d_after = d_block[...] + norm_back(after[...].astype(F32), d_second)
    d_after_out[...] = d_after
    d_att_out[...] = d_after.astype(BF)


def token_column(grid):
    tok = iota((TP, 14), 0)
    rho = (tok * 4682) >> 16
    place = iota((TP, 14), 1)
    pick = jnp.where(rho == place, 1.0, 0.0).astype(BF)
    high, mid, low = split3(grid[...].reshape(14, 14))
    rows = dot(pick, high) + dot(pick, mid) + dot(pick, low)
    return jnp.sum(jnp.where(tok - 14 * rho == place, rows, 0.0), axis=1, keepdims=True)


def lay_rows(tokens, wide, x):
    wide[TOK - 4:, :] = jnp.zeros((TP - TOK + 4, C), F32)
    for i in range(14):
        wide[14 * i:14 * i + 14, :] = tokens[0, i].astype(F32)
    x[...] = wide[...].astype(BF)


def expert_chunk(j, recv, part, ups, downs, flat, act_out, slope_out):
    here = pl.ds(8 * j, 8)
    rows_here = pl.ds(256 * j, 256)
    low, high = unpack_rows(recv[:, here].reshape(32, 16, HC), 32)
    rows = jnp.concatenate([low, high], axis=1).astype(BF)
    flat[rows_here, :] = rows
    total = jnp.zeros((256, C), F32)
    for k in range(4):
        pre = dot(rows, ups[k])
        cdf = 0.5 * (1.0 + lax.erf(pre * np.float32(2.0 ** -0.5)))
        act = (pre * cdf).astype(BF)
        slope = cdf + pre * jnp.exp(-0.5 * pre * pre) * np.float32((2.0 * np.pi) ** -0.5)
        act_out[rows_here, k * 256:(k + 1) * 256] = act
        slope_out[rows_here, k * 256:(k + 1) * 256] = slope.astype(BF)
        total = total + dot(act, downs[k])
    part[:, here] = pack_rows(total[:, :HC], total[:, HC:], 32).reshape(4, 8, 16, HC)


def expert_chunk_back(j, recv, part, ups, downs, flat, slope):
    here = pl.ds(8 * j, 8)
    rows_here = pl.ds(256 * j, 256)
    low, high = unpack_rows(recv[:, here].reshape(32, 16, HC), 32)
    rows = jnp.concatenate([low, high], axis=1).astype(BF)
    flat[rows_here, :] = rows
    total = jnp.zeros((256, C), F32)
    for k in range(4):
        span = slice(k * 256, (k + 1) * 256)
        d_pre = (slope[rows_here, span].astype(F32) * dot(rows, downs[k], 1, 1)).astype(BF)
        slope[rows_here, span] = d_pre
        total = total + dot(d_pre, ups[k], 1, 1)
    part[:, here] = pack_rows(total[:, :HC], total[:, HC:], 32).reshape(4, 8, 16, HC)


def coords():
    s = lax.axis_index("scene")
    row = lax.axis_index("row")
    z, m = row // 4, row % 4
    return s, z, m // 2, m % 2


def at(s, z, y, c):
    return (s, z * 4 + y * 2 + c)


def greet(s, z, y, c, total=64):
    barrier = pltpu.get_barrier_semaphore()
    mine = s * 4 + z

    def hail(k, carry):
        peer = (mine + k) % 32
        pl.semaphore_signal(barrier, inc=1, device_id=at(peer // 4, peer % 4, y, c), device_id_type=MESH)
        pl.semaphore_signal(barrier, inc=1, device_id=at(peer // 4, peer % 4, 1 - y, c), device_id_type=MESH)
        return carry

    lax.fori_loop(1, 32, hail, 0)
    pl.semaphore_signal(barrier, inc=1, device_id=at(s, z, 1 - y, c), device_id_type=MESH)
    pl.semaphore_signal(barrier, inc=1, device_id=at(s, z, y, 1 - c), device_id_type=MESH)
    pl.semaphore_wait(barrier, total)


def greet_all(place):
    s, z, y, c = place
    barrier = pltpu.get_barrier_semaphore()
    row = z * 4 + y * 2 + c
    pl.semaphore_signal(barrier, inc=1, device_id=(s, (row + 1) % 16), device_id_type=MESH)
    pl.semaphore_signal(barrier, inc=1, device_id=(s, (row + 15) % 16), device_id_type=MESH)
    greet(s, z, y, c, 66)


def remote(src, dst, send, recv, device):
    return pltpu.make_async_remote_copy(
        src_ref=src, dst_ref=dst, send_sem=send, recv_sem=recv, device_id=device, device_id_type=MESH
    )


def await_bytes(ref, sem):
    pltpu.make_async_copy(ref, ref, sem).wait()


SLOT_SEMS = [
    pltpu.SemaphoreType.DMA,
    pltpu.SemaphoreType.DMA((2, 4)),
    pltpu.SemaphoreType.DMA((2, 4)),
    pltpu.SemaphoreType.DMA((2, 4)),
    pltpu.SemaphoreType.DMA((2, 4)),
    pltpu.SemaphoreType.DMA((2, 4)),
    pltpu.SemaphoreType.DMA,
    pltpu.SemaphoreType.DMA,
]


def slots_through(place, slots, recv, part, other, total, ret, sems, compute, meanwhile=None):
    s, z, y, c = place
    mine = s * 4 + z
    send, arrive, f_send, f_recv, p_send, p_recv, r_send, r_recv = sems
    pair = at(s, z, y, 1 - c)

    def to_peer(k, peer, yy):
        remote(slots.at[peer], recv.at[y * 2 + c, k], send, arrive.at[y, k // 8], at(peer // 4, peer % 4, yy, c)).start()

    def push(k, carry):
        peer = (mine + k) % 32
        to_peer(k, peer, y)
        to_peer(k, peer, 1 - y)
        return carry

    pltpu.make_async_copy(slots.at[mine], recv.at[y * 2 + c, 0], arrive.at[y, 0]).start()
    to_peer(0, mine, 1 - y)
    lax.fori_loop(1, 32, push, 0)
    forwards, partials = {}, {}

    def forward(j):
        for yy in range(2):
            block = recv.at[yy * 2 + c, pl.ds(8 * j, 8)]
            await_bytes(block, arrive.at[yy, j])
            forwards[yy, j] = remote(block, block, f_send.at[yy, j], f_recv.at[yy, j], pair)
            forwards[yy, j].start()

    def work(j):
        for yy in range(2):
            forwards[yy, j].wait_recv()
        compute(j)
        for yy in range(2):
            here = pl.ds(8 * j, 8)
            partials[yy, j] = remote(
                part.at[yy * 2 + (1 - c), here], other.at[yy, here], p_send.at[yy, j], p_recv.at[yy, j], pair
            )
            partials[yy, j].start()

    def give(k, yy):
        peer = (mine - k + 32) % 32
        remote(total.at[yy, k], ret.at[y, mine], r_send, r_recv, at(peer // 4, peer % 4, yy, c)).start()

    def give_both(k, carry):
        give(k, 1 - y)
        give(k, y)
        return carry

    def back(j):
        here = pl.ds(8 * j, 8)
        for yy in range(2):
            partials[yy, j].wait_recv()
            total[yy, here] = (part[yy * 2 + c, here].astype(F32) + other[yy, here].astype(F32)).astype(BF)
        if j == 0:
            give(0, 1 - y)
            pltpu.make_async_copy(total.at[y, 0], ret.at[y, mine], r_recv).start()
        lax.fori_loop(max(1, 8 * j), 8 * j + 8, give_both, 0)

    forward(0)
    forward(1)
    work(0)
    forward(2)
    work(1)
    back(0)
    forward(3)
    work(2)
    back(1)
    work(3)
    back(2)
    back(3)

    def finish_sends():
        for copy in list(forwards.values()) + list(partials.values()):
            copy.wait_send()
        for sem in (send, r_send):
            await_bytes(total.at[0], sem)
            await_bytes(total.at[0, pl.ds(0, 31)], sem)

    if meanwhile is not None:
        meanwhile()
    await_bytes(ret, r_recv)
    return finish_sends


def front(
    shift, tokens, choice_in, gate_in, position_bias, pairs, merged_grad, qkv_weight, out_weight, expert_up, expert_down, reduce_weight,
    after, table, merge_norm, mn_tail, d_block, d_slots, qkv_out, probs_out, flat_out, act_out, slope_out, up_out, down_out,
    x, x_wide, bias, table_of, grad_wide, halo, halo2, normed, mask, ecol, erow, acc, att, wqkv, wo, wred, qkv, probs,
    d_send, d_relay, d_direct, d_summed, d_across, t_wide, t_send, t_recv, ups, downs, relay_up, relay_down,
    slots, recv, part, other, total, ret, flat, act, slope, spread,
    io_sem, halo_sem, w_send, w_recv, d_sem, *slot_sems,
):
    place = coords()
    s, z, y, c = place
    row = z * 4 + y * 2 + c
    r, cc = shift[0], shift[1]
    last = jnp.where(row == 15, 1, 0)
    ins = [
        pltpu.make_async_copy(reduce_weight, wred, io_sem.at[0]),
        pltpu.make_async_copy(qkv_weight, wqkv, io_sem.at[1]),
        pltpu.make_async_copy(out_weight, wo, io_sem.at[2]),
        pltpu.make_async_copy(expert_up.at[z], ups.at[0], io_sem.at[3]),
        pltpu.make_async_copy(expert_down.at[z], downs.at[0], io_sem.at[4]),
        pltpu.make_async_copy(pairs, table_of, io_sem.at[14]),
    ]
    for copy in ins:
        copy.start()
    lay_rows(tokens, x_wide, x)
    greet_all(place)

    nxt = (s, (row + 1) % 16)
    prv = (s, (row + 15) % 16)
    z_up, z_down = at(s, (z + 1) % 4, y, c), at(s, (z + 3) % 4, y, c)
    halo_copy = remote(x.at[pl.ds(0, HALO)], halo, halo_sem.at[0], halo_sem.at[1], prv)
    halo_copy.start()
    weights = [
        remote(expert_up.at[(z + 2) % 4], relay_up, w_send.at[0], w_recv.at[0], z_up),
        remote(expert_down.at[(z + 2) % 4], relay_down, w_send.at[1], w_recv.at[1], z_down),
        remote(expert_up.at[(z + 1) % 4], ups.at[1], w_send.at[2], w_recv.at[2], z_up),
        remote(expert_up.at[(z + 3) % 4], ups.at[3], w_send.at[3], w_recv.at[3], z_down),
        remote(expert_down.at[(z + 1) % 4], downs.at[1], w_send.at[4], w_recv.at[4], z_up),
        remote(expert_down.at[(z + 3) % 4], downs.at[3], w_send.at[5], w_recv.at[5], z_down),
    ]
    for copy in weights:
        copy.start()
    relayed = [
        remote(relay_up, ups.at[2], w_send.at[6], w_recv.at[6], z_up),
        remote(relay_down, downs.at[2], w_send.at[7], w_recv.at[7], z_down),
    ]

    by_place = merged_grad[...].astype(F32).reshape(49, 8, 256)
    for n in range(8):
        grad_wide[n] = by_place[:, n, :]
    grad48 = grad_wide[:, :48, :].astype(BF).reshape(8 * 48, 256)
    grad_tail = jnp.concatenate([grad_wide[:, 48, :], jnp.zeros((8, 256), F32)], axis=0).astype(BF)
    ins[0].wait()
    for half in range(4):
        span = pl.ds(half * C, C)
        d_send[:, :, span] = dot(grad48, wred[span, :], 1, 1).astype(BF).reshape(8, 48, C)
        tail = dot(grad_tail, wred[span, :], 1, 1)
        for i in range(4):
            t_wide[:, 4 * half + i, :] = tail[:8, i * 256:(i + 1) * 256]
    t_send[...] = t_wide[...].astype(BF)
    yh, xx = s // 4, s % 4
    x_up, x_down, x_far = (xx + 1) % 4, (xx + 3) % 4, (xx + 2) % 4
    to_up, to_down = at(yh * 4 + x_up, z, y, c), at(yh * 4 + x_down, z, y, c)
    first = [
        remote(d_send.at[x_far], d_relay.at[0], d_sem.at[0, 0], d_sem.at[1, 0], to_up),
        remote(d_send.at[4 + x_far], d_relay.at[1], d_sem.at[0, 1], d_sem.at[1, 1], to_down),
        remote(d_send.at[4 + x_up], d_direct.at[1], d_sem.at[0, 2], d_sem.at[1, 2], to_up),
        remote(d_send.at[x_down], d_direct.at[0], d_sem.at[0, 3], d_sem.at[1, 3], to_down),
    ]
    second = [
        remote(d_send.at[x_up], d_summed.at[0], d_sem.at[0, 4], d_sem.at[1, 4], to_up),
        remote(d_send.at[4 + x_down], d_summed.at[1], d_sem.at[0, 5], d_sem.at[1, 5], to_down),
    ]
    other_yh = 1 - yh
    across = remote(
        d_send.at[other_yh * 4 + xx], d_across, d_sem.at[0, 6], d_sem.at[1, 6], at(other_yh * 4 + xx, z, y, c)
    )
    gifts = []
    for k in range(1, 8):
        peer = (s + k) % 8
        gifts.append(remote(t_send.at[peer], t_recv.at[s], d_sem.at[2, k], d_sem.at[3, k], at(peer, z, y, c)))
    for copy in first + gifts:
        copy.start()
    own = pltpu.make_async_copy(t_send.at[s], t_recv.at[s], io_sem.at[6])
    own.start()

    def pass_on():
        for i, mine_at in enumerate((x_up, 4 + x_down)):
            first[i].wait_recv()
            d_send[mine_at] = (d_send[mine_at].astype(F32) + d_relay[i].astype(F32)).astype(BF)
            second[i].start()

    def cross():
        for copy in first[2:] + second:
            copy.wait_recv()
        there = other_yh * 4 + xx
        d_send[there] = (
            d_send[there].astype(F32) + d_direct[other_yh].astype(F32) + d_summed[other_yh].astype(F32)
        ).astype(BF)
        across.start()

    attn_masks(r, cc, last, mask, ecol, erow)
    ins[5].wait()
    bias[...] = jnp.zeros_like(bias)
    parts3 = jnp.concatenate(split3(position_bias[...]), axis=0)
    for pair in range(25):
        wide = dot(parts3, table_of[:, pair * 256:(pair + 1) * 256])
        wide = wide[:32] + wide[32:64] + wide[64:]
        for i in range(2):
            if 2 * pair + i < 49:
                bias[:, 2 * pair + i, :] = wide[:, i * 128:(i + 1) * 128]
    normed[HALO:, :] = norm_parts(x[HALO:, :].astype(F32))[0].astype(BF)
    acc[...] = jnp.zeros_like(acc)
    halo_copy.wait_recv()
    top = jnp.where(iota((HALO, C), 0) < 14 * r, halo[...].astype(F32), x[:HALO, :].astype(F32))
    normed[:HALO, :] = norm_parts(top)[0].astype(BF)
    ins[1].wait()
    ins[2].wait()

    def group(g, carry):
        attn_group(g, normed, wqkv, wo, bias, mask, ecol, erow, qkv, probs, acc)
        return carry

    lax.fori_loop(0, 1, group, 0)
    pass_on()
    lax.fori_loop(1, 3, group, 0)
    for arrived, onward in zip(weights, relayed):
        arrived.wait_recv()
        onward.start()
    lax.fori_loop(3, 4, group, 0)
    att[...] = acc[...].astype(BF)
    halo2_copy = remote(att.at[pl.ds(0, HALO)], halo2, halo_sem.at[2], halo_sem.at[3], nxt)
    halo2_copy.start()
    outs = [
        pltpu.make_async_copy(qkv, qkv_out, io_sem.at[7]),
        pltpu.make_async_copy(probs, probs_out, io_sem.at[8]),
    ]
    for copy in outs:
        copy.start()
    cross()
    halo2_copy.wait_recv()
    choice = token_column(choice_in[...].astype(F32))
    route(r, x, att, halo2, choice, after, slots, table)

    def compute(j):
        if j == 0:
            for copy in weights[2:] + relayed:
                copy.wait_recv()
            ins[3].wait()
            ins[4].wait()
        expert_chunk(j, recv, part, ups, downs, flat, act, slope)

    finish_sends = slots_through(place, slots, recv, part, other, total, ret, slot_sems, compute)
    more = [
        pltpu.make_async_copy(flat, flat_out, io_sem.at[9]),
        pltpu.make_async_copy(act, act_out, io_sem.at[10]),
        pltpu.make_async_copy(slope, slope_out, io_sem.at[11]),
        pltpu.make_async_copy(ups, up_out, io_sem.at[12]),
        pltpu.make_async_copy(downs, down_out, io_sem.at[13]),
    ]
    for copy in more:
        copy.start()
    for copy in gifts + [across]:
        copy.wait_recv()
    own.wait()
    parts = (d_send.at[s], d_direct.at[yh], d_summed.at[yh], d_across)
    merge_mid(after, ret, table, token_column(gate_in), parts, t_recv, merge_norm, mn_tail, d_block, d_slots, spread, t_wide)
    for copy in outs + more:
        copy.wait()
    finish_sends()
    for copy in weights + relayed + gifts + first + second + [across, halo_copy, halo2_copy]:
        copy.wait_send()


def back(
    shift, tokens, after, table, merge_norm, mn_tail, d_block, d_slots,
    qkv_weight, out_weight, reduce_weight, qkv_in, probs_in, flat_in, act_in, slope_in, up_in, down_in,
    tokens_grad, merged, up_grad, down_grad,
    x, x_wide, halo, halo2, d_att, acc, d_after, d_shift, wqkv, wo, wred, qkv, probs, flat, act, slope, ups, downs,
    recv, part, other, total, ret, flat_d, send_up, send_down, relay_up, relay_down,
    mn_all, mt_all, merged_wide, merged_rows,
    io_sem, halo_sem, g_send, g_recv, m_sem, *slot_sems,
):
    place = coords()
    s, z, y, c = place
    row = z * 4 + y * 2 + c
    r = shift[0]
    loads = [
        (down_in, downs), (slope_in, slope), (up_in, ups), (act_in, act), (flat_in, flat),
        (out_weight, wo), (qkv_in, qkv), (probs_in, probs), (qkv_weight, wqkv), (reduce_weight, wred),
    ]
    ins = [pltpu.make_async_copy(a, b, io_sem.at[i]) for i, (a, b) in enumerate(loads)]
    for copy in ins:
        copy.start()
    greet_all(place)
    nxt = (s, (row + 1) % 16)
    prv = (s, (row + 15) % 16)
    z_up, z_down = at(s, (z + 1) % 4, y, c), at(s, (z + 3) % 4, y, c)

    def compute(j):
        if j == 0:
            for copy in ins[:3]:
                copy.wait()
        expert_chunk_back(j, recv, part, ups, downs, flat_d, slope)

    returns = [
        remote(send_up.at[1], relay_up, g_send.at[0], g_recv.at[0], z_up),
        remote(send_down.at[1], relay_down, g_send.at[1], g_recv.at[1], z_down),
        remote(send_up.at[0], up_grad.at[z], g_send.at[2], g_recv.at[2], z_down),
        remote(send_down.at[0], down_grad.at[z], g_send.at[3], g_recv.at[3], z_down),
        remote(send_up.at[2], up_grad.at[z], g_send.at[4], g_recv.at[4], z_up),
        remote(send_down.at[2], down_grad.at[z], g_send.at[5], g_recv.at[5], z_up),
    ]
    relayed = [
        remote(relay_up, up_grad.at[(z + 3) % 4], g_send.at[6], g_recv.at[6], z_up),
        remote(relay_down, down_grad.at[(z + 1) % 4], g_send.at[7], g_recv.at[7], z_down),
    ]
    yh, xx = s // 4, s % 4
    x_up, x_down = (xx + 1) % 4, (xx + 3) % 4
    to_up, to_down = at(yh * 4 + x_up, z, y, c), at(yh * 4 + x_down, z, y, c)
    across = (1 - yh) * 4 + xx
    half = (pl.ds(0, 2 * C), pl.ds(2 * C, 2 * C))

    def neighbours(source, slot, n):
        return [
            remote(source, mn_all.at[slot], m_sem.at[0, n], m_sem.at[1, n], to_up),
            remote(source, mn_all.at[slot], m_sem.at[0, n + 1], m_sem.at[1, n + 1], to_down),
        ]

    def halves(base, n):
        below, above = base * 4 + x_down, base * 4 + x_up
        low, high = mn_all.at[below, :, half[0]], mn_all.at[above, :, half[1]]
        return [
            remote(low, low, m_sem.at[0, n], m_sem.at[1, n], to_up),
            remote(high, high, m_sem.at[0, n + 1], m_sem.at[1, n + 1], to_down),
        ]

    spread_own = neighbours(merge_norm, s, 0)
    spread_across = neighbours(mn_all.at[across], across, 2)
    far_own = halves(yh, 4)
    far_across = halves(1 - yh, 6)
    partner = remote(merge_norm, mn_all.at[s], m_sem.at[0, 8], m_sem.at[1, 8], at(across, z, y, c))
    tail_copies = []
    for k in range(1, 8):
        peer = (s + k) % 8
        tail_copies.append(remote(mn_tail, mt_all.at[s], m_sem.at[2, k], m_sem.at[3, k], at(peer, z, y, c)))
    gifts = spread_own + spread_across + far_own + far_across + [partner] + tail_copies
    own = [
        pltpu.make_async_copy(merge_norm, mn_all.at[s], io_sem.at[10]),
        pltpu.make_async_copy(mn_tail, mt_all.at[s], io_sem.at[11]),
    ]
    own_out = [
        pltpu.make_async_copy(send_up.at[3], up_grad.at[z], io_sem.at[12]),
        pltpu.make_async_copy(send_down.at[3], down_grad.at[z], io_sem.at[13]),
    ]

    def grads():
        for copy in ins[3:5]:
            copy.wait()
        for k in (2, 1, 3, 0):
            span = slice(k * 256, (k + 1) * 256)
            up_part = dot(flat[...], slope[:, span], 0, 0)
            down_part = dot(act[:, span], flat_d[...], 0, 0)
            send_up[(k + 3) % 4] = up_part.astype(BF)
            send_down[(k + 3) % 4] = down_part.astype(BF)
            if k:
                first = {2: 0, 1: 2, 3: 4}[k]
                returns[first].start()
                returns[first + 1].start()
            else:
                for copy in own_out:
                    copy.start()

    finish_sends = slots_through(place, d_slots, recv, part, other, total, ret, slot_sems, compute, grads)
    for copy in spread_own + [partner] + tail_copies + own:
        copy.start()
    after_back(after, ret, table, d_block, d_after, d_att)
    halo_copy = remote(d_att.at[pl.ds(0, HALO)], halo, halo_sem.at[0], halo_sem.at[1], prv)
    halo_copy.start()
    lay_rows(tokens, x_wide, x)
    acc[...] = jnp.zeros_like(acc)
    for copy in ins[5:9]:
        copy.wait()
    halo_copy.wait_recv()
    halo_copy.wait_send()
    top = jnp.where(iota((HALO, C), 0) < 14 * r, halo[...].astype(F32), d_att[:HALO, :].astype(F32))
    d_att[:HALO, :] = top.astype(BF)

    def group(g, carry):
        attn_group_back(g, d_att, wqkv, wo, qkv, probs, acc)
        return carry

    lax.fori_loop(0, 1, group, 0)
    for arrived, onward in zip(spread_own, far_own):
        arrived.wait_recv()
        onward.start()
    lax.fori_loop(1, 2, group, 0)
    partner.wait_recv()
    for onward in spread_across:
        onward.start()
    lax.fori_loop(2, 3, group, 0)
    for arrived, onward in zip(returns, relayed):
        arrived.wait_recv()
        onward.start()
    lax.fori_loop(3, 4, group, 0)
    d_shift[...] = acc[...].astype(BF)
    halo2_copy = remote(d_shift.at[pl.ds(0, HALO)], halo2, halo_sem.at[2], halo_sem.at[3], nxt)
    halo2_copy.start()

    for arrived, onward in zip(spread_across, far_across):
        arrived.wait_recv()
        onward.start()
    halo2_copy.wait_recv()
    top = jnp.where(iota((HALO, C), 0) < 14 * r, halo2[...].astype(F32), d_shift[:HALO, :].astype(F32))
    x_wide[:HALO, :] = d_after[:HALO, :] + norm_back(x[:HALO, :].astype(F32), top)
    x_wide[HALO:, :] = d_after[HALO:, :] + norm_back(x[HALO:, :].astype(F32), d_shift[HALO:, :].astype(F32))
    for i in range(14):
        tokens_grad[0, i] = x_wide[14 * i:14 * i + 14, :].astype(BF)

    for copy in far_own + far_across + tail_copies:
        copy.wait_recv()
    for copy in own + [ins[9]]:
        copy.wait()
    merged_wide[:, :48, :] = dot(mn_all[...].reshape(8 * 48, 4 * C), wred[...]).reshape(8, 48, 256)
    tails = mt_all[...].astype(F32)
    last = jnp.concatenate([tails[:, i, :] for i in range(16)], axis=1)
    last = jnp.concatenate([last, jnp.zeros_like(last)], axis=0).astype(BF)
    merged_wide[:, 48, :] = dot(last, wred[...])[:8]
    for n in range(8):
        merged_rows[:, n, :] = merged_wide[n]
    merged[...] = merged_rows[...].reshape(7, 7, 8, 256).astype(BF)

    for copy in returns[2:] + relayed:
        copy.wait_recv()
    for copy in own_out:
        copy.wait()
    finish_sends()
    for copy in returns + relayed + gifts + [halo2_copy]:
        copy.wait_send()


def bias_pairs():
    spot = np.arange(49)
    py, px = spot // 7, spot % 7
    relative = (py[:, None] - py[None, :] + 6) * 13 + (px[:, None] - px[None, :] + 6)
    table = np.zeros((169, 50, 128), np.float32)
    a, b = np.meshgrid(spot, spot, indexing="ij")
    table[relative.reshape(-1), a.reshape(-1), b.reshape(-1)] = 1.0
    return table.reshape(169, 6400)


def local(
    tokens,
    qkv_weight,
    out_weight,
    position_bias,
    window_shift,
    expert_up,
    expert_down,
    expert_choice,
    combine_weight,
    reduce_weight,
    merged_grad,
):
    choice = jnp.transpose(expert_choice, (1, 0, 3, 2)).reshape(14, 1, 14)
    gate = jnp.transpose(combine_weight, (1, 0, 2))
    pairs = jnp.asarray(bias_pairs(), dtype=BF)
    V = pltpu.VMEM
    D = pltpu.SemaphoreType.DMA

    after, table, merge_norm, mn_tail, d_block, d_slots, qkv, probs, flat_in, act, slope, ups, downs = pl.pallas_call(
        front,
        out_shape=[
            sds((TP, C), BF), sds((TP, 256), BF), sds((48, 4 * C), BF), sds((16, 256), BF), sds((TP, C), F32),
            sds((32, 16, HC), BF), sds((3, 4, TP, GRP), BF), sds((32 * TP, TP), BF), sds((C, C), BF), sds((C, C), BF),
            sds((C, C), BF), sds((4, C, 256), BF), sds((4, 256, C), BF),
        ],
        in_specs=[SM, VM, VM, VM, VM, HB, VM] + [HB] * 5,
        out_specs=[VM] * 6 + [HB] * 7,
        scratch_shapes=[
            V((TP, C), BF), V((TP, C), F32), V((32, 64, 128), F32), V((169, 6400), BF), V((8, 49, 256), F32),
            V((HALO, C), BF), V((HALO, C), BF), V((TP, C), BF), V((TP, TP), F32),
            V((192, TP), BF), V((TP, 192), BF), V((TP, C), F32), V((TP, C), BF),
            V((C, 3 * C), BF), V((C, C), BF), V((4 * C, 256), BF),
            V((3, 4, TP, GRP), BF), V((32 * TP, TP), BF),
            V((8, 48, 4 * C), BF), V((2, 48, 4 * C), BF), V((2, 48, 4 * C), BF), V((2, 48, 4 * C), BF),
            V((48, 4 * C), BF), V((8, 16, 256), F32),
            V((8, 16, 256), BF), V((8, 16, 256), BF),
            V((4, C, 256), BF), V((4, 256, C), BF), V((C, 256), BF), V((256, C), BF),
            V((32, 16, HC), BF), V((4, 32, 16, HC), BF), V((4, 32, 16, HC), BF),
            V((2, 32, 16, HC), BF), V((2, 32, 16, HC), BF), V((2, 32, 16, HC), BF),
            V((C, C), BF), V((C, C), BF), V((C, C), BF), V((256, C), F32),
            D((15,)), D((4,)), D((8,)), D((8,)), D((4, 8)), *SLOT_SEMS,
        ],
        compiler_params=params(collective_id=0, has_side_effects=True),
        cost_estimate=cost(12 << 30, 60 << 20),
        name="front",
    )(window_shift, tokens, choice, gate, position_bias, pairs, jnp.transpose(merged_grad, (1, 2, 0, 3)), qkv_weight, out_weight,
      expert_up, expert_down, reduce_weight)

    tokens_grad, merged, up_grad, down_grad = pl.pallas_call(
        back,
        out_shape=[
            sds(tokens.shape, BF), sds((7, 7, 8, 256), BF), sds((4, C, 256), BF), sds((4, 256, C), BF),
        ],
        in_specs=[SM] + [VM] * 7 + [HB] * 10,
        out_specs=[VM] * 2 + [HB] * 2,
        scratch_shapes=[
            V((TP, C), BF), V((TP, C), F32), V((HALO, C), BF), V((HALO, C), BF), V((TP, C), BF), V((TP, C), F32),
            V((TP, C), F32), V((TP, C), BF), V((C, 3 * C), BF), V((C, C), BF), V((4 * C, 256), BF),
            V((3, 4, TP, GRP), BF), V((32 * TP, TP), BF), V((C, C), BF), V((C, C), BF), V((C, C), BF),
            V((4, C, 256), BF), V((4, 256, C), BF),
            V((4, 32, 16, HC), BF), V((4, 32, 16, HC), BF), V((2, 32, 16, HC), BF), V((2, 32, 16, HC), BF),
            V((2, 32, 16, HC), BF), V((C, C), BF), V((4, C, 256), BF), V((4, 256, C), BF), V((C, 256), BF), V((256, C), BF),
            V((8, 48, 4 * C), BF), V((8, 16, 256), BF), V((8, 49, 256), F32), V((49, 8, 256), F32),
            D((20,)), D((4,)), D((8,)), D((8,)), D((4, 9)), *SLOT_SEMS,
        ],
        compiler_params=pltpu.CompilerParams(
            vmem_limit_bytes=60 * 1024 * 1024, collective_id=1, has_side_effects=True
        ),
        cost_estimate=cost(16 << 30, 60 << 20),
        name="back",
    )(window_shift, tokens, after, table, merge_norm, mn_tail, d_block, d_slots, qkv_weight, out_weight, reduce_weight,
      qkv, probs, flat_in, act, slope, ups, downs)
    return (jnp.transpose(merged, (2, 0, 1, 3)), tokens_grad, up_grad.astype(F32), down_grad.astype(F32))


def solution(mesh):
    placed = (
        P("scene", "row", None, None),
        P(),
        P(),
        P(),
        P(),
        P("scene", None, "row"),
        P("scene", "row", None),
        P("scene", "row", None, None),
        P("scene", "row", None),
        P(None, "scene"),
        P(None, "row", None, "scene"),
    )
    return jax.shard_map(
        local,
        mesh=mesh,
        in_specs=placed,
        out_specs=(
            P(None, "row", None, "scene"),
            P("scene", "row", None, None),
            P("scene", None, "row"),
            P("scene", "row", None),
        ),
        check_vma=False,
    )
```

```python
import functools

import jax
import jax.numpy as jnp
import numpy as np
from jax import lax
from jax.experimental import pallas as pl
from jax.experimental.pallas import tpu as pltpu
from jax.sharding import PartitionSpec as P

MESH = pl.DeviceIdType.MESH
F32 = jnp.float32
BF = jnp.bfloat16
EPS = 1e-5
C = 1024
HC = C // 2
TOK = 196
TP = 208
HALO = 96
GRP = 256
NEG = -1e30
VMEM_BIG = 56 * 1024 * 1024
VM = pl.BlockSpec(memory_space=pltpu.VMEM)
SM = pl.BlockSpec(memory_space=pltpu.SMEM)
HB = pl.BlockSpec(memory_space=pl.ANY)


def sds(shape, dtype):
    return jax.ShapeDtypeStruct(shape, dtype)


def params(**kw):
    return pltpu.CompilerParams(vmem_limit_bytes=VMEM_BIG, **kw)


def cost(flops, nbytes):
    return pl.CostEstimate(flops=flops, bytes_accessed=nbytes, transcendentals=0)


def dot(a, b, da=1, db=0):
    return lax.dot_general(a, b, (((da,), (db,)), ((), ())), preferred_element_type=F32)


def iota(shape, dim):
    return lax.broadcasted_iota(jnp.int32, shape, dim)


def norm_parts(values):
    centre = jnp.mean(values, axis=-1, keepdims=True)
    centred = values - centre
    spread = jnp.mean(centred * centred, axis=-1, keepdims=True)
    scale = lax.rsqrt(spread + EPS)
    return centred * scale, scale


def norm_back(values, cot):
    unit, scale = norm_parts(values)
    mean_cot = jnp.mean(cot, axis=-1, keepdims=True)
    mean_dot = jnp.mean(cot * unit, axis=-1, keepdims=True)
    return scale * (cot - mean_cot - unit * mean_dot)


def split3(values):
    high = values.astype(BF)
    rest = values - high.astype(F32)
    mid = rest.astype(BF)
    low = (rest - mid.astype(F32)).astype(BF)
    return high, mid, low


def place_of(tok, r, c):
    rho = (tok * 4682) >> 16
    gam = tok - 14 * rho
    i = rho - r
    i = jnp.where(i < 0, i + 14, i)
    j = gam - c
    j = jnp.where(j < 0, j + 14, j)
    a = jnp.where(i >= 7, 1, 0)
    b = jnp.where(j >= 7, 1, 0)
    return i, j, a, b


def pos_of(tok, r, c):
    i, j, a, b = place_of(tok, r, c)
    return (i - 7 * a) * 7 + (j - 7 * b)


def group_of(tok, r, c, last):
    i, j, a, b = place_of(tok, r, c)
    la = jnp.where(i >= 7, jnp.where(i < 14 - r, 1, 2), 0) * last
    lb = jnp.where(j >= 7, jnp.where(j < 14 - c, 1, 2), 0)
    return a * 2 + b, la * 3 + lb


def pack_rows(low, high, blocks):
    return jnp.concatenate([low.reshape(blocks, 8, HC), high.reshape(blocks, 8, HC)], axis=1).astype(BF)


def unpack_rows(packed, blocks):
    wide = packed.astype(F32)
    low = wide[:, :8, :].reshape(blocks * 8, HC)
    high = wide[:, 8:, :].reshape(blocks * 8, HC)
    return low, high


def attn_masks(r, c, last, mask, ecol, erow):
    tq, tk = iota((TP, TP), 0), iota((TP, TP), 1)
    wq_, lq = group_of(tq, r, c, last)
    wk_, lk = group_of(tk, r, c, last)
    seen = jnp.where(wq_ == wk_, jnp.where(lq == lk, 0.0, -100.0), NEG)
    mask[...] = jnp.where(tq < TOK, seen, NEG)
    row_pos = pos_of(iota((TP, 192), 0), r, c)
    erow[...] = jnp.where(row_pos == (iota((TP, 192), 1) & 63), 1.0, 0.0).astype(BF)
    col_pos = pos_of(iota((192, TP), 1), r, c)
    ecol[...] = jnp.where(col_pos == (iota((192, TP), 0) & 63), 1.0, 0.0).astype(BF)


def cols(start):
    return pl.ds(pl.multiple_of(start, GRP), GRP)


def turned(values, eye):
    return dot(eye, values, 1, 1)


def unit_table():
    return jnp.where(iota((GRP, GRP), 0) == iota((GRP, GRP), 1), 1.0, 0.0).astype(BF)


def attn_group(g, normed, wqkv, wo, bias, mask, ecol, erow, qkv, probs, mixed, acc):
    n = normed[...]
    q = dot(n, wqkv[:, cols(g * GRP)]).astype(BF)
    k = dot(n, wqkv[:, cols(C + g * GRP)]).astype(BF)
    v = dot(n, wqkv[:, cols(2 * C + g * GRP)]).astype(BF)
    qkv[0, g] = q
    qkv[1, g] = k
    qkv[2, g] = v
    eye = unit_table()
    q_t = turned(q, eye).astype(BF)
    v_t = turned(v, eye).astype(BF)
    wide = dot(jnp.concatenate(split3(bias[pl.ds(g * 8, 8)][:, :, :64].reshape(8 * 64, 64)), axis=1), ecol[...])
    w_hi, w_mid, w_lo = split3(wide)
    lane_head = iota((TP, GRP), 1) >> 5
    k32 = k.astype(F32)
    outs = []
    for h in range(8):
        km = jnp.where(lane_head == h, k32, 0.0).astype(BF)
        part = slice(h * 64, h * 64 + 64)
        s = dot(km, q_t) * (32.0 ** -0.5)
        s = s + dot(erow[...], jnp.concatenate([w_hi[part], w_mid[part], w_lo[part]], axis=0)) + mask[...]
        e = jnp.exp(s - jnp.max(s, axis=0, keepdims=True))
        p = (e * (1.0 / jnp.sum(e, axis=0, keepdims=True))).astype(BF)
        probs[pl.ds(pl.multiple_of((g * 8 + h) * TP, 16), TP), :] = p
        outs.append(dot(v_t[32 * h:32 * h + 32], p))
    mixed_t = jnp.concatenate(outs, axis=0).astype(BF)
    mixed[g] = mixed_t
    acc[...] += dot(mixed_t, wo[pl.ds(pl.multiple_of(g * GRP, GRP), GRP), :], 0, 0)


def attn_group_back(g, d_att, wqkv, wo, qkv, probs, mixed, acc):
    q, k, v = qkv[0, g], qkv[1, g], qkv[2, g]
    eye = unit_table()
    d_out = dot(d_att[...], wo[pl.ds(pl.multiple_of(g * GRP, GRP), GRP), :], 1, 1).astype(BF)
    d_out_t = turned(d_out, eye)
    weighed = d_out_t * mixed[g].astype(F32)
    d_out_t = d_out_t.astype(BF)
    k_t = turned(k, eye).astype(BF)
    v32 = v.astype(F32)
    lane_head = iota((TP, GRP), 1) >> 5
    dq_t = []
    dk = jnp.zeros((TP, GRP), F32)
    dv = jnp.zeros((TP, GRP), F32)
    for h in range(8):
        mine = lane_head == h
        vm = jnp.where(mine, v32, 0.0).astype(BF)
        p = probs[pl.ds(pl.multiple_of((g * 8 + h) * TP, 16), TP), :]
        shared = jnp.sum(weighed[32 * h:32 * h + 32], axis=0, keepdims=True)
        ds = (p.astype(F32) * (dot(vm, d_out_t) - shared)).astype(BF)
        dq_t.append(dot(k_t[32 * h:32 * h + 32], ds))
        dk = jnp.where(mine, dot(ds, q), dk)
        dv = jnp.where(mine, dot(p, d_out), dv)
    scale = 32.0 ** -0.5
    dq = jnp.transpose(jnp.concatenate(dq_t, axis=0) * scale)
    acc[...] += (
        dot(dq.astype(BF), wqkv[:, cols(g * GRP)], 1, 1)
        + dot((dk * scale).astype(BF), wqkv[:, cols(C + g * GRP)], 1, 1)
        + dot(dv.astype(BF), wqkv[:, cols(2 * C + g * GRP)], 1, 1)
    )


def route(r, x, att, halo, choice, after_out, slots, table_out):
    top = jnp.where(iota((HALO, C), 0) < 14 * r, halo[...].astype(F32), att[:HALO, :].astype(F32))
    after_out[:HALO, :] = (x[:HALO, :].astype(F32) + top).astype(BF)
    after_out[HALO:, :] = (x[HALO:, :].astype(F32) + att[HALO:, :].astype(F32)).astype(BF)
    after = after_out[...].astype(F32)
    n2 = norm_parts(after)[0].astype(BF)
    tok, other = iota((TP, TP), 0), iota((TP, TP), 1)
    col = jnp.where(iota((TP, 1), 0) < TOK, choice, -1000.0)
    line = jnp.sum(jnp.where(tok == other, col, 0.0), axis=0, keepdims=True)
    same = jnp.where(col == line, 1.0, 0.0)
    same = jnp.where(other < tok, same, 0.0)
    rank = jnp.sum(same, axis=1, keepdims=True).astype(jnp.int32)
    table = jnp.where(col.astype(jnp.int32) * 8 + rank == iota((TP, 256), 1), 1.0, 0.0).astype(BF)
    table_out[...] = table
    slots[...] = pack_rows(dot(table, n2[:, :HC], 0, 0), dot(table, n2[:, HC:], 0, 0), 32)


def quad_table():
    row = iota((256, TP), 0)
    tok = iota((256, TP), 1)
    q = row >> 6
    n = row & 63
    a = (n * 9363) >> 16
    b = n - 7 * a
    want = (2 * a + (q & 1)) * 14 + 2 * b + (q >> 1)
    hit = jnp.where(want == tok, 1.0, 0.0)
    return jnp.where(n < 49, hit, 0.0).astype(BF)


def gathered(ret, table):
    low, high = unpack_rows(ret[0].astype(F32) + ret[1].astype(F32), 32)
    return jnp.concatenate([dot(table, low.astype(BF)), dot(table, high.astype(BF))], axis=1)


def merge_mid(after, ret, table_in, gate, parts, tail, mn_out, mn_tail, d_block_out, slots, spread, t_wide):
    table = table_in[...]
    block = (after[...].astype(F32) + gate * gathered(ret, table)).astype(BF)
    perm = quad_table()
    quads = dot(perm, block)
    vals = [quads[64 * q:64 * q + 49, :] for q in range(4)]
    inv = 1.0 / (4 * C)
    centre = sum(jnp.sum(v, axis=-1, keepdims=True) for v in vals) * inv
    cent = [v - centre for v in vals]
    var = sum(jnp.sum(v * v, axis=-1, keepdims=True) for v in cent) * inv
    scale = lax.rsqrt(var + EPS)
    unit = [v * scale for v in cent]
    for q in range(4):
        mn_out[:, q * C:(q + 1) * C] = unit[q][:48].astype(BF)
        for i in range(4):
            t_wide[0, 4 * q + i:4 * q + i + 1, :] = unit[q][48:49, i * 256:(i + 1) * 256]
    mn_tail[...] = t_wide[0].astype(BF)
    tails = jnp.sum(tail[...].astype(F32), axis=0)
    cots = []
    for q in range(4):
        tot = sum(part[:, q * C:(q + 1) * C].astype(F32) for part in parts)
        last = jnp.concatenate([tails[4 * q + i:4 * q + i + 1, :] for i in range(4)], axis=1)
        cots.append(jnp.concatenate([tot, last], axis=0))
    mean_cot = sum(jnp.sum(v, axis=-1, keepdims=True) for v in cots) * inv
    mean_dot = sum(jnp.sum(v * u, axis=-1, keepdims=True) for v, u in zip(cots, unit)) * inv
    spread[...] = jnp.zeros_like(spread)
    for q in range(4):
        spread[64 * q:64 * q + 49, :] = scale * (cots[q] - mean_cot - unit[q] * mean_dot)
    high, mid, low = split3(spread[...])
    d_block = dot(perm, high, 0, 0) + dot(perm, mid, 0, 0) + dot(perm, low, 0, 0)
    d_block_out[...] = d_block
    scaled = (gate * d_block).astype(BF)
    slots[...] = pack_rows(dot(table, scaled[:, :HC], 0, 0), dot(table, scaled[:, HC:], 0, 0), 32)


def after_back(after, ret, table, d_block, d_after_out, d_att_out):
    d_second = gathered(ret, table[...])
    d_after = d_block[...] + norm_back(after[...].astype(F32), d_second)
    d_after_out[...] = d_after
    d_att_out[...] = d_after.astype(BF)


def token_column(grid):
    tok = iota((TP, 14), 0)
    rho = (tok * 4682) >> 16
    place = iota((TP, 14), 1)
    pick = jnp.where(rho == place, 1.0, 0.0).astype(BF)
    high, mid, low = split3(grid[...].reshape(14, 14))
    rows = dot(pick, high) + dot(pick, mid) + dot(pick, low)
    return jnp.sum(jnp.where(tok - 14 * rho == place, rows, 0.0), axis=1, keepdims=True)


def lay_rows(tokens, wide, x):
    wide[TOK - 4:, :] = jnp.zeros((TP - TOK + 4, C), F32)
    for i in range(14):
        wide[14 * i:14 * i + 14, :] = tokens[0, i].astype(F32)
    x[...] = wide[...].astype(BF)


def expert_chunk(j, recv, part, ups, downs, flat, act_out, slope_out):
    here = pl.ds(8 * j, 8)
    rows_here = pl.ds(256 * j, 256)
    low, high = unpack_rows(recv[:, here].reshape(32, 16, HC), 32)
    rows = jnp.concatenate([low, high], axis=1).astype(BF)
    flat[rows_here, :] = rows
    total = jnp.zeros((256, C), F32)
    for k in range(4):
        pre = dot(rows, ups[k])
        cdf = 0.5 * (1.0 + lax.erf(pre * np.float32(2.0 ** -0.5)))
        act = (pre * cdf).astype(BF)
        slope = cdf + pre * jnp.exp(-0.5 * pre * pre) * np.float32((2.0 * np.pi) ** -0.5)
        act_out[rows_here, k * 256:(k + 1) * 256] = act
        slope_out[rows_here, k * 256:(k + 1) * 256] = slope.astype(BF)
        total = total + dot(act, downs[k])
    part[:, here] = pack_rows(total[:, :HC], total[:, HC:], 32).reshape(4, 8, 16, HC)


def expert_chunk_back(j, recv, part, ups, downs, flat, slope):
    here = pl.ds(8 * j, 8)
    rows_here = pl.ds(256 * j, 256)
    low, high = unpack_rows(recv[:, here].reshape(32, 16, HC), 32)
    rows = jnp.concatenate([low, high], axis=1).astype(BF)
    flat[rows_here, :] = rows
    total = jnp.zeros((256, C), F32)
    for k in range(4):
        span = slice(k * 256, (k + 1) * 256)
        d_pre = (slope[rows_here, span].astype(F32) * dot(rows, downs[k], 1, 1)).astype(BF)
        slope[rows_here, span] = d_pre
        total = total + dot(d_pre, ups[k], 1, 1)
    part[:, here] = pack_rows(total[:, :HC], total[:, HC:], 32).reshape(4, 8, 16, HC)


def coords():
    s = lax.axis_index("scene")
    row = lax.axis_index("row")
    z, m = row // 4, row % 4
    return s, z, m // 2, m % 2


def at(s, z, y, c):
    return (s, z * 4 + y * 2 + c)


def greet(s, z, y, c, total=64):
    barrier = pltpu.get_barrier_semaphore()
    mine = s * 4 + z

    def hail(k, carry):
        peer = (mine + k) % 32
        pl.semaphore_signal(barrier, inc=1, device_id=at(peer // 4, peer % 4, y, c), device_id_type=MESH)
        pl.semaphore_signal(barrier, inc=1, device_id=at(peer // 4, peer % 4, 1 - y, c), device_id_type=MESH)
        return carry

    lax.fori_loop(1, 32, hail, 0)
    pl.semaphore_signal(barrier, inc=1, device_id=at(s, z, 1 - y, c), device_id_type=MESH)
    pl.semaphore_signal(barrier, inc=1, device_id=at(s, z, y, 1 - c), device_id_type=MESH)
    pl.semaphore_wait(barrier, total)


def greet_all(place):
    s, z, y, c = place
    barrier = pltpu.get_barrier_semaphore()
    row = z * 4 + y * 2 + c
    pl.semaphore_signal(barrier, inc=1, device_id=(s, (row + 1) % 16), device_id_type=MESH)
    pl.semaphore_signal(barrier, inc=1, device_id=(s, (row + 15) % 16), device_id_type=MESH)
    greet(s, z, y, c, 66)


def remote(src, dst, send, recv, device):
    return pltpu.make_async_remote_copy(
        src_ref=src, dst_ref=dst, send_sem=send, recv_sem=recv, device_id=device, device_id_type=MESH
    )


def await_bytes(ref, sem):
    pltpu.make_async_copy(ref, ref, sem).wait()


SLOT_SEMS = [
    pltpu.SemaphoreType.DMA,
    pltpu.SemaphoreType.DMA((2, 4)),
    pltpu.SemaphoreType.DMA((2, 4)),
    pltpu.SemaphoreType.DMA((2, 4)),
    pltpu.SemaphoreType.DMA((2, 4)),
    pltpu.SemaphoreType.DMA((2, 4)),
    pltpu.SemaphoreType.DMA,
    pltpu.SemaphoreType.DMA,
]


def slots_through(place, slots, recv, part, other, total, ret, sems, compute, meanwhile=None):
    s, z, y, c = place
    mine = s * 4 + z
    yh, xx = s // 4, s % 4

    def steps(k):
        dx = k % 4
        return (k % 8) // 4, dx, (k // 8 + 4 - dx) % 4

    def ahead(k):
        dy, dx, dz = steps(k)
        return ((yh + dy) % 2 * 4 + (xx + dx) % 4) * 4 + (z + dz) % 4

    def behind(k):
        dy, dx, dz = steps(k)
        return ((yh + dy) % 2 * 4 + (xx + 4 - dx) % 4) * 4 + (z + 4 - dz) % 4

    send, arrive, f_send, f_recv, p_send, p_recv, r_send, r_recv = sems
    pair = at(s, z, y, 1 - c)

    def to_peer(k, peer, yy):
        remote(slots.at[peer], recv.at[y * 2 + c, k], send, arrive.at[y, k // 8], at(peer // 4, peer % 4, yy, c)).start()

    def push(k, carry):
        peer = ahead(k)
        to_peer(k, peer, y)
        to_peer(k, peer, 1 - y)
        return carry

    pltpu.make_async_copy(slots.at[mine], recv.at[y * 2 + c, 0], arrive.at[y, 0]).start()
    to_peer(0, mine, 1 - y)
    lax.fori_loop(1, 32, push, 0)
    forwards, partials = {}, {}

    def forward(j):
        for yy in range(2):
            block = recv.at[yy * 2 + c, pl.ds(8 * j, 8)]
            await_bytes(block, arrive.at[yy, j])
            forwards[yy, j] = remote(block, block, f_send.at[yy, j], f_recv.at[yy, j], pair)
            forwards[yy, j].start()

    def work(j):
        for yy in range(2):
            forwards[yy, j].wait_recv()
        compute(j)
        for yy in range(2):
            here = pl.ds(8 * j, 8)
            partials[yy, j] = remote(
                part.at[yy * 2 + (1 - c), here], other.at[yy, here], p_send.at[yy, j], p_recv.at[yy, j], pair
            )
            partials[yy, j].start()

    def give(k, yy):
        peer = behind(k)
        remote(total.at[yy, k], ret.at[y, mine], r_send, r_recv, at(peer // 4, peer % 4, yy, c)).start()

    def give_both(k, carry):
        give(k, 1 - y)
        give(k, y)
        return carry

    def back(j):
        here = pl.ds(8 * j, 8)
        for yy in range(2):
            partials[yy, j].wait_recv()
            total[yy, here] = (part[yy * 2 + c, here].astype(F32) + other[yy, here].astype(F32)).astype(BF)
        if j == 0:
            give(0, 1 - y)
            pltpu.make_async_copy(total.at[y, 0], ret.at[y, mine], r_recv).start()
        lax.fori_loop(max(1, 8 * j), 8 * j + 8, give_both, 0)

    forward(0)
    forward(1)
    work(0)
    forward(2)
    work(1)
    back(0)
    forward(3)
    work(2)
    back(1)
    work(3)
    back(2)
    back(3)

    def finish_sends():
        for copy in list(forwards.values()) + list(partials.values()):
            copy.wait_send()
        for sem in (send, r_send):
            await_bytes(total.at[0], sem)
            await_bytes(total.at[0, pl.ds(0, 31)], sem)

    if meanwhile is not None:
        meanwhile()
    await_bytes(ret, r_recv)
    return finish_sends


def front(
    shift, tokens, choice_in, gate_in, position_bias, pairs, merged_grad, qkv_weight, out_weight, expert_up, expert_down, reduce_weight,
    after, table, merge_norm, mn_tail, d_block, d_slots, qkv_out, probs_out, mixed_out, flat_out, act_out, slope_out, up_out, down_out,
    x, x_wide, bias, table_of, grad_wide, halo, halo2, normed, mask, ecol, erow, acc, att, wqkv, wo, wred, qkv, probs, mixed,
    d_send, d_relay, d_direct, d_summed, d_across, t_wide, t_send, t_recv, ups, downs, relay_up, relay_down,
    slots, recv, part, other, total, ret, flat, act, slope, spread,
    io_sem, halo_sem, w_send, w_recv, d_sem, *slot_sems,
):
    place = coords()
    s, z, y, c = place
    row = z * 4 + y * 2 + c
    r, cc = shift[0], shift[1]
    last = jnp.where(row == 15, 1, 0)
    ins = [
        pltpu.make_async_copy(reduce_weight, wred, io_sem.at[0]),
        pltpu.make_async_copy(qkv_weight, wqkv, io_sem.at[1]),
        pltpu.make_async_copy(out_weight, wo, io_sem.at[2]),
        pltpu.make_async_copy(expert_up.at[z], ups.at[0], io_sem.at[3]),
        pltpu.make_async_copy(expert_down.at[z], downs.at[0], io_sem.at[4]),
        pltpu.make_async_copy(pairs, table_of, io_sem.at[14]),
    ]
    for copy in ins:
        copy.start()
    lay_rows(tokens, x_wide, x)
    greet_all(place)

    nxt = (s, (row + 1) % 16)
    prv = (s, (row + 15) % 16)
    z_up, z_down = at(s, (z + 1) % 4, y, c), at(s, (z + 3) % 4, y, c)
    halo_copy = remote(x.at[pl.ds(0, HALO)], halo, halo_sem.at[0], halo_sem.at[1], prv)
    halo_copy.start()
    weights = [
        remote(expert_up.at[(z + 2) % 4], relay_up, w_send.at[0], w_recv.at[0], z_up),
        remote(expert_down.at[(z + 2) % 4], relay_down, w_send.at[1], w_recv.at[1], z_down),
        remote(expert_up.at[(z + 1) % 4], ups.at[1], w_send.at[2], w_recv.at[2], z_up),
        remote(expert_up.at[(z + 3) % 4], ups.at[3], w_send.at[3], w_recv.at[3], z_down),
        remote(expert_down.at[(z + 1) % 4], downs.at[1], w_send.at[4], w_recv.at[4], z_up),
        remote(expert_down.at[(z + 3) % 4], downs.at[3], w_send.at[5], w_recv.at[5], z_down),
    ]
    for copy in weights:
        copy.start()
    relayed = [
        remote(relay_up, ups.at[2], w_send.at[6], w_recv.at[6], z_up),
        remote(relay_down, downs.at[2], w_send.at[7], w_recv.at[7], z_down),
    ]

    by_place = merged_grad[...].astype(F32).reshape(49, 8, 256)
    for n in range(8):
        grad_wide[n] = by_place[:, n, :]
    grad48 = grad_wide[:, :48, :].astype(BF).reshape(8 * 48, 256)
    grad_tail = jnp.concatenate([grad_wide[:, 48, :], jnp.zeros((8, 256), F32)], axis=0).astype(BF)
    ins[0].wait()
    for half in range(4):
        span = pl.ds(half * C, C)
        d_send[:, :, span] = dot(grad48, wred[span, :], 1, 1).astype(BF).reshape(8, 48, C)
        tail = dot(grad_tail, wred[span, :], 1, 1)
        for i in range(4):
            t_wide[:, 4 * half + i, :] = tail[:8, i * 256:(i + 1) * 256]
    t_send[...] = t_wide[...].astype(BF)
    yh, xx = s // 4, s % 4
    x_up, x_down, x_far = (xx + 1) % 4, (xx + 3) % 4, (xx + 2) % 4
    to_up, to_down = at(yh * 4 + x_up, z, y, c), at(yh * 4 + x_down, z, y, c)
    first = [
        remote(d_send.at[x_far], d_relay.at[0], d_sem.at[0, 0], d_sem.at[1, 0], to_up),
        remote(d_send.at[4 + x_far], d_relay.at[1], d_sem.at[0, 1], d_sem.at[1, 1], to_down),
        remote(d_send.at[4 + x_up], d_direct.at[1], d_sem.at[0, 2], d_sem.at[1, 2], to_up),
        remote(d_send.at[x_down], d_direct.at[0], d_sem.at[0, 3], d_sem.at[1, 3], to_down),
    ]
    second = [
        remote(d_send.at[x_up], d_summed.at[0], d_sem.at[0, 4], d_sem.at[1, 4], to_up),
        remote(d_send.at[4 + x_down], d_summed.at[1], d_sem.at[0, 5], d_sem.at[1, 5], to_down),
    ]
    other_yh = 1 - yh
    across = remote(
        d_send.at[other_yh * 4 + xx], d_across, d_sem.at[0, 6], d_sem.at[1, 6], at(other_yh * 4 + xx, z, y, c)
    )
    gifts = []
    for k in range(1, 8):
        peer = (s + k) % 8
        gifts.append(remote(t_send.at[peer], t_recv.at[s], d_sem.at[2, k], d_sem.at[3, k], at(peer, z, y, c)))
    for copy in first + gifts:
        copy.start()
    own = pltpu.make_async_copy(t_send.at[s], t_recv.at[s], io_sem.at[6])
    own.start()

    def pass_on():
        for i, mine_at in enumerate((x_up, 4 + x_down)):
            first[i].wait_recv()
            d_send[mine_at] = (d_send[mine_at].astype(F32) + d_relay[i].astype(F32)).astype(BF)
            second[i].start()

    def cross():
        for copy in first[2:] + second:
            copy.wait_recv()
        there = other_yh * 4 + xx
        d_send[there] = (
            d_send[there].astype(F32) + d_direct[other_yh].astype(F32) + d_summed[other_yh].astype(F32)
        ).astype(BF)
        across.start()

    attn_masks(r, cc, last, mask, ecol, erow)
    ins[5].wait()
    bias[...] = jnp.zeros_like(bias)
    parts3 = jnp.concatenate(split3(position_bias[...]), axis=0)
    for pair in range(25):
        wide = dot(parts3, table_of[:, pair * 256:(pair + 1) * 256])
        wide = wide[:32] + wide[32:64] + wide[64:]
        for i in range(2):
            if 2 * pair + i < 49:
                bias[:, 2 * pair + i, :] = wide[:, i * 128:(i + 1) * 128]
    normed[HALO:, :] = norm_parts(x[HALO:, :].astype(F32))[0].astype(BF)
    acc[...] = jnp.zeros_like(acc)
    halo_copy.wait_recv()
    top = jnp.where(iota((HALO, C), 0) < 14 * r, halo[...].astype(F32), x[:HALO, :].astype(F32))
    normed[:HALO, :] = norm_parts(top)[0].astype(BF)
    ins[1].wait()
    ins[2].wait()

    def group(g, carry):
        attn_group(g, normed, wqkv, wo, bias, mask, ecol, erow, qkv, probs, mixed, acc)
        return carry

    lax.fori_loop(0, 1, group, 0)
    pass_on()
    lax.fori_loop(1, 3, group, 0)
    for arrived, onward in zip(weights, relayed):
        arrived.wait_recv()
        onward.start()
    lax.fori_loop(3, 4, group, 0)
    att[...] = acc[...].astype(BF)
    halo2_copy = remote(att.at[pl.ds(0, HALO)], halo2, halo_sem.at[2], halo_sem.at[3], nxt)
    halo2_copy.start()
    outs = [
        pltpu.make_async_copy(qkv, qkv_out, io_sem.at[7]),
        pltpu.make_async_copy(probs, probs_out, io_sem.at[8]),
        pltpu.make_async_copy(mixed, mixed_out, io_sem.at[15]),
    ]
    for copy in outs:
        copy.start()
    cross()
    halo2_copy.wait_recv()
    choice = token_column(choice_in[...].astype(F32))
    route(r, x, att, halo2, choice, after, slots, table)

    def compute(j):
        if j == 0:
            for copy in weights[2:] + relayed:
                copy.wait_recv()
            ins[3].wait()
            ins[4].wait()
        expert_chunk(j, recv, part, ups, downs, flat, act, slope)

    finish_sends = slots_through(place, slots, recv, part, other, total, ret, slot_sems, compute)
    more = [
        pltpu.make_async_copy(flat, flat_out, io_sem.at[9]),
        pltpu.make_async_copy(act, act_out, io_sem.at[10]),
        pltpu.make_async_copy(slope, slope_out, io_sem.at[11]),
        pltpu.make_async_copy(ups, up_out, io_sem.at[12]),
        pltpu.make_async_copy(downs, down_out, io_sem.at[13]),
    ]
    for copy in more:
        copy.start()
    for copy in gifts + [across]:
        copy.wait_recv()
    own.wait()
    parts = (d_send.at[s], d_direct.at[yh], d_summed.at[yh], d_across)
    merge_mid(after, ret, table, token_column(gate_in), parts, t_recv, merge_norm, mn_tail, d_block, d_slots, spread, t_wide)
    for copy in outs + more:
        copy.wait()
    finish_sends()
    for copy in weights + relayed + gifts + first + second + [across, halo_copy, halo2_copy]:
        copy.wait_send()


def back(
    shift, tokens, after, table, merge_norm, mn_tail, d_block, d_slots,
    qkv_weight, out_weight, reduce_weight, qkv_in, probs_in, mixed_in, flat_in, act_in, slope_in, up_in, down_in,
    tokens_grad, merged, up_grad, down_grad,
    x, x_wide, halo, halo2, d_att, acc, d_after, d_shift, wqkv, wo, wred, qkv, probs, mixed, flat, act, slope, ups, downs,
    recv, part, other, total, ret, flat_d, send_up, send_down, relay_up, relay_down,
    mn_all, mt_all, merged_wide, merged_rows,
    io_sem, halo_sem, g_send, g_recv, m_sem, *slot_sems,
):
    place = coords()
    s, z, y, c = place
    row = z * 4 + y * 2 + c
    r = shift[0]
    loads = [
        (down_in, downs), (slope_in, slope), (up_in, ups), (act_in, act), (flat_in, flat),
        (out_weight, wo), (qkv_in, qkv), (probs_in, probs), (qkv_weight, wqkv), (reduce_weight, wred), (mixed_in, mixed),
    ]
    ins = [pltpu.make_async_copy(a, b, io_sem.at[i]) for i, (a, b) in enumerate(loads)]
    for copy in ins:
        copy.start()
    greet_all(place)
    nxt = (s, (row + 1) % 16)
    prv = (s, (row + 15) % 16)
    z_up, z_down = at(s, (z + 1) % 4, y, c), at(s, (z + 3) % 4, y, c)

    def compute(j):
        if j == 0:
            for copy in ins[:3]:
                copy.wait()
        expert_chunk_back(j, recv, part, ups, downs, flat_d, slope)

    returns = [
        remote(send_up.at[1], relay_up, g_send.at[0], g_recv.at[0], z_up),
        remote(send_down.at[1], relay_down, g_send.at[1], g_recv.at[1], z_down),
        remote(send_up.at[0], up_grad.at[z], g_send.at[2], g_recv.at[2], z_down),
        remote(send_down.at[0], down_grad.at[z], g_send.at[3], g_recv.at[3], z_down),
        remote(send_up.at[2], up_grad.at[z], g_send.at[4], g_recv.at[4], z_up),
        remote(send_down.at[2], down_grad.at[z], g_send.at[5], g_recv.at[5], z_up),
    ]
    relayed = [
        remote(relay_up, up_grad.at[(z + 3) % 4], g_send.at[6], g_recv.at[6], z_up),
        remote(relay_down, down_grad.at[(z + 1) % 4], g_send.at[7], g_recv.at[7], z_down),
    ]
    yh, xx = s // 4, s % 4
    x_up, x_down = (xx + 1) % 4, (xx + 3) % 4
    to_up, to_down = at(yh * 4 + x_up, z, y, c), at(yh * 4 + x_down, z, y, c)
    across = (1 - yh) * 4 + xx
    half = (pl.ds(0, 2 * C), pl.ds(2 * C, 2 * C))

    def neighbours(source, slot, n):
        return [
            remote(source, mn_all.at[slot], m_sem.at[0, n], m_sem.at[1, n], to_up),
            remote(source, mn_all.at[slot], m_sem.at[0, n + 1], m_sem.at[1, n + 1], to_down),
        ]

    def halves(base, n):
        below, above = base * 4 + x_down, base * 4 + x_up
        low, high = mn_all.at[below, :, half[0]], mn_all.at[above, :, half[1]]
        return [
            remote(low, low, m_sem.at[0, n], m_sem.at[1, n], to_up),
            remote(high, high, m_sem.at[0, n + 1], m_sem.at[1, n + 1], to_down),
        ]

    spread_own = neighbours(merge_norm, s, 0)
    spread_across = neighbours(mn_all.at[across], across, 2)
    far_own = halves(yh, 4)
    far_across = halves(1 - yh, 6)
    partner = remote(merge_norm, mn_all.at[s], m_sem.at[0, 8], m_sem.at[1, 8], at(across, z, y, c))
    tail_copies = []
    for k in range(1, 8):
        peer = (s + k) % 8
        tail_copies.append(remote(mn_tail, mt_all.at[s], m_sem.at[2, k], m_sem.at[3, k], at(peer, z, y, c)))
    gifts = spread_own + spread_across + far_own + far_across + [partner] + tail_copies
    own = [
        pltpu.make_async_copy(merge_norm, mn_all.at[s], io_sem.at[14]),
        pltpu.make_async_copy(mn_tail, mt_all.at[s], io_sem.at[11]),
    ]
    own_out = [
        pltpu.make_async_copy(send_up.at[3], up_grad.at[z], io_sem.at[12]),
        pltpu.make_async_copy(send_down.at[3], down_grad.at[z], io_sem.at[13]),
    ]

    def grads():
        for copy in ins[3:5]:
            copy.wait()
        for k in (2, 1, 3, 0):
            span = slice(k * 256, (k + 1) * 256)
            up_part = dot(flat[...], slope[:, span], 0, 0)
            down_part = dot(act[:, span], flat_d[...], 0, 0)
            send_up[(k + 3) % 4] = up_part.astype(BF)
            send_down[(k + 3) % 4] = down_part.astype(BF)
            if k:
                first = {2: 0, 1: 2, 3: 4}[k]
                returns[first].start()
                returns[first + 1].start()
            else:
                for copy in own_out:
                    copy.start()

    finish_sends = slots_through(place, d_slots, recv, part, other, total, ret, slot_sems, compute, grads)
    for copy in spread_own + [partner] + tail_copies + own:
        copy.start()
    after_back(after, ret, table, d_block, d_after, d_att)
    halo_copy = remote(d_att.at[pl.ds(0, HALO)], halo, halo_sem.at[0], halo_sem.at[1], prv)
    halo_copy.start()
    lay_rows(tokens, x_wide, x)
    acc[...] = jnp.zeros_like(acc)
    for copy in ins[5:9] + ins[10:]:
        copy.wait()
    halo_copy.wait_recv()
    halo_copy.wait_send()
    top = jnp.where(iota((HALO, C), 0) < 14 * r, halo[...].astype(F32), d_att[:HALO, :].astype(F32))
    d_att[:HALO, :] = top.astype(BF)

    def group(g, carry):
        attn_group_back(g, d_att, wqkv, wo, qkv, probs, mixed, acc)
        return carry

    lax.fori_loop(0, 1, group, 0)
    for arrived, onward in zip(spread_own, far_own):
        arrived.wait_recv()
        onward.start()
    lax.fori_loop(1, 2, group, 0)
    partner.wait_recv()
    for onward in spread_across:
        onward.start()
    lax.fori_loop(2, 3, group, 0)
    for arrived, onward in zip(returns, relayed):
        arrived.wait_recv()
        onward.start()
    lax.fori_loop(3, 4, group, 0)
    d_shift[...] = acc[...].astype(BF)
    halo2_copy = remote(d_shift.at[pl.ds(0, HALO)], halo2, halo_sem.at[2], halo_sem.at[3], nxt)
    halo2_copy.start()

    for arrived, onward in zip(spread_across, far_across):
        arrived.wait_recv()
        onward.start()
    halo2_copy.wait_recv()
    top = jnp.where(iota((HALO, C), 0) < 14 * r, halo2[...].astype(F32), d_shift[:HALO, :].astype(F32))
    x_wide[:HALO, :] = d_after[:HALO, :] + norm_back(x[:HALO, :].astype(F32), top)
    x_wide[HALO:, :] = d_after[HALO:, :] + norm_back(x[HALO:, :].astype(F32), d_shift[HALO:, :].astype(F32))
    for i in range(14):
        tokens_grad[0, i] = x_wide[14 * i:14 * i + 14, :].astype(BF)

    for copy in far_own + far_across + tail_copies:
        copy.wait_recv()
    for copy in own + [ins[9]]:
        copy.wait()
    merged_wide[:, :48, :] = dot(mn_all[...].reshape(8 * 48, 4 * C), wred[...]).reshape(8, 48, 256)
    tails = mt_all[...].astype(F32)
    last = jnp.concatenate([tails[:, i, :] for i in range(16)], axis=1)
    last = jnp.concatenate([last, jnp.zeros_like(last)], axis=0).astype(BF)
    merged_wide[:, 48, :] = dot(last, wred[...])[:8]
    for n in range(8):
        merged_rows[:, n, :] = merged_wide[n]
    merged[...] = merged_rows[...].reshape(7, 7, 8, 256).astype(BF)

    for copy in returns[2:] + relayed:
        copy.wait_recv()
    for copy in own_out:
        copy.wait()
    finish_sends()
    for copy in returns + relayed + gifts + [halo2_copy]:
        copy.wait_send()


def widen(up_in, down_in, grad_in, merged_in, up_out, down_out, grad_out, merged_out):
    up_out[...] = up_in[...].astype(F32)
    down_out[...] = down_in[...].astype(F32)

    @pl.when(pl.program_id(0) == 0)
    def _():
        grad_out[...] = grad_in[...]
        merged_out[...] = merged_in[...]


def bias_pairs():
    spot = np.arange(49)
    py, px = spot // 7, spot % 7
    relative = (py[:, None] - py[None, :] + 6) * 13 + (px[:, None] - px[None, :] + 6)
    table = np.zeros((169, 50, 128), np.float32)
    a, b = np.meshgrid(spot, spot, indexing="ij")
    table[relative.reshape(-1), b.reshape(-1), a.reshape(-1)] = 1.0
    return table.reshape(169, 6400)


def local(
    tokens,
    qkv_weight,
    out_weight,
    position_bias,
    window_shift,
    expert_up,
    expert_down,
    expert_choice,
    combine_weight,
    reduce_weight,
    merged_grad,
):
    choice = jnp.transpose(expert_choice, (1, 0, 3, 2)).reshape(14, 1, 14)
    gate = jnp.transpose(combine_weight, (1, 0, 2))
    pairs = jnp.asarray(bias_pairs(), dtype=BF)
    V = pltpu.VMEM
    D = pltpu.SemaphoreType.DMA

    after, table, merge_norm, mn_tail, d_block, d_slots, qkv, probs, mixed, flat_in, act, slope, ups, downs = pl.pallas_call(
        front,
        out_shape=[
            sds((TP, C), BF), sds((TP, 256), BF), sds((48, 4 * C), BF), sds((16, 256), BF), sds((TP, C), F32),
            sds((32, 16, HC), BF), sds((3, 4, TP, GRP), BF), sds((32 * TP, TP), BF), sds((4, GRP, TP), BF), sds((C, C), BF), sds((C, C), BF),
            sds((C, C), BF), sds((4, C, 256), BF), sds((4, 256, C), BF),
        ],
        in_specs=[SM, VM, VM, VM, VM, HB, VM] + [HB] * 5,
        out_specs=[VM] * 6 + [HB] * 8,
        scratch_shapes=[
            V((TP, C), BF), V((TP, C), F32), V((32, 64, 128), F32), V((169, 6400), BF), V((8, 49, 256), F32),
            V((HALO, C), BF), V((HALO, C), BF), V((TP, C), BF), V((TP, TP), F32),
            V((192, TP), BF), V((TP, 192), BF), V((TP, C), F32), V((TP, C), BF),
            V((C, 3 * C), BF), V((C, C), BF), V((4 * C, 256), BF),
            V((3, 4, TP, GRP), BF), V((32 * TP, TP), BF), V((4, GRP, TP), BF),
            V((8, 48, 4 * C), BF), V((2, 48, 4 * C), BF), V((2, 48, 4 * C), BF), V((2, 48, 4 * C), BF),
            V((48, 4 * C), BF), V((8, 16, 256), F32),
            V((8, 16, 256), BF), V((8, 16, 256), BF),
            V((4, C, 256), BF), V((4, 256, C), BF), V((C, 256), BF), V((256, C), BF),
            V((32, 16, HC), BF), V((4, 32, 16, HC), BF), V((4, 32, 16, HC), BF),
            V((2, 32, 16, HC), BF), V((2, 32, 16, HC), BF), V((2, 32, 16, HC), BF),
            V((C, C), BF), V((C, C), BF), V((C, C), BF), V((256, C), F32),
            D((16,)), D((4,)), D((8,)), D((8,)), D((4, 8)), *SLOT_SEMS,
        ],
        compiler_params=params(collective_id=0, has_side_effects=True),
        cost_estimate=cost(12 << 30, 60 << 20),
        name="front",
    )(window_shift, tokens, choice, gate, position_bias, pairs, jnp.transpose(merged_grad, (1, 2, 0, 3)), qkv_weight, out_weight,
      expert_up, expert_down, reduce_weight)

    tokens_grad, merged, up_grad, down_grad = pl.pallas_call(
        back,
        out_shape=[
            sds(tokens.shape, BF), sds((7, 7, 8, 256), BF), sds((4, C, 256), BF), sds((4, 256, C), BF),
        ],
        in_specs=[SM] + [VM] * 7 + [HB] * 11,
        out_specs=[VM] * 2 + [HB] * 2,
        scratch_shapes=[
            V((TP, C), BF), V((TP, C), F32), V((HALO, C), BF), V((HALO, C), BF), V((TP, C), BF), V((TP, C), F32),
            V((TP, C), F32), V((TP, C), BF), V((C, 3 * C), BF), V((C, C), BF), V((4 * C, 256), BF),
            V((3, 4, TP, GRP), BF), V((32 * TP, TP), BF), V((4, GRP, TP), BF), V((C, C), BF), V((C, C), BF), V((C, C), BF),
            V((4, C, 256), BF), V((4, 256, C), BF),
            V((4, 32, 16, HC), BF), V((4, 32, 16, HC), BF), V((2, 32, 16, HC), BF), V((2, 32, 16, HC), BF),
            V((2, 32, 16, HC), BF), V((C, C), BF), V((4, C, 256), BF), V((4, 256, C), BF), V((C, 256), BF), V((256, C), BF),
            V((8, 48, 4 * C), BF), V((8, 16, 256), BF), V((8, 49, 256), F32), V((49, 8, 256), F32),
            D((20,)), D((4,)), D((8,)), D((8,)), D((4, 9)), *SLOT_SEMS,
        ],
        compiler_params=pltpu.CompilerParams(
            vmem_limit_bytes=60 * 1024 * 1024, collective_id=1, has_side_effects=True
        ),
        cost_estimate=cost(16 << 30, 60 << 20),
        name="back",
    )(window_shift, tokens, after, table, merge_norm, mn_tail, d_block, d_slots, qkv_weight, out_weight, reduce_weight,
      qkv, probs, mixed, flat_in, act, slope, ups, downs)
    whole = lambda shape: pl.BlockSpec(shape, lambda e: (0,) * len(shape))
    blocks = [
        pl.BlockSpec((1, C, 256), lambda e: (e, 0, 0)), pl.BlockSpec((1, 256, C), lambda e: (e, 0, 0)),
        whole(tokens_grad.shape), whole(merged.shape),
    ]
    up_grad, down_grad, tokens_grad, merged = pl.pallas_call(
        widen,
        grid=(4,),
        out_shape=[
            sds((4, C, 256), F32), sds((4, 256, C), F32), sds(tokens_grad.shape, BF), sds(merged.shape, BF),
        ],
        in_specs=blocks,
        out_specs=blocks,
        compiler_params=params(),
        cost_estimate=cost(0, 14 << 20),
        name="widen",
    )(up_grad, down_grad, tokens_grad, merged)
    return (jnp.transpose(merged, (2, 0, 1, 3)), tokens_grad, up_grad, down_grad)


def solution(mesh):
    placed = (
        P("scene", "row", None, None),
        P(),
        P(),
        P(),
        P(),
        P("scene", None, "row"),
        P("scene", "row", None),
        P("scene", "row", None, None),
        P("scene", "row", None),
        P(None, "scene"),
        P(None, "row", None, "scene"),
    )
    return jax.shard_map(
        local,
        mesh=mesh,
        in_specs=placed,
        out_specs=(
            P(None, "row", None, "scene"),
            P("scene", "row", None, None),
            P("scene", None, "row"),
            P("scene", "row", None),
        ),
        check_vma=False,
    )
```

```python
import functools

import jax
import jax.numpy as jnp
import numpy as np
from jax import lax
from jax.experimental import pallas as pl
from jax.experimental.pallas import tpu as pltpu
from jax.sharding import PartitionSpec as P

MESH = pl.DeviceIdType.MESH
F32 = jnp.float32
BF = jnp.bfloat16
EPS = 1e-5
C = 1024
HC = C // 2
TOK = 196
TP = 208
HALO = 96
GRP = 256
NEG = -1e30
VMEM_BIG = 56 * 1024 * 1024
VM = pl.BlockSpec(memory_space=pltpu.VMEM)
SM = pl.BlockSpec(memory_space=pltpu.SMEM)
HB = pl.BlockSpec(memory_space=pl.ANY)


def sds(shape, dtype):
    return jax.ShapeDtypeStruct(shape, dtype)


def params(**kw):
    return pltpu.CompilerParams(vmem_limit_bytes=VMEM_BIG, **kw)


def cost(flops, nbytes):
    return pl.CostEstimate(flops=flops, bytes_accessed=nbytes, transcendentals=0)


def dot(a, b, da=1, db=0):
    return lax.dot_general(a, b, (((da,), (db,)), ((), ())), preferred_element_type=F32)


def iota(shape, dim):
    return lax.broadcasted_iota(jnp.int32, shape, dim)


def norm_parts(values):
    centre = jnp.mean(values, axis=-1, keepdims=True)
    centred = values - centre
    spread = jnp.mean(centred * centred, axis=-1, keepdims=True)
    scale = lax.rsqrt(spread + EPS)
    return centred * scale, scale


def norm_back(values, cot):
    unit, scale = norm_parts(values)
    mean_cot = jnp.mean(cot, axis=-1, keepdims=True)
    mean_dot = jnp.mean(cot * unit, axis=-1, keepdims=True)
    return scale * (cot - mean_cot - unit * mean_dot)


def split3(values):
    high = values.astype(BF)
    rest = values - high.astype(F32)
    mid = rest.astype(BF)
    low = (rest - mid.astype(F32)).astype(BF)
    return high, mid, low


def place_of(tok, r, c):
    rho = (tok * 4682) >> 16
    gam = tok - 14 * rho
    i = rho - r
    i = jnp.where(i < 0, i + 14, i)
    j = gam - c
    j = jnp.where(j < 0, j + 14, j)
    a = jnp.where(i >= 7, 1, 0)
    b = jnp.where(j >= 7, 1, 0)
    return i, j, a, b


def pos_of(tok, r, c):
    i, j, a, b = place_of(tok, r, c)
    return (i - 7 * a) * 7 + (j - 7 * b)


def group_of(tok, r, c, last):
    i, j, a, b = place_of(tok, r, c)
    la = jnp.where(i >= 7, jnp.where(i < 14 - r, 1, 2), 0) * last
    lb = jnp.where(j >= 7, jnp.where(j < 14 - c, 1, 2), 0)
    return a * 2 + b, la * 3 + lb


def pack_rows(low, high, blocks):
    return jnp.concatenate([low.reshape(blocks, 8, HC), high.reshape(blocks, 8, HC)], axis=1).astype(BF)


def unpack_rows(packed, blocks):
    wide = packed.astype(F32)
    low = wide[:, :8, :].reshape(blocks * 8, HC)
    high = wide[:, 8:, :].reshape(blocks * 8, HC)
    return low, high


def attn_masks(r, c, last, mask, ecol, erow):
    tq, tk = iota((TP, TP), 0), iota((TP, TP), 1)
    wq_, lq = group_of(tq, r, c, last)
    wk_, lk = group_of(tk, r, c, last)
    seen = jnp.where(wq_ == wk_, jnp.where(lq == lk, 0.0, -100.0), NEG)
    mask[...] = jnp.where(tq < TOK, seen, NEG)
    row_pos = pos_of(iota((TP, 192), 0), r, c)
    erow[...] = jnp.where(row_pos == (iota((TP, 192), 1) & 63), 1.0, 0.0).astype(BF)
    col_pos = pos_of(iota((192, TP), 1), r, c)
    ecol[...] = jnp.where(col_pos == (iota((192, TP), 0) & 63), 1.0, 0.0).astype(BF)


def cols(start):
    return pl.ds(pl.multiple_of(start, GRP), GRP)


def turned(values, eye):
    return dot(eye, values, 1, 1)


def unit_table():
    return jnp.where(iota((GRP, GRP), 0) == iota((GRP, GRP), 1), 1.0, 0.0).astype(BF)


def attn_group(g, normed, wqkv, wo, bias, mask, ecol, erow, qkv, probs, mixed, acc):
    n = normed[...]
    q = dot(n, wqkv[:, cols(g * GRP)]).astype(BF)
    k = dot(n, wqkv[:, cols(C + g * GRP)]).astype(BF)
    v = dot(n, wqkv[:, cols(2 * C + g * GRP)]).astype(BF)
    qkv[0, g] = q
    qkv[1, g] = k
    qkv[2, g] = v
    eye = unit_table()
    q_t = turned(q, eye).astype(BF)
    v_t = turned(v, eye).astype(BF)
    wide = dot(jnp.concatenate(split3(bias[pl.ds(g * 8, 8)][:, :, :64].reshape(8 * 64, 64)), axis=1), ecol[...])
    w_hi, w_mid, w_lo = split3(wide)
    lane_head = iota((TP, GRP), 1) >> 5
    k32 = k.astype(F32)
    outs = []
    for h in range(8):
        km = jnp.where(lane_head == h, k32, 0.0).astype(BF)
        part = slice(h * 64, h * 64 + 64)
        s = dot(km, q_t) * (32.0 ** -0.5)
        s = s + dot(erow[...], jnp.concatenate([w_hi[part], w_mid[part], w_lo[part]], axis=0)) + mask[...]
        e = jnp.exp(s - jnp.max(s, axis=0, keepdims=True))
        p = (e * (1.0 / jnp.sum(e, axis=0, keepdims=True))).astype(BF)
        probs[pl.ds(pl.multiple_of((g * 8 + h) * TP, 16), TP), :] = p
        outs.append(dot(v_t[32 * h:32 * h + 32], p))
    mixed_t = jnp.concatenate(outs, axis=0).astype(BF)
    mixed[g] = mixed_t
    acc[...] += dot(mixed_t, wo[pl.ds(pl.multiple_of(g * GRP, GRP), GRP), :], 0, 0)


def attn_group_back(g, d_att, wqkv, wo, qkv, probs, mixed, acc):
    q, k, v = qkv[0, g], qkv[1, g], qkv[2, g]
    eye = unit_table()
    d_out = dot(d_att[...], wo[pl.ds(pl.multiple_of(g * GRP, GRP), GRP), :], 1, 1).astype(BF)
    d_out_t = turned(d_out, eye)
    weighed = d_out_t * mixed[g].astype(F32)
    d_out_t = d_out_t.astype(BF)
    k_t = turned(k, eye).astype(BF)
    v32 = v.astype(F32)
    lane_head = iota((TP, GRP), 1) >> 5
    dq_t = []
    dk = jnp.zeros((TP, GRP), F32)
    dv = jnp.zeros((TP, GRP), F32)
    for h in range(8):
        mine = lane_head == h
        vm = jnp.where(mine, v32, 0.0).astype(BF)
        p = probs[pl.ds(pl.multiple_of((g * 8 + h) * TP, 16), TP), :]
        shared = jnp.sum(weighed[32 * h:32 * h + 32], axis=0, keepdims=True)
        ds = (p.astype(F32) * (dot(vm, d_out_t) - shared)).astype(BF)
        dq_t.append(dot(k_t[32 * h:32 * h + 32], ds))
        dk = jnp.where(mine, dot(ds, q), dk)
        dv = jnp.where(mine, dot(p, d_out), dv)
    scale = 32.0 ** -0.5
    dq = jnp.transpose(jnp.concatenate(dq_t, axis=0) * scale)
    acc[...] += (
        dot(dq.astype(BF), wqkv[:, cols(g * GRP)], 1, 1)
        + dot((dk * scale).astype(BF), wqkv[:, cols(C + g * GRP)], 1, 1)
        + dot(dv.astype(BF), wqkv[:, cols(2 * C + g * GRP)], 1, 1)
    )


def route(r, x, att, halo, choice, after_out, slots, table_out):
    top = jnp.where(iota((HALO, C), 0) < 14 * r, halo[...].astype(F32), att[:HALO, :].astype(F32))
    after_out[:HALO, :] = (x[:HALO, :].astype(F32) + top).astype(BF)
    after_out[HALO:, :] = (x[HALO:, :].astype(F32) + att[HALO:, :].astype(F32)).astype(BF)
    after = after_out[...].astype(F32)
    n2 = norm_parts(after)[0].astype(BF)
    tok, other = iota((TP, TP), 0), iota((TP, TP), 1)
    col = jnp.where(iota((TP, 1), 0) < TOK, choice, -1000.0)
    line = jnp.sum(jnp.where(tok == other, col, 0.0), axis=0, keepdims=True)
    same = jnp.where(col == line, 1.0, 0.0)
    same = jnp.where(other < tok, same, 0.0)
    rank = jnp.sum(same, axis=1, keepdims=True).astype(jnp.int32)
    table = jnp.where(col.astype(jnp.int32) * 8 + rank == iota((TP, 256), 1), 1.0, 0.0).astype(BF)
    table_out[...] = table
    slots[...] = pack_rows(dot(table, n2[:, :HC], 0, 0), dot(table, n2[:, HC:], 0, 0), 32)


def quad_table():
    row = iota((256, TP), 0)
    tok = iota((256, TP), 1)
    q = row >> 6
    n = row & 63
    a = (n * 9363) >> 16
    b = n - 7 * a
    want = (2 * a + (q & 1)) * 14 + 2 * b + (q >> 1)
    hit = jnp.where(want == tok, 1.0, 0.0)
    return jnp.where(n < 49, hit, 0.0).astype(BF)


def gathered(ret, table):
    low, high = unpack_rows(ret[...], 32)
    return jnp.concatenate([dot(table, low.astype(BF)), dot(table, high.astype(BF))], axis=1)


def merge_mid(after, ret, table_in, gate, parts, tail, mn_out, mn_tail, d_block_out, slots, spread, t_wide):
    table = table_in[...]
    block = (after[...].astype(F32) + gate * gathered(ret, table)).astype(BF)
    perm = quad_table()
    quads = dot(perm, block)
    vals = [quads[64 * q:64 * q + 49, :] for q in range(4)]
    inv = 1.0 / (4 * C)
    centre = sum(jnp.sum(v, axis=-1, keepdims=True) for v in vals) * inv
    cent = [v - centre for v in vals]
    var = sum(jnp.sum(v * v, axis=-1, keepdims=True) for v in cent) * inv
    scale = lax.rsqrt(var + EPS)
    unit = [v * scale for v in cent]
    for q in range(4):
        mn_out[:, q * C:(q + 1) * C] = unit[q][:48].astype(BF)
        for i in range(4):
            t_wide[0, 4 * q + i:4 * q + i + 1, :] = unit[q][48:49, i * 256:(i + 1) * 256]
    mn_tail[...] = t_wide[0].astype(BF)
    tails = jnp.sum(tail[...].astype(F32), axis=0)
    cots = []
    for q in range(4):
        tot = sum(part[:, q * C:(q + 1) * C].astype(F32) for part in parts)
        last = jnp.concatenate([tails[4 * q + i:4 * q + i + 1, :] for i in range(4)], axis=1)
        cots.append(jnp.concatenate([tot, last], axis=0))
    mean_cot = sum(jnp.sum(v, axis=-1, keepdims=True) for v in cots) * inv
    mean_dot = sum(jnp.sum(v * u, axis=-1, keepdims=True) for v, u in zip(cots, unit)) * inv
    spread[...] = jnp.zeros_like(spread)
    for q in range(4):
        spread[64 * q:64 * q + 49, :] = scale * (cots[q] - mean_cot - unit[q] * mean_dot)
    high, mid, low = split3(spread[...])
    d_block = dot(perm, high, 0, 0) + dot(perm, mid, 0, 0) + dot(perm, low, 0, 0)
    d_block_out[...] = d_block
    scaled = (gate * d_block).astype(BF)
    slots[...] = pack_rows(dot(table, scaled[:, :HC], 0, 0), dot(table, scaled[:, HC:], 0, 0), 32)


def after_back(after, ret, table, d_block, d_after_out, d_att_out):
    d_second = gathered(ret, table[...])
    d_after = d_block[...] + norm_back(after[...].astype(F32), d_second)
    d_after_out[...] = d_after
    d_att_out[...] = d_after.astype(BF)


def token_column(grid):
    tok = iota((TP, 14), 0)
    rho = (tok * 4682) >> 16
    place = iota((TP, 14), 1)
    pick = jnp.where(rho == place, 1.0, 0.0).astype(BF)
    high, mid, low = split3(grid[...].reshape(14, 14))
    rows = dot(pick, high) + dot(pick, mid) + dot(pick, low)
    return jnp.sum(jnp.where(tok - 14 * rho == place, rows, 0.0), axis=1, keepdims=True)


def lay_rows(tokens, wide, x):
    wide[TOK - 4:, :] = jnp.zeros((TP - TOK + 4, C), F32)
    for i in range(14):
        wide[14 * i:14 * i + 14, :] = tokens[0, i].astype(F32)
    x[...] = wide[...].astype(BF)


def expert_chunk(j, recv, part, ups, downs, flat, act_out, slope_out):
    here = pl.ds(8 * j, 8)
    rows_here = pl.ds(256 * j, 256)
    low, high = unpack_rows(recv[:, here].reshape(32, 16, HC), 32)
    rows = jnp.concatenate([low, high], axis=1).astype(BF)
    flat[rows_here, :] = rows
    total = jnp.zeros((256, C), F32)
    for k in range(4):
        pre = dot(rows, ups[k])
        cdf = 0.5 * (1.0 + lax.erf(pre * np.float32(2.0 ** -0.5)))
        act = (pre * cdf).astype(BF)
        slope = cdf + pre * jnp.exp(-0.5 * pre * pre) * np.float32((2.0 * np.pi) ** -0.5)
        act_out[rows_here, k * 256:(k + 1) * 256] = act
        slope_out[rows_here, k * 256:(k + 1) * 256] = slope.astype(BF)
        total = total + dot(act, downs[k])
    part[:, here] = pack_rows(total[:, :HC], total[:, HC:], 32).reshape(4, 8, 16, HC)


def expert_chunk_back(j, recv, part, ups, downs, flat, slope):
    here = pl.ds(8 * j, 8)
    rows_here = pl.ds(256 * j, 256)
    low, high = unpack_rows(recv[:, here].reshape(32, 16, HC), 32)
    rows = jnp.concatenate([low, high], axis=1).astype(BF)
    flat[rows_here, :] = rows
    total = jnp.zeros((256, C), F32)
    for k in range(4):
        span = slice(k * 256, (k + 1) * 256)
        d_pre = (slope[rows_here, span].astype(F32) * dot(rows, downs[k], 1, 1)).astype(BF)
        slope[rows_here, span] = d_pre
        total = total + dot(d_pre, ups[k], 1, 1)
    part[:, here] = pack_rows(total[:, :HC], total[:, HC:], 32).reshape(4, 8, 16, HC)


def coords():
    s = lax.axis_index("scene")
    row = lax.axis_index("row")
    z, m = row // 4, row % 4
    return s, z, m // 2, m % 2


def at(s, z, y, c):
    return (s, z * 4 + y * 2 + c)


def steps(k):
    dx = k % 4
    return (k % 8) // 4, dx, (k // 8 + 4 - dx) % 4


def ahead(place, k):
    s, z, y, c = place
    dy, dx, dz = steps(k)
    scene, zz = (s // 4 + dy) % 2 * 4 + (s % 4 + dx) % 4, (z + dz) % 4
    return scene * 4 + zz, at(scene, zz, (y + dy) % 2, c)


def behind(place, k):
    s, z, y, c = place
    dy, dx, dz = steps(k)
    return at((s // 4 + dy) % 2 * 4 + (s % 4 + 4 - dx) % 4, (z + 4 - dz) % 4, (y + dy) % 2, c)


def greet_all(place):
    s, z, y, c = place
    barrier = pltpu.get_barrier_semaphore()
    row = z * 4 + y * 2 + c

    def hail(device):
        pl.semaphore_signal(barrier, inc=1, device_id=device, device_id_type=MESH)

    def hail_step(k, carry):
        hail(ahead(place, k)[1])
        return carry

    hail((s, (row + 1) % 16))
    hail((s, (row + 15) % 16))
    hail(at(s, z, 1 - y, c))
    hail(at(s, z, y, 1 - c))
    lax.fori_loop(1, 32, hail_step, 0)
    for dx in range(4):
        hail(at((1 - s // 4) * 4 + (s % 4 + dx) % 4, z, y, c))
    pl.semaphore_wait(barrier, 39)


def remote(src, dst, send, recv, device):
    return pltpu.make_async_remote_copy(
        src_ref=src, dst_ref=dst, send_sem=send, recv_sem=recv, device_id=device, device_id_type=MESH
    )


def await_bytes(ref, sem):
    pltpu.make_async_copy(ref, ref, sem).wait()


SLOT_SEMS = [pltpu.SemaphoreType.DMA] + [pltpu.SemaphoreType.DMA((4,))] * 3 + [pltpu.SemaphoreType.DMA((2, 4))] * 4 + [
    pltpu.SemaphoreType.DMA((4,)), pltpu.SemaphoreType.DMA((4,)), pltpu.SemaphoreType.DMA, pltpu.SemaphoreType.DMA,
]


def slots_through(place, slots, recv, part, other, total, across, ret, sems, compute, meanwhile=None):
    s, z, y, c = place
    mine = s * 4 + z
    send, arrive, y_send, y_recv, c_send, c_recv, p_send, p_recv, t_send, t_recv, r_send, r_recv = sems
    pair = at(s, z, y, 1 - c)
    beside = at(s, z, 1 - y, c)
    own, next_own = y * 2 + c, (1 - y) * 2 + c

    def push(k, carry):
        index, device = ahead(place, k)
        remote(slots.at[index], recv.at[(y + steps(k)[0]) % 2 * 2 + c, k], send, arrive.at[k // 8], device).start()
        return carry

    pltpu.make_async_copy(slots.at[mine], recv.at[own, 0], arrive.at[0]).start()
    lax.fori_loop(1, 32, push, 0)
    y_copies, c_copies, partials, t_copies = {}, {}, {}, {}

    def here(j):
        return pl.ds(8 * j, 8)

    def pass_pair(j, which, member):
        block = recv.at[member, here(j)]
        c_copies[which, j] = remote(block, block, c_send.at[which, j], c_recv.at[which, j], pair)
        c_copies[which, j].start()

    def arrived(j):
        block = recv.at[own, here(j)]
        await_bytes(block, arrive.at[j])
        y_copies[j] = remote(block, block, y_send.at[j], y_recv.at[j], beside)
        y_copies[j].start()
        pass_pair(j, 0, own)

    def passed(j):
        y_copies[j].wait_recv()
        pass_pair(j, 1, next_own)

    def work(j):
        for which in range(2):
            c_copies[which, j].wait_recv()
        compute(j)
        for yy in range(2):
            partials[yy, j] = remote(
                part.at[yy * 2 + (1 - c), here(j)], other.at[yy, here(j)], p_send.at[yy, j], p_recv.at[yy, j], pair
            )
            partials[yy, j].start()

    def add_pair(j):
        for yy in range(2):
            partials[yy, j].wait_recv()
        total[1, here(j)] = (
            part[next_own, here(j)].astype(F32) + other[1 - y, here(j)].astype(F32)
        ).astype(BF)
        t_copies[j] = remote(total.at[1, here(j)], across.at[here(j)], t_send.at[j], t_recv.at[j], beside)
        t_copies[j].start()

    def give(k, carry):
        remote(total.at[0, k], ret.at[mine], r_send, r_recv, behind(place, k)).start()
        return carry

    def back_home(j):
        t_copies[j].wait_recv()
        total[0, here(j)] = (
            part[own, here(j)].astype(F32) + other[y, here(j)].astype(F32) + across[here(j)].astype(F32)
        ).astype(BF)
        if j == 0:
            pltpu.make_async_copy(total.at[0, 0], ret.at[mine], r_recv).start()
        lax.fori_loop(max(1, 8 * j), 8 * j + 8, give, 0)

    arrived(0)
    arrived(1)
    passed(0)
    work(0)
    arrived(2)
    passed(1)
    add_pair(0)
    work(1)
    arrived(3)
    passed(2)
    back_home(0)
    add_pair(1)
    work(2)
    passed(3)
    back_home(1)
    add_pair(2)
    work(3)
    back_home(2)
    add_pair(3)
    back_home(3)

    def finish_sends():
        for copies in (y_copies, c_copies, partials, t_copies):
            for copy in copies.values():
                copy.wait_send()
        for sem in (send, r_send):
            await_bytes(total.at[0, pl.ds(0, 31)], sem)

    if meanwhile is not None:
        meanwhile()
    await_bytes(ret, r_recv)
    return finish_sends


def front(
    shift, tokens, choice_in, gate_in, position_bias, pairs, merged_grad, qkv_weight, out_weight, expert_up, expert_down, reduce_weight,
    after, table, merge_norm, mn_tail, d_block, d_slots, qkv_out, probs_out, mixed_out, flat_out, act_out, slope_out, up_out, down_out,
    x, x_wide, bias, table_of, grad_wide, halo, halo2, normed, mask, ecol, erow, acc, att, wqkv, wo, wred, qkv, probs, mixed,
    d_send, d_relay, d_direct, d_summed, d_across, t_wide, t_send, t_recv, ups, downs, relay_up, relay_down,
    slots, recv, part, other, total, across_sum, ret, flat, act, slope, spread,
    io_sem, halo_sem, w_send, w_recv, d_sem, *slot_sems,
):
    place = coords()
    s, z, y, c = place
    row = z * 4 + y * 2 + c
    r, cc = shift[0], shift[1]
    last = jnp.where(row == 15, 1, 0)
    ins = [
        pltpu.make_async_copy(reduce_weight, wred, io_sem.at[0]),
        pltpu.make_async_copy(qkv_weight, wqkv, io_sem.at[1]),
        pltpu.make_async_copy(out_weight, wo, io_sem.at[2]),
        pltpu.make_async_copy(expert_up.at[z], ups.at[0], io_sem.at[3]),
        pltpu.make_async_copy(expert_down.at[z], downs.at[0], io_sem.at[4]),
        pltpu.make_async_copy(pairs, table_of, io_sem.at[14]),
    ]
    for copy in ins:
        copy.start()
    lay_rows(tokens, x_wide, x)
    greet_all(place)

    nxt = (s, (row + 1) % 16)
    prv = (s, (row + 15) % 16)
    z_up, z_down = at(s, (z + 1) % 4, y, c), at(s, (z + 3) % 4, y, c)
    halo_copy = remote(x.at[pl.ds(0, HALO)], halo, halo_sem.at[0], halo_sem.at[1], prv)
    halo_copy.start()
    weights = [
        remote(expert_up.at[(z + 2) % 4], relay_up, w_send.at[0], w_recv.at[0], z_up),
        remote(expert_down.at[(z + 2) % 4], relay_down, w_send.at[1], w_recv.at[1], z_down),
        remote(expert_up.at[(z + 1) % 4], ups.at[1], w_send.at[2], w_recv.at[2], z_up),
        remote(expert_up.at[(z + 3) % 4], ups.at[3], w_send.at[3], w_recv.at[3], z_down),
        remote(expert_down.at[(z + 1) % 4], downs.at[1], w_send.at[4], w_recv.at[4], z_up),
        remote(expert_down.at[(z + 3) % 4], downs.at[3], w_send.at[5], w_recv.at[5], z_down),
    ]
    for copy in weights:
        copy.start()
    relayed = [
        remote(relay_up, ups.at[2], w_send.at[6], w_recv.at[6], z_up),
        remote(relay_down, downs.at[2], w_send.at[7], w_recv.at[7], z_down),
    ]

    by_place = merged_grad[...].astype(F32).reshape(49, 8, 256)
    for n in range(8):
        grad_wide[n] = by_place[:, n, :]
    grad48 = grad_wide[:, :48, :].astype(BF).reshape(8 * 48, 256)
    grad_tail = jnp.concatenate([grad_wide[:, 48, :], jnp.zeros((8, 256), F32)], axis=0).astype(BF)
    ins[0].wait()
    for half in range(4):
        span = pl.ds(half * C, C)
        d_send[:, :, span] = dot(grad48, wred[span, :], 1, 1).astype(BF).reshape(8, 48, C)
        tail = dot(grad_tail, wred[span, :], 1, 1)
        for i in range(4):
            t_wide[:, 4 * half + i, :] = tail[:8, i * 256:(i + 1) * 256]
    t_send[...] = t_wide[...].astype(BF)
    yh, xx = s // 4, s % 4
    x_up, x_down, x_far = (xx + 1) % 4, (xx + 3) % 4, (xx + 2) % 4
    to_up, to_down = at(yh * 4 + x_up, z, y, c), at(yh * 4 + x_down, z, y, c)
    first = [
        remote(d_send.at[x_far], d_relay.at[0], d_sem.at[0, 0], d_sem.at[1, 0], to_up),
        remote(d_send.at[4 + x_far], d_relay.at[1], d_sem.at[0, 1], d_sem.at[1, 1], to_down),
        remote(d_send.at[4 + x_up], d_direct.at[1], d_sem.at[0, 2], d_sem.at[1, 2], to_up),
        remote(d_send.at[x_down], d_direct.at[0], d_sem.at[0, 3], d_sem.at[1, 3], to_down),
    ]
    second = [
        remote(d_send.at[x_up], d_summed.at[0], d_sem.at[0, 4], d_sem.at[1, 4], to_up),
        remote(d_send.at[4 + x_down], d_summed.at[1], d_sem.at[0, 5], d_sem.at[1, 5], to_down),
    ]
    other_yh = 1 - yh
    across = remote(
        d_send.at[other_yh * 4 + xx], d_across, d_sem.at[0, 6], d_sem.at[1, 6], at(other_yh * 4 + xx, z, y, c)
    )
    gifts = []
    for k in range(1, 8):
        peer = (s + k) % 8
        gifts.append(remote(t_send.at[peer], t_recv.at[s], d_sem.at[2, k], d_sem.at[3, k], at(peer, z, y, c)))
    for copy in first + gifts:
        copy.start()
    own = pltpu.make_async_copy(t_send.at[s], t_recv.at[s], io_sem.at[6])
    own.start()

    def pass_on():
        for i, mine_at in enumerate((x_up, 4 + x_down)):
            first[i].wait_recv()
            d_send[mine_at] = (d_send[mine_at].astype(F32) + d_relay[i].astype(F32)).astype(BF)
            second[i].start()

    def cross():
        for copy in first[2:] + second:
            copy.wait_recv()
        there = other_yh * 4 + xx
        d_send[there] = (
            d_send[there].astype(F32) + d_direct[other_yh].astype(F32) + d_summed[other_yh].astype(F32)
        ).astype(BF)
        across.start()

    attn_masks(r, cc, last, mask, ecol, erow)
    ins[5].wait()
    bias[...] = jnp.zeros_like(bias)
    parts3 = jnp.concatenate(split3(position_bias[...]), axis=0)
    for pair in range(25):
        wide = dot(parts3, table_of[:, pair * 256:(pair + 1) * 256])
        wide = wide[:32] + wide[32:64] + wide[64:]
        for i in range(2):
            if 2 * pair + i < 49:
                bias[:, 2 * pair + i, :] = wide[:, i * 128:(i + 1) * 128]
    normed[HALO:, :] = norm_parts(x[HALO:, :].astype(F32))[0].astype(BF)
    acc[...] = jnp.zeros_like(acc)
    halo_copy.wait_recv()
    top = jnp.where(iota((HALO, C), 0) < 14 * r, halo[...].astype(F32), x[:HALO, :].astype(F32))
    normed[:HALO, :] = norm_parts(top)[0].astype(BF)
    ins[1].wait()
    ins[2].wait()

    def group(g, carry):
        attn_group(g, normed, wqkv, wo, bias, mask, ecol, erow, qkv, probs, mixed, acc)
        return carry

    lax.fori_loop(0, 1, group, 0)
    pass_on()
    lax.fori_loop(1, 3, group, 0)
    for arrived, onward in zip(weights, relayed):
        arrived.wait_recv()
        onward.start()
    lax.fori_loop(3, 4, group, 0)
    att[...] = acc[...].astype(BF)
    halo2_copy = remote(att.at[pl.ds(0, HALO)], halo2, halo_sem.at[2], halo_sem.at[3], nxt)
    halo2_copy.start()
    outs = [
        pltpu.make_async_copy(qkv, qkv_out, io_sem.at[7]),
        pltpu.make_async_copy(probs, probs_out, io_sem.at[8]),
        pltpu.make_async_copy(mixed, mixed_out, io_sem.at[15]),
    ]
    for copy in outs:
        copy.start()
    cross()
    halo2_copy.wait_recv()
    choice = token_column(choice_in[...].astype(F32))
    route(r, x, att, halo2, choice, after, slots, table)

    def compute(j):
        if j == 0:
            for copy in weights[2:] + relayed:
                copy.wait_recv()
            ins[3].wait()
            ins[4].wait()
        expert_chunk(j, recv, part, ups, downs, flat, act, slope)

    finish_sends = slots_through(place, slots, recv, part, other, total, across_sum, ret, slot_sems, compute)
    more = [
        pltpu.make_async_copy(flat, flat_out, io_sem.at[9]),
        pltpu.make_async_copy(act, act_out, io_sem.at[10]),
        pltpu.make_async_copy(slope, slope_out, io_sem.at[11]),
        pltpu.make_async_copy(ups, up_out, io_sem.at[12]),
        pltpu.make_async_copy(downs, down_out, io_sem.at[13]),
    ]
    for copy in more:
        copy.start()
    for copy in gifts + [across]:
        copy.wait_recv()
    own.wait()
    parts = (d_send.at[s], d_direct.at[yh], d_summed.at[yh], d_across)
    merge_mid(after, ret, table, token_column(gate_in), parts, t_recv, merge_norm, mn_tail, d_block, d_slots, spread, t_wide)
    for copy in outs + more:
        copy.wait()
    finish_sends()
    for copy in weights + relayed + gifts + first + second + [across, halo_copy, halo2_copy]:
        copy.wait_send()


def back(
    shift, tokens, after, table, merge_norm, mn_tail, d_block, d_slots,
    qkv_weight, out_weight, reduce_weight, qkv_in, probs_in, mixed_in, flat_in, act_in, slope_in, up_in, down_in,
    tokens_grad, merged, up_grad, down_grad,
    x, x_wide, halo, halo2, d_att, acc, d_after, d_shift, wqkv, wo, wred, qkv, probs, mixed, flat, act, slope, ups, downs,
    recv, part, other, total, across_sum, ret, flat_d, send_up, send_down, relay_up, relay_down,
    mn_all, mt_all, merged_wide, merged_rows,
    io_sem, halo_sem, g_send, g_recv, m_sem, *slot_sems,
):
    place = coords()
    s, z, y, c = place
    row = z * 4 + y * 2 + c
    r = shift[0]
    loads = [
        (down_in, downs), (slope_in, slope), (up_in, ups), (act_in, act), (flat_in, flat),
        (out_weight, wo), (qkv_in, qkv), (probs_in, probs), (qkv_weight, wqkv), (reduce_weight, wred), (mixed_in, mixed),
    ]
    ins = [pltpu.make_async_copy(a, b, io_sem.at[i]) for i, (a, b) in enumerate(loads)]
    for copy in ins:
        copy.start()
    greet_all(place)
    nxt = (s, (row + 1) % 16)
    prv = (s, (row + 15) % 16)
    z_up, z_down = at(s, (z + 1) % 4, y, c), at(s, (z + 3) % 4, y, c)

    def compute(j):
        if j == 0:
            for copy in ins[:3]:
                copy.wait()
        expert_chunk_back(j, recv, part, ups, downs, flat_d, slope)

    returns = [
        remote(send_up.at[1], relay_up, g_send.at[0], g_recv.at[0], z_up),
        remote(send_down.at[1], relay_down, g_send.at[1], g_recv.at[1], z_down),
        remote(send_up.at[0], up_grad.at[z], g_send.at[2], g_recv.at[2], z_down),
        remote(send_down.at[0], down_grad.at[z], g_send.at[3], g_recv.at[3], z_down),
        remote(send_up.at[2], up_grad.at[z], g_send.at[4], g_recv.at[4], z_up),
        remote(send_down.at[2], down_grad.at[z], g_send.at[5], g_recv.at[5], z_up),
    ]
    relayed = [
        remote(relay_up, up_grad.at[(z + 3) % 4], g_send.at[6], g_recv.at[6], z_up),
        remote(relay_down, down_grad.at[(z + 1) % 4], g_send.at[7], g_recv.at[7], z_down),
    ]
    yh, xx = s // 4, s % 4
    x_up, x_down = (xx + 1) % 4, (xx + 3) % 4
    to_up, to_down = at(yh * 4 + x_up, z, y, c), at(yh * 4 + x_down, z, y, c)
    across = (1 - yh) * 4 + xx
    half = (pl.ds(0, 2 * C), pl.ds(2 * C, 2 * C))

    def neighbours(source, slot, n):
        return [
            remote(source, mn_all.at[slot], m_sem.at[0, n], m_sem.at[1, n], to_up),
            remote(source, mn_all.at[slot], m_sem.at[0, n + 1], m_sem.at[1, n + 1], to_down),
        ]

    def halves(base, n):
        below, above = base * 4 + x_down, base * 4 + x_up
        low, high = mn_all.at[below, :, half[0]], mn_all.at[above, :, half[1]]
        return [
            remote(low, low, m_sem.at[0, n], m_sem.at[1, n], to_up),
            remote(high, high, m_sem.at[0, n + 1], m_sem.at[1, n + 1], to_down),
        ]

    spread_own = neighbours(merge_norm, s, 0)
    spread_across = neighbours(mn_all.at[across], across, 2)
    far_own = halves(yh, 4)
    far_across = halves(1 - yh, 6)
    partner = remote(merge_norm, mn_all.at[s], m_sem.at[0, 8], m_sem.at[1, 8], at(across, z, y, c))
    tail_copies = []
    for k in range(1, 8):
        peer = (s + k) % 8
        tail_copies.append(remote(mn_tail, mt_all.at[s], m_sem.at[2, k], m_sem.at[3, k], at(peer, z, y, c)))
    gifts = spread_own + spread_across + far_own + far_across + [partner] + tail_copies
    own = [
        pltpu.make_async_copy(merge_norm, mn_all.at[s], io_sem.at[14]),
        pltpu.make_async_copy(mn_tail, mt_all.at[s], io_sem.at[11]),
    ]
    own_out = [
        pltpu.make_async_copy(send_up.at[3], up_grad.at[z], io_sem.at[12]),
        pltpu.make_async_copy(send_down.at[3], down_grad.at[z], io_sem.at[13]),
    ]

    def grads():
        for copy in ins[3:5]:
            copy.wait()
        for k in (2, 1, 3, 0):
            span = slice(k * 256, (k + 1) * 256)
            up_part = dot(flat[...], slope[:, span], 0, 0)
            down_part = dot(act[:, span], flat_d[...], 0, 0)
            send_up[(k + 3) % 4] = up_part.astype(BF)
            send_down[(k + 3) % 4] = down_part.astype(BF)
            if k:
                first = {2: 0, 1: 2, 3: 4}[k]
                returns[first].start()
                returns[first + 1].start()
            else:
                for copy in own_out:
                    copy.start()

    finish_sends = slots_through(place, d_slots, recv, part, other, total, across_sum, ret, slot_sems, compute, grads)
    for copy in spread_own + [partner] + tail_copies + own:
        copy.start()
    after_back(after, ret, table, d_block, d_after, d_att)
    halo_copy = remote(d_att.at[pl.ds(0, HALO)], halo, halo_sem.at[0], halo_sem.at[1], prv)
    halo_copy.start()
    lay_rows(tokens, x_wide, x)
    acc[...] = jnp.zeros_like(acc)
    for copy in ins[5:9] + ins[10:]:
        copy.wait()
    halo_copy.wait_recv()
    halo_copy.wait_send()
    top = jnp.where(iota((HALO, C), 0) < 14 * r, halo[...].astype(F32), d_att[:HALO, :].astype(F32))
    d_att[:HALO, :] = top.astype(BF)

    def group(g, carry):
        attn_group_back(g, d_att, wqkv, wo, qkv, probs, mixed, acc)
        return carry

    lax.fori_loop(0, 1, group, 0)
    for arrived, onward in zip(spread_own, far_own):
        arrived.wait_recv()
        onward.start()
    lax.fori_loop(1, 2, group, 0)
    partner.wait_recv()
    for onward in spread_across:
        onward.start()
    lax.fori_loop(2, 3, group, 0)
    for arrived, onward in zip(returns, relayed):
        arrived.wait_recv()
        onward.start()
    lax.fori_loop(3, 4, group, 0)
    d_shift[...] = acc[...].astype(BF)
    halo2_copy = remote(d_shift.at[pl.ds(0, HALO)], halo2, halo_sem.at[2], halo_sem.at[3], nxt)
    halo2_copy.start()

    for arrived, onward in zip(spread_across, far_across):
        arrived.wait_recv()
        onward.start()
    halo2_copy.wait_recv()
    top = jnp.where(iota((HALO, C), 0) < 14 * r, halo2[...].astype(F32), d_shift[:HALO, :].astype(F32))
    x_wide[:HALO, :] = d_after[:HALO, :] + norm_back(x[:HALO, :].astype(F32), top)
    x_wide[HALO:, :] = d_after[HALO:, :] + norm_back(x[HALO:, :].astype(F32), d_shift[HALO:, :].astype(F32))
    for i in range(14):
        tokens_grad[0, i] = x_wide[14 * i:14 * i + 14, :].astype(BF)

    for copy in far_own + far_across + tail_copies:
        copy.wait_recv()
    for copy in own + [ins[9]]:
        copy.wait()
    merged_wide[:, :48, :] = dot(mn_all[...].reshape(8 * 48, 4 * C), wred[...]).reshape(8, 48, 256)
    tails = mt_all[...].astype(F32)
    last = jnp.concatenate([tails[:, i, :] for i in range(16)], axis=1)
    last = jnp.concatenate([last, jnp.zeros_like(last)], axis=0).astype(BF)
    merged_wide[:, 48, :] = dot(last, wred[...])[:8]
    for n in range(8):
        merged_rows[:, n, :] = merged_wide[n]
    merged[...] = merged_rows[...].reshape(7, 7, 8, 256).astype(BF)

    for copy in returns[2:] + relayed:
        copy.wait_recv()
    for copy in own_out:
        copy.wait()
    finish_sends()
    for copy in returns + relayed + gifts + [halo2_copy]:
        copy.wait_send()


def widen(up_in, down_in, grad_in, merged_in, up_out, down_out, grad_out, merged_out, wide_up, wide_down, sems):
    copies = [
        pltpu.make_async_copy(grad_in, grad_out, sems.at[8]), pltpu.make_async_copy(merged_in, merged_out, sems.at[9]),
    ]
    for e in range(4):
        for n, (source, wide, out) in enumerate(((up_in, wide_up, up_out), (down_in, wide_down, down_out))):
            wide[e] = source[e].astype(F32)
            copies.append(pltpu.make_async_copy(wide.at[e], out.at[e], sems.at[2 * e + n]))
            copies[-1].start()
    for copy in copies[:2]:
        copy.start()
    for copy in copies:
        copy.wait()


def bias_pairs():
    spot = np.arange(49)
    py, px = spot // 7, spot % 7
    relative = (py[:, None] - py[None, :] + 6) * 13 + (px[:, None] - px[None, :] + 6)
    table = np.zeros((169, 50, 128), np.float32)
    a, b = np.meshgrid(spot, spot, indexing="ij")
    table[relative.reshape(-1), b.reshape(-1), a.reshape(-1)] = 1.0
    return table.reshape(169, 6400)


def local(
    tokens,
    qkv_weight,
    out_weight,
    position_bias,
    window_shift,
    expert_up,
    expert_down,
    expert_choice,
    combine_weight,
    reduce_weight,
    merged_grad,
):
    choice = jnp.transpose(expert_choice, (1, 0, 3, 2)).reshape(14, 1, 14)
    gate = jnp.transpose(combine_weight, (1, 0, 2))
    pairs = jnp.asarray(bias_pairs(), dtype=BF)
    V = pltpu.VMEM
    D = pltpu.SemaphoreType.DMA

    after, table, merge_norm, mn_tail, d_block, d_slots, qkv, probs, mixed, flat_in, act, slope, ups, downs = pl.pallas_call(
        front,
        out_shape=[
            sds((TP, C), BF), sds((TP, 256), BF), sds((48, 4 * C), BF), sds((16, 256), BF), sds((TP, C), F32),
            sds((32, 16, HC), BF), sds((3, 4, TP, GRP), BF), sds((32 * TP, TP), BF), sds((4, GRP, TP), BF), sds((C, C), BF), sds((C, C), BF),
            sds((C, C), BF), sds((4, C, 256), BF), sds((4, 256, C), BF),
        ],
        in_specs=[SM, VM, VM, VM, VM, HB, VM] + [HB] * 5,
        out_specs=[VM] * 6 + [HB] * 8,
        scratch_shapes=[
            V((TP, C), BF), V((TP, C), F32), V((32, 64, 128), F32), V((169, 6400), BF), V((8, 49, 256), F32),
            V((HALO, C), BF), V((HALO, C), BF), V((TP, C), BF), V((TP, TP), F32),
            V((192, TP), BF), V((TP, 192), BF), V((TP, C), F32), V((TP, C), BF),
            V((C, 3 * C), BF), V((C, C), BF), V((4 * C, 256), BF),
            V((3, 4, TP, GRP), BF), V((32 * TP, TP), BF), V((4, GRP, TP), BF),
            V((8, 48, 4 * C), BF), V((2, 48, 4 * C), BF), V((2, 48, 4 * C), BF), V((2, 48, 4 * C), BF),
            V((48, 4 * C), BF), V((8, 16, 256), F32),
            V((8, 16, 256), BF), V((8, 16, 256), BF),
            V((4, C, 256), BF), V((4, 256, C), BF), V((C, 256), BF), V((256, C), BF),
            V((32, 16, HC), BF), V((4, 32, 16, HC), BF), V((4, 32, 16, HC), BF),
            V((2, 32, 16, HC), BF), V((2, 32, 16, HC), BF), V((32, 16, HC), BF), V((32, 16, HC), BF),
            V((C, C), BF), V((C, C), BF), V((C, C), BF), V((256, C), F32),
            D((16,)), D((4,)), D((8,)), D((8,)), D((4, 8)), *SLOT_SEMS,
        ],
        compiler_params=params(collective_id=0, has_side_effects=True),
        cost_estimate=cost(12 << 30, 60 << 20),
        name="front",
    )(window_shift, tokens, choice, gate, position_bias, pairs, jnp.transpose(merged_grad, (1, 2, 0, 3)), qkv_weight, out_weight,
      expert_up, expert_down, reduce_weight)

    tokens_grad, merged, up_grad, down_grad = pl.pallas_call(
        back,
        out_shape=[
            sds(tokens.shape, BF), sds((7, 7, 8, 256), BF), sds((4, C, 256), BF), sds((4, 256, C), BF),
        ],
        in_specs=[SM] + [VM] * 7 + [HB] * 11,
        out_specs=[VM] * 4,
        scratch_shapes=[
            V((TP, C), BF), V((TP, C), F32), V((HALO, C), BF), V((HALO, C), BF), V((TP, C), BF), V((TP, C), F32),
            V((TP, C), F32), V((TP, C), BF), V((C, 3 * C), BF), V((C, C), BF), V((4 * C, 256), BF),
            V((3, 4, TP, GRP), BF), V((32 * TP, TP), BF), V((4, GRP, TP), BF), V((C, C), BF), V((C, C), BF), V((C, C), BF),
            V((4, C, 256), BF), V((4, 256, C), BF),
            V((4, 32, 16, HC), BF), V((4, 32, 16, HC), BF), V((2, 32, 16, HC), BF), V((2, 32, 16, HC), BF),
            V((32, 16, HC), BF), V((32, 16, HC), BF), V((C, C), BF), V((4, C, 256), BF), V((4, 256, C), BF), V((C, 256), BF), V((256, C), BF),
            V((8, 48, 4 * C), BF), V((8, 16, 256), BF), V((8, 49, 256), F32), V((49, 8, 256), F32),
            D((20,)), D((4,)), D((8,)), D((8,)), D((4, 9)), *SLOT_SEMS,
        ],
        compiler_params=pltpu.CompilerParams(
            vmem_limit_bytes=60 * 1024 * 1024, collective_id=1, has_side_effects=True
        ),
        cost_estimate=cost(16 << 30, 60 << 20),
        name="back",
    )(window_shift, tokens, after, table, merge_norm, mn_tail, d_block, d_slots, qkv_weight, out_weight, reduce_weight,
      qkv, probs, mixed, flat_in, act, slope, ups, downs)
    up_grad, down_grad, tokens_grad, merged = pl.pallas_call(
        widen,
        out_shape=[
            sds((4, C, 256), F32), sds((4, 256, C), F32), sds(tokens_grad.shape, BF), sds(merged.shape, BF),
        ],
        in_specs=[VM] * 4,
        out_specs=[HB] * 4,
        scratch_shapes=[V((4, C, 256), F32), V((4, 256, C), F32), D((10,))],
        compiler_params=params(),
        cost_estimate=cost(0, 14 << 20),
        name="widen",
    )(up_grad, down_grad, tokens_grad, merged)
    return (jnp.transpose(merged, (2, 0, 1, 3)), tokens_grad, up_grad, down_grad)


def solution(mesh):
    placed = (
        P("scene", "row", None, None),
        P(),
        P(),
        P(),
        P(),
        P("scene", None, "row"),
        P("scene", "row", None),
        P("scene", "row", None, None),
        P("scene", "row", None),
        P(None, "scene"),
        P(None, "row", None, "scene"),
    )
    return jax.shard_map(
        local,
        mesh=mesh,
        in_specs=placed,
        out_specs=(
            P(None, "row", None, "scene"),
            P("scene", "row", None, None),
            P("scene", None, "row"),
            P("scene", "row", None),
        ),
        check_vma=False,
    )
```

```python
import functools

import jax
import jax.numpy as jnp
import numpy as np
from jax import lax
from jax.experimental import pallas as pl
from jax.experimental.pallas import tpu as pltpu
from jax.sharding import PartitionSpec as P

MESH = pl.DeviceIdType.MESH
F32 = jnp.float32
BF = jnp.bfloat16
EPS = 1e-5
C = 1024
HC = C // 2
TOK = 196
TP = 208
HALO = 96
GRP = 256
NEG = -1e30
VMEM_BIG = 56 * 1024 * 1024
VM = pl.BlockSpec(memory_space=pltpu.VMEM)
SM = pl.BlockSpec(memory_space=pltpu.SMEM)
HB = pl.BlockSpec(memory_space=pl.ANY)


def sds(shape, dtype):
    return jax.ShapeDtypeStruct(shape, dtype)


def params(**kw):
    return pltpu.CompilerParams(vmem_limit_bytes=VMEM_BIG, **kw)


def cost(flops, nbytes):
    return pl.CostEstimate(flops=flops, bytes_accessed=nbytes, transcendentals=0)


def dot(a, b, da=1, db=0):
    return lax.dot_general(a, b, (((da,), (db,)), ((), ())), preferred_element_type=F32)


def iota(shape, dim):
    return lax.broadcasted_iota(jnp.int32, shape, dim)


def norm_parts(values):
    centre = jnp.mean(values, axis=-1, keepdims=True)
    centred = values - centre
    spread = jnp.mean(centred * centred, axis=-1, keepdims=True)
    scale = lax.rsqrt(spread + EPS)
    return centred * scale, scale


def norm_back(values, cot):
    unit, scale = norm_parts(values)
    mean_cot = jnp.mean(cot, axis=-1, keepdims=True)
    mean_dot = jnp.mean(cot * unit, axis=-1, keepdims=True)
    return scale * (cot - mean_cot - unit * mean_dot)


def split3(values):
    high = values.astype(BF)
    rest = values - high.astype(F32)
    mid = rest.astype(BF)
    low = (rest - mid.astype(F32)).astype(BF)
    return high, mid, low


def place_of(tok, r, c):
    rho = (tok * 4682) >> 16
    gam = tok - 14 * rho
    i = rho - r
    i = jnp.where(i < 0, i + 14, i)
    j = gam - c
    j = jnp.where(j < 0, j + 14, j)
    a = jnp.where(i >= 7, 1, 0)
    b = jnp.where(j >= 7, 1, 0)
    return i, j, a, b


def pos_of(tok, r, c):
    i, j, a, b = place_of(tok, r, c)
    return (i - 7 * a) * 7 + (j - 7 * b)


def group_of(tok, r, c, last):
    i, j, a, b = place_of(tok, r, c)
    la = jnp.where(i >= 7, jnp.where(i < 14 - r, 1, 2), 0) * last
    lb = jnp.where(j >= 7, jnp.where(j < 14 - c, 1, 2), 0)
    return a * 2 + b, la * 3 + lb


def pack_rows(low, high, blocks):
    return jnp.concatenate([low.reshape(blocks, 8, HC), high.reshape(blocks, 8, HC)], axis=1).astype(BF)


def unpack_rows(packed, blocks):
    wide = packed.astype(F32)
    low = wide[:, :8, :].reshape(blocks * 8, HC)
    high = wide[:, 8:, :].reshape(blocks * 8, HC)
    return low, high


def attn_masks(r, c, last, mask, ecol, erow):
    tq, tk = iota((TP, TP), 0), iota((TP, TP), 1)
    wq_, lq = group_of(tq, r, c, last)
    wk_, lk = group_of(tk, r, c, last)
    seen = jnp.where(wq_ == wk_, jnp.where(lq == lk, 0.0, -100.0), NEG)
    mask[...] = jnp.where(tq < TOK, seen, NEG)
    row_pos = pos_of(iota((TP, 192), 0), r, c)
    erow[...] = jnp.where(row_pos == (iota((TP, 192), 1) & 63), 1.0, 0.0).astype(BF)
    col_pos = pos_of(iota((192, TP), 1), r, c)
    ecol[...] = jnp.where(col_pos == (iota((192, TP), 0) & 63), 1.0, 0.0).astype(BF)


def cols(start):
    return pl.ds(pl.multiple_of(start, GRP), GRP)


def turned(values, eye):
    return dot(eye, values, 1, 1)


def unit_table():
    return jnp.where(iota((GRP, GRP), 0) == iota((GRP, GRP), 1), 1.0, 0.0).astype(BF)


def attn_group(g, normed, wqkv, wo, bias, mask, ecol, erow, qkv, probs, mixed, acc):
    n = normed[...]
    q = dot(n, wqkv[:, cols(g * GRP)]).astype(BF)
    k = dot(n, wqkv[:, cols(C + g * GRP)]).astype(BF)
    v = dot(n, wqkv[:, cols(2 * C + g * GRP)]).astype(BF)
    qkv[0, g] = q
    qkv[1, g] = k
    qkv[2, g] = v
    eye = unit_table()
    q_t = turned(q, eye).astype(BF)
    v_t = turned(v, eye).astype(BF)
    wide = dot(jnp.concatenate(split3(bias[pl.ds(g * 8, 8)][:, :, :64].reshape(8 * 64, 64)), axis=1), ecol[...])
    w_hi, w_mid, w_lo = split3(wide)
    lane_head = iota((TP, GRP), 1) >> 5
    k32 = k.astype(F32)
    outs = []
    for h in range(8):
        km = jnp.where(lane_head == h, k32, 0.0).astype(BF)
        part = slice(h * 64, h * 64 + 64)
        s = dot(km, q_t) * (32.0 ** -0.5)
        s = s + dot(erow[...], jnp.concatenate([w_hi[part], w_mid[part], w_lo[part]], axis=0)) + mask[...]
        e = jnp.exp(s - jnp.max(s, axis=0, keepdims=True))
        p = (e * (1.0 / jnp.sum(e, axis=0, keepdims=True))).astype(BF)
        probs[pl.ds(pl.multiple_of((g * 8 + h) * TP, 16), TP), :] = p
        outs.append(dot(v_t[32 * h:32 * h + 32], p))
    mixed_t = jnp.concatenate(outs, axis=0).astype(BF)
    mixed[g] = mixed_t
    acc[...] += dot(mixed_t, wo[pl.ds(pl.multiple_of(g * GRP, GRP), GRP), :], 0, 0)


def attn_group_back(g, d_att, wqkv, wo, qkv, probs, mixed, acc):
    q, k, v = qkv[0, g], qkv[1, g], qkv[2, g]
    eye = unit_table()
    d_out = dot(d_att[...], wo[pl.ds(pl.multiple_of(g * GRP, GRP), GRP), :], 1, 1).astype(BF)
    d_out_t = turned(d_out, eye)
    weighed = d_out_t * mixed[g].astype(F32)
    d_out_t = d_out_t.astype(BF)
    k_t = turned(k, eye).astype(BF)
    v32 = v.astype(F32)
    lane_head = iota((TP, GRP), 1) >> 5
    dq_t = []
    dk = jnp.zeros((TP, GRP), F32)
    dv = jnp.zeros((TP, GRP), F32)
    for h in range(8):
        mine = lane_head == h
        vm = jnp.where(mine, v32, 0.0).astype(BF)
        p = probs[pl.ds(pl.multiple_of((g * 8 + h) * TP, 16), TP), :]
        shared = jnp.sum(weighed[32 * h:32 * h + 32], axis=0, keepdims=True)
        ds = (p.astype(F32) * (dot(vm, d_out_t) - shared)).astype(BF)
        dq_t.append(dot(k_t[32 * h:32 * h + 32], ds))
        dk = jnp.where(mine, dot(ds, q), dk)
        dv = jnp.where(mine, dot(p, d_out), dv)
    scale = 32.0 ** -0.5
    dq = jnp.transpose(jnp.concatenate(dq_t, axis=0) * scale)
    acc[...] += (
        dot(dq.astype(BF), wqkv[:, cols(g * GRP)], 1, 1)
        + dot((dk * scale).astype(BF), wqkv[:, cols(C + g * GRP)], 1, 1)
        + dot(dv.astype(BF), wqkv[:, cols(2 * C + g * GRP)], 1, 1)
    )


def route(r, x, att, halo, choice, after_out, slots, table_out):
    top = jnp.where(iota((HALO, C), 0) < 14 * r, halo[...].astype(F32), att[:HALO, :].astype(F32))
    after_out[:HALO, :] = (x[:HALO, :].astype(F32) + top).astype(BF)
    after_out[HALO:, :] = (x[HALO:, :].astype(F32) + att[HALO:, :].astype(F32)).astype(BF)
    after = after_out[...].astype(F32)
    n2 = norm_parts(after)[0].astype(BF)
    tok, other = iota((TP, TP), 0), iota((TP, TP), 1)
    col = jnp.where(iota((TP, 1), 0) < TOK, choice, -1000.0)
    line = jnp.sum(jnp.where(tok == other, col, 0.0), axis=0, keepdims=True)
    same = jnp.where(col == line, 1.0, 0.0)
    same = jnp.where(other < tok, same, 0.0)
    rank = jnp.sum(same, axis=1, keepdims=True).astype(jnp.int32)
    table = jnp.where(col.astype(jnp.int32) * 8 + rank == iota((TP, 256), 1), 1.0, 0.0).astype(BF)
    table_out[...] = table
    slots[...] = pack_rows(dot(table, n2[:, :HC], 0, 0), dot(table, n2[:, HC:], 0, 0), 32)


def quad_table():
    row = iota((256, TP), 0)
    tok = iota((256, TP), 1)
    q = row >> 6
    n = row & 63
    a = (n * 9363) >> 16
    b = n - 7 * a
    want = (2 * a + (q & 1)) * 14 + 2 * b + (q >> 1)
    hit = jnp.where(want == tok, 1.0, 0.0)
    return jnp.where(n < 49, hit, 0.0).astype(BF)


def gathered(ret, table):
    low, high = unpack_rows(ret[0].astype(F32) + ret[1].astype(F32), 32)
    return jnp.concatenate([dot(table, low.astype(BF)), dot(table, high.astype(BF))], axis=1)


def merge_mid(after, ret, table_in, gate, parts, tail, mn_out, mn_tail, d_block_out, slots, spread, t_wide):
    table = table_in[...]
    block = (after[...].astype(F32) + gate * gathered(ret, table)).astype(BF)
    perm = quad_table()
    quads = dot(perm, block)
    vals = [quads[64 * q:64 * q + 49, :] for q in range(4)]
    inv = 1.0 / (4 * C)
    centre = sum(jnp.sum(v, axis=-1, keepdims=True) for v in vals) * inv
    cent = [v - centre for v in vals]
    var = sum(jnp.sum(v * v, axis=-1, keepdims=True) for v in cent) * inv
    scale = lax.rsqrt(var + EPS)
    unit = [v * scale for v in cent]
    for q in range(4):
        mn_out[:, q * C:(q + 1) * C] = unit[q][:48].astype(BF)
        for i in range(4):
            t_wide[0, 4 * q + i:4 * q + i + 1, :] = unit[q][48:49, i * 256:(i + 1) * 256]
    mn_tail[...] = t_wide[0].astype(BF)
    tails = jnp.sum(tail[...].astype(F32), axis=0)
    cots = []
    for q in range(4):
        tot = sum(part[:, q * C:(q + 1) * C].astype(F32) for part in parts)
        last = jnp.concatenate([tails[4 * q + i:4 * q + i + 1, :] for i in range(4)], axis=1)
        cots.append(jnp.concatenate([tot, last], axis=0))
    mean_cot = sum(jnp.sum(v, axis=-1, keepdims=True) for v in cots) * inv
    mean_dot = sum(jnp.sum(v * u, axis=-1, keepdims=True) for v, u in zip(cots, unit)) * inv
    spread[...] = jnp.zeros_like(spread)
    for q in range(4):
        spread[64 * q:64 * q + 49, :] = scale * (cots[q] - mean_cot - unit[q] * mean_dot)
    high, mid, low = split3(spread[...])
    d_block = dot(perm, high, 0, 0) + dot(perm, mid, 0, 0) + dot(perm, low, 0, 0)
    d_block_out[...] = d_block
    scaled = (gate * d_block).astype(BF)
    slots[...] = pack_rows(dot(table, scaled[:, :HC], 0, 0), dot(table, scaled[:, HC:], 0, 0), 32)


def after_back(after, ret, table, d_block, d_after_out, d_att_out):
    d_second = gathered(ret, table[...])
    d_after = d_block[...] + norm_back(after[...].astype(F32), d_second)
    d_after_out[...] = d_after
    d_att_out[...] = d_after.astype(BF)


def token_column(grid):
    tok = iota((TP, 14), 0)
    rho = (tok * 4682) >> 16
    place = iota((TP, 14), 1)
    pick = jnp.where(rho == place, 1.0, 0.0).astype(BF)
    high, mid, low = split3(grid[...].reshape(14, 14))
    rows = dot(pick, high) + dot(pick, mid) + dot(pick, low)
    return jnp.sum(jnp.where(tok - 14 * rho == place, rows, 0.0), axis=1, keepdims=True)


def lay_rows(tokens, wide, x):
    wide[TOK - 4:, :] = jnp.zeros((TP - TOK + 4, C), F32)
    for i in range(14):
        wide[14 * i:14 * i + 14, :] = tokens[0, i].astype(F32)
    x[...] = wide[...].astype(BF)


SHARES = (0, 4, 1, 5, 3, 7, 2, 6)


def expert_chunk(j, recv, part, ups, downs, flat, act_out, slope_out, ready):
    here = pl.ds(8 * j, 8)
    rows_here = pl.ds(128 * j, 128)
    low, high = unpack_rows(recv[:, here].reshape(16, 16, HC), 16)
    rows = jnp.concatenate([low, high], axis=1).astype(BF)
    flat[rows_here, :] = rows
    total = jnp.zeros((128, C), F32)
    for k in SHARES:
        ready(k)
        pre = dot(rows, ups[k])
        cdf = 0.5 * (1.0 + lax.erf(pre * np.float32(2.0 ** -0.5)))
        act = (pre * cdf).astype(BF)
        slope = cdf + pre * jnp.exp(-0.5 * pre * pre) * np.float32((2.0 * np.pi) ** -0.5)
        act_out[rows_here, k * 256:(k + 1) * 256] = act
        slope_out[rows_here, k * 256:(k + 1) * 256] = slope.astype(BF)
        total = total + dot(act, downs[k])
    part[:, here] = pack_rows(total[:, :HC], total[:, HC:], 16).reshape(2, 8, 16, HC)


def expert_chunk_back(j, recv, part, ups, downs, flat, slope):
    here = pl.ds(8 * j, 8)
    rows_here = pl.ds(128 * j, 128)
    low, high = unpack_rows(recv[:, here].reshape(16, 16, HC), 16)
    rows = jnp.concatenate([low, high], axis=1).astype(BF)
    flat[rows_here, :] = rows
    total = jnp.zeros((128, C), F32)
    for k in range(8):
        span = slice(k * 256, (k + 1) * 256)
        d_pre = (slope[rows_here, span].astype(F32) * dot(rows, downs[k], 1, 1)).astype(BF)
        slope[rows_here, span] = d_pre
        total = total + dot(d_pre, ups[k], 1, 1)
    part[:, here] = pack_rows(total[:, :HC], total[:, HC:], 16).reshape(2, 8, 16, HC)


def coords():
    s = lax.axis_index("scene")
    row = lax.axis_index("row")
    z, m = row // 4, row % 4
    return s, z, m // 2, m % 2


def at(s, z, y, c):
    return (s, z * 4 + y * 2 + c)


def greet(s, z, y, c, total=64):
    barrier = pltpu.get_barrier_semaphore()
    mine = s * 4 + z

    def hail(k, carry):
        peer = (mine + k) % 32
        pl.semaphore_signal(barrier, inc=1, device_id=at(peer // 4, peer % 4, y, c), device_id_type=MESH)
        pl.semaphore_signal(barrier, inc=1, device_id=at(peer // 4, peer % 4, 1 - y, c), device_id_type=MESH)
        return carry

    lax.fori_loop(1, 32, hail, 0)
    pl.semaphore_signal(barrier, inc=1, device_id=at(s, z, 1 - y, c), device_id_type=MESH)
    pl.semaphore_signal(barrier, inc=1, device_id=at(s, z, y, 1 - c), device_id_type=MESH)
    pl.semaphore_wait(barrier, total)


def greet_all(place):
    s, z, y, c = place
    barrier = pltpu.get_barrier_semaphore()
    row = z * 4 + y * 2 + c
    pl.semaphore_signal(barrier, inc=1, device_id=(s, (row + 1) % 16), device_id_type=MESH)
    pl.semaphore_signal(barrier, inc=1, device_id=(s, (row + 15) % 16), device_id_type=MESH)
    greet(s, z, y, c, 66)


def remote(src, dst, send, recv, device):
    return pltpu.make_async_remote_copy(
        src_ref=src, dst_ref=dst, send_sem=send, recv_sem=recv, device_id=device, device_id_type=MESH
    )


def await_bytes(ref, sem):
    pltpu.make_async_copy(ref, ref, sem).wait()


SLOT_SEMS = [
    pltpu.SemaphoreType.DMA, pltpu.SemaphoreType.DMA((2, 4)), pltpu.SemaphoreType.DMA, pltpu.SemaphoreType.DMA,
]


def slots_through(place, slots, recv, part, ret, sems, compute, meanwhile=None):
    s, z, y, c = place
    mine = s * 4 + z
    send, arrive, r_send, r_recv = sems
    yh, xx = s // 4, s % 4

    def steps(k):
        dx = k % 4
        return (k % 8) // 4, dx, (k // 8 + 4 - dx) % 4

    def ahead(k):
        dy, dx, dz = steps(k)
        return ((yh + dy) % 2 * 4 + (xx + dx) % 4) * 4 + (z + dz) % 4

    def behind(k):
        dy, dx, dz = steps(k)
        return ((yh + dy) % 2 * 4 + (xx + 4 - dx) % 4) * 4 + (z + 4 - dz) % 4

    def to_peer(k, peer, yy):
        remote(slots.at[peer], recv.at[y, k], send, arrive.at[y, k // 8], at(peer // 4, peer % 4, yy, c)).start()

    def push(k, carry):
        peer = ahead(k)
        to_peer(k, peer, y)
        to_peer(k, peer, 1 - y)
        return carry

    pltpu.make_async_copy(slots.at[mine], recv.at[y, 0], arrive.at[y, 0]).start()
    to_peer(0, mine, 1 - y)
    lax.fori_loop(1, 32, push, 0)

    def give(k, yy):
        peer = behind(k)
        remote(part.at[yy, k], ret.at[y, mine], r_send, r_recv, at(peer // 4, peer % 4, yy, c)).start()

    def give_both(k, carry):
        give(k, 1 - y)
        give(k, y)
        return carry

    for j in range(4):
        for yy in range(2):
            await_bytes(recv.at[yy, pl.ds(8 * j, 8)], arrive.at[yy, j])
        compute(j)
        if j == 0:
            give(0, 1 - y)
            pltpu.make_async_copy(part.at[y, 0], ret.at[y, mine], r_recv).start()
        lax.fori_loop(max(1, 8 * j), 8 * j + 8, give_both, 0)

    def finish_sends():
        for sem in (send, r_send):
            await_bytes(part.at[0], sem)
            await_bytes(part.at[0, pl.ds(0, 31)], sem)

    if meanwhile is not None:
        meanwhile()
    await_bytes(ret, r_recv)
    return finish_sends


def front(
    shift, tokens, choice_in, gate_in, position_bias, pairs, merged_grad, qkv_weight, out_weight, expert_up, expert_down, reduce_weight,
    after, table, merge_norm, mn_tail, d_block, d_slots, qkv_out, probs_out, mixed_out, flat_out, act_out, slope_out, up_out, down_out,
    x, x_wide, bias, table_of, grad_wide, halo, halo2, normed, mask, ecol, erow, acc, att, wqkv, wo, wred, qkv, probs, mixed,
    d_send, d_relay, d_direct, d_summed, d_across, t_wide, t_send, t_recv, ups, downs, relay_up, relay_down,
    slots, recv, part, ret, flat, act, slope, spread,
    io_sem, halo_sem, w_send, w_recv, c_send, c_recv, d_sem, *slot_sems,
):
    place = coords()
    s, z, y, c = place
    row = z * 4 + y * 2 + c
    r, cc = shift[0], shift[1]
    last = jnp.where(row == 15, 1, 0)
    ins = [
        pltpu.make_async_copy(reduce_weight, wred, io_sem.at[0]),
        pltpu.make_async_copy(qkv_weight, wqkv, io_sem.at[1]),
        pltpu.make_async_copy(out_weight, wo, io_sem.at[2]),
        pltpu.make_async_copy(expert_up.at[z], ups.at[0], io_sem.at[3]),
        pltpu.make_async_copy(expert_down.at[z], downs.at[0], io_sem.at[4]),
        pltpu.make_async_copy(pairs, table_of, io_sem.at[14]),
    ]
    for copy in ins:
        copy.start()
    lay_rows(tokens, x_wide, x)
    greet_all(place)

    nxt = (s, (row + 1) % 16)
    prv = (s, (row + 15) % 16)
    z_up, z_down = at(s, (z + 1) % 4, y, c), at(s, (z + 3) % 4, y, c)
    halo_copy = remote(x.at[pl.ds(0, HALO)], halo, halo_sem.at[0], halo_sem.at[1], prv)
    halo_copy.start()
    weights = [
        remote(expert_up.at[(z + 2) % 4], relay_up, w_send.at[0], w_recv.at[0], z_up),
        remote(expert_down.at[(z + 2) % 4], relay_down, w_send.at[1], w_recv.at[1], z_down),
        remote(expert_up.at[(z + 1) % 4], ups.at[1], w_send.at[2], w_recv.at[2], z_up),
        remote(expert_up.at[(z + 3) % 4], ups.at[3], w_send.at[3], w_recv.at[3], z_down),
        remote(expert_down.at[(z + 1) % 4], downs.at[1], w_send.at[4], w_recv.at[4], z_up),
        remote(expert_down.at[(z + 3) % 4], downs.at[3], w_send.at[5], w_recv.at[5], z_down),
    ]
    for copy in weights:
        copy.start()
    pair = at(s, z, y, 1 - c)
    doubled = [
        [
            remote(ups.at[k], ups.at[4 + k], c_send.at[0, k], c_recv.at[0, k], pair),
            remote(downs.at[k], downs.at[4 + k], c_send.at[1, k], c_recv.at[1, k], pair),
        ]
        for k in range(4)
    ]
    relayed = [
        remote(relay_up, ups.at[2], w_send.at[6], w_recv.at[6], z_up),
        remote(relay_down, downs.at[2], w_send.at[7], w_recv.at[7], z_down),
    ]

    by_place = merged_grad[...].astype(F32).reshape(49, 8, 256)
    for n in range(8):
        grad_wide[n] = by_place[:, n, :]
    grad48 = grad_wide[:, :48, :].astype(BF).reshape(8 * 48, 256)
    grad_tail = jnp.concatenate([grad_wide[:, 48, :], jnp.zeros((8, 256), F32)], axis=0).astype(BF)
    ins[0].wait()
    for half in range(4):
        span = pl.ds(half * C, C)
        d_send[:, :, span] = dot(grad48, wred[span, :], 1, 1).astype(BF).reshape(8, 48, C)
        tail = dot(grad_tail, wred[span, :], 1, 1)
        for i in range(4):
            t_wide[:, 4 * half + i, :] = tail[:8, i * 256:(i + 1) * 256]
    t_send[...] = t_wide[...].astype(BF)
    yh, xx = s // 4, s % 4
    x_up, x_down, x_far = (xx + 1) % 4, (xx + 3) % 4, (xx + 2) % 4
    to_up, to_down = at(yh * 4 + x_up, z, y, c), at(yh * 4 + x_down, z, y, c)
    first = [
        remote(d_send.at[x_far], d_relay.at[0], d_sem.at[0, 0], d_sem.at[1, 0], to_up),
        remote(d_send.at[4 + x_far], d_relay.at[1], d_sem.at[0, 1], d_sem.at[1, 1], to_down),
        remote(d_send.at[4 + x_up], d_direct.at[1], d_sem.at[0, 2], d_sem.at[1, 2], to_up),
        remote(d_send.at[x_down], d_direct.at[0], d_sem.at[0, 3], d_sem.at[1, 3], to_down),
    ]
    second = [
        remote(d_send.at[x_up], d_summed.at[0], d_sem.at[0, 4], d_sem.at[1, 4], to_up),
        remote(d_send.at[4 + x_down], d_summed.at[1], d_sem.at[0, 5], d_sem.at[1, 5], to_down),
    ]
    other_yh = 1 - yh
    across = remote(
        d_send.at[other_yh * 4 + xx], d_across, d_sem.at[0, 6], d_sem.at[1, 6], at(other_yh * 4 + xx, z, y, c)
    )
    gifts = []
    for k in range(1, 8):
        peer = (s + k) % 8
        gifts.append(remote(t_send.at[peer], t_recv.at[s], d_sem.at[2, k], d_sem.at[3, k], at(peer, z, y, c)))
    for copy in first + gifts:
        copy.start()
    own = pltpu.make_async_copy(t_send.at[s], t_recv.at[s], io_sem.at[6])
    own.start()

    def pass_on():
        for i, mine_at in enumerate((x_up, 4 + x_down)):
            first[i].wait_recv()
            d_send[mine_at] = (d_send[mine_at].astype(F32) + d_relay[i].astype(F32)).astype(BF)
            second[i].start()

    def cross():
        for copy in first[2:] + second:
            copy.wait_recv()
        there = other_yh * 4 + xx
        d_send[there] = (
            d_send[there].astype(F32) + d_direct[other_yh].astype(F32) + d_summed[other_yh].astype(F32)
        ).astype(BF)
        across.start()

    attn_masks(r, cc, last, mask, ecol, erow)
    ins[5].wait()
    bias[...] = jnp.zeros_like(bias)
    parts3 = jnp.concatenate(split3(position_bias[...]), axis=0)
    for pair in range(25):
        wide = dot(parts3, table_of[:, pair * 256:(pair + 1) * 256])
        wide = wide[:32] + wide[32:64] + wide[64:]
        for i in range(2):
            if 2 * pair + i < 49:
                bias[:, 2 * pair + i, :] = wide[:, i * 128:(i + 1) * 128]
    normed[HALO:, :] = norm_parts(x[HALO:, :].astype(F32))[0].astype(BF)
    acc[...] = jnp.zeros_like(acc)
    halo_copy.wait_recv()
    top = jnp.where(iota((HALO, C), 0) < 14 * r, halo[...].astype(F32), x[:HALO, :].astype(F32))
    normed[:HALO, :] = norm_parts(top)[0].astype(BF)
    ins[1].wait()
    ins[2].wait()

    def group(g, carry):
        attn_group(g, normed, wqkv, wo, bias, mask, ecol, erow, qkv, probs, mixed, acc)
        return carry

    lax.fori_loop(0, 1, group, 0)
    pass_on()
    lax.fori_loop(1, 3, group, 0)
    for arrived, onward in zip(weights, relayed):
        arrived.wait_recv()
        onward.start()
    ins[3].wait()
    ins[4].wait()
    for copy in doubled[0]:
        copy.start()
    lax.fori_loop(3, 4, group, 0)
    att[...] = acc[...].astype(BF)
    halo2_copy = remote(att.at[pl.ds(0, HALO)], halo2, halo_sem.at[2], halo_sem.at[3], nxt)
    halo2_copy.start()
    outs = [
        pltpu.make_async_copy(qkv, qkv_out, io_sem.at[7]),
        pltpu.make_async_copy(probs, probs_out, io_sem.at[8]),
        pltpu.make_async_copy(mixed, mixed_out, io_sem.at[15]),
    ]
    for copy in outs:
        copy.start()
    cross()
    halo2_copy.wait_recv()
    choice = token_column(choice_in[...].astype(F32))
    route(r, x, att, halo2, choice, after, slots, table)

    for k, pieces in ((1, (weights[2], weights[4])), (3, (weights[3], weights[5]))):
        for copy in pieces:
            copy.wait_recv()
        for copy in doubled[k]:
            copy.start()

    def ready(k):
        if k == 2:
            for copy in relayed:
                copy.wait_recv()
            for copy in doubled[2]:
                copy.start()
        elif k >= 4:
            for copy in doubled[k - 4]:
                copy.wait_recv()

    def compute(j):
        expert_chunk(j, recv, part, ups, downs, flat, act, slope, ready if j == 0 else lambda k: None)

    finish_sends = slots_through(place, slots, recv, part, ret, slot_sems, compute)
    more = [
        pltpu.make_async_copy(flat, flat_out, io_sem.at[9]),
        pltpu.make_async_copy(act, act_out, io_sem.at[10]),
        pltpu.make_async_copy(slope, slope_out, io_sem.at[11]),
        pltpu.make_async_copy(ups, up_out, io_sem.at[12]),
        pltpu.make_async_copy(downs, down_out, io_sem.at[13]),
    ]
    for copy in more:
        copy.start()
    for copy in gifts + [across]:
        copy.wait_recv()
    own.wait()
    parts = (d_send.at[s], d_direct.at[yh], d_summed.at[yh], d_across)
    merge_mid(after, ret, table, token_column(gate_in), parts, t_recv, merge_norm, mn_tail, d_block, d_slots, spread, t_wide)
    for copy in outs + more:
        copy.wait()
    finish_sends()
    for copy in weights + relayed + sum(doubled, []) + gifts + first + second + [across, halo_copy, halo2_copy]:
        copy.wait_send()


def back(
    shift, tokens, after, table, merge_norm, mn_tail, d_block, d_slots,
    qkv_weight, out_weight, reduce_weight, qkv_in, probs_in, mixed_in, flat_in, act_in, slope_in, up_in, down_in,
    tokens_grad, merged, up_grad, down_grad,
    x, x_wide, halo, halo2, d_att, acc, d_after, d_shift, wqkv, wo, wred, qkv, probs, mixed, flat, act, slope, ups, downs,
    recv, part, ret, flat_d, pair_up, pair_down, relay_up, relay_down,
    mn_all, mt_all, merged_wide, merged_rows,
    io_sem, halo_sem, g_send, g_recv, c_send, c_recv, m_sem, *slot_sems,
):
    place = coords()
    s, z, y, c = place
    row = z * 4 + y * 2 + c
    r = shift[0]
    loads = [
        (down_in, downs), (slope_in, slope), (up_in, ups), (act_in, act), (flat_in, flat),
        (out_weight, wo), (qkv_in, qkv), (probs_in, probs), (qkv_weight, wqkv), (reduce_weight, wred), (mixed_in, mixed),
    ]
    ins = [pltpu.make_async_copy(a, b, io_sem.at[i]) for i, (a, b) in enumerate(loads)]
    for copy in ins:
        copy.start()
    greet_all(place)
    nxt = (s, (row + 1) % 16)
    prv = (s, (row + 15) % 16)
    z_up, z_down = at(s, (z + 1) % 4, y, c), at(s, (z + 3) % 4, y, c)

    def compute(j):
        if j == 0:
            for copy in ins[:3]:
                copy.wait()
        expert_chunk_back(j, recv, part, ups, downs, flat_d, slope)

    returns = [
        remote(ups.at[2], relay_up, g_send.at[0], g_recv.at[0], z_up),
        remote(downs.at[2], relay_down, g_send.at[1], g_recv.at[1], z_down),
        remote(ups.at[1], up_grad.at[z], g_send.at[2], g_recv.at[2], z_down),
        remote(downs.at[1], down_grad.at[z], g_send.at[3], g_recv.at[3], z_down),
        remote(ups.at[3], up_grad.at[z], g_send.at[4], g_recv.at[4], z_up),
        remote(downs.at[3], down_grad.at[z], g_send.at[5], g_recv.at[5], z_up),
    ]
    relayed = [
        remote(relay_up, up_grad.at[(z + 3) % 4], g_send.at[6], g_recv.at[6], z_up),
        remote(relay_down, down_grad.at[(z + 1) % 4], g_send.at[7], g_recv.at[7], z_down),
    ]
    yh, xx = s // 4, s % 4
    x_up, x_down = (xx + 1) % 4, (xx + 3) % 4
    to_up, to_down = at(yh * 4 + x_up, z, y, c), at(yh * 4 + x_down, z, y, c)
    across = (1 - yh) * 4 + xx
    half = (pl.ds(0, 2 * C), pl.ds(2 * C, 2 * C))

    def neighbours(source, slot, n):
        return [
            remote(source, mn_all.at[slot], m_sem.at[0, n], m_sem.at[1, n], to_up),
            remote(source, mn_all.at[slot], m_sem.at[0, n + 1], m_sem.at[1, n + 1], to_down),
        ]

    def halves(base, n):
        below, above = base * 4 + x_down, base * 4 + x_up
        low, high = mn_all.at[below, :, half[0]], mn_all.at[above, :, half[1]]
        return [
            remote(low, low, m_sem.at[0, n], m_sem.at[1, n], to_up),
            remote(high, high, m_sem.at[0, n + 1], m_sem.at[1, n + 1], to_down),
        ]

    spread_own = neighbours(merge_norm, s, 0)
    spread_across = neighbours(mn_all.at[across], across, 2)
    far_own = halves(yh, 4)
    far_across = halves(1 - yh, 6)
    partner = remote(merge_norm, mn_all.at[s], m_sem.at[0, 8], m_sem.at[1, 8], at(across, z, y, c))
    tail_copies = []
    for k in range(1, 8):
        peer = (s + k) % 8
        tail_copies.append(remote(mn_tail, mt_all.at[s], m_sem.at[2, k], m_sem.at[3, k], at(peer, z, y, c)))
    gifts = spread_own + spread_across + far_own + far_across + [partner] + tail_copies
    own = [
        pltpu.make_async_copy(merge_norm, mn_all.at[s], io_sem.at[14]),
        pltpu.make_async_copy(mn_tail, mt_all.at[s], io_sem.at[11]),
    ]
    own_out = [
        pltpu.make_async_copy(ups.at[0], up_grad.at[z], io_sem.at[12]),
        pltpu.make_async_copy(downs.at[0], down_grad.at[z], io_sem.at[13]),
    ]

    pair = at(s, z, y, 1 - c)
    halves_over = [
        [
            remote(ups.at[4 + k], pair_up.at[k], c_send.at[0, k], c_recv.at[0, k], pair),
            remote(downs.at[4 + k], pair_down.at[k], c_send.at[1, k], c_recv.at[1, k], pair),
        ]
        for k in range(4)
    ]

    def grads():
        for copy in ins[3:5]:
            copy.wait()

        def both(k):
            span = slice(k * 256, (k + 1) * 256)
            return dot(flat[...], slope[:, span], 0, 0), dot(act[:, span], flat_d[...], 0, 0)

        for k in (2, 1, 3, 0):
            up_part, down_part = both(4 + k)
            ups[4 + k] = up_part.astype(BF)
            downs[4 + k] = down_part.astype(BF)
            for copy in halves_over[k]:
                copy.start()
        for k in (2, 1, 3, 0):
            up_part, down_part = both(k)
            for copy in halves_over[k]:
                copy.wait_recv()
            ups[k] = (up_part + pair_up[k].astype(F32)).astype(BF)
            downs[k] = (down_part + pair_down[k].astype(F32)).astype(BF)
            if k:
                first = {2: 0, 1: 2, 3: 4}[k]
                returns[first].start()
                returns[first + 1].start()
            else:
                for copy in own_out:
                    copy.start()

    finish_sends = slots_through(place, d_slots, recv, part, ret, slot_sems, compute, grads)
    for copy in spread_own + [partner] + tail_copies:
        copy.start()
    for copy in own:
        copy.start()
    after_back(after, ret, table, d_block, d_after, d_att)
    halo_copy = remote(d_att.at[pl.ds(0, HALO)], halo, halo_sem.at[0], halo_sem.at[1], prv)
    halo_copy.start()
    lay_rows(tokens, x_wide, x)
    acc[...] = jnp.zeros_like(acc)
    for copy in ins[5:9] + ins[10:]:
        copy.wait()
    halo_copy.wait_recv()
    halo_copy.wait_send()
    top = jnp.where(iota((HALO, C), 0) < 14 * r, halo[...].astype(F32), d_att[:HALO, :].astype(F32))
    d_att[:HALO, :] = top.astype(BF)

    def group(g, carry):
        attn_group_back(g, d_att, wqkv, wo, qkv, probs, mixed, acc)
        return carry

    lax.fori_loop(0, 1, group, 0)
    for arrived, onward in zip(spread_own, far_own):
        arrived.wait_recv()
        onward.start()
    lax.fori_loop(1, 2, group, 0)
    partner.wait_recv()
    for onward in spread_across:
        onward.start()
    lax.fori_loop(2, 3, group, 0)
    for arrived, onward in zip(returns, relayed):
        arrived.wait_recv()
        onward.start()
    lax.fori_loop(3, 4, group, 0)
    d_shift[...] = acc[...].astype(BF)
    halo2_copy = remote(d_shift.at[pl.ds(0, HALO)], halo2, halo_sem.at[2], halo_sem.at[3], nxt)
    halo2_copy.start()

    for arrived, onward in zip(spread_across, far_across):
        arrived.wait_recv()
        onward.start()
    halo2_copy.wait_recv()
    top = jnp.where(iota((HALO, C), 0) < 14 * r, halo2[...].astype(F32), d_shift[:HALO, :].astype(F32))
    x_wide[:HALO, :] = d_after[:HALO, :] + norm_back(x[:HALO, :].astype(F32), top)
    x_wide[HALO:, :] = d_after[HALO:, :] + norm_back(x[HALO:, :].astype(F32), d_shift[HALO:, :].astype(F32))
    for i in range(14):
        tokens_grad[0, i] = x_wide[14 * i:14 * i + 14, :].astype(BF)

    for copy in far_own + far_across + tail_copies:
        copy.wait_recv()
    for copy in own + [ins[9]]:
        copy.wait()
    merged_wide[:, :48, :] = dot(mn_all[...].reshape(8 * 48, 4 * C), wred[...]).reshape(8, 48, 256)
    tails = mt_all[...].astype(F32)
    last = jnp.concatenate([tails[:, i, :] for i in range(16)], axis=1)
    last = jnp.concatenate([last, jnp.zeros_like(last)], axis=0).astype(BF)
    merged_wide[:, 48, :] = dot(last, wred[...])[:8]
    for n in range(8):
        merged_rows[:, n, :] = merged_wide[n]
    merged[...] = merged_rows[...].reshape(7, 7, 8, 256).astype(BF)

    for copy in returns[2:] + relayed:
        copy.wait_recv()
    for copy in own_out:
        copy.wait()
    finish_sends()
    for copy in returns + relayed + sum(halves_over, []) + gifts + [halo2_copy]:
        copy.wait_send()


def widen(up_in, down_in, grad_in, merged_in, up_out, down_out, grad_out, merged_out):
    up_out[...] = up_in[...].astype(F32)
    down_out[...] = down_in[...].astype(F32)

    @pl.when(pl.program_id(0) == 0)
    def _():
        grad_out[...] = grad_in[...]
        merged_out[...] = merged_in[...]


def bias_pairs():
    spot = np.arange(49)
    py, px = spot // 7, spot % 7
    relative = (py[:, None] - py[None, :] + 6) * 13 + (px[:, None] - px[None, :] + 6)
    table = np.zeros((169, 50, 128), np.float32)
    a, b = np.meshgrid(spot, spot, indexing="ij")
    table[relative.reshape(-1), b.reshape(-1), a.reshape(-1)] = 1.0
    return table.reshape(169, 6400)


def local(
    tokens,
    qkv_weight,
    out_weight,
    position_bias,
    window_shift,
    expert_up,
    expert_down,
    expert_choice,
    combine_weight,
    reduce_weight,
    merged_grad,
):
    choice = jnp.transpose(expert_choice, (1, 0, 3, 2)).reshape(14, 1, 14)
    gate = jnp.transpose(combine_weight, (1, 0, 2))
    pairs = jnp.asarray(bias_pairs(), dtype=BF)
    V = pltpu.VMEM
    D = pltpu.SemaphoreType.DMA

    after, table, merge_norm, mn_tail, d_block, d_slots, qkv, probs, mixed, flat_in, act, slope, ups, downs = pl.pallas_call(
        front,
        out_shape=[
            sds((TP, C), BF), sds((TP, 256), BF), sds((48, 4 * C), BF), sds((16, 256), BF), sds((TP, C), F32),
            sds((32, 16, HC), BF), sds((3, 4, TP, GRP), BF), sds((32 * TP, TP), BF), sds((4, GRP, TP), BF), sds((512, C), BF), sds((512, 2 * C), BF),
            sds((512, 2 * C), BF), sds((8, C, 256), BF), sds((8, 256, C), BF),
        ],
        in_specs=[SM, VM, VM, VM, VM, HB, VM] + [HB] * 5,
        out_specs=[VM] * 6 + [HB] * 8,
        scratch_shapes=[
            V((TP, C), BF), V((TP, C), F32), V((32, 64, 128), F32), V((169, 6400), BF), V((8, 49, 256), F32),
            V((HALO, C), BF), V((HALO, C), BF), V((TP, C), BF), V((TP, TP), F32),
            V((192, TP), BF), V((TP, 192), BF), V((TP, C), F32), V((TP, C), BF),
            V((C, 3 * C), BF), V((C, C), BF), V((4 * C, 256), BF),
            V((3, 4, TP, GRP), BF), V((32 * TP, TP), BF), V((4, GRP, TP), BF),
            V((8, 48, 4 * C), BF), V((2, 48, 4 * C), BF), V((2, 48, 4 * C), BF), V((2, 48, 4 * C), BF),
            V((48, 4 * C), BF), V((8, 16, 256), F32),
            V((8, 16, 256), BF), V((8, 16, 256), BF),
            V((8, C, 256), BF), V((8, 256, C), BF), V((C, 256), BF), V((256, C), BF),
            V((32, 16, HC), BF), V((2, 32, 16, HC), BF), V((2, 32, 16, HC), BF), V((2, 32, 16, HC), BF),
            V((512, C), BF), V((512, 2 * C), BF), V((512, 2 * C), BF), V((256, C), F32),
            D((16,)), D((4,)), D((8,)), D((8,)), D((2, 4)), D((2, 4)), D((4, 8)), *SLOT_SEMS,
        ],
        compiler_params=params(collective_id=0, has_side_effects=True),
        cost_estimate=cost(12 << 30, 60 << 20),
        name="front",
    )(window_shift, tokens, choice, gate, position_bias, pairs, jnp.transpose(merged_grad, (1, 2, 0, 3)), qkv_weight, out_weight,
      expert_up, expert_down, reduce_weight)

    tokens_grad, merged, up_grad, down_grad = pl.pallas_call(
        back,
        out_shape=[
            sds(tokens.shape, BF), sds((7, 7, 8, 256), BF), sds((4, C, 256), BF), sds((4, 256, C), BF),
        ],
        in_specs=[SM] + [VM] * 7 + [HB] * 11,
        out_specs=[VM] * 2 + [HB] * 2,
        scratch_shapes=[
            V((TP, C), BF), V((TP, C), F32), V((HALO, C), BF), V((HALO, C), BF), V((TP, C), BF), V((TP, C), F32),
            V((TP, C), F32), V((TP, C), BF), V((C, 3 * C), BF), V((C, C), BF), V((4 * C, 256), BF),
            V((3, 4, TP, GRP), BF), V((32 * TP, TP), BF), V((4, GRP, TP), BF), V((512, C), BF), V((512, 2 * C), BF), V((512, 2 * C), BF),
            V((8, C, 256), BF), V((8, 256, C), BF),
            V((2, 32, 16, HC), BF), V((2, 32, 16, HC), BF), V((2, 32, 16, HC), BF),
            V((512, C), BF), V((4, C, 256), BF), V((4, 256, C), BF), V((C, 256), BF), V((256, C), BF),
            V((8, 48, 4 * C), BF), V((8, 16, 256), BF), V((8, 49, 256), F32), V((49, 8, 256), F32),
            D((20,)), D((4,)), D((8,)), D((8,)), D((2, 4)), D((2, 4)), D((4, 9)), *SLOT_SEMS,
        ],
        compiler_params=pltpu.CompilerParams(
            vmem_limit_bytes=60 * 1024 * 1024, collective_id=1, has_side_effects=True
        ),
        cost_estimate=cost(16 << 30, 60 << 20),
        name="back",
    )(window_shift, tokens, after, table, merge_norm, mn_tail, d_block, d_slots, qkv_weight, out_weight, reduce_weight,
      qkv, probs, mixed, flat_in, act, slope, ups, downs)
    whole = lambda shape: pl.BlockSpec(shape, lambda e: (0,) * len(shape))
    blocks = [
        pl.BlockSpec((1, C, 256), lambda e: (e, 0, 0)), pl.BlockSpec((1, 256, C), lambda e: (e, 0, 0)),
        whole(tokens_grad.shape), whole(merged.shape),
    ]
    up_grad, down_grad, tokens_grad, merged = pl.pallas_call(
        widen,
        grid=(4,),
        out_shape=[
            sds((4, C, 256), F32), sds((4, 256, C), F32), sds(tokens_grad.shape, BF), sds(merged.shape, BF),
        ],
        in_specs=blocks,
        out_specs=blocks,
        compiler_params=params(),
        cost_estimate=cost(0, 14 << 20),
        name="widen",
    )(up_grad, down_grad, tokens_grad, merged)
    return (jnp.transpose(merged, (2, 0, 1, 3)), tokens_grad, up_grad, down_grad)


def solution(mesh):
    placed = (
        P("scene", "row", None, None),
        P(),
        P(),
        P(),
        P(),
        P("scene", None, "row"),
        P("scene", "row", None),
        P("scene", "row", None, None),
        P("scene", "row", None),
        P(None, "scene"),
        P(None, "row", None, "scene"),
    )
    return jax.shard_map(
        local,
        mesh=mesh,
        in_specs=placed,
        out_specs=(
            P(None, "row", None, "scene"),
            P("scene", "row", None, None),
            P("scene", None, "row"),
            P("scene", "row", None),
        ),
        check_vma=False,
    )
```

```python
import functools

import jax
import jax.numpy as jnp
import numpy as np
from jax import lax
from jax.experimental import pallas as pl
from jax.experimental.pallas import tpu as pltpu
from jax.sharding import PartitionSpec as P

MESH = pl.DeviceIdType.MESH
F32 = jnp.float32
BF = jnp.bfloat16
EPS = 1e-5
C = 1024
HC = C // 2
TOK = 196
TP = 208
HALO = 96
GRP = 256
NEG = -1e30
VMEM_BIG = 56 * 1024 * 1024
VM = pl.BlockSpec(memory_space=pltpu.VMEM)
SM = pl.BlockSpec(memory_space=pltpu.SMEM)
HB = pl.BlockSpec(memory_space=pl.ANY)


def sds(shape, dtype):
    return jax.ShapeDtypeStruct(shape, dtype)


def params(**kw):
    return pltpu.CompilerParams(vmem_limit_bytes=VMEM_BIG, **kw)


def cost(flops, nbytes):
    return pl.CostEstimate(flops=flops, bytes_accessed=nbytes, transcendentals=0)


def dot(a, b, da=1, db=0):
    return lax.dot_general(a, b, (((da,), (db,)), ((), ())), preferred_element_type=F32)


def iota(shape, dim):
    return lax.broadcasted_iota(jnp.int32, shape, dim)


def norm_parts(values):
    centre = jnp.mean(values, axis=-1, keepdims=True)
    centred = values - centre
    spread = jnp.mean(centred * centred, axis=-1, keepdims=True)
    scale = lax.rsqrt(spread + EPS)
    return centred * scale, scale


def norm_back(values, cot):
    unit, scale = norm_parts(values)
    mean_cot = jnp.mean(cot, axis=-1, keepdims=True)
    mean_dot = jnp.mean(cot * unit, axis=-1, keepdims=True)
    return scale * (cot - mean_cot - unit * mean_dot)


def split3(values):
    high = values.astype(BF)
    rest = values - high.astype(F32)
    mid = rest.astype(BF)
    low = (rest - mid.astype(F32)).astype(BF)
    return high, mid, low


def place_of(tok, r, c):
    rho = (tok * 4682) >> 16
    gam = tok - 14 * rho
    i = rho - r
    i = jnp.where(i < 0, i + 14, i)
    j = gam - c
    j = jnp.where(j < 0, j + 14, j)
    a = jnp.where(i >= 7, 1, 0)
    b = jnp.where(j >= 7, 1, 0)
    return i, j, a, b


def pos_of(tok, r, c):
    i, j, a, b = place_of(tok, r, c)
    return (i - 7 * a) * 7 + (j - 7 * b)


def group_of(tok, r, c, last):
    i, j, a, b = place_of(tok, r, c)
    la = jnp.where(i >= 7, jnp.where(i < 14 - r, 1, 2), 0) * last
    lb = jnp.where(j >= 7, jnp.where(j < 14 - c, 1, 2), 0)
    return a * 2 + b, la * 3 + lb


def pack_rows(low, high, blocks):
    return jnp.concatenate([low.reshape(blocks, 8, HC), high.reshape(blocks, 8, HC)], axis=1).astype(BF)


def unpack_rows(packed, blocks):
    wide = packed.astype(F32)
    low = wide[:, :8, :].reshape(blocks * 8, HC)
    high = wide[:, 8:, :].reshape(blocks * 8, HC)
    return low, high


def attn_masks(r, c, last, mask, ecol, erow):
    tq, tk = iota((TP, TP), 0), iota((TP, TP), 1)
    wq_, lq = group_of(tq, r, c, last)
    wk_, lk = group_of(tk, r, c, last)
    seen = jnp.where(wq_ == wk_, jnp.where(lq == lk, 0.0, -100.0), NEG)
    mask[...] = jnp.where(tq < TOK, seen, NEG)
    row_pos = pos_of(iota((TP, 192), 0), r, c)
    erow[...] = jnp.where(row_pos == (iota((TP, 192), 1) & 63), 1.0, 0.0).astype(BF)
    col_pos = pos_of(iota((192, TP), 1), r, c)
    ecol[...] = jnp.where(col_pos == (iota((192, TP), 0) & 63), 1.0, 0.0).astype(BF)


def cols(start):
    return pl.ds(pl.multiple_of(start, GRP), GRP)


def turned(values, eye):
    return dot(eye, values, 1, 1)


def unit_table():
    return jnp.where(iota((GRP, GRP), 0) == iota((GRP, GRP), 1), 1.0, 0.0).astype(BF)


def attn_group(g, normed, wqkv, wo, bias, mask, ecol, erow, qkv, probs, mixed, acc):
    n = normed[...]
    q = dot(n, wqkv[:, cols(g * GRP)]).astype(BF)
    k = dot(n, wqkv[:, cols(C + g * GRP)]).astype(BF)
    v = dot(n, wqkv[:, cols(2 * C + g * GRP)]).astype(BF)
    qkv[0, g] = q
    qkv[1, g] = k
    qkv[2, g] = v
    eye = unit_table()
    q_t = turned(q, eye).astype(BF)
    v_t = turned(v, eye).astype(BF)
    wide = dot(jnp.concatenate(split3(bias[pl.ds(g * 8, 8)][:, :, :64].reshape(8 * 64, 64)), axis=1), ecol[...])
    w_hi, w_mid, w_lo = split3(wide)
    lane_head = iota((TP, GRP), 1) >> 5
    k32 = k.astype(F32)
    outs = []
    for h in range(8):
        km = jnp.where(lane_head == h, k32, 0.0).astype(BF)
        part = slice(h * 64, h * 64 + 64)
        s = dot(km, q_t) * (32.0 ** -0.5)
        s = s + dot(erow[...], jnp.concatenate([w_hi[part], w_mid[part], w_lo[part]], axis=0)) + mask[...]
        e = jnp.exp(s - jnp.max(s, axis=0, keepdims=True))
        p = (e * (1.0 / jnp.sum(e, axis=0, keepdims=True))).astype(BF)
        probs[pl.ds(pl.multiple_of((g * 8 + h) * TP, 16), TP), :] = p
        outs.append(dot(v_t[32 * h:32 * h + 32], p))
    mixed_t = jnp.concatenate(outs, axis=0).astype(BF)
    mixed[g] = mixed_t
    acc[...] += dot(mixed_t, wo[pl.ds(pl.multiple_of(g * GRP, GRP), GRP), :], 0, 0)


def attn_group_back(g, d_att, wqkv, wo, qkv, probs, mixed, acc):
    q, k, v = qkv[0, g], qkv[1, g], qkv[2, g]
    eye = unit_table()
    d_out = dot(d_att[...], wo[pl.ds(pl.multiple_of(g * GRP, GRP), GRP), :], 1, 1).astype(BF)
    d_out_t = turned(d_out, eye)
    weighed = d_out_t * mixed[g].astype(F32)
    d_out_t = d_out_t.astype(BF)
    k_t = turned(k, eye).astype(BF)
    v32 = v.astype(F32)
    lane_head = iota((TP, GRP), 1) >> 5
    dq_t = []
    dk = jnp.zeros((TP, GRP), F32)
    dv = jnp.zeros((TP, GRP), F32)
    for h in range(8):
        mine = lane_head == h
        vm = jnp.where(mine, v32, 0.0).astype(BF)
        p = probs[pl.ds(pl.multiple_of((g * 8 + h) * TP, 16), TP), :]
        shared = jnp.sum(weighed[32 * h:32 * h + 32], axis=0, keepdims=True)
        ds = (p.astype(F32) * (dot(vm, d_out_t) - shared)).astype(BF)
        dq_t.append(dot(k_t[32 * h:32 * h + 32], ds))
        dk = jnp.where(mine, dot(ds, q), dk)
        dv = jnp.where(mine, dot(p, d_out), dv)
    scale = 32.0 ** -0.5
    dq = jnp.transpose(jnp.concatenate(dq_t, axis=0) * scale)
    acc[...] += (
        dot(dq.astype(BF), wqkv[:, cols(g * GRP)], 1, 1)
        + dot((dk * scale).astype(BF), wqkv[:, cols(C + g * GRP)], 1, 1)
        + dot(dv.astype(BF), wqkv[:, cols(2 * C + g * GRP)], 1, 1)
    )


def route(r, x, att, halo, choice, after_out, slots, table_out):
    top = jnp.where(iota((HALO, C), 0) < 14 * r, halo[...].astype(F32), att[:HALO, :].astype(F32))
    after_out[:HALO, :] = (x[:HALO, :].astype(F32) + top).astype(BF)
    after_out[HALO:, :] = (x[HALO:, :].astype(F32) + att[HALO:, :].astype(F32)).astype(BF)
    after = after_out[...].astype(F32)
    n2 = norm_parts(after)[0].astype(BF)
    tok, other = iota((TP, TP), 0), iota((TP, TP), 1)
    col = jnp.where(iota((TP, 1), 0) < TOK, choice, -1000.0)
    line = jnp.sum(jnp.where(tok == other, col, 0.0), axis=0, keepdims=True)
    same = jnp.where(col == line, 1.0, 0.0)
    same = jnp.where(other < tok, same, 0.0)
    rank = jnp.sum(same, axis=1, keepdims=True).astype(jnp.int32)
    table = jnp.where(col.astype(jnp.int32) * 8 + rank == iota((TP, 256), 1), 1.0, 0.0).astype(BF)
    table_out[...] = table
    slots[...] = pack_rows(dot(table, n2[:, :HC], 0, 0), dot(table, n2[:, HC:], 0, 0), 32)


def quad_table():
    row = iota((256, TP), 0)
    tok = iota((256, TP), 1)
    q = row >> 6
    n = row & 63
    a = (n * 9363) >> 16
    b = n - 7 * a
    want = (2 * a + (q & 1)) * 14 + 2 * b + (q >> 1)
    hit = jnp.where(want == tok, 1.0, 0.0)
    return jnp.where(n < 49, hit, 0.0).astype(BF)


def gathered(ret, table):
    low, high = unpack_rows(ret[0].astype(F32) + ret[1].astype(F32), 32)
    return jnp.concatenate([dot(table, low.astype(BF)), dot(table, high.astype(BF))], axis=1)


def merge_mid(after, ret, table_in, gate, parts, tail, mn_out, mn_tail, d_block_out, slots, spread, t_wide):
    table = table_in[...]
    block = (after[...].astype(F32) + gate * gathered(ret, table)).astype(BF)
    perm = quad_table()
    quads = dot(perm, block)
    vals = [quads[64 * q:64 * q + 49, :] for q in range(4)]
    inv = 1.0 / (4 * C)
    centre = sum(jnp.sum(v, axis=-1, keepdims=True) for v in vals) * inv
    cent = [v - centre for v in vals]
    var = sum(jnp.sum(v * v, axis=-1, keepdims=True) for v in cent) * inv
    scale = lax.rsqrt(var + EPS)
    unit = [v * scale for v in cent]
    for q in range(4):
        mn_out[:, q * C:(q + 1) * C] = unit[q][:48].astype(BF)
        for i in range(4):
            t_wide[0, 4 * q + i:4 * q + i + 1, :] = unit[q][48:49, i * 256:(i + 1) * 256]
    mn_tail[...] = t_wide[0].astype(BF)
    tails = jnp.sum(tail[...].astype(F32), axis=0)
    cots = []
    for q in range(4):
        tot = sum(part[:, q * C:(q + 1) * C].astype(F32) for part in parts)
        last = jnp.concatenate([tails[4 * q + i:4 * q + i + 1, :] for i in range(4)], axis=1)
        cots.append(jnp.concatenate([tot, last], axis=0))
    mean_cot = sum(jnp.sum(v, axis=-1, keepdims=True) for v in cots) * inv
    mean_dot = sum(jnp.sum(v * u, axis=-1, keepdims=True) for v, u in zip(cots, unit)) * inv
    spread[...] = jnp.zeros_like(spread)
    for q in range(4):
        spread[64 * q:64 * q + 49, :] = scale * (cots[q] - mean_cot - unit[q] * mean_dot)
    high, mid, low = split3(spread[...])
    d_block = dot(perm, high, 0, 0) + dot(perm, mid, 0, 0) + dot(perm, low, 0, 0)
    d_block_out[...] = d_block
    scaled = (gate * d_block).astype(BF)
    slots[...] = pack_rows(dot(table, scaled[:, :HC], 0, 0), dot(table, scaled[:, HC:], 0, 0), 32)


def after_back(after, ret, table, d_block, d_after_out, d_att_out):
    d_second = gathered(ret, table[...])
    d_after = d_block[...] + norm_back(after[...].astype(F32), d_second)
    d_after_out[...] = d_after
    d_att_out[...] = d_after.astype(BF)


def token_column(grid):
    tok = iota((TP, 14), 0)
    rho = (tok * 4682) >> 16
    place = iota((TP, 14), 1)
    pick = jnp.where(rho == place, 1.0, 0.0).astype(BF)
    high, mid, low = split3(grid[...].reshape(14, 14))
    rows = dot(pick, high) + dot(pick, mid) + dot(pick, low)
    return jnp.sum(jnp.where(tok - 14 * rho == place, rows, 0.0), axis=1, keepdims=True)


def lay_rows(tokens, wide, x):
    wide[TOK - 4:, :] = jnp.zeros((TP - TOK + 4, C), F32)
    for i in range(14):
        wide[14 * i:14 * i + 14, :] = tokens[0, i].astype(F32)
    x[...] = wide[...].astype(BF)


def expert_chunk(j, recv, part, ups, downs, flat, act_out, slope_out, ready):
    here = pl.ds(8 * j, 8)
    rows_here = pl.ds(256 * j, 256)
    low, high = unpack_rows(recv[:, here].reshape(32, 16, HC), 32)
    rows = jnp.concatenate([low, high], axis=1).astype(BF)
    flat[rows_here, :] = rows
    total = jnp.zeros((256, C), F32)
    for k in (0, 1, 3, 2):
        ready(k)
        pre = dot(rows, ups[k])
        cdf = 0.5 * (1.0 + lax.erf(pre * np.float32(2.0 ** -0.5)))
        act = (pre * cdf).astype(BF)
        slope = cdf + pre * jnp.exp(-0.5 * pre * pre) * np.float32((2.0 * np.pi) ** -0.5)
        act_out[rows_here, k * 256:(k + 1) * 256] = act
        slope_out[rows_here, k * 256:(k + 1) * 256] = slope.astype(BF)
        total = total + dot(act, downs[k])
    part[:, here] = pack_rows(total[:, :HC], total[:, HC:], 32).reshape(4, 8, 16, HC)


def expert_chunk_back(j, recv, part, ups, downs, flat, slope):
    here = pl.ds(8 * j, 8)
    rows_here = pl.ds(256 * j, 256)
    low, high = unpack_rows(recv[:, here].reshape(32, 16, HC), 32)
    rows = jnp.concatenate([low, high], axis=1).astype(BF)
    flat[rows_here, :] = rows
    total = jnp.zeros((256, C), F32)
    for k in range(4):
        span = slice(k * 256, (k + 1) * 256)
        d_pre = (slope[rows_here, span].astype(F32) * dot(rows, downs[k], 1, 1)).astype(BF)
        slope[rows_here, span] = d_pre
        total = total + dot(d_pre, ups[k], 1, 1)
    part[:, here] = pack_rows(total[:, :HC], total[:, HC:], 32).reshape(4, 8, 16, HC)


def coords():
    s = lax.axis_index("scene")
    row = lax.axis_index("row")
    z, m = row // 4, row % 4
    return s, z, m // 2, m % 2


def at(s, z, y, c):
    return (s, z * 4 + y * 2 + c)


def greet(s, z, y, c, total=64):
    barrier = pltpu.get_barrier_semaphore()
    mine = s * 4 + z

    def hail(k, carry):
        peer = (mine + k) % 32
        pl.semaphore_signal(barrier, inc=1, device_id=at(peer // 4, peer % 4, y, c), device_id_type=MESH)
        pl.semaphore_signal(barrier, inc=1, device_id=at(peer // 4, peer % 4, 1 - y, c), device_id_type=MESH)
        return carry

    lax.fori_loop(1, 32, hail, 0)
    pl.semaphore_signal(barrier, inc=1, device_id=at(s, z, 1 - y, c), device_id_type=MESH)
    pl.semaphore_signal(barrier, inc=1, device_id=at(s, z, y, 1 - c), device_id_type=MESH)
    pl.semaphore_wait(barrier, total)


def greet_all(place):
    s, z, y, c = place
    barrier = pltpu.get_barrier_semaphore()
    row = z * 4 + y * 2 + c
    pl.semaphore_signal(barrier, inc=1, device_id=(s, (row + 1) % 16), device_id_type=MESH)
    pl.semaphore_signal(barrier, inc=1, device_id=(s, (row + 15) % 16), device_id_type=MESH)
    greet(s, z, y, c, 66)


def remote(src, dst, send, recv, device):
    return pltpu.make_async_remote_copy(
        src_ref=src, dst_ref=dst, send_sem=send, recv_sem=recv, device_id=device, device_id_type=MESH
    )


def await_bytes(ref, sem):
    pltpu.make_async_copy(ref, ref, sem).wait()


SLOT_SEMS = [
    pltpu.SemaphoreType.DMA,
    pltpu.SemaphoreType.DMA((2, 4)),
    pltpu.SemaphoreType.DMA((2, 4)),
    pltpu.SemaphoreType.DMA((2, 4)),
    pltpu.SemaphoreType.DMA((2, 4)),
    pltpu.SemaphoreType.DMA((2, 4)),
    pltpu.SemaphoreType.DMA((4,)),
    pltpu.SemaphoreType.DMA,
    pltpu.SemaphoreType.DMA,
]
FIRST, FAR = 1, 2


def slots_through(place, slots, recv, part, other, total, across, ret, sems, compute, meanwhile=None):
    s, z, y, c = place
    mine = s * 4 + z
    send, arrive, f_send, f_recv, p_send, p_recv, y_sems, r_send, r_recv = sems
    pair, beside = at(s, z, y, 1 - c), at(s, z, 1 - y, c)
    yh, xx = s // 4, s % 4
    own, next_own = y * 2 + c, (1 - y) * 2 + c
    far = pl.ds(8 * FAR, 8)

    def ahead(j, i):
        return ((yh + i // 4) % 2 * 4 + (xx + i % 4) % 4) * 4 + (z + j) % 4

    def behind(j, i):
        return ((yh + i // 4) % 2 * 4 + (xx + 4 - i % 4) % 4) * 4 + (z + 4 - j) % 4

    def to_peer(j, i, peer, yy):
        remote(slots.at[peer], recv.at[own, 8 * j + i], send, arrive.at[y, j], at(peer // 4, peer % 4, yy, c)).start()

    def push_far(i, carry):
        to_peer(FAR, i, ahead(FAR, i), y)
        return carry

    def push(i, carry):
        for j in (1, 3):
            to_peer(j, i, ahead(j, i), y)
            to_peer(j, i, ahead(j, i), 1 - y)
        return carry

    def push_near(i, carry):
        to_peer(0, i, ahead(0, i), y)
        to_peer(0, i, ahead(0, i), 1 - y)
        return carry

    lax.fori_loop(0, 8, push_far, 0)
    lax.fori_loop(0, 8, push, 0)
    pltpu.make_async_copy(slots.at[mine], recv.at[own, 0], arrive.at[y, 0]).start()
    to_peer(0, 0, mine, 1 - y)
    lax.fori_loop(1, 8, push_near, 0)

    def clear(scene, carry):
        ret[1 - y, scene * 4 + (z + 2) % 4] = jnp.zeros((16, HC), BF)
        return carry

    lax.fori_loop(0, 8, clear, 0)
    forwards, partials, y_copies = {}, {}, []

    def to_pair(yy, j):
        block = recv.at[yy * 2 + c, pl.ds(8 * j, 8)]
        forwards[yy, j] = remote(block, block, f_send.at[yy, j], f_recv.at[yy, j], pair)
        forwards[yy, j].start()

    def forward(j):
        for yy in range(2):
            await_bytes(recv.at[yy * 2 + c, pl.ds(8 * j, 8)], arrive.at[yy, j])
            to_pair(yy, j)

    def forward_far():
        block = recv.at[own, far]
        await_bytes(block, arrive.at[y, FAR])
        y_copies.append(remote(block, block, y_sems.at[0], y_sems.at[1], beside))
        y_copies[0].start()

    def forward_beside():
        y_copies[0].wait_recv()
        for yy in range(2):
            to_pair(yy, FAR)

    def work(j):
        for yy in range(2):
            forwards[yy, j].wait_recv()
        compute(j)
        for yy in range(2):
            here = pl.ds(8 * j, 8)
            partials[yy, j] = remote(
                part.at[yy * 2 + (1 - c), here], other.at[yy, here], p_send.at[yy, j], p_recv.at[yy, j], pair
            )
            partials[yy, j].start()

    def give(j, i, yy):
        peer = behind(j, i)
        remote(total.at[yy, 8 * j + i], ret.at[y, mine], r_send, r_recv, at(peer // 4, peer % 4, yy, c)).start()

    def back(j):
        here = pl.ds(8 * j, 8)
        for yy in range(2):
            partials[yy, j].wait_recv()
            total[yy, here] = (part[yy * 2 + c, here].astype(F32) + other[yy, here].astype(F32)).astype(BF)

        def give_both(i, carry):
            give(j, i, 1 - y)
            give(j, i, y)
            return carry

        if j == 0:
            give(0, 0, 1 - y)
            pltpu.make_async_copy(total.at[y, 0], ret.at[y, mine], r_recv).start()
        lax.fori_loop(0 if j else 1, 8, give_both, 0)

    def back_beside():
        for yy in range(2):
            partials[yy, FAR].wait_recv()
        total[1 - y, far] = (part[next_own, far].astype(F32) + other[1 - y, far].astype(F32)).astype(BF)
        y_copies.append(remote(total.at[1 - y, far], across, y_sems.at[2], y_sems.at[3], beside))
        y_copies[1].start()

    def back_far():
        y_copies[1].wait_recv()
        total[y, far] = (
            part[own, far].astype(F32) + other[y, far].astype(F32) + across[...].astype(F32)
        ).astype(BF)

        def give_one(i, carry):
            give(FAR, i, y)
            return carry

        lax.fori_loop(0, 8, give_one, 0)

    forward_far()
    forward(1)
    forward_beside()
    work(1)
    forward(3)
    work(2)
    back(1)
    back_beside()
    forward(0)
    work(3)
    back(3)
    back_far()
    work(0)
    back(0)

    def finish_sends():
        for copy in list(forwards.values()) + list(partials.values()) + y_copies:
            copy.wait_send()
        for sem in (send, r_send):
            await_bytes(total.at[0], sem)
            await_bytes(total.at[0, pl.ds(0, 23)], sem)

    if meanwhile is not None:
        meanwhile()
    await_bytes(total.at[:, pl.ds(0, 28)], r_recv)
    return finish_sends


def front(
    shift, tokens, choice_in, gate_in, position_bias, pairs, merged_grad, qkv_weight, out_weight, expert_up, expert_down, reduce_weight,
    after, table, merge_norm, mn_tail, d_block, d_slots, qkv_out, probs_out, mixed_out, flat_out, act_out, slope_out, up_out, down_out,
    x, x_wide, bias, table_of, grad_wide, halo, halo2, normed, mask, ecol, erow, acc, att, wqkv, wo, wred, qkv, probs, mixed,
    d_send, d_relay, d_direct, d_summed, d_across, t_wide, t_send, t_recv, ups, downs, relay_up, relay_down,
    slots, recv, part, other, total, across_sum, ret, flat, act, slope, spread,
    io_sem, halo_sem, w_send, w_recv, d_sem, *slot_sems,
):
    place = coords()
    s, z, y, c = place
    row = z * 4 + y * 2 + c
    r, cc = shift[0], shift[1]
    last = jnp.where(row == 15, 1, 0)
    ins = [
        pltpu.make_async_copy(reduce_weight, wred, io_sem.at[0]),
        pltpu.make_async_copy(qkv_weight, wqkv, io_sem.at[1]),
        pltpu.make_async_copy(out_weight, wo, io_sem.at[2]),
        pltpu.make_async_copy(expert_up.at[z], ups.at[0], io_sem.at[3]),
        pltpu.make_async_copy(expert_down.at[z], downs.at[0], io_sem.at[4]),
        pltpu.make_async_copy(pairs, table_of, io_sem.at[14]),
    ]
    for copy in ins:
        copy.start()
    lay_rows(tokens, x_wide, x)
    greet_all(place)

    nxt = (s, (row + 1) % 16)
    prv = (s, (row + 15) % 16)
    z_up, z_down = at(s, (z + 1) % 4, y, c), at(s, (z + 3) % 4, y, c)
    halo_copy = remote(x.at[pl.ds(0, HALO)], halo, halo_sem.at[0], halo_sem.at[1], prv)
    halo_copy.start()
    weights = [
        remote(expert_up.at[(z + 2) % 4], relay_up, w_send.at[0], w_recv.at[0], z_up),
        remote(expert_down.at[(z + 2) % 4], relay_down, w_send.at[1], w_recv.at[1], z_down),
        remote(expert_up.at[(z + 1) % 4], ups.at[1], w_send.at[2], w_recv.at[2], z_up),
        remote(expert_up.at[(z + 3) % 4], ups.at[3], w_send.at[3], w_recv.at[3], z_down),
        remote(expert_down.at[(z + 1) % 4], downs.at[1], w_send.at[4], w_recv.at[4], z_up),
        remote(expert_down.at[(z + 3) % 4], downs.at[3], w_send.at[5], w_recv.at[5], z_down),
    ]
    for copy in weights:
        copy.start()
    relayed = [
        remote(relay_up, ups.at[2], w_send.at[6], w_recv.at[6], z_up),
        remote(relay_down, downs.at[2], w_send.at[7], w_recv.at[7], z_down),
    ]

    by_place = merged_grad[...].astype(F32).reshape(49, 8, 256)
    for n in range(8):
        grad_wide[n] = by_place[:, n, :]
    grad48 = grad_wide[:, :48, :].astype(BF).reshape(8 * 48, 256)
    grad_tail = jnp.concatenate([grad_wide[:, 48, :], jnp.zeros((8, 256), F32)], axis=0).astype(BF)
    ins[0].wait()
    for half in range(4):
        span = pl.ds(half * C, C)
        d_send[:, :, span] = dot(grad48, wred[span, :], 1, 1).astype(BF).reshape(8, 48, C)
        tail = dot(grad_tail, wred[span, :], 1, 1)
        for i in range(4):
            t_wide[:, 4 * half + i, :] = tail[:8, i * 256:(i + 1) * 256]
    t_send[...] = t_wide[...].astype(BF)
    yh, xx = s // 4, s % 4
    x_up, x_down, x_far = (xx + 1) % 4, (xx + 3) % 4, (xx + 2) % 4
    to_up, to_down = at(yh * 4 + x_up, z, y, c), at(yh * 4 + x_down, z, y, c)
    first = [
        remote(d_send.at[x_far], d_relay.at[0], d_sem.at[0, 0], d_sem.at[1, 0], to_up),
        remote(d_send.at[4 + x_far], d_relay.at[1], d_sem.at[0, 1], d_sem.at[1, 1], to_down),
        remote(d_send.at[4 + x_up], d_direct.at[1], d_sem.at[0, 2], d_sem.at[1, 2], to_up),
        remote(d_send.at[x_down], d_direct.at[0], d_sem.at[0, 3], d_sem.at[1, 3], to_down),
    ]
    second = [
        remote(d_send.at[x_up], d_summed.at[0], d_sem.at[0, 4], d_sem.at[1, 4], to_up),
        remote(d_send.at[4 + x_down], d_summed.at[1], d_sem.at[0, 5], d_sem.at[1, 5], to_down),
    ]
    other_yh = 1 - yh
    across = remote(
        d_send.at[other_yh * 4 + xx], d_across, d_sem.at[0, 6], d_sem.at[1, 6], at(other_yh * 4 + xx, z, y, c)
    )
    gifts = []
    for k in range(1, 8):
        peer = (s + k) % 8
        gifts.append(remote(t_send.at[peer], t_recv.at[s], d_sem.at[2, k], d_sem.at[3, k], at(peer, z, y, c)))
    for copy in first + gifts:
        copy.start()
    own = pltpu.make_async_copy(t_send.at[s], t_recv.at[s], io_sem.at[6])
    own.start()

    def pass_on():
        for i, mine_at in enumerate((x_up, 4 + x_down)):
            first[i].wait_recv()
            d_send[mine_at] = (d_send[mine_at].astype(F32) + d_relay[i].astype(F32)).astype(BF)
            second[i].start()

    def cross():
        for copy in first[2:] + second:
            copy.wait_recv()
        there = other_yh * 4 + xx
        d_send[there] = (
            d_send[there].astype(F32) + d_direct[other_yh].astype(F32) + d_summed[other_yh].astype(F32)
        ).astype(BF)
        across.start()

    attn_masks(r, cc, last, mask, ecol, erow)
    ins[5].wait()
    bias[...] = jnp.zeros_like(bias)
    parts3 = jnp.concatenate(split3(position_bias[...]), axis=0)
    for pair in range(25):
        wide = dot(parts3, table_of[:, pair * 256:(pair + 1) * 256])
        wide = wide[:32] + wide[32:64] + wide[64:]
        for i in range(2):
            if 2 * pair + i < 49:
                bias[:, 2 * pair + i, :] = wide[:, i * 128:(i + 1) * 128]
    normed[HALO:, :] = norm_parts(x[HALO:, :].astype(F32))[0].astype(BF)
    acc[...] = jnp.zeros_like(acc)
    halo_copy.wait_recv()
    top = jnp.where(iota((HALO, C), 0) < 14 * r, halo[...].astype(F32), x[:HALO, :].astype(F32))
    normed[:HALO, :] = norm_parts(top)[0].astype(BF)
    ins[1].wait()
    ins[2].wait()

    def group(g, carry):
        attn_group(g, normed, wqkv, wo, bias, mask, ecol, erow, qkv, probs, mixed, acc)
        return carry

    lax.fori_loop(0, 1, group, 0)
    pass_on()
    lax.fori_loop(1, 3, group, 0)
    for arrived, onward in zip(weights, relayed):
        arrived.wait_recv()
        onward.start()
    lax.fori_loop(3, 4, group, 0)
    att[...] = acc[...].astype(BF)
    halo2_copy = remote(att.at[pl.ds(0, HALO)], halo2, halo_sem.at[2], halo_sem.at[3], nxt)
    halo2_copy.start()
    outs = [
        pltpu.make_async_copy(qkv, qkv_out, io_sem.at[7]),
        pltpu.make_async_copy(probs, probs_out, io_sem.at[8]),
        pltpu.make_async_copy(mixed, mixed_out, io_sem.at[15]),
    ]
    for copy in outs:
        copy.start()
    cross()
    halo2_copy.wait_recv()
    choice = token_column(choice_in[...].astype(F32))
    route(r, x, att, halo2, choice, after, slots, table)

    def ready(k):
        pieces = {0: (), 1: (weights[2], weights[4]), 3: (weights[3], weights[5]), 2: relayed}[k]
        for copy in pieces:
            copy.wait_recv()
        if k == 0:
            ins[3].wait()
            ins[4].wait()

    def compute(j):
        expert_chunk(j, recv, part, ups, downs, flat, act, slope, ready if j == FIRST else lambda k: None)

    finish_sends = slots_through(place, slots, recv, part, other, total, across_sum, ret, slot_sems, compute)
    more = [
        pltpu.make_async_copy(flat, flat_out, io_sem.at[9]),
        pltpu.make_async_copy(act, act_out, io_sem.at[10]),
        pltpu.make_async_copy(slope, slope_out, io_sem.at[11]),
        pltpu.make_async_copy(ups, up_out, io_sem.at[12]),
        pltpu.make_async_copy(downs, down_out, io_sem.at[13]),
    ]
    for copy in more:
        copy.start()
    for copy in gifts + [across]:
        copy.wait_recv()
    own.wait()
    parts = (d_send.at[s], d_direct.at[yh], d_summed.at[yh], d_across)
    merge_mid(after, ret, table, token_column(gate_in), parts, t_recv, merge_norm, mn_tail, d_block, d_slots, spread, t_wide)
    for copy in outs + more:
        copy.wait()
    finish_sends()
    for copy in weights + relayed + gifts + first + second + [across, halo_copy, halo2_copy]:
        copy.wait_send()


def back(
    shift, tokens, after, table, merge_norm, mn_tail, d_block, d_slots,
    qkv_weight, out_weight, reduce_weight, qkv_in, probs_in, mixed_in, flat_in, act_in, slope_in, up_in, down_in,
    tokens_grad, merged, up_grad, down_grad,
    x, x_wide, halo, halo2, d_att, acc, d_after, d_shift, wqkv, wo, wred, qkv, probs, mixed, flat, act, slope, ups, downs,
    recv, part, other, total, across_sum, ret, flat_d, send_up, send_down, relay_up, relay_down,
    mn_all, mt_all, merged_wide, merged_rows,
    io_sem, halo_sem, g_send, g_recv, m_sem, *slot_sems,
):
    place = coords()
    s, z, y, c = place
    row = z * 4 + y * 2 + c
    r = shift[0]
    loads = [
        (down_in, downs), (slope_in, slope), (up_in, ups), (act_in, act), (flat_in, flat),
        (out_weight, wo), (qkv_in, qkv), (probs_in, probs), (qkv_weight, wqkv), (reduce_weight, wred), (mixed_in, mixed),
    ]
    ins = [pltpu.make_async_copy(a, b, io_sem.at[i]) for i, (a, b) in enumerate(loads)]
    for copy in ins:
        copy.start()
    greet_all(place)
    nxt = (s, (row + 1) % 16)
    prv = (s, (row + 15) % 16)
    z_up, z_down = at(s, (z + 1) % 4, y, c), at(s, (z + 3) % 4, y, c)

    def compute(j):
        if j == FIRST:
            for copy in ins[:3]:
                copy.wait()
        expert_chunk_back(j, recv, part, ups, downs, flat_d, slope)

    returns = [
        remote(send_up.at[1], relay_up, g_send.at[0], g_recv.at[0], z_up),
        remote(send_down.at[1], relay_down, g_send.at[1], g_recv.at[1], z_down),
        remote(send_up.at[0], up_grad.at[z], g_send.at[2], g_recv.at[2], z_down),
        remote(send_down.at[0], down_grad.at[z], g_send.at[3], g_recv.at[3], z_down),
        remote(send_up.at[2], up_grad.at[z], g_send.at[4], g_recv.at[4], z_up),
        remote(send_down.at[2], down_grad.at[z], g_send.at[5], g_recv.at[5], z_up),
    ]
    relayed = [
        remote(relay_up, up_grad.at[(z + 3) % 4], g_send.at[6], g_recv.at[6], z_up),
        remote(relay_down, down_grad.at[(z + 1) % 4], g_send.at[7], g_recv.at[7], z_down),
    ]
    yh, xx = s // 4, s % 4
    x_up, x_down = (xx + 1) % 4, (xx + 3) % 4
    to_up, to_down = at(yh * 4 + x_up, z, y, c), at(yh * 4 + x_down, z, y, c)
    across = (1 - yh) * 4 + xx
    half = (pl.ds(0, 2 * C), pl.ds(2 * C, 2 * C))

    def neighbours(source, slot, n):
        return [
            remote(source, mn_all.at[slot], m_sem.at[0, n], m_sem.at[1, n], to_up),
            remote(source, mn_all.at[slot], m_sem.at[0, n + 1], m_sem.at[1, n + 1], to_down),
        ]

    def halves(base, n):
        below, above = base * 4 + x_down, base * 4 + x_up
        low, high = mn_all.at[below, :, half[0]], mn_all.at[above, :, half[1]]
        return [
            remote(low, low, m_sem.at[0, n], m_sem.at[1, n], to_up),
            remote(high, high, m_sem.at[0, n + 1], m_sem.at[1, n + 1], to_down),
        ]

    spread_own = neighbours(merge_norm, s, 0)
    spread_across = neighbours(mn_all.at[across], across, 2)
    far_own = halves(yh, 4)
    far_across = halves(1 - yh, 6)
    partner = remote(merge_norm, mn_all.at[s], m_sem.at[0, 8], m_sem.at[1, 8], at(across, z, y, c))
    tail_copies = []
    for k in range(1, 8):
        peer = (s + k) % 8
        tail_copies.append(remote(mn_tail, mt_all.at[s], m_sem.at[2, k], m_sem.at[3, k], at(peer, z, y, c)))
    gifts = spread_own + spread_across + far_own + far_across + [partner] + tail_copies
    own = [
        pltpu.make_async_copy(merge_norm, mn_all.at[s], io_sem.at[14]),
        pltpu.make_async_copy(mn_tail, mt_all.at[s], io_sem.at[11]),
    ]
    own_out = [
        pltpu.make_async_copy(send_up.at[3], up_grad.at[z], io_sem.at[12]),
        pltpu.make_async_copy(send_down.at[3], down_grad.at[z], io_sem.at[13]),
    ]

    def grads():
        for copy in ins[3:5]:
            copy.wait()
        for k in (2, 1, 3, 0):
            span = slice(k * 256, (k + 1) * 256)
            up_part = dot(flat[...], slope[:, span], 0, 0)
            down_part = dot(act[:, span], flat_d[...], 0, 0)
            send_up[(k + 3) % 4] = up_part.astype(BF)
            send_down[(k + 3) % 4] = down_part.astype(BF)
            if k:
                first = {2: 0, 1: 2, 3: 4}[k]
                returns[first].start()
                returns[first + 1].start()
            else:
                for copy in own_out:
                    copy.start()

    finish_sends = slots_through(place, d_slots, recv, part, other, total, across_sum, ret, slot_sems, compute, grads)
    for copy in spread_own + [partner] + tail_copies + own:
        copy.start()
    after_back(after, ret, table, d_block, d_after, d_att)
    halo_copy = remote(d_att.at[pl.ds(0, HALO)], halo, halo_sem.at[0], halo_sem.at[1], prv)
    halo_copy.start()
    lay_rows(tokens, x_wide, x)
    acc[...] = jnp.zeros_like(acc)
    for copy in ins[5:9] + ins[10:]:
        copy.wait()
    halo_copy.wait_recv()
    halo_copy.wait_send()
    top = jnp.where(iota((HALO, C), 0) < 14 * r, halo[...].astype(F32), d_att[:HALO, :].astype(F32))
    d_att[:HALO, :] = top.astype(BF)

    def group(g, carry):
        attn_group_back(g, d_att, wqkv, wo, qkv, probs, mixed, acc)
        return carry

    lax.fori_loop(0, 1, group, 0)
    for arrived, onward in zip(spread_own, far_own):
        arrived.wait_recv()
        onward.start()
    lax.fori_loop(1, 2, group, 0)
    partner.wait_recv()
    for onward in spread_across:
        onward.start()
    lax.fori_loop(2, 3, group, 0)
    for arrived, onward in zip(returns, relayed):
        arrived.wait_recv()
        onward.start()
    lax.fori_loop(3, 4, group, 0)
    d_shift[...] = acc[...].astype(BF)
    halo2_copy = remote(d_shift.at[pl.ds(0, HALO)], halo2, halo_sem.at[2], halo_sem.at[3], nxt)
    halo2_copy.start()

    for arrived, onward in zip(spread_across, far_across):
        arrived.wait_recv()
        onward.start()
    halo2_copy.wait_recv()
    top = jnp.where(iota((HALO, C), 0) < 14 * r, halo2[...].astype(F32), d_shift[:HALO, :].astype(F32))
    x_wide[:HALO, :] = d_after[:HALO, :] + norm_back(x[:HALO, :].astype(F32), top)
    x_wide[HALO:, :] = d_after[HALO:, :] + norm_back(x[HALO:, :].astype(F32), d_shift[HALO:, :].astype(F32))
    for i in range(14):
        tokens_grad[0, i] = x_wide[14 * i:14 * i + 14, :].astype(BF)

    for copy in far_own + far_across + tail_copies:
        copy.wait_recv()
    for copy in own + [ins[9]]:
        copy.wait()
    merged_wide[:, :48, :] = dot(mn_all[...].reshape(8 * 48, 4 * C), wred[...]).reshape(8, 48, 256)
    tails = mt_all[...].astype(F32)
    last = jnp.concatenate([tails[:, i, :] for i in range(16)], axis=1)
    last = jnp.concatenate([last, jnp.zeros_like(last)], axis=0).astype(BF)
    merged_wide[:, 48, :] = dot(last, wred[...])[:8]
    for n in range(8):
        merged_rows[:, n, :] = merged_wide[n]
    merged[...] = merged_rows[...].reshape(7, 7, 8, 256).astype(BF)

    for copy in returns[2:] + relayed:
        copy.wait_recv()
    for copy in own_out:
        copy.wait()
    finish_sends()
    for copy in returns + relayed + gifts + [halo2_copy]:
        copy.wait_send()


def widen(up_in, down_in, grad_in, merged_in, up_out, down_out, grad_out, merged_out):
    up_out[...] = up_in[...].astype(F32)
    down_out[...] = down_in[...].astype(F32)

    @pl.when(pl.program_id(0) == 0)
    def _():
        grad_out[...] = grad_in[...]
        merged_out[...] = merged_in[...]


def bias_pairs():
    spot = np.arange(49)
    py, px = spot // 7, spot % 7
    relative = (py[:, None] - py[None, :] + 6) * 13 + (px[:, None] - px[None, :] + 6)
    table = np.zeros((169, 50, 128), np.float32)
    a, b = np.meshgrid(spot, spot, indexing="ij")
    table[relative.reshape(-1), b.reshape(-1), a.reshape(-1)] = 1.0
    return table.reshape(169, 6400)


def local(
    tokens,
    qkv_weight,
    out_weight,
    position_bias,
    window_shift,
    expert_up,
    expert_down,
    expert_choice,
    combine_weight,
    reduce_weight,
    merged_grad,
):
    choice = jnp.transpose(expert_choice, (1, 0, 3, 2)).reshape(14, 1, 14)
    gate = jnp.transpose(combine_weight, (1, 0, 2))
    pairs = jnp.asarray(bias_pairs(), dtype=BF)
    V = pltpu.VMEM
    D = pltpu.SemaphoreType.DMA

    after, table, merge_norm, mn_tail, d_block, d_slots, qkv, probs, mixed, flat_in, act, slope, ups, downs = pl.pallas_call(
        front,
        out_shape=[
            sds((TP, C), BF), sds((TP, 256), BF), sds((48, 4 * C), BF), sds((16, 256), BF), sds((TP, C), F32),
            sds((32, 16, HC), BF), sds((3, 4, TP, GRP), BF), sds((32 * TP, TP), BF), sds((4, GRP, TP), BF), sds((C, C), BF), sds((C, C), BF),
            sds((C, C), BF), sds((4, C, 256), BF), sds((4, 256, C), BF),
        ],
        in_specs=[SM, VM, VM, VM, VM, HB, VM] + [HB] * 5,
        out_specs=[VM] * 6 + [HB] * 8,
        scratch_shapes=[
            V((TP, C), BF), V((TP, C), F32), V((32, 64, 128), F32), V((169, 6400), BF), V((8, 49, 256), F32),
            V((HALO, C), BF), V((HALO, C), BF), V((TP, C), BF), V((TP, TP), F32),
            V((192, TP), BF), V((TP, 192), BF), V((TP, C), F32), V((TP, C), BF),
            V((C, 3 * C), BF), V((C, C), BF), V((4 * C, 256), BF),
            V((3, 4, TP, GRP), BF), V((32 * TP, TP), BF), V((4, GRP, TP), BF),
            V((8, 48, 4 * C), BF), V((2, 48, 4 * C), BF), V((2, 48, 4 * C), BF), V((2, 48, 4 * C), BF),
            V((48, 4 * C), BF), V((8, 16, 256), F32),
            V((8, 16, 256), BF), V((8, 16, 256), BF),
            V((4, C, 256), BF), V((4, 256, C), BF), V((C, 256), BF), V((256, C), BF),
            V((32, 16, HC), BF), V((4, 32, 16, HC), BF), V((4, 32, 16, HC), BF),
            V((2, 32, 16, HC), BF), V((2, 32, 16, HC), BF), V((8, 16, HC), BF), V((2, 32, 16, HC), BF),
            V((C, C), BF), V((C, C), BF), V((C, C), BF), V((256, C), F32),
            D((16,)), D((4,)), D((8,)), D((8,)), D((4, 8)), *SLOT_SEMS,
        ],
        compiler_params=params(collective_id=0, has_side_effects=True),
        cost_estimate=cost(12 << 30, 60 << 20),
        name="front",
    )(window_shift, tokens, choice, gate, position_bias, pairs, jnp.transpose(merged_grad, (1, 2, 0, 3)), qkv_weight, out_weight,
      expert_up, expert_down, reduce_weight)

    tokens_grad, merged, up_grad, down_grad = pl.pallas_call(
        back,
        out_shape=[
            sds(tokens.shape, BF), sds((7, 7, 8, 256), BF), sds((4, C, 256), BF), sds((4, 256, C), BF),
        ],
        in_specs=[SM] + [VM] * 7 + [HB] * 11,
        out_specs=[VM] * 2 + [HB] * 2,
        scratch_shapes=[
            V((TP, C), BF), V((TP, C), F32), V((HALO, C), BF), V((HALO, C), BF), V((TP, C), BF), V((TP, C), F32),
            V((TP, C), F32), V((TP, C), BF), V((C, 3 * C), BF), V((C, C), BF), V((4 * C, 256), BF),
            V((3, 4, TP, GRP), BF), V((32 * TP, TP), BF), V((4, GRP, TP), BF), V((C, C), BF), V((C, C), BF), V((C, C), BF),
            V((4, C, 256), BF), V((4, 256, C), BF),
            V((4, 32, 16, HC), BF), V((4, 32, 16, HC), BF), V((2, 32, 16, HC), BF), V((2, 32, 16, HC), BF),
            V((8, 16, HC), BF), V((2, 32, 16, HC), BF), V((C, C), BF), V((4, C, 256), BF), V((4, 256, C), BF), V((C, 256), BF), V((256, C), BF),
            V((8, 48, 4 * C), BF), V((8, 16, 256), BF), V((8, 49, 256), F32), V((49, 8, 256), F32),
            D((20,)), D((4,)), D((8,)), D((8,)), D((4, 9)), *SLOT_SEMS,
        ],
        compiler_params=pltpu.CompilerParams(
            vmem_limit_bytes=60 * 1024 * 1024, collective_id=1, has_side_effects=True
        ),
        cost_estimate=cost(16 << 30, 60 << 20),
        name="back",
    )(window_shift, tokens, after, table, merge_norm, mn_tail, d_block, d_slots, qkv_weight, out_weight, reduce_weight,
      qkv, probs, mixed, flat_in, act, slope, ups, downs)
    whole = lambda shape: pl.BlockSpec(shape, lambda e: (0,) * len(shape))
    blocks = [
        pl.BlockSpec((1, C // 2, 256), lambda e: (e // 2, e % 2, 0)), pl.BlockSpec((1, 128, C), lambda e: (e // 2, e % 2, 0)),
        whole(tokens_grad.shape), whole(merged.shape),
    ]
    up_grad, down_grad, tokens_grad, merged = pl.pallas_call(
        widen,
        grid=(8,),
        out_shape=[
            sds((4, C, 256), F32), sds((4, 256, C), F32), sds(tokens_grad.shape, BF), sds(merged.shape, BF),
        ],
        in_specs=blocks,
        out_specs=blocks,
        compiler_params=params(),
        cost_estimate=cost(0, 14 << 20),
        name="widen",
    )(up_grad, down_grad, tokens_grad, merged)
    return (jnp.transpose(merged, (2, 0, 1, 3)), tokens_grad, up_grad, down_grad)


def solution(mesh):
    placed = (
        P("scene", "row", None, None),
        P(),
        P(),
        P(),
        P(),
        P("scene", None, "row"),
        P("scene", "row", None),
        P("scene", "row", None, None),
        P("scene", "row", None),
        P(None, "scene"),
        P(None, "row", None, "scene"),
    )
    return jax.shard_map(
        local,
        mesh=mesh,
        in_specs=placed,
        out_specs=(
            P(None, "row", None, "scene"),
            P("scene", "row", None, None),
            P("scene", None, "row"),
            P("scene", "row", None),
        ),
        check_vma=False,
    )
```

```python
import functools

import jax
import jax.numpy as jnp
import numpy as np
from jax import lax
from jax.experimental import pallas as pl
from jax.experimental.pallas import tpu as pltpu
from jax.sharding import PartitionSpec as P

MESH = pl.DeviceIdType.MESH
F32 = jnp.float32
BF = jnp.bfloat16
EPS = 1e-5
C = 1024
HC = C // 2
TOK = 196
TP = 208
HALO = 96
GRP = 256
NEG = -1e30
VMEM_BIG = 60 * 1024 * 1024
VM = pl.BlockSpec(memory_space=pltpu.VMEM)
SM = pl.BlockSpec(memory_space=pltpu.SMEM)
HB = pl.BlockSpec(memory_space=pl.ANY)


def sds(shape, dtype):
    return jax.ShapeDtypeStruct(shape, dtype)


def params(**kw):
    return pltpu.CompilerParams(vmem_limit_bytes=VMEM_BIG, **kw)


def cost(flops, nbytes):
    return pl.CostEstimate(flops=flops, bytes_accessed=nbytes, transcendentals=0)


def dot(a, b, da=1, db=0):
    return lax.dot_general(a, b, (((da,), (db,)), ((), ())), preferred_element_type=F32)


def iota(shape, dim):
    return lax.broadcasted_iota(jnp.int32, shape, dim)


def norm_parts(values):
    centre = jnp.mean(values, axis=-1, keepdims=True)
    centred = values - centre
    spread = jnp.mean(centred * centred, axis=-1, keepdims=True)
    scale = lax.rsqrt(spread + EPS)
    return centred * scale, scale


def norm_back(values, cot):
    unit, scale = norm_parts(values)
    mean_cot = jnp.mean(cot, axis=-1, keepdims=True)
    mean_dot = jnp.mean(cot * unit, axis=-1, keepdims=True)
    return scale * (cot - mean_cot - unit * mean_dot)


def split3(values):
    high = values.astype(BF)
    rest = values - high.astype(F32)
    mid = rest.astype(BF)
    low = (rest - mid.astype(F32)).astype(BF)
    return high, mid, low


def place_of(tok, r, c):
    rho = (tok * 4682) >> 16
    gam = tok - 14 * rho
    i = rho - r
    i = jnp.where(i < 0, i + 14, i)
    j = gam - c
    j = jnp.where(j < 0, j + 14, j)
    a = jnp.where(i >= 7, 1, 0)
    b = jnp.where(j >= 7, 1, 0)
    return i, j, a, b


def pos_of(tok, r, c):
    i, j, a, b = place_of(tok, r, c)
    return (i - 7 * a) * 7 + (j - 7 * b)


def group_of(tok, r, c, last):
    i, j, a, b = place_of(tok, r, c)
    la = jnp.where(i >= 7, jnp.where(i < 14 - r, 1, 2), 0) * last
    lb = jnp.where(j >= 7, jnp.where(j < 14 - c, 1, 2), 0)
    return a * 2 + b, la * 3 + lb


def pack_rows(low, high, blocks):
    return jnp.concatenate([low.reshape(blocks, 8, HC), high.reshape(blocks, 8, HC)], axis=1).astype(BF)


def unpack_rows(packed, blocks):
    wide = packed.astype(F32)
    low = wide[:, :8, :].reshape(blocks * 8, HC)
    high = wide[:, 8:, :].reshape(blocks * 8, HC)
    return low, high


def attn_masks(r, c, last, mask, ecol, spots):
    tq, tk = iota((TP, TP), 0), iota((TP, TP), 1)
    wq_, lq = group_of(tq, r, c, last)
    wk_, lk = group_of(tk, r, c, last)
    seen = jnp.where(wq_ == wk_, jnp.where(lq == lk, 0.0, -100.0), NEG)
    mask[...] = jnp.where(tq < TOK, seen, NEG)
    row_pos = pos_of(iota((TP, GRP), 0), r, c)
    for h in range(8):
        lane = (iota((TP, GRP), 1) + (224 - 32 * h)) & 255
        spots[h] = jnp.where(lane < 192, jnp.where(row_pos == (lane & 63), 1.0, 0.0), 0.0).astype(BF)
    col_pos = pos_of(iota((192, TP), 1), r, c)
    ecol[...] = jnp.where(col_pos == (iota((192, TP), 0) & 63), 1.0, 0.0).astype(BF)


def cols(start):
    return pl.ds(pl.multiple_of(start, GRP), GRP)


def turned(values, eye):
    return dot(eye, values, 1, 1)


def unit_table():
    return jnp.where(iota((GRP, GRP), 0) == iota((GRP, GRP), 1), 1.0, 0.0).astype(BF)


def attn_group(g, normed, wqkv, wo, bias, mask, ecol, spots, qkv, probs, mixed, acc):
    n = normed[...]
    q = dot(n, wqkv[:, cols(g * GRP)]).astype(BF)
    k = dot(n, wqkv[:, cols(C + g * GRP)]).astype(BF)
    v = dot(n, wqkv[:, cols(2 * C + g * GRP)]).astype(BF)
    qkv[0, g] = q
    qkv[1, g] = k
    qkv[2, g] = v
    eye = unit_table()
    q_t = turned(q, eye).astype(BF)
    v_t = turned(v, eye).astype(BF)
    wide = dot(jnp.concatenate(split3(bias[pl.ds(g * 8, 8)][:, :, :64].reshape(8 * 64, 64)), axis=1), ecol[...])
    w_hi, w_mid, w_lo = split3(wide)
    lane_head = iota((TP, GRP), 1) >> 5
    k32 = k.astype(F32)
    outs = []
    for h in range(8):
        km = jnp.where(lane_head == h, k32, 0.0).astype(BF) + spots[h]
        part = slice(h * 64, h * 64 + 64)
        table = jnp.concatenate([w_hi[part], w_mid[part], w_lo[part], jnp.zeros((32, TP), BF)], axis=0)
        own = [q_t[32 * h:32 * h + 32]]
        if h < 7:
            own = own + [table[:224 - 32 * h]]
        if h:
            own = [table[224 - 32 * h:]] + own
        s = dot(km, jnp.concatenate(own, axis=0)) * (32.0 ** -0.5) + mask[...]
        e = jnp.exp(s - jnp.max(s, axis=0, keepdims=True))
        p = (e * (1.0 / jnp.sum(e, axis=0, keepdims=True))).astype(BF)
        probs[pl.ds(pl.multiple_of((g * 8 + h) * TP, 16), TP), :] = p
        outs.append(dot(v_t[32 * h:32 * h + 32], p))
    mixed_t = jnp.concatenate(outs, axis=0).astype(BF)
    mixed[g] = mixed_t
    acc[...] += dot(mixed_t, wo[pl.ds(pl.multiple_of(g * GRP, GRP), GRP), :], 0, 0)


def attn_group_back(g, d_att, wqkv, wo, qkv, probs, mixed, acc):
    q, k, v = qkv[0, g], qkv[1, g], qkv[2, g]
    eye = unit_table()
    d_out = dot(d_att[...], wo[pl.ds(pl.multiple_of(g * GRP, GRP), GRP), :], 1, 1).astype(BF)
    d_out_t = turned(d_out, eye)
    weighed = d_out_t * mixed[g].astype(F32)
    d_out_t = d_out_t.astype(BF)
    k_t = turned(k, eye).astype(BF)
    v32 = v.astype(F32)
    lane_head = iota((TP, GRP), 1) >> 5
    dq_t = []
    dk = jnp.zeros((TP, GRP), F32)
    dv = jnp.zeros((TP, GRP), F32)
    for h in range(8):
        mine = lane_head == h
        vm = jnp.where(mine, v32, 0.0).astype(BF)
        p = probs[pl.ds(pl.multiple_of((g * 8 + h) * TP, 16), TP), :]
        shared = jnp.sum(weighed[32 * h:32 * h + 32], axis=0, keepdims=True)
        ds = (p.astype(F32) * (dot(vm, d_out_t) - shared)).astype(BF)
        dq_t.append(dot(k_t[32 * h:32 * h + 32], ds))
        dk = jnp.where(mine, dot(ds, q), dk)
        dv = jnp.where(mine, dot(p, d_out), dv)
    scale = 32.0 ** -0.5
    dq = jnp.transpose(jnp.concatenate(dq_t, axis=0) * scale)
    acc[...] += (
        dot(dq.astype(BF), wqkv[:, cols(g * GRP)], 1, 1)
        + dot((dk * scale).astype(BF), wqkv[:, cols(C + g * GRP)], 1, 1)
        + dot(dv.astype(BF), wqkv[:, cols(2 * C + g * GRP)], 1, 1)
    )


def route(r, x, att, halo, choice, after_out, slots, table_out):
    top = jnp.where(iota((HALO, C), 0) < 14 * r, halo[...].astype(F32), att[:HALO, :].astype(F32))
    after_out[:HALO, :] = (x[:HALO, :].astype(F32) + top).astype(BF)
    after_out[HALO:, :] = (x[HALO:, :].astype(F32) + att[HALO:, :].astype(F32)).astype(BF)
    after = after_out[...].astype(F32)
    n2 = norm_parts(after)[0].astype(BF)
    tok, other = iota((TP, TP), 0), iota((TP, TP), 1)
    col = jnp.where(iota((TP, 1), 0) < TOK, choice, -1000.0)
    line = jnp.sum(jnp.where(tok == other, col, 0.0), axis=0, keepdims=True)
    same = jnp.where(col == line, 1.0, 0.0)
    same = jnp.where(other < tok, same, 0.0)
    rank = jnp.sum(same, axis=1, keepdims=True).astype(jnp.int32)
    table = jnp.where(col.astype(jnp.int32) * 8 + rank == iota((TP, 256), 1), 1.0, 0.0).astype(BF)
    table_out[...] = table
    slots[...] = pack_rows(dot(table, n2[:, :HC], 0, 0), dot(table, n2[:, HC:], 0, 0), 32)


def quad_table():
    row = iota((256, TP), 0)
    tok = iota((256, TP), 1)
    q = row >> 6
    n = row & 63
    a = (n * 9363) >> 16
    b = n - 7 * a
    want = (2 * a + (q & 1)) * 14 + 2 * b + (q >> 1)
    hit = jnp.where(want == tok, 1.0, 0.0)
    return jnp.where(n < 49, hit, 0.0).astype(BF)


def gathered(ret, table):
    low, high = unpack_rows(ret[0].astype(F32) + ret[1].astype(F32), 32)
    return jnp.concatenate([dot(table, low.astype(BF)), dot(table, high.astype(BF))], axis=1)


def merge_mid(after, ret, table_in, gate, parts, tail, mn_out, mn_tail, d_block_out, slots, spread, t_wide):
    table = table_in[...]
    block = (after[...].astype(F32) + gate * gathered(ret, table)).astype(BF)
    perm = quad_table()
    quads = dot(perm, block)
    vals = [quads[64 * q:64 * q + 49, :] for q in range(4)]
    inv = 1.0 / (4 * C)
    centre = sum(jnp.sum(v, axis=-1, keepdims=True) for v in vals) * inv
    cent = [v - centre for v in vals]
    var = sum(jnp.sum(v * v, axis=-1, keepdims=True) for v in cent) * inv
    scale = lax.rsqrt(var + EPS)
    unit = [v * scale for v in cent]
    for q in range(4):
        mn_out[:, q * C:(q + 1) * C] = unit[q][:48].astype(BF)
        for i in range(4):
            t_wide[0, 4 * q + i:4 * q + i + 1, :] = unit[q][48:49, i * 256:(i + 1) * 256]
    mn_tail[...] = t_wide[0].astype(BF)
    tails = jnp.sum(tail[...].astype(F32), axis=0)
    cots = []
    for q in range(4):
        tot = sum(part[:, q * C:(q + 1) * C].astype(F32) for part in parts)
        last = jnp.concatenate([tails[4 * q + i:4 * q + i + 1, :] for i in range(4)], axis=1)
        cots.append(jnp.concatenate([tot, last], axis=0))
    mean_cot = sum(jnp.sum(v, axis=-1, keepdims=True) for v in cots) * inv
    mean_dot = sum(jnp.sum(v * u, axis=-1, keepdims=True) for v, u in zip(cots, unit)) * inv
    spread[...] = jnp.zeros_like(spread)
    for q in range(4):
        spread[64 * q:64 * q + 49, :] = scale * (cots[q] - mean_cot - unit[q] * mean_dot)
    high, mid, low = split3(spread[...])
    d_block = dot(perm, high, 0, 0) + dot(perm, mid, 0, 0) + dot(perm, low, 0, 0)
    d_block_out[...] = d_block
    scaled = (gate * d_block).astype(BF)
    slots[...] = pack_rows(dot(table, scaled[:, :HC], 0, 0), dot(table, scaled[:, HC:], 0, 0), 32)


def after_back(after, ret, table, d_block, d_after_out, d_att_out):
    d_second = gathered(ret, table[...])
    d_after = d_block[...] + norm_back(after[...].astype(F32), d_second)
    d_after_out[...] = d_after
    d_att_out[...] = d_after.astype(BF)


def token_column(grid):
    tok = iota((TP, 14), 0)
    rho = (tok * 4682) >> 16
    place = iota((TP, 14), 1)
    pick = jnp.where(rho == place, 1.0, 0.0).astype(BF)
    high, mid, low = split3(grid[...].reshape(14, 14))
    rows = dot(pick, high) + dot(pick, mid) + dot(pick, low)
    return jnp.sum(jnp.where(tok - 14 * rho == place, rows, 0.0), axis=1, keepdims=True)


def lay_rows(tokens, wide, x):
    wide[TOK - 4:, :] = jnp.zeros((TP - TOK + 4, C), F32)
    for i in range(14):
        wide[14 * i:14 * i + 14, :] = tokens[0, i].astype(F32)
    x[...] = wide[...].astype(BF)


def expert_chunk(j, recv, part, ups, downs, flat, act_out, slope_out, ready):
    here = pl.ds(8 * j, 8)
    rows_here = pl.ds(256 * j, 256)
    low, high = unpack_rows(recv[:, here].reshape(32, 16, HC), 32)
    rows = jnp.concatenate([low, high], axis=1).astype(BF)
    flat[rows_here, :] = rows
    total = jnp.zeros((256, C), F32)
    for k in (0, 1, 3, 2):
        ready(k)
        pre = dot(rows, ups[k])
        cdf = 0.5 * (1.0 + lax.erf(pre * np.float32(2.0 ** -0.5)))
        act = (pre * cdf).astype(BF)
        slope = cdf + pre * jnp.exp(-0.5 * pre * pre) * np.float32((2.0 * np.pi) ** -0.5)
        act_out[rows_here, k * 256:(k + 1) * 256] = act
        slope_out[rows_here, k * 256:(k + 1) * 256] = slope.astype(BF)
        total = total + dot(act, downs[k])
    part[:, here] = pack_rows(total[:, :HC], total[:, HC:], 32).reshape(4, 8, 16, HC)


def expert_chunk_back(j, recv, part, ups, downs, flat, slope):
    here = pl.ds(8 * j, 8)
    rows_here = pl.ds(256 * j, 256)
    low, high = unpack_rows(recv[:, here].reshape(32, 16, HC), 32)
    rows = jnp.concatenate([low, high], axis=1).astype(BF)
    flat[rows_here, :] = rows
    total = jnp.zeros((256, C), F32)
    for k in range(4):
        span = slice(k * 256, (k + 1) * 256)
        d_pre = (slope[rows_here, span].astype(F32) * dot(rows, downs[k], 1, 1)).astype(BF)
        slope[rows_here, span] = d_pre
        total = total + dot(d_pre, ups[k], 1, 1)
    part[:, here] = pack_rows(total[:, :HC], total[:, HC:], 32).reshape(4, 8, 16, HC)


def coords():
    s = lax.axis_index("scene")
    row = lax.axis_index("row")
    z, m = row // 4, row % 4
    return s, z, m // 2, m % 2


def at(s, z, y, c):
    return (s, z * 4 + y * 2 + c)


def greet(s, z, y, c, total=64):
    barrier = pltpu.get_barrier_semaphore()
    mine = s * 4 + z

    def hail(k, carry):
        peer = (mine + k) % 32
        pl.semaphore_signal(barrier, inc=1, device_id=at(peer // 4, peer % 4, y, c), device_id_type=MESH)
        pl.semaphore_signal(barrier, inc=1, device_id=at(peer // 4, peer % 4, 1 - y, c), device_id_type=MESH)
        return carry

    lax.fori_loop(1, 32, hail, 0)
    pl.semaphore_signal(barrier, inc=1, device_id=at(s, z, 1 - y, c), device_id_type=MESH)
    pl.semaphore_signal(barrier, inc=1, device_id=at(s, z, y, 1 - c), device_id_type=MESH)
    pl.semaphore_wait(barrier, total)


def greet_all(place):
    s, z, y, c = place
    barrier = pltpu.get_barrier_semaphore()
    row = z * 4 + y * 2 + c
    pl.semaphore_signal(barrier, inc=1, device_id=(s, (row + 1) % 16), device_id_type=MESH)
    pl.semaphore_signal(barrier, inc=1, device_id=(s, (row + 15) % 16), device_id_type=MESH)
    greet(s, z, y, c, 66)


def remote(src, dst, send, recv, device):
    return pltpu.make_async_remote_copy(
        src_ref=src, dst_ref=dst, send_sem=send, recv_sem=recv, device_id=device, device_id_type=MESH
    )


def await_bytes(ref, sem):
    pltpu.make_async_copy(ref, ref, sem).wait()


SLOT_SEMS = [
    pltpu.SemaphoreType.DMA,
    pltpu.SemaphoreType.DMA((2, 4)),
    pltpu.SemaphoreType.DMA((2, 4)),
    pltpu.SemaphoreType.DMA((2, 4)),
    pltpu.SemaphoreType.DMA((2, 4)),
    pltpu.SemaphoreType.DMA((2, 4)),
    pltpu.SemaphoreType.DMA,
    pltpu.SemaphoreType.DMA,
]


def slots_through(place, slots, recv, part, other, total, ret, sems, compute, meanwhile=None):
    s, z, y, c = place
    mine = s * 4 + z
    yh, xx = s // 4, s % 4

    def steps(k):
        dx = k % 4
        return (k % 8) // 4, dx, (k // 8 + 4 - dx) % 4

    def ahead(k):
        dy, dx, dz = steps(k)
        return ((yh + dy) % 2 * 4 + (xx + dx) % 4) * 4 + (z + dz) % 4

    def behind(k):
        dy, dx, dz = steps(k)
        return ((yh + dy) % 2 * 4 + (xx + 4 - dx) % 4) * 4 + (z + 4 - dz) % 4

    send, arrive, f_send, f_recv, p_send, p_recv, r_send, r_recv = sems
    pair = at(s, z, y, 1 - c)

    def to_peer(k, peer, yy):
        remote(slots.at[peer], recv.at[y * 2 + c, k], send, arrive.at[y, k // 8], at(peer // 4, peer % 4, yy, c)).start()

    def push(k, carry):
        peer = ahead(k)
        to_peer(k, peer, y)
        to_peer(k, peer, 1 - y)
        return carry

    pltpu.make_async_copy(slots.at[mine], recv.at[y * 2 + c, 0], arrive.at[y, 0]).start()
    to_peer(0, mine, 1 - y)
    lax.fori_loop(1, 32, push, 0)
    forwards, partials = {}, {}

    def forward(j):
        for yy in range(2):
            block = recv.at[yy * 2 + c, pl.ds(8 * j, 8)]
            await_bytes(block, arrive.at[yy, j])
            forwards[yy, j] = remote(block, block, f_send.at[yy, j], f_recv.at[yy, j], pair)
            forwards[yy, j].start()

    def work(j):
        for yy in range(2):
            forwards[yy, j].wait_recv()
        compute(j)
        for yy in range(2):
            here = pl.ds(8 * j, 8)
            partials[yy, j] = remote(
                part.at[yy * 2 + (1 - c), here], other.at[yy, here], p_send.at[yy, j], p_recv.at[yy, j], pair
            )
            partials[yy, j].start()

    def give(k, yy):
        peer = behind(k)
        remote(total.at[yy, k], ret.at[y, mine], r_send, r_recv, at(peer // 4, peer % 4, yy, c)).start()

    def give_both(k, carry):
        give(k, 1 - y)
        give(k, y)
        return carry

    def back(j):
        here = pl.ds(8 * j, 8)
        for yy in range(2):
            partials[yy, j].wait_recv()
            total[yy, here] = (part[yy * 2 + c, here].astype(F32) + other[yy, here].astype(F32)).astype(BF)
        if j == 0:
            give(0, 1 - y)
            pltpu.make_async_copy(total.at[y, 0], ret.at[y, mine], r_recv).start()
        lax.fori_loop(max(1, 8 * j), 8 * j + 8, give_both, 0)

    forward(0)
    forward(1)
    work(0)
    forward(2)
    work(1)
    back(0)
    forward(3)
    work(2)
    back(1)
    work(3)
    back(2)
    back(3)

    def finish_sends():
        for copy in list(forwards.values()) + list(partials.values()):
            copy.wait_send()
        for sem in (send, r_send):
            await_bytes(total.at[0], sem)
            await_bytes(total.at[0, pl.ds(0, 31)], sem)

    if meanwhile is not None:
        meanwhile()
    await_bytes(ret, r_recv)
    return finish_sends


def front(
    shift, tokens, choice_in, gate_in, position_bias, pairs, merged_grad, qkv_weight, out_weight, expert_up, expert_down, reduce_weight,
    after, table, merge_norm, mn_tail, d_block, d_slots, qkv_out, probs_out, mixed_out, flat_out, act_out, slope_out, up_out, down_out,
    x, x_wide, bias, table_of, grad_wide, halo, halo2, normed, mask, ecol, spots, acc, att, wqkv, wo, wred, qkv, probs, mixed,
    d_send, d_relay, d_direct, d_summed, d_across, t_wide, t_send, t_recv, ups, downs, relay_up, relay_down,
    slots, recv, part, other, total, ret, flat, act, slope, spread,
    io_sem, halo_sem, w_send, w_recv, d_sem, *slot_sems,
):
    place = coords()
    s, z, y, c = place
    row = z * 4 + y * 2 + c
    r, cc = shift[0], shift[1]
    last = jnp.where(row == 15, 1, 0)
    ins = [
        pltpu.make_async_copy(reduce_weight, wred, io_sem.at[0]),
        pltpu.make_async_copy(qkv_weight, wqkv, io_sem.at[1]),
        pltpu.make_async_copy(out_weight, wo, io_sem.at[2]),
        pltpu.make_async_copy(expert_up.at[z], ups.at[0], io_sem.at[3]),
        pltpu.make_async_copy(expert_down.at[z], downs.at[0], io_sem.at[4]),
        pltpu.make_async_copy(pairs, table_of, io_sem.at[14]),
    ]
    for copy in ins:
        copy.start()
    lay_rows(tokens, x_wide, x)
    greet_all(place)

    nxt = (s, (row + 1) % 16)
    prv = (s, (row + 15) % 16)
    z_up, z_down = at(s, (z + 1) % 4, y, c), at(s, (z + 3) % 4, y, c)
    halo_copy = remote(x.at[pl.ds(0, HALO)], halo, halo_sem.at[0], halo_sem.at[1], prv)
    halo_copy.start()
    weights = [
        remote(expert_up.at[(z + 2) % 4], relay_up, w_send.at[0], w_recv.at[0], z_up),
        remote(expert_down.at[(z + 2) % 4], relay_down, w_send.at[1], w_recv.at[1], z_down),
        remote(expert_up.at[(z + 1) % 4], ups.at[1], w_send.at[2], w_recv.at[2], z_up),
        remote(expert_up.at[(z + 3) % 4], ups.at[3], w_send.at[3], w_recv.at[3], z_down),
        remote(expert_down.at[(z + 1) % 4], downs.at[1], w_send.at[4], w_recv.at[4], z_up),
        remote(expert_down.at[(z + 3) % 4], downs.at[3], w_send.at[5], w_recv.at[5], z_down),
    ]
    for copy in weights:
        copy.start()
    relayed = [
        remote(relay_up, ups.at[2], w_send.at[6], w_recv.at[6], z_up),
        remote(relay_down, downs.at[2], w_send.at[7], w_recv.at[7], z_down),
    ]

    by_place = merged_grad[...].astype(F32).reshape(49, 8, 256)
    for n in range(8):
        grad_wide[n] = by_place[:, n, :]
    grad48 = grad_wide[:, :48, :].astype(BF).reshape(8 * 48, 256)
    grad_tail = jnp.concatenate([grad_wide[:, 48, :], jnp.zeros((8, 256), F32)], axis=0).astype(BF)
    ins[0].wait()
    for half in range(4):
        span = pl.ds(half * C, C)
        d_send[:, :, span] = dot(grad48, wred[span, :], 1, 1).astype(BF).reshape(8, 48, C)
        tail = dot(grad_tail, wred[span, :], 1, 1)
        for i in range(4):
            t_wide[:, 4 * half + i, :] = tail[:8, i * 256:(i + 1) * 256]
    t_send[...] = t_wide[...].astype(BF)
    yh, xx = s // 4, s % 4
    x_up, x_down, x_far = (xx + 1) % 4, (xx + 3) % 4, (xx + 2) % 4
    to_up, to_down = at(yh * 4 + x_up, z, y, c), at(yh * 4 + x_down, z, y, c)
    first = [
        remote(d_send.at[x_far], d_relay.at[0], d_sem.at[0, 0], d_sem.at[1, 0], to_up),
        remote(d_send.at[4 + x_far], d_relay.at[1], d_sem.at[0, 1], d_sem.at[1, 1], to_down),
        remote(d_send.at[4 + x_up], d_direct.at[1], d_sem.at[0, 2], d_sem.at[1, 2], to_up),
        remote(d_send.at[x_down], d_direct.at[0], d_sem.at[0, 3], d_sem.at[1, 3], to_down),
    ]
    second = [
        remote(d_send.at[x_up], d_summed.at[0], d_sem.at[0, 4], d_sem.at[1, 4], to_up),
        remote(d_send.at[4 + x_down], d_summed.at[1], d_sem.at[0, 5], d_sem.at[1, 5], to_down),
    ]
    other_yh = 1 - yh
    across = remote(
        d_send.at[other_yh * 4 + xx], d_across, d_sem.at[0, 6], d_sem.at[1, 6], at(other_yh * 4 + xx, z, y, c)
    )
    gifts = []
    for k in range(1, 8):
        peer = (s + k) % 8
        gifts.append(remote(t_send.at[peer], t_recv.at[s], d_sem.at[2, k], d_sem.at[3, k], at(peer, z, y, c)))
    for copy in first + gifts:
        copy.start()
    own = pltpu.make_async_copy(t_send.at[s], t_recv.at[s], io_sem.at[6])
    own.start()

    def pass_on():
        for i, mine_at in enumerate((x_up, 4 + x_down)):
            first[i].wait_recv()
            d_send[mine_at] = (d_send[mine_at].astype(F32) + d_relay[i].astype(F32)).astype(BF)
            second[i].start()

    def cross():
        for copy in first[2:] + second:
            copy.wait_recv()
        there = other_yh * 4 + xx
        d_send[there] = (
            d_send[there].astype(F32) + d_direct[other_yh].astype(F32) + d_summed[other_yh].astype(F32)
        ).astype(BF)
        across.start()

    attn_masks(r, cc, last, mask, ecol, spots)
    ins[5].wait()
    bias[...] = jnp.zeros_like(bias)
    parts3 = jnp.concatenate(split3(position_bias[...]), axis=0)
    for pair in range(25):
        wide = dot(parts3, table_of[:, pair * 256:(pair + 1) * 256])
        wide = wide[:32] + wide[32:64] + wide[64:]
        for i in range(2):
            if 2 * pair + i < 49:
                bias[:, 2 * pair + i, :] = wide[:, i * 128:(i + 1) * 128] * np.float32(32.0 ** 0.5)
    normed[HALO:, :] = norm_parts(x[HALO:, :].astype(F32))[0].astype(BF)
    acc[...] = jnp.zeros_like(acc)
    halo_copy.wait_recv()
    top = jnp.where(iota((HALO, C), 0) < 14 * r, halo[...].astype(F32), x[:HALO, :].astype(F32))
    normed[:HALO, :] = norm_parts(top)[0].astype(BF)
    ins[1].wait()
    ins[2].wait()

    def group(g, carry):
        attn_group(g, normed, wqkv, wo, bias, mask, ecol, spots, qkv, probs, mixed, acc)
        return carry

    lax.fori_loop(0, 1, group, 0)
    pass_on()
    lax.fori_loop(1, 3, group, 0)
    for arrived, onward in zip(weights, relayed):
        arrived.wait_recv()
        onward.start()
    lax.fori_loop(3, 4, group, 0)
    att[...] = acc[...].astype(BF)
    halo2_copy = remote(att.at[pl.ds(0, HALO)], halo2, halo_sem.at[2], halo_sem.at[3], nxt)
    halo2_copy.start()
    outs = [
        pltpu.make_async_copy(qkv, qkv_out, io_sem.at[7]),
        pltpu.make_async_copy(probs, probs_out, io_sem.at[8]),
        pltpu.make_async_copy(mixed, mixed_out, io_sem.at[15]),
    ]
    for copy in outs:
        copy.start()
    halo2_copy.wait_recv()
    choice = token_column(choice_in[...].astype(F32))
    route(r, x, att, halo2, choice, after, slots, table)

    def ready(k):
        pieces = {0: (), 1: (weights[2], weights[4]), 3: (weights[3], weights[5]), 2: relayed}[k]
        for copy in pieces:
            copy.wait_recv()
        if k == 0:
            ins[3].wait()
            ins[4].wait()

    def compute(j):
        expert_chunk(j, recv, part, ups, downs, flat, act, slope, ready if j == 0 else lambda k: None)
        if j == 1:
            cross()

    finish_sends = slots_through(place, slots, recv, part, other, total, ret, slot_sems, compute)
    more = [
        pltpu.make_async_copy(flat, flat_out, io_sem.at[9]),
        pltpu.make_async_copy(act, act_out, io_sem.at[10]),
        pltpu.make_async_copy(slope, slope_out, io_sem.at[11]),
        pltpu.make_async_copy(ups, up_out, io_sem.at[12]),
        pltpu.make_async_copy(downs, down_out, io_sem.at[13]),
    ]
    for copy in more:
        copy.start()
    for copy in gifts + [across]:
        copy.wait_recv()
    own.wait()
    parts = (d_send.at[s], d_direct.at[yh], d_summed.at[yh], d_across)
    merge_mid(after, ret, table, token_column(gate_in), parts, t_recv, merge_norm, mn_tail, d_block, d_slots, spread, t_wide)
    for copy in outs + more:
        copy.wait()
    finish_sends()
    for copy in weights + relayed + gifts + first + second + [across, halo_copy, halo2_copy]:
        copy.wait_send()


def back(
    shift, tokens, after, table, merge_norm, mn_tail, d_block, d_slots,
    qkv_weight, out_weight, reduce_weight, qkv_in, probs_in, mixed_in, flat_in, act_in, slope_in, up_in, down_in,
    tokens_grad, merged, up_grad, down_grad,
    x, x_wide, halo, halo2, d_att, acc, d_after, d_shift, wqkv, wo, wred, qkv, probs, mixed, flat, act, slope, ups, downs,
    recv, part, other, total, ret, flat_d, send_up, send_down, relay_up, relay_down,
    mn_all, mt_all, merged_wide, merged_rows,
    io_sem, halo_sem, g_send, g_recv, m_sem, *slot_sems,
):
    place = coords()
    s, z, y, c = place
    row = z * 4 + y * 2 + c
    r = shift[0]
    loads = [
        (down_in, downs), (slope_in, slope), (up_in, ups), (act_in, act), (flat_in, flat),
        (out_weight, wo), (qkv_in, qkv), (probs_in, probs), (qkv_weight, wqkv), (reduce_weight, wred), (mixed_in, mixed),
    ]
    ins = [pltpu.make_async_copy(a, b, io_sem.at[i]) for i, (a, b) in enumerate(loads)]
    for copy in ins:
        copy.start()
    greet_all(place)
    nxt = (s, (row + 1) % 16)
    prv = (s, (row + 15) % 16)
    z_up, z_down = at(s, (z + 1) % 4, y, c), at(s, (z + 3) % 4, y, c)

    returns = [
        remote(send_up.at[1], relay_up, g_send.at[0], g_recv.at[0], z_up),
        remote(send_down.at[1], relay_down, g_send.at[1], g_recv.at[1], z_down),
        remote(send_up.at[0], up_grad.at[z], g_send.at[2], g_recv.at[2], z_down),
        remote(send_down.at[0], down_grad.at[z], g_send.at[3], g_recv.at[3], z_down),
        remote(send_up.at[2], up_grad.at[z], g_send.at[4], g_recv.at[4], z_up),
        remote(send_down.at[2], down_grad.at[z], g_send.at[5], g_recv.at[5], z_up),
    ]
    relayed = [
        remote(relay_up, up_grad.at[(z + 3) % 4], g_send.at[6], g_recv.at[6], z_up),
        remote(relay_down, down_grad.at[(z + 1) % 4], g_send.at[7], g_recv.at[7], z_down),
    ]
    yh, xx = s // 4, s % 4
    x_up, x_down = (xx + 1) % 4, (xx + 3) % 4
    to_up, to_down = at(yh * 4 + x_up, z, y, c), at(yh * 4 + x_down, z, y, c)
    across = (1 - yh) * 4 + xx
    half = (pl.ds(0, 2 * C), pl.ds(2 * C, 2 * C))

    def neighbours(source, slot, n):
        return [
            remote(source, mn_all.at[slot], m_sem.at[0, n], m_sem.at[1, n], to_up),
            remote(source, mn_all.at[slot], m_sem.at[0, n + 1], m_sem.at[1, n + 1], to_down),
        ]

    def halves(base, n):
        below, above = base * 4 + x_down, base * 4 + x_up
        low, high = mn_all.at[below, :, half[0]], mn_all.at[above, :, half[1]]
        return [
            remote(low, low, m_sem.at[0, n], m_sem.at[1, n], to_up),
            remote(high, high, m_sem.at[0, n + 1], m_sem.at[1, n + 1], to_down),
        ]

    spread_own = neighbours(merge_norm, s, 0)
    spread_across = neighbours(mn_all.at[across], across, 2)
    far_own = halves(yh, 4)
    far_across = halves(1 - yh, 6)
    partner = remote(merge_norm, mn_all.at[s], m_sem.at[0, 8], m_sem.at[1, 8], at(across, z, y, c))
    tail_copies = []
    for k in range(1, 8):
        peer = (s + k) % 8
        tail_copies.append(remote(mn_tail, mt_all.at[s], m_sem.at[2, k], m_sem.at[3, k], at(peer, z, y, c)))
    gifts = spread_own + spread_across + far_own + far_across + [partner] + tail_copies
    own = [
        pltpu.make_async_copy(merge_norm, mn_all.at[s], io_sem.at[14]),
        pltpu.make_async_copy(mn_tail, mt_all.at[s], io_sem.at[11]),
    ]
    own_out = [
        pltpu.make_async_copy(send_up.at[3], up_grad.at[z], io_sem.at[12]),
        pltpu.make_async_copy(send_down.at[3], down_grad.at[z], io_sem.at[13]),
    ]

    def grads():
        for copy in ins[3:5]:
            copy.wait()
        for k in (2, 1, 3, 0):
            span = slice(k * 256, (k + 1) * 256)
            up_part = dot(flat[...], slope[:, span], 0, 0)
            down_part = dot(act[:, span], flat_d[...], 0, 0)
            send_up[(k + 3) % 4] = up_part.astype(BF)
            send_down[(k + 3) % 4] = down_part.astype(BF)
            if k:
                first = {2: 0, 1: 2, 3: 4}[k]
                returns[first].start()
                returns[first + 1].start()
            else:
                for copy in own_out:
                    copy.start()

    partner.start()

    def compute(j):
        if j == 0:
            for copy in ins[:3]:
                copy.wait()
        expert_chunk_back(j, recv, part, ups, downs, flat_d, slope)

    finish_sends = slots_through(place, d_slots, recv, part, other, total, ret, slot_sems, compute, grads)
    partner.wait_recv()
    for copy in spread_own + spread_across + tail_copies + own:
        copy.start()
    after_back(after, ret, table, d_block, d_after, d_att)
    halo_copy = remote(d_att.at[pl.ds(0, HALO)], halo, halo_sem.at[0], halo_sem.at[1], prv)
    halo_copy.start()
    lay_rows(tokens, x_wide, x)
    acc[...] = jnp.zeros_like(acc)
    for copy in ins[5:9] + ins[10:]:
        copy.wait()
    halo_copy.wait_recv()
    halo_copy.wait_send()
    top = jnp.where(iota((HALO, C), 0) < 14 * r, halo[...].astype(F32), d_att[:HALO, :].astype(F32))
    d_att[:HALO, :] = top.astype(BF)

    def group(g, carry):
        attn_group_back(g, d_att, wqkv, wo, qkv, probs, mixed, acc)
        return carry

    lax.fori_loop(0, 1, group, 0)
    for arrived, onward in zip(spread_own, far_own):
        arrived.wait_recv()
        onward.start()
    lax.fori_loop(1, 3, group, 0)
    for arrived, onward in zip(returns, relayed):
        arrived.wait_recv()
        onward.start()
    lax.fori_loop(3, 4, group, 0)
    d_shift[...] = acc[...].astype(BF)
    halo2_copy = remote(d_shift.at[pl.ds(0, HALO)], halo2, halo_sem.at[2], halo_sem.at[3], nxt)
    halo2_copy.start()

    halo2_copy.wait_recv()
    for arrived, onward in zip(spread_across, far_across):
        arrived.wait_recv()
        onward.start()
    top = jnp.where(iota((HALO, C), 0) < 14 * r, halo2[...].astype(F32), d_shift[:HALO, :].astype(F32))
    x_wide[:HALO, :] = d_after[:HALO, :] + norm_back(x[:HALO, :].astype(F32), top)
    x_wide[HALO:, :] = d_after[HALO:, :] + norm_back(x[HALO:, :].astype(F32), d_shift[HALO:, :].astype(F32))
    for i in range(14):
        tokens_grad[0, i] = x_wide[14 * i:14 * i + 14, :].astype(BF)

    for copy in far_own + far_across + tail_copies:
        copy.wait_recv()
    for copy in own + [ins[9]]:
        copy.wait()
    merged_wide[:, :48, :] = dot(mn_all[...].reshape(8 * 48, 4 * C), wred[...]).reshape(8, 48, 256)
    tails = mt_all[...].astype(F32)
    last = jnp.concatenate([tails[:, i, :] for i in range(16)], axis=1)
    last = jnp.concatenate([last, jnp.zeros_like(last)], axis=0).astype(BF)
    merged_wide[:, 48, :] = dot(last, wred[...])[:8]
    for n in range(8):
        merged_rows[:, n, :] = merged_wide[n]
    merged[...] = merged_rows[...].reshape(7, 7, 8, 256).astype(BF)

    for copy in returns[2:] + relayed:
        copy.wait_recv()
    for copy in own_out:
        copy.wait()
    finish_sends()
    for copy in returns + relayed + gifts + [halo2_copy]:
        copy.wait_send()


def widen(up_in, down_in, grad_in, merged_in, up_out, down_out, grad_out, merged_out):
    up_out[...] = up_in[...].astype(F32)
    down_out[...] = down_in[...].astype(F32)

    @pl.when(pl.program_id(0) == 0)
    def _():
        grad_out[...] = grad_in[...]
        merged_out[...] = merged_in[...]


def bias_pairs():
    spot = np.arange(49)
    py, px = spot // 7, spot % 7
    relative = (py[:, None] - py[None, :] + 6) * 13 + (px[:, None] - px[None, :] + 6)
    table = np.zeros((169, 50, 128), np.float32)
    a, b = np.meshgrid(spot, spot, indexing="ij")
    table[relative.reshape(-1), b.reshape(-1), a.reshape(-1)] = 1.0
    return table.reshape(169, 6400)


def local(
    tokens,
    qkv_weight,
    out_weight,
    position_bias,
    window_shift,
    expert_up,
    expert_down,
    expert_choice,
    combine_weight,
    reduce_weight,
    merged_grad,
):
    choice = jnp.transpose(expert_choice, (1, 0, 3, 2)).reshape(14, 1, 14)
    gate = jnp.transpose(combine_weight, (1, 0, 2))
    pairs = jnp.asarray(bias_pairs(), dtype=BF)
    V = pltpu.VMEM
    D = pltpu.SemaphoreType.DMA

    after, table, merge_norm, mn_tail, d_block, d_slots, qkv, probs, mixed, flat_in, act, slope, ups, downs = pl.pallas_call(
        front,
        out_shape=[
            sds((TP, C), BF), sds((TP, 256), BF), sds((48, 4 * C), BF), sds((16, 256), BF), sds((TP, C), F32),
            sds((32, 16, HC), BF), sds((3, 4, TP, GRP), BF), sds((32 * TP, TP), BF), sds((4, GRP, TP), BF), sds((C, C), BF), sds((C, C), BF),
            sds((C, C), BF), sds((4, C, 256), BF), sds((4, 256, C), BF),
        ],
        in_specs=[SM, VM, VM, VM, VM, HB, VM] + [HB] * 5,
        out_specs=[VM] * 6 + [HB] * 8,
        scratch_shapes=[
            V((TP, C), BF), V((TP, C), F32), V((32, 64, 128), F32), V((169, 6400), BF), V((8, 49, 256), F32),
            V((HALO, C), BF), V((HALO, C), BF), V((TP, C), BF), V((TP, TP), F32),
            V((192, TP), BF), V((8, TP, GRP), BF), V((TP, C), F32), V((TP, C), BF),
            V((C, 3 * C), BF), V((C, C), BF), V((4 * C, 256), BF),
            V((3, 4, TP, GRP), BF), V((32 * TP, TP), BF), V((4, GRP, TP), BF),
            V((8, 48, 4 * C), BF), V((2, 48, 4 * C), BF), V((2, 48, 4 * C), BF), V((2, 48, 4 * C), BF),
            V((48, 4 * C), BF), V((8, 16, 256), F32),
            V((8, 16, 256), BF), V((8, 16, 256), BF),
            V((4, C, 256), BF), V((4, 256, C), BF), V((C, 256), BF), V((256, C), BF),
            V((32, 16, HC), BF), V((4, 32, 16, HC), BF), V((4, 32, 16, HC), BF),
            V((2, 32, 16, HC), BF), V((2, 32, 16, HC), BF), V((2, 32, 16, HC), BF),
            V((C, C), BF), V((C, C), BF), V((C, C), BF), V((256, C), F32),
            D((16,)), D((4,)), D((8,)), D((8,)), D((4, 8)), *SLOT_SEMS,
        ],
        compiler_params=params(collective_id=0, has_side_effects=True),
        cost_estimate=cost(12 << 30, 60 << 20),
        name="front",
    )(window_shift, tokens, choice, gate, position_bias, pairs, jnp.transpose(merged_grad, (1, 2, 0, 3)), qkv_weight, out_weight,
      expert_up, expert_down, reduce_weight)

    tokens_grad, merged, up_grad, down_grad = pl.pallas_call(
        back,
        out_shape=[
            sds(tokens.shape, BF), sds((7, 7, 8, 256), BF), sds((4, C, 256), BF), sds((4, 256, C), BF),
        ],
        in_specs=[SM] + [VM] * 7 + [HB] * 11,
        out_specs=[VM] * 2 + [HB] * 2,
        scratch_shapes=[
            V((TP, C), BF), V((TP, C), F32), V((HALO, C), BF), V((HALO, C), BF), V((TP, C), BF), V((TP, C), F32),
            V((TP, C), F32), V((TP, C), BF), V((C, 3 * C), BF), V((C, C), BF), V((4 * C, 256), BF),
            V((3, 4, TP, GRP), BF), V((32 * TP, TP), BF), V((4, GRP, TP), BF), V((C, C), BF), V((C, C), BF), V((C, C), BF),
            V((4, C, 256), BF), V((4, 256, C), BF),
            V((4, 32, 16, HC), BF), V((4, 32, 16, HC), BF), V((2, 32, 16, HC), BF), V((2, 32, 16, HC), BF),
            V((2, 32, 16, HC), BF), V((C, C), BF), V((4, C, 256), BF), V((4, 256, C), BF), V((C, 256), BF), V((256, C), BF),
            V((8, 48, 4 * C), BF), V((8, 16, 256), BF), V((8, 49, 256), F32), V((49, 8, 256), F32),
            D((20,)), D((4,)), D((8,)), D((8,)), D((4, 9)), *SLOT_SEMS,
        ],
        compiler_params=pltpu.CompilerParams(
            vmem_limit_bytes=60 * 1024 * 1024, collective_id=1, has_side_effects=True
        ),
        cost_estimate=cost(16 << 30, 60 << 20),
        name="back",
    )(window_shift, tokens, after, table, merge_norm, mn_tail, d_block, d_slots, qkv_weight, out_weight, reduce_weight,
      qkv, probs, mixed, flat_in, act, slope, ups, downs)
    whole = lambda shape: pl.BlockSpec(shape, lambda e: (0,) * len(shape))
    blocks = [
        pl.BlockSpec((1, C, 256), lambda e: (e, 0, 0)), pl.BlockSpec((1, 256, C), lambda e: (e, 0, 0)),
        whole(tokens_grad.shape), whole(merged.shape),
    ]
    up_grad, down_grad, tokens_grad, merged = pl.pallas_call(
        widen,
        grid=(4,),
        out_shape=[
            sds((4, C, 256), F32), sds((4, 256, C), F32), sds(tokens_grad.shape, BF), sds(merged.shape, BF),
        ],
        in_specs=blocks,
        out_specs=blocks,
        compiler_params=params(),
        cost_estimate=cost(0, 14 << 20),
        name="widen",
    )(up_grad, down_grad, tokens_grad, merged)
    return (jnp.transpose(merged, (2, 0, 1, 3)), tokens_grad, up_grad, down_grad)


def solution(mesh):
    placed = (
        P("scene", "row", None, None),
        P(),
        P(),
        P(),
        P(),
        P("scene", None, "row"),
        P("scene", "row", None),
        P("scene", "row", None, None),
        P("scene", "row", None),
        P(None, "scene"),
        P(None, "row", None, "scene"),
    )
    return jax.shard_map(
        local,
        mesh=mesh,
        in_specs=placed,
        out_specs=(
            P(None, "row", None, "scene"),
            P("scene", "row", None, None),
            P("scene", None, "row"),
            P("scene", "row", None),
        ),
        check_vma=False,
    )
```

```python
import functools

import jax
import jax.numpy as jnp
import numpy as np
from jax import lax
from jax.experimental import pallas as pl
from jax.experimental.pallas import tpu as pltpu
from jax.sharding import PartitionSpec as P

MESH = pl.DeviceIdType.MESH
F32 = jnp.float32
BF = jnp.bfloat16
EPS = 1e-5
C = 1024
HC = C // 2
TOK = 196
TP = 208
HALO = 96
GRP = 256
NEG = -1e30
VMEM_BIG = 60 * 1024 * 1024
VM = pl.BlockSpec(memory_space=pltpu.VMEM)
SM = pl.BlockSpec(memory_space=pltpu.SMEM)
HB = pl.BlockSpec(memory_space=pl.ANY)


def sds(shape, dtype):
    return jax.ShapeDtypeStruct(shape, dtype)


def params(**kw):
    return pltpu.CompilerParams(vmem_limit_bytes=VMEM_BIG, **kw)


def cost(flops, nbytes):
    return pl.CostEstimate(flops=flops, bytes_accessed=nbytes, transcendentals=0)


def dot(a, b, da=1, db=0):
    return lax.dot_general(a, b, (((da,), (db,)), ((), ())), preferred_element_type=F32)


def iota(shape, dim):
    return lax.broadcasted_iota(jnp.int32, shape, dim)


def norm_parts(values):
    centre = jnp.mean(values, axis=-1, keepdims=True)
    centred = values - centre
    spread = jnp.mean(centred * centred, axis=-1, keepdims=True)
    scale = lax.rsqrt(spread + EPS)
    return centred * scale, scale


def norm_back(values, cot):
    unit, scale = norm_parts(values)
    mean_cot = jnp.mean(cot, axis=-1, keepdims=True)
    mean_dot = jnp.mean(cot * unit, axis=-1, keepdims=True)
    return scale * (cot - mean_cot - unit * mean_dot)


def split3(values):
    high = values.astype(BF)
    rest = values - high.astype(F32)
    mid = rest.astype(BF)
    low = (rest - mid.astype(F32)).astype(BF)
    return high, mid, low


def place_of(tok, r, c):
    rho = (tok * 4682) >> 16
    gam = tok - 14 * rho
    i = rho - r
    i = jnp.where(i < 0, i + 14, i)
    j = gam - c
    j = jnp.where(j < 0, j + 14, j)
    a = jnp.where(i >= 7, 1, 0)
    b = jnp.where(j >= 7, 1, 0)
    return i, j, a, b


def pos_of(tok, r, c):
    i, j, a, b = place_of(tok, r, c)
    return (i - 7 * a) * 7 + (j - 7 * b)


def group_of(tok, r, c, last):
    i, j, a, b = place_of(tok, r, c)
    la = jnp.where(i >= 7, jnp.where(i < 14 - r, 1, 2), 0) * last
    lb = jnp.where(j >= 7, jnp.where(j < 14 - c, 1, 2), 0)
    return a * 2 + b, la * 3 + lb


def pack_rows(low, high, blocks):
    return jnp.concatenate([low.reshape(blocks, 8, HC), high.reshape(blocks, 8, HC)], axis=1).astype(BF)


def unpack_rows(packed, blocks):
    wide = packed.astype(F32)
    low = wide[:, :8, :].reshape(blocks * 8, HC)
    high = wide[:, 8:, :].reshape(blocks * 8, HC)
    return low, high


def attn_masks(r, c, last, mask, ecol, spots):
    tq, tk = iota((TP, TP), 0), iota((TP, TP), 1)
    wq_, lq = group_of(tq, r, c, last)
    wk_, lk = group_of(tk, r, c, last)
    seen = jnp.where(wq_ == wk_, jnp.where(lq == lk, 0.0, -100.0), NEG)
    mask[...] = jnp.where(tq < TOK, seen, NEG)
    row_pos = pos_of(iota((TP, GRP), 0), r, c)
    for h in range(8):
        lane = (iota((TP, GRP), 1) + (224 - 32 * h)) & 255
        spots[h] = jnp.where(lane < 192, jnp.where(row_pos == (lane & 63), 1.0, 0.0), 0.0).astype(BF)
    col_pos = pos_of(iota((192, TP), 1), r, c)
    ecol[...] = jnp.where(col_pos == (iota((192, TP), 0) & 63), 1.0, 0.0).astype(BF)


def cols(start):
    return pl.ds(pl.multiple_of(start, GRP), GRP)


def turned(values, eye):
    return dot(eye, values, 1, 1)


def unit_table():
    return jnp.where(iota((GRP, GRP), 0) == iota((GRP, GRP), 1), 1.0, 0.0).astype(BF)


def attn_group(g, normed, wqkv, wo, bias, mask, ecol, spots, qkv, probs, mixed, acc):
    n = normed[...]
    q = dot(n, wqkv[:, cols(g * GRP)]).astype(BF)
    k = dot(n, wqkv[:, cols(C + g * GRP)]).astype(BF)
    v = dot(n, wqkv[:, cols(2 * C + g * GRP)]).astype(BF)
    qkv[0, g] = q
    qkv[1, g] = k
    qkv[2, g] = v
    eye = unit_table()
    q_t = turned(q, eye).astype(BF)
    v_t = turned(v, eye).astype(BF)
    wide = dot(jnp.concatenate(split3(bias[pl.ds(g * 8, 8)][:, :, :64].reshape(8 * 64, 64)), axis=1), ecol[...])
    w_hi, w_mid, w_lo = split3(wide)
    lane_head = iota((TP, GRP), 1) >> 5
    k32 = k.astype(F32)
    outs = []
    for h in range(8):
        km = jnp.where(lane_head == h, k32, 0.0).astype(BF) + spots[h]
        part = slice(h * 64, h * 64 + 64)
        table = jnp.concatenate([w_hi[part], w_mid[part], w_lo[part], jnp.zeros((32, TP), BF)], axis=0)
        own = [q_t[32 * h:32 * h + 32]]
        if h < 7:
            own = own + [table[:224 - 32 * h]]
        if h:
            own = [table[224 - 32 * h:]] + own
        s = dot(km, jnp.concatenate(own, axis=0)) * (32.0 ** -0.5) + mask[...]
        e = jnp.exp(s - jnp.max(s, axis=0, keepdims=True))
        p = (e * (1.0 / jnp.sum(e, axis=0, keepdims=True))).astype(BF)
        probs[pl.ds(pl.multiple_of((g * 8 + h) * TP, 16), TP), :] = p
        outs.append(dot(v_t[32 * h:32 * h + 32], p))
    mixed_t = jnp.concatenate(outs, axis=0).astype(BF)
    mixed[g] = mixed_t
    acc[...] += dot(mixed_t, wo[pl.ds(pl.multiple_of(g * GRP, GRP), GRP), :], 0, 0)


def attn_group_back(g, d_att, wqkv, wo, qkv, probs, mixed, acc):
    q, k, v = qkv[0, g], qkv[1, g], qkv[2, g]
    eye = unit_table()
    d_out = dot(d_att[...], wo[pl.ds(pl.multiple_of(g * GRP, GRP), GRP), :], 1, 1).astype(BF)
    d_out_t = turned(d_out, eye)
    weighed = d_out_t * mixed[g].astype(F32)
    d_out_t = d_out_t.astype(BF)
    k_t = turned(k, eye).astype(BF)
    v32 = v.astype(F32)
    lane_head = iota((TP, GRP), 1) >> 5
    dq_t = []
    dk = jnp.zeros((TP, GRP), F32)
    dv = jnp.zeros((TP, GRP), F32)
    for h in range(8):
        mine = lane_head == h
        vm = jnp.where(mine, v32, 0.0).astype(BF)
        p = probs[pl.ds(pl.multiple_of((g * 8 + h) * TP, 16), TP), :]
        shared = jnp.sum(weighed[32 * h:32 * h + 32], axis=0, keepdims=True)
        ds = (p.astype(F32) * (dot(vm, d_out_t) - shared)).astype(BF)
        dq_t.append(dot(k_t[32 * h:32 * h + 32], ds))
        dk = jnp.where(mine, dot(ds, q), dk)
        dv = jnp.where(mine, dot(p, d_out), dv)
    scale = 32.0 ** -0.5
    dq = jnp.transpose(jnp.concatenate(dq_t, axis=0) * scale)
    acc[...] += (
        dot(dq.astype(BF), wqkv[:, cols(g * GRP)], 1, 1)
        + dot((dk * scale).astype(BF), wqkv[:, cols(C + g * GRP)], 1, 1)
        + dot(dv.astype(BF), wqkv[:, cols(2 * C + g * GRP)], 1, 1)
    )


def route(r, x, att, halo, choice, after_out, slots, table_out):
    top = jnp.where(iota((HALO, C), 0) < 14 * r, halo[...].astype(F32), att[:HALO, :].astype(F32))
    after_out[:HALO, :] = (x[:HALO, :].astype(F32) + top).astype(BF)
    after_out[HALO:, :] = (x[HALO:, :].astype(F32) + att[HALO:, :].astype(F32)).astype(BF)
    after = after_out[...].astype(F32)
    n2 = norm_parts(after)[0].astype(BF)
    tok, other = iota((TP, TP), 0), iota((TP, TP), 1)
    col = jnp.where(iota((TP, 1), 0) < TOK, choice, -1000.0)
    line = jnp.sum(jnp.where(tok == other, col, 0.0), axis=0, keepdims=True)
    same = jnp.where(col == line, 1.0, 0.0)
    same = jnp.where(other < tok, same, 0.0)
    rank = jnp.sum(same, axis=1, keepdims=True).astype(jnp.int32)
    table = jnp.where(col.astype(jnp.int32) * 8 + rank == iota((TP, 256), 1), 1.0, 0.0).astype(BF)
    table_out[...] = table
    slots[...] = pack_rows(dot(table, n2[:, :HC], 0, 0), dot(table, n2[:, HC:], 0, 0), 32)


def quad_table():
    row = iota((256, TP), 0)
    tok = iota((256, TP), 1)
    q = row >> 6
    n = row & 63
    a = (n * 9363) >> 16
    b = n - 7 * a
    want = (2 * a + (q & 1)) * 14 + 2 * b + (q >> 1)
    hit = jnp.where(want == tok, 1.0, 0.0)
    return jnp.where(n < 49, hit, 0.0).astype(BF)


def gathered(ret, table):
    low, high = unpack_rows(ret[0].astype(F32) + ret[1].astype(F32), 32)
    return jnp.concatenate([dot(table, low.astype(BF)), dot(table, high.astype(BF))], axis=1)


def merge_mid(after, ret, table_in, gate, parts, tail, mn_out, mn_tail, d_block_out, slots, spread, t_wide):
    table = table_in[...]
    block = (after[...].astype(F32) + gate * gathered(ret, table)).astype(BF)
    perm = quad_table()
    quads = dot(perm, block)
    vals = [quads[64 * q:64 * q + 49, :] for q in range(4)]
    inv = 1.0 / (4 * C)
    centre = sum(jnp.sum(v, axis=-1, keepdims=True) for v in vals) * inv
    cent = [v - centre for v in vals]
    var = sum(jnp.sum(v * v, axis=-1, keepdims=True) for v in cent) * inv
    scale = lax.rsqrt(var + EPS)
    unit = [v * scale for v in cent]
    for q in range(4):
        mn_out[:, q * C:(q + 1) * C] = unit[q][:48].astype(BF)
        for i in range(4):
            t_wide[0, 4 * q + i:4 * q + i + 1, :] = unit[q][48:49, i * 256:(i + 1) * 256]
    mn_tail[...] = t_wide[0].astype(BF)
    tails = jnp.sum(tail[...].astype(F32), axis=0)
    cots = []
    for q in range(4):
        tot = sum(part[:, q * C:(q + 1) * C].astype(F32) for part in parts)
        last = jnp.concatenate([tails[4 * q + i:4 * q + i + 1, :] for i in range(4)], axis=1)
        cots.append(jnp.concatenate([tot, last], axis=0))
    mean_cot = sum(jnp.sum(v, axis=-1, keepdims=True) for v in cots) * inv
    mean_dot = sum(jnp.sum(v * u, axis=-1, keepdims=True) for v, u in zip(cots, unit)) * inv
    spread[...] = jnp.zeros_like(spread)
    for q in range(4):
        spread[64 * q:64 * q + 49, :] = scale * (cots[q] - mean_cot - unit[q] * mean_dot)
    high, mid, low = split3(spread[...])
    d_block = dot(perm, high, 0, 0) + dot(perm, mid, 0, 0) + dot(perm, low, 0, 0)
    d_block_out[...] = d_block
    scaled = (gate * d_block).astype(BF)
    slots[...] = pack_rows(dot(table, scaled[:, :HC], 0, 0), dot(table, scaled[:, HC:], 0, 0), 32)


def after_back(after, ret, table, d_block, d_after_out, d_att_out):
    d_second = gathered(ret, table[...])
    d_after = d_block[...] + norm_back(after[...].astype(F32), d_second)
    d_after_out[...] = d_after
    d_att_out[...] = d_after.astype(BF)


def token_column(grid):
    tok = iota((TP, 14), 0)
    rho = (tok * 4682) >> 16
    place = iota((TP, 14), 1)
    pick = jnp.where(rho == place, 1.0, 0.0).astype(BF)
    high, mid, low = split3(grid[...].reshape(14, 14))
    rows = dot(pick, high) + dot(pick, mid) + dot(pick, low)
    return jnp.sum(jnp.where(tok - 14 * rho == place, rows, 0.0), axis=1, keepdims=True)


def lay_rows(tokens, wide, x):
    wide[TOK - 4:, :] = jnp.zeros((TP - TOK + 4, C), F32)
    for i in range(14):
        wide[14 * i:14 * i + 14, :] = tokens[0, i].astype(F32)
    x[...] = wide[...].astype(BF)


def expert_chunk(j, recv, part, ups, downs, flat, act_out, slope_out, ready):
    here = pl.ds(8 * j, 8)
    rows_here = pl.ds(256 * j, 256)
    low, high = unpack_rows(recv[:, here].reshape(32, 16, HC), 32)
    rows = jnp.concatenate([low, high], axis=1).astype(BF)
    flat[rows_here, :] = rows
    total = jnp.zeros((256, C), F32)
    for k in (0, 1, 3, 2):
        ready(k)
        pre = dot(rows, ups[k])
        cdf = 0.5 * (1.0 + lax.erf(pre * np.float32(2.0 ** -0.5)))
        act = (pre * cdf).astype(BF)
        slope = cdf + pre * jnp.exp(-0.5 * pre * pre) * np.float32((2.0 * np.pi) ** -0.5)
        act_out[rows_here, k * 256:(k + 1) * 256] = act
        slope_out[rows_here, k * 256:(k + 1) * 256] = slope.astype(BF)
        total = total + dot(act, downs[k])
    part[:, here] = pack_rows(total[:, :HC], total[:, HC:], 32).reshape(4, 8, 16, HC)


def expert_chunk_back(j, recv, part, ups, downs, flat, slope):
    here = pl.ds(8 * j, 8)
    rows_here = pl.ds(256 * j, 256)
    low, high = unpack_rows(recv[:, here].reshape(32, 16, HC), 32)
    rows = jnp.concatenate([low, high], axis=1).astype(BF)
    flat[rows_here, :] = rows
    total = jnp.zeros((256, C), F32)
    for k in range(4):
        span = slice(k * 256, (k + 1) * 256)
        d_pre = (slope[rows_here, span].astype(F32) * dot(rows, downs[k], 1, 1)).astype(BF)
        slope[rows_here, span] = d_pre
        total = total + dot(d_pre, ups[k], 1, 1)
    part[:, here] = pack_rows(total[:, :HC], total[:, HC:], 32).reshape(4, 8, 16, HC)


def coords():
    s = lax.axis_index("scene")
    row = lax.axis_index("row")
    z, m = row // 4, row % 4
    return s, z, m // 2, m % 2


def at(s, z, y, c):
    return (s, z * 4 + y * 2 + c)


def greet(s, z, y, c, total=64):
    barrier = pltpu.get_barrier_semaphore()
    mine = s * 4 + z

    def hail(k, carry):
        peer = (mine + k) % 32
        pl.semaphore_signal(barrier, inc=1, device_id=at(peer // 4, peer % 4, y, c), device_id_type=MESH)
        pl.semaphore_signal(barrier, inc=1, device_id=at(peer // 4, peer % 4, 1 - y, c), device_id_type=MESH)
        return carry

    lax.fori_loop(1, 32, hail, 0)
    pl.semaphore_signal(barrier, inc=1, device_id=at(s, z, 1 - y, c), device_id_type=MESH)
    pl.semaphore_signal(barrier, inc=1, device_id=at(s, z, y, 1 - c), device_id_type=MESH)
    pl.semaphore_wait(barrier, total)


def greet_all(place):
    s, z, y, c = place
    barrier = pltpu.get_barrier_semaphore()
    row = z * 4 + y * 2 + c
    pl.semaphore_signal(barrier, inc=1, device_id=(s, (row + 1) % 16), device_id_type=MESH)
    pl.semaphore_signal(barrier, inc=1, device_id=(s, (row + 15) % 16), device_id_type=MESH)
    greet(s, z, y, c, 66)


def remote(src, dst, send, recv, device):
    return pltpu.make_async_remote_copy(
        src_ref=src, dst_ref=dst, send_sem=send, recv_sem=recv, device_id=device, device_id_type=MESH
    )


def await_bytes(ref, sem):
    pltpu.make_async_copy(ref, ref, sem).wait()


SLOT_SEMS = [
    pltpu.SemaphoreType.DMA,
    pltpu.SemaphoreType.DMA((2, 4)),
    pltpu.SemaphoreType.DMA((2, 4)),
    pltpu.SemaphoreType.DMA((2, 4)),
    pltpu.SemaphoreType.DMA((2, 4)),
    pltpu.SemaphoreType.DMA((2, 4)),
    pltpu.SemaphoreType.DMA,
    pltpu.SemaphoreType.DMA,
]


def slots_through(place, slots, recv, part, other, total, ret, sems, compute, meanwhile=None):
    s, z, y, c = place
    mine = s * 4 + z
    yh, xx = s // 4, s % 4

    def steps(k):
        dx = k % 4
        return (k % 8) // 4, dx, (k // 8 + 4 - dx) % 4

    def ahead(k):
        dy, dx, dz = steps(k)
        return ((yh + dy) % 2 * 4 + (xx + dx) % 4) * 4 + (z + dz) % 4

    def behind(k):
        dy, dx, dz = steps(k)
        return ((yh + dy) % 2 * 4 + (xx + 4 - dx) % 4) * 4 + (z + 4 - dz) % 4

    send, arrive, f_send, f_recv, p_send, p_recv, r_send, r_recv = sems
    pair = at(s, z, y, 1 - c)

    def to_peer(k, peer, yy):
        remote(slots.at[peer], recv.at[y * 2 + c, k], send, arrive.at[y, k // 8], at(peer // 4, peer % 4, yy, c)).start()

    def push(k, carry):
        peer = ahead(k)
        to_peer(k, peer, y)
        to_peer(k, peer, 1 - y)
        return carry

    pltpu.make_async_copy(slots.at[mine], recv.at[y * 2 + c, 0], arrive.at[y, 0]).start()
    to_peer(0, mine, 1 - y)
    lax.fori_loop(1, 32, push, 0)
    forwards, partials = {}, {}

    def forward(j):
        for yy in range(2):
            block = recv.at[yy * 2 + c, pl.ds(8 * j, 8)]
            await_bytes(block, arrive.at[yy, j])
            forwards[yy, j] = remote(block, block, f_send.at[yy, j], f_recv.at[yy, j], pair)
            forwards[yy, j].start()

    def work(j):
        for yy in range(2):
            forwards[yy, j].wait_recv()
        compute(j)
        for yy in range(2):
            here = pl.ds(8 * j, 8)
            partials[yy, j] = remote(
                part.at[yy * 2 + (1 - c), here], other.at[yy, here], p_send.at[yy, j], p_recv.at[yy, j], pair
            )
            partials[yy, j].start()

    def give(k, yy):
        peer = behind(k)
        remote(total.at[yy, k], ret.at[y, mine], r_send, r_recv, at(peer // 4, peer % 4, yy, c)).start()

    def give_both(k, carry):
        give(k, 1 - y)
        give(k, y)
        return carry

    def back(j):
        here = pl.ds(8 * j, 8)
        for yy in range(2):
            partials[yy, j].wait_recv()
            total[yy, here] = (part[yy * 2 + c, here].astype(F32) + other[yy, here].astype(F32)).astype(BF)
        if j == 0:
            give(0, 1 - y)
            pltpu.make_async_copy(total.at[y, 0], ret.at[y, mine], r_recv).start()
        lax.fori_loop(max(1, 8 * j), 8 * j + 8, give_both, 0)

    forward(0)
    forward(1)
    work(0)
    forward(2)
    work(1)
    back(0)
    forward(3)
    work(2)
    back(1)
    work(3)
    back(2)
    back(3)

    def finish_sends():
        for copy in list(forwards.values()) + list(partials.values()):
            copy.wait_send()
        for sem in (send, r_send):
            await_bytes(total.at[0], sem)
            await_bytes(total.at[0, pl.ds(0, 31)], sem)

    if meanwhile is not None:
        meanwhile()
    await_bytes(ret, r_recv)
    return finish_sends


def front(
    shift, tokens, choice_in, gate_in, position_bias, pairs, merged_grad, qkv_weight, out_weight, expert_up, expert_down, reduce_weight,
    after, table, merge_norm, mn_tail, d_block, d_slots, qkv_out, probs_out, mixed_out, flat_out, act_out, slope_out, up_out, down_out,
    x, x_wide, bias, table_of, grad_wide, halo, halo2, normed, mask, ecol, spots, acc, att, wqkv, wo, wred, qkv, probs, mixed,
    d_send, d_relay, d_direct, d_summed, d_across, t_wide, t_send, t_recv, ups, downs, relay_up, relay_down,
    slots, recv, part, other, total, ret, flat, act, slope, spread,
    io_sem, halo_sem, w_send, w_recv, d_sem, *slot_sems,
):
    place = coords()
    s, z, y, c = place
    row = z * 4 + y * 2 + c
    r, cc = shift[0], shift[1]
    last = jnp.where(row == 15, 1, 0)
    ins = [
        pltpu.make_async_copy(reduce_weight, wred, io_sem.at[0]),
        pltpu.make_async_copy(qkv_weight, wqkv, io_sem.at[1]),
        pltpu.make_async_copy(out_weight, wo, io_sem.at[2]),
        pltpu.make_async_copy(expert_up.at[z], ups.at[0], io_sem.at[3]),
        pltpu.make_async_copy(expert_down.at[z], downs.at[0], io_sem.at[4]),
        pltpu.make_async_copy(pairs, table_of, io_sem.at[14]),
    ]
    for copy in ins:
        copy.start()
    lay_rows(tokens, x_wide, x)
    greet_all(place)

    nxt = (s, (row + 1) % 16)
    prv = (s, (row + 15) % 16)
    z_up, z_down = at(s, (z + 1) % 4, y, c), at(s, (z + 3) % 4, y, c)
    halo_copy = remote(x.at[pl.ds(0, HALO)], halo, halo_sem.at[0], halo_sem.at[1], prv)
    halo_copy.start()
    weights = [
        remote(expert_up.at[(z + 2) % 4], relay_up, w_send.at[0], w_recv.at[0], z_up),
        remote(expert_down.at[(z + 2) % 4], relay_down, w_send.at[1], w_recv.at[1], z_down),
        remote(expert_up.at[(z + 1) % 4], ups.at[1], w_send.at[2], w_recv.at[2], z_up),
        remote(expert_up.at[(z + 3) % 4], ups.at[3], w_send.at[3], w_recv.at[3], z_down),
        remote(expert_down.at[(z + 1) % 4], downs.at[1], w_send.at[4], w_recv.at[4], z_up),
        remote(expert_down.at[(z + 3) % 4], downs.at[3], w_send.at[5], w_recv.at[5], z_down),
    ]
    for copy in weights:
        copy.start()
    relayed = [
        remote(relay_up, ups.at[2], w_send.at[6], w_recv.at[6], z_up),
        remote(relay_down, downs.at[2], w_send.at[7], w_recv.at[7], z_down),
    ]

    by_place = merged_grad[...].astype(F32).reshape(49, 8, 256)
    for n in range(8):
        grad_wide[n] = by_place[:, n, :]
    grad48 = grad_wide[:, :48, :].astype(BF).reshape(8 * 48, 256)
    grad_tail = jnp.concatenate([grad_wide[:, 48, :], jnp.zeros((8, 256), F32)], axis=0).astype(BF)
    ins[0].wait()
    for half in range(4):
        span = pl.ds(half * C, C)
        d_send[:, :, span] = dot(grad48, wred[span, :], 1, 1).astype(BF).reshape(8, 48, C)
        tail = dot(grad_tail, wred[span, :], 1, 1)
        for i in range(4):
            t_wide[:, 4 * half + i, :] = tail[:8, i * 256:(i + 1) * 256]
    t_send[...] = t_wide[...].astype(BF)
    yh, xx = s // 4, s % 4
    x_up, x_down, x_far = (xx + 1) % 4, (xx + 3) % 4, (xx + 2) % 4
    to_up, to_down = at(yh * 4 + x_up, z, y, c), at(yh * 4 + x_down, z, y, c)
    first = [
        remote(d_send.at[x_far], d_relay.at[0], d_sem.at[0, 0], d_sem.at[1, 0], to_up),
        remote(d_send.at[4 + x_far], d_relay.at[1], d_sem.at[0, 1], d_sem.at[1, 1], to_down),
        remote(d_send.at[4 + x_up], d_direct.at[1], d_sem.at[0, 2], d_sem.at[1, 2], to_up),
        remote(d_send.at[x_down], d_direct.at[0], d_sem.at[0, 3], d_sem.at[1, 3], to_down),
    ]
    second = [
        remote(d_send.at[x_up], d_summed.at[0], d_sem.at[0, 4], d_sem.at[1, 4], to_up),
        remote(d_send.at[4 + x_down], d_summed.at[1], d_sem.at[0, 5], d_sem.at[1, 5], to_down),
    ]
    other_yh = 1 - yh
    across = remote(
        d_send.at[other_yh * 4 + xx], d_across, d_sem.at[0, 6], d_sem.at[1, 6], at(other_yh * 4 + xx, z, y, c)
    )
    gifts = []
    for k in range(1, 8):
        peer = (s + k) % 8
        gifts.append(remote(t_send.at[peer], t_recv.at[s], d_sem.at[2, k], d_sem.at[3, k], at(peer, z, y, c)))
    for copy in first + gifts:
        copy.start()
    own = pltpu.make_async_copy(t_send.at[s], t_recv.at[s], io_sem.at[6])
    own.start()

    def pass_on():
        for i, mine_at in enumerate((x_up, 4 + x_down)):
            first[i].wait_recv()
            d_send[mine_at] = (d_send[mine_at].astype(F32) + d_relay[i].astype(F32)).astype(BF)
            second[i].start()

    def cross():
        for copy in first[2:] + second:
            copy.wait_recv()
        there = other_yh * 4 + xx
        d_send[there] = (
            d_send[there].astype(F32) + d_direct[other_yh].astype(F32) + d_summed[other_yh].astype(F32)
        ).astype(BF)
        across.start()

    attn_masks(r, cc, last, mask, ecol, spots)
    ins[5].wait()
    bias[...] = jnp.zeros_like(bias)
    parts3 = jnp.concatenate(split3(position_bias[...]), axis=0)
    for pair in range(25):
        wide = dot(parts3, table_of[:, pair * 256:(pair + 1) * 256])
        wide = wide[:32] + wide[32:64] + wide[64:]
        for i in range(2):
            if 2 * pair + i < 49:
                bias[:, 2 * pair + i, :] = wide[:, i * 128:(i + 1) * 128] * np.float32(32.0 ** 0.5)
    normed[HALO:, :] = norm_parts(x[HALO:, :].astype(F32))[0].astype(BF)
    acc[...] = jnp.zeros_like(acc)
    halo_copy.wait_recv()
    top = jnp.where(iota((HALO, C), 0) < 14 * r, halo[...].astype(F32), x[:HALO, :].astype(F32))
    normed[:HALO, :] = norm_parts(top)[0].astype(BF)
    ins[1].wait()
    ins[2].wait()

    def group(g, carry):
        attn_group(g, normed, wqkv, wo, bias, mask, ecol, spots, qkv, probs, mixed, acc)
        return carry

    lax.fori_loop(0, 1, group, 0)
    pass_on()
    lax.fori_loop(1, 3, group, 0)
    for arrived, onward in zip(weights, relayed):
        arrived.wait_recv()
        onward.start()
    lax.fori_loop(3, 4, group, 0)
    att[...] = acc[...].astype(BF)
    halo2_copy = remote(att.at[pl.ds(0, HALO)], halo2, halo_sem.at[2], halo_sem.at[3], nxt)
    halo2_copy.start()
    outs = [
        pltpu.make_async_copy(qkv, qkv_out, io_sem.at[7]),
        pltpu.make_async_copy(probs, probs_out, io_sem.at[8]),
        pltpu.make_async_copy(mixed, mixed_out, io_sem.at[15]),
    ]
    for copy in outs:
        copy.start()
    cross()
    halo2_copy.wait_recv()
    choice = token_column(choice_in[...].astype(F32))
    route(r, x, att, halo2, choice, after, slots, table)

    def ready(k):
        pieces = {0: (), 1: (weights[2], weights[4]), 3: (weights[3], weights[5]), 2: relayed}[k]
        for copy in pieces:
            copy.wait_recv()
        if k == 0:
            ins[3].wait()
            ins[4].wait()

    def compute(j):
        expert_chunk(j, recv, part, ups, downs, flat, act, slope, ready if j == 0 else lambda k: None)

    finish_sends = slots_through(place, slots, recv, part, other, total, ret, slot_sems, compute)
    more = [
        pltpu.make_async_copy(flat, flat_out, io_sem.at[9]),
        pltpu.make_async_copy(act, act_out, io_sem.at[10]),
        pltpu.make_async_copy(slope, slope_out, io_sem.at[11]),
        pltpu.make_async_copy(ups, up_out, io_sem.at[12]),
        pltpu.make_async_copy(downs, down_out, io_sem.at[13]),
    ]
    for copy in more:
        copy.start()
    for copy in gifts + [across]:
        copy.wait_recv()
    own.wait()
    parts = (d_send.at[s], d_direct.at[yh], d_summed.at[yh], d_across)
    merge_mid(after, ret, table, token_column(gate_in), parts, t_recv, merge_norm, mn_tail, d_block, d_slots, spread, t_wide)
    for copy in outs + more:
        copy.wait()
    finish_sends()
    for copy in weights + relayed + gifts + first + second + [across, halo_copy, halo2_copy]:
        copy.wait_send()


def back(
    shift, tokens, after, table, merge_norm, mn_tail, d_block, d_slots,
    qkv_weight, out_weight, reduce_weight, qkv_in, probs_in, mixed_in, flat_in, act_in, slope_in, up_in, down_in,
    tokens_grad, merged, up_grad, down_grad,
    x, x_wide, halo, halo2, d_att, acc, d_after, d_shift, wqkv, wo, wred, qkv, probs, mixed, flat, act, slope, ups, downs,
    recv, part, other, total, ret, flat_d, send_up, send_down, relay_up, relay_down,
    mn_all, mt_all, merged_wide, merged_rows,
    io_sem, halo_sem, g_send, g_recv, m_sem, *slot_sems,
):
    place = coords()
    s, z, y, c = place
    row = z * 4 + y * 2 + c
    r = shift[0]
    loads = [
        (down_in, downs), (slope_in, slope), (up_in, ups), (act_in, act), (flat_in, flat),
        (out_weight, wo), (qkv_in, qkv), (probs_in, probs), (qkv_weight, wqkv), (reduce_weight, wred), (mixed_in, mixed),
    ]
    ins = [pltpu.make_async_copy(a, b, io_sem.at[i]) for i, (a, b) in enumerate(loads)]
    for copy in ins:
        copy.start()
    greet_all(place)
    nxt = (s, (row + 1) % 16)
    prv = (s, (row + 15) % 16)
    z_up, z_down = at(s, (z + 1) % 4, y, c), at(s, (z + 3) % 4, y, c)

    def compute(j):
        if j == 0:
            for copy in ins[:3]:
                copy.wait()
        expert_chunk_back(j, recv, part, ups, downs, flat_d, slope)

    returns = [
        remote(send_up.at[1], relay_up, g_send.at[0], g_recv.at[0], z_up),
        remote(send_down.at[1], relay_down, g_send.at[1], g_recv.at[1], z_down),
        remote(send_up.at[0], up_grad.at[z], g_send.at[2], g_recv.at[2], z_down),
        remote(send_down.at[0], down_grad.at[z], g_send.at[3], g_recv.at[3], z_down),
        remote(send_up.at[2], up_grad.at[z], g_send.at[4], g_recv.at[4], z_up),
        remote(send_down.at[2], down_grad.at[z], g_send.at[5], g_recv.at[5], z_up),
    ]
    relayed = [
        remote(relay_up, up_grad.at[(z + 3) % 4], g_send.at[6], g_recv.at[6], z_up),
        remote(relay_down, down_grad.at[(z + 1) % 4], g_send.at[7], g_recv.at[7], z_down),
    ]
    yh, xx = s // 4, s % 4
    x_up, x_down = (xx + 1) % 4, (xx + 3) % 4
    to_up, to_down = at(yh * 4 + x_up, z, y, c), at(yh * 4 + x_down, z, y, c)
    across = (1 - yh) * 4 + xx
    half = (pl.ds(0, 2 * C), pl.ds(2 * C, 2 * C))

    def neighbours(source, slot, n):
        return [
            remote(source, mn_all.at[slot], m_sem.at[0, n], m_sem.at[1, n], to_up),
            remote(source, mn_all.at[slot], m_sem.at[0, n + 1], m_sem.at[1, n + 1], to_down),
        ]

    def halves(base, n):
        below, above = base * 4 + x_down, base * 4 + x_up
        low, high = mn_all.at[below, :, half[0]], mn_all.at[above, :, half[1]]
        return [
            remote(low, low, m_sem.at[0, n], m_sem.at[1, n], to_up),
            remote(high, high, m_sem.at[0, n + 1], m_sem.at[1, n + 1], to_down),
        ]

    spread_own = neighbours(merge_norm, s, 0)
    spread_across = neighbours(mn_all.at[across], across, 2)
    far_own = halves(yh, 4)
    far_across = halves(1 - yh, 6)
    partner = remote(merge_norm, mn_all.at[s], m_sem.at[0, 8], m_sem.at[1, 8], at(across, z, y, c))
    tail_copies = []
    for k in range(1, 8):
        peer = (s + k) % 8
        tail_copies.append(remote(mn_tail, mt_all.at[s], m_sem.at[2, k], m_sem.at[3, k], at(peer, z, y, c)))
    gifts = spread_own + spread_across + far_own + far_across + [partner] + tail_copies
    own = [
        pltpu.make_async_copy(merge_norm, mn_all.at[s], io_sem.at[14]),
        pltpu.make_async_copy(mn_tail, mt_all.at[s], io_sem.at[11]),
    ]
    own_out = [
        pltpu.make_async_copy(send_up.at[3], up_grad.at[z], io_sem.at[12]),
        pltpu.make_async_copy(send_down.at[3], down_grad.at[z], io_sem.at[13]),
    ]

    def grads():
        for copy in ins[3:5]:
            copy.wait()
        for k in (2, 1, 3, 0):
            span = slice(k * 256, (k + 1) * 256)
            up_part = dot(flat[...], slope[:, span], 0, 0)
            down_part = dot(act[:, span], flat_d[...], 0, 0)
            send_up[(k + 3) % 4] = up_part.astype(BF)
            send_down[(k + 3) % 4] = down_part.astype(BF)
            if k:
                first = {2: 0, 1: 2, 3: 4}[k]
                returns[first].start()
                returns[first + 1].start()
            else:
                for copy in own_out:
                    copy.start()

    finish_sends = slots_through(place, d_slots, recv, part, other, total, ret, slot_sems, compute, grads)
    for copy in spread_own + [partner] + tail_copies + own:
        copy.start()
    after_back(after, ret, table, d_block, d_after, d_att)
    halo_copy = remote(d_att.at[pl.ds(0, HALO)], halo, halo_sem.at[0], halo_sem.at[1], prv)
    halo_copy.start()
    lay_rows(tokens, x_wide, x)
    acc[...] = jnp.zeros_like(acc)
    for copy in ins[5:9] + ins[10:]:
        copy.wait()
    halo_copy.wait_recv()
    halo_copy.wait_send()
    top = jnp.where(iota((HALO, C), 0) < 14 * r, halo[...].astype(F32), d_att[:HALO, :].astype(F32))
    d_att[:HALO, :] = top.astype(BF)

    def group(g, carry):
        attn_group_back(g, d_att, wqkv, wo, qkv, probs, mixed, acc)
        return carry

    lax.fori_loop(0, 1, group, 0)
    for arrived, onward in zip(spread_own, far_own):
        arrived.wait_recv()
        onward.start()
    lax.fori_loop(1, 2, group, 0)
    partner.wait_recv()
    for onward in spread_across:
        onward.start()
    lax.fori_loop(2, 3, group, 0)
    for arrived, onward in zip(returns, relayed):
        arrived.wait_recv()
        onward.start()
    lax.fori_loop(3, 4, group, 0)
    d_shift[...] = acc[...].astype(BF)
    halo2_copy = remote(d_shift.at[pl.ds(0, HALO)], halo2, halo_sem.at[2], halo_sem.at[3], nxt)
    halo2_copy.start()

    for arrived, onward in zip(spread_across, far_across):
        arrived.wait_recv()
        onward.start()
    halo2_copy.wait_recv()
    top = jnp.where(iota((HALO, C), 0) < 14 * r, halo2[...].astype(F32), d_shift[:HALO, :].astype(F32))
    x_wide[:HALO, :] = d_after[:HALO, :] + norm_back(x[:HALO, :].astype(F32), top)
    x_wide[HALO:, :] = d_after[HALO:, :] + norm_back(x[HALO:, :].astype(F32), d_shift[HALO:, :].astype(F32))
    for i in range(14):
        tokens_grad[0, i] = x_wide[14 * i:14 * i + 14, :].astype(BF)

    for copy in far_own + far_across + tail_copies:
        copy.wait_recv()
    for copy in own + [ins[9]]:
        copy.wait()
    merged_wide[:, :48, :] = dot(mn_all[...].reshape(8 * 48, 4 * C), wred[...]).reshape(8, 48, 256)
    tails = mt_all[...].astype(F32)
    last = jnp.concatenate([tails[:, i, :] for i in range(16)], axis=1)
    last = jnp.concatenate([last, jnp.zeros_like(last)], axis=0).astype(BF)
    merged_wide[:, 48, :] = dot(last, wred[...])[:8]
    for n in range(8):
        merged_rows[:, n, :] = merged_wide[n]
    merged[...] = merged_rows[...].reshape(7, 7, 8, 256).astype(BF)

    for copy in returns[2:] + relayed:
        copy.wait_recv()
    for copy in own_out:
        copy.wait()
    finish_sends()
    for copy in returns + relayed + gifts + [halo2_copy]:
        copy.wait_send()


def widen(up_in, down_in, grad_in, merged_in, up_out, down_out, grad_out, merged_out):
    up_out[...] = up_in[...].astype(F32)
    down_out[...] = down_in[...].astype(F32)

    @pl.when(pl.program_id(0) == 0)
    def _():
        grad_out[...] = grad_in[...]
        merged_out[...] = merged_in[...]


def bias_pairs():
    spot = np.arange(49)
    py, px = spot // 7, spot % 7
    relative = (py[:, None] - py[None, :] + 6) * 13 + (px[:, None] - px[None, :] + 6)
    table = np.zeros((169, 50, 128), np.float32)
    a, b = np.meshgrid(spot, spot, indexing="ij")
    table[relative.reshape(-1), b.reshape(-1), a.reshape(-1)] = 1.0
    return table.reshape(169, 6400)


def local(
    tokens,
    qkv_weight,
    out_weight,
    position_bias,
    window_shift,
    expert_up,
    expert_down,
    expert_choice,
    combine_weight,
    reduce_weight,
    merged_grad,
):
    choice = jnp.transpose(expert_choice, (1, 0, 3, 2)).reshape(14, 1, 14)
    gate = jnp.transpose(combine_weight, (1, 0, 2))
    pairs = jnp.asarray(bias_pairs(), dtype=BF)
    V = pltpu.VMEM
    D = pltpu.SemaphoreType.DMA

    after, table, merge_norm, mn_tail, d_block, d_slots, qkv, probs, mixed, flat_in, act, slope, ups, downs = pl.pallas_call(
        front,
        out_shape=[
            sds((TP, C), BF), sds((TP, 256), BF), sds((48, 4 * C), BF), sds((16, 256), BF), sds((TP, C), F32),
            sds((32, 16, HC), BF), sds((3, 4, TP, GRP), BF), sds((32 * TP, TP), BF), sds((4, GRP, TP), BF), sds((C, C), BF), sds((C, C), BF),
            sds((C, C), BF), sds((4, C, 256), BF), sds((4, 256, C), BF),
        ],
        in_specs=[SM, VM, VM, VM, VM, HB, VM] + [HB] * 5,
        out_specs=[VM] * 6 + [HB] * 8,
        scratch_shapes=[
            V((TP, C), BF), V((TP, C), F32), V((32, 64, 128), F32), V((169, 6400), BF), V((8, 49, 256), F32),
            V((HALO, C), BF), V((HALO, C), BF), V((TP, C), BF), V((TP, TP), F32),
            V((192, TP), BF), V((8, TP, GRP), BF), V((TP, C), F32), V((TP, C), BF),
            V((C, 3 * C), BF), V((C, C), BF), V((4 * C, 256), BF),
            V((3, 4, TP, GRP), BF), V((32 * TP, TP), BF), V((4, GRP, TP), BF),
            V((8, 48, 4 * C), BF), V((2, 48, 4 * C), BF), V((2, 48, 4 * C), BF), V((2, 48, 4 * C), BF),
            V((48, 4 * C), BF), V((8, 16, 256), F32),
            V((8, 16, 256), BF), V((8, 16, 256), BF),
            V((4, C, 256), BF), V((4, 256, C), BF), V((C, 256), BF), V((256, C), BF),
            V((32, 16, HC), BF), V((4, 32, 16, HC), BF), V((4, 32, 16, HC), BF),
            V((2, 32, 16, HC), BF), V((2, 32, 16, HC), BF), V((2, 32, 16, HC), BF),
            V((C, C), BF), V((C, C), BF), V((C, C), BF), V((256, C), F32),
            D((16,)), D((4,)), D((8,)), D((8,)), D((4, 8)), *SLOT_SEMS,
        ],
        compiler_params=params(collective_id=0, has_side_effects=True),
        cost_estimate=cost(12 << 30, 60 << 20),
        name="front",
    )(window_shift, tokens, choice, gate, position_bias, pairs, jnp.transpose(merged_grad, (1, 2, 0, 3)), qkv_weight, out_weight,
      expert_up, expert_down, reduce_weight)

    tokens_grad, merged, up_grad, down_grad = pl.pallas_call(
        back,
        out_shape=[
            sds(tokens.shape, BF), sds((7, 7, 8, 256), BF), sds((4, C, 256), BF), sds((4, 256, C), BF),
        ],
        in_specs=[SM] + [VM] * 7 + [HB] * 11,
        out_specs=[VM] * 2 + [HB] * 2,
        scratch_shapes=[
            V((TP, C), BF), V((TP, C), F32), V((HALO, C), BF), V((HALO, C), BF), V((TP, C), BF), V((TP, C), F32),
            V((TP, C), F32), V((TP, C), BF), V((C, 3 * C), BF), V((C, C), BF), V((4 * C, 256), BF),
            V((3, 4, TP, GRP), BF), V((32 * TP, TP), BF), V((4, GRP, TP), BF), V((C, C), BF), V((C, C), BF), V((C, C), BF),
            V((4, C, 256), BF), V((4, 256, C), BF),
            V((4, 32, 16, HC), BF), V((4, 32, 16, HC), BF), V((2, 32, 16, HC), BF), V((2, 32, 16, HC), BF),
            V((2, 32, 16, HC), BF), V((C, C), BF), V((4, C, 256), BF), V((4, 256, C), BF), V((C, 256), BF), V((256, C), BF),
            V((8, 48, 4 * C), BF), V((8, 16, 256), BF), V((8, 49, 256), F32), V((49, 8, 256), F32),
            D((20,)), D((4,)), D((8,)), D((8,)), D((4, 9)), *SLOT_SEMS,
        ],
        compiler_params=pltpu.CompilerParams(
            vmem_limit_bytes=60 * 1024 * 1024, collective_id=1, has_side_effects=True
        ),
        cost_estimate=cost(16 << 30, 60 << 20),
        name="back",
    )(window_shift, tokens, after, table, merge_norm, mn_tail, d_block, d_slots, qkv_weight, out_weight, reduce_weight,
      qkv, probs, mixed, flat_in, act, slope, ups, downs)
    whole = lambda shape: pl.BlockSpec(shape, lambda e: (0,) * len(shape))
    blocks = [
        pl.BlockSpec((1, C, 256), lambda e: (e, 0, 0)), pl.BlockSpec((1, 256, C), lambda e: (e, 0, 0)),
        whole(tokens_grad.shape), whole(merged.shape),
    ]
    up_grad, down_grad, tokens_grad, merged = pl.pallas_call(
        widen,
        grid=(4,),
        out_shape=[
            sds((4, C, 256), F32), sds((4, 256, C), F32), sds(tokens_grad.shape, BF), sds(merged.shape, BF),
        ],
        in_specs=blocks,
        out_specs=blocks,
        compiler_params=params(),
        cost_estimate=cost(0, 14 << 20),
        name="widen",
    )(up_grad, down_grad, tokens_grad, merged)
    return (jnp.transpose(merged, (2, 0, 1, 3)), tokens_grad, up_grad, down_grad)


def solution(mesh):
    placed = (
        P("scene", "row", None, None),
        P(),
        P(),
        P(),
        P(),
        P("scene", None, "row"),
        P("scene", "row", None),
        P("scene", "row", None, None),
        P("scene", "row", None),
        P(None, "scene"),
        P(None, "row", None, "scene"),
    )
    return jax.shard_map(
        local,
        mesh=mesh,
        in_specs=placed,
        out_specs=(
            P(None, "row", None, "scene"),
            P("scene", "row", None, None),
            P("scene", None, "row"),
            P("scene", "row", None),
        ),
        check_vma=False,
    )
```

```python
import functools

import jax
import jax.numpy as jnp
import numpy as np
from jax import lax
from jax.experimental import pallas as pl
from jax.experimental.pallas import tpu as pltpu
from jax.sharding import PartitionSpec as P

MESH = pl.DeviceIdType.MESH
F32 = jnp.float32
BF = jnp.bfloat16
EPS = 1e-5
C = 1024
HC = C // 2
TOK = 196
TP = 208
HALO = 96
GRP = 256
NEG = -1e30
VMEM_BIG = 60 * 1024 * 1024
VM = pl.BlockSpec(memory_space=pltpu.VMEM)
SM = pl.BlockSpec(memory_space=pltpu.SMEM)
HB = pl.BlockSpec(memory_space=pl.ANY)


def sds(shape, dtype):
    return jax.ShapeDtypeStruct(shape, dtype)


def params(**kw):
    return pltpu.CompilerParams(vmem_limit_bytes=VMEM_BIG, **kw)


def cost(flops, nbytes):
    return pl.CostEstimate(flops=flops, bytes_accessed=nbytes, transcendentals=0)


def dot(a, b, da=1, db=0):
    return lax.dot_general(a, b, (((da,), (db,)), ((), ())), preferred_element_type=F32)


def iota(shape, dim):
    return lax.broadcasted_iota(jnp.int32, shape, dim)


def norm_parts(values):
    centre = jnp.mean(values, axis=-1, keepdims=True)
    centred = values - centre
    spread = jnp.mean(centred * centred, axis=-1, keepdims=True)
    scale = lax.rsqrt(spread + EPS)
    return centred * scale, scale


def norm_back(values, cot):
    unit, scale = norm_parts(values)
    mean_cot = jnp.mean(cot, axis=-1, keepdims=True)
    mean_dot = jnp.mean(cot * unit, axis=-1, keepdims=True)
    return scale * (cot - mean_cot - unit * mean_dot)


def split3(values):
    high = values.astype(BF)
    rest = values - high.astype(F32)
    mid = rest.astype(BF)
    low = (rest - mid.astype(F32)).astype(BF)
    return high, mid, low


def place_of(tok, r, c):
    rho = (tok * 4682) >> 16
    gam = tok - 14 * rho
    i = rho - r
    i = jnp.where(i < 0, i + 14, i)
    j = gam - c
    j = jnp.where(j < 0, j + 14, j)
    a = jnp.where(i >= 7, 1, 0)
    b = jnp.where(j >= 7, 1, 0)
    return i, j, a, b


def pos_of(tok, r, c):
    i, j, a, b = place_of(tok, r, c)
    return (i - 7 * a) * 7 + (j - 7 * b)


def group_of(tok, r, c, last):
    i, j, a, b = place_of(tok, r, c)
    la = jnp.where(i >= 7, jnp.where(i < 14 - r, 1, 2), 0) * last
    lb = jnp.where(j >= 7, jnp.where(j < 14 - c, 1, 2), 0)
    return a * 2 + b, la * 3 + lb


def pack_rows(low, high, blocks):
    return jnp.concatenate([low.reshape(blocks, 8, HC), high.reshape(blocks, 8, HC)], axis=1).astype(BF)


def unpack_rows(packed, blocks):
    wide = packed.astype(F32)
    low = wide[:, :8, :].reshape(blocks * 8, HC)
    high = wide[:, 8:, :].reshape(blocks * 8, HC)
    return low, high


def attn_masks(r, c, last, mask, ecol, spots):
    tq, tk = iota((TP, TP), 0), iota((TP, TP), 1)
    wq_, lq = group_of(tq, r, c, last)
    wk_, lk = group_of(tk, r, c, last)
    seen = jnp.where(wq_ == wk_, jnp.where(lq == lk, 0.0, -100.0), NEG)
    mask[...] = jnp.where(tq < TOK, seen, NEG)
    row_pos = pos_of(iota((TP, GRP), 0), r, c)
    for h in range(8):
        lane = (iota((TP, GRP), 1) + (224 - 32 * h)) & 255
        spots[h] = jnp.where(lane < 192, jnp.where(row_pos == (lane & 63), 1.0, 0.0), 0.0).astype(BF)
    col_pos = pos_of(iota((192, TP), 1), r, c)
    ecol[...] = jnp.where(col_pos == (iota((192, TP), 0) & 63), 1.0, 0.0).astype(BF)


def cols(start):
    return pl.ds(pl.multiple_of(start, GRP), GRP)


def turned(values, eye):
    return dot(eye, values, 1, 1)


def unit_table():
    return jnp.where(iota((GRP, GRP), 0) == iota((GRP, GRP), 1), 1.0, 0.0).astype(BF)


def attn_group(g, normed, wqkv, wo, bias, mask, ecol, spots, qkv, probs, mixed, acc):
    n = normed[...]
    q = dot(n, wqkv[:, cols(g * GRP)]).astype(BF)
    k = dot(n, wqkv[:, cols(C + g * GRP)]).astype(BF)
    v = dot(n, wqkv[:, cols(2 * C + g * GRP)]).astype(BF)
    qkv[0, g] = q
    qkv[1, g] = k
    qkv[2, g] = v
    eye = unit_table()
    q_t = turned(q, eye).astype(BF)
    v_t = turned(v, eye).astype(BF)
    wide = dot(jnp.concatenate(split3(bias[pl.ds(g * 8, 8)][:, :, :64].reshape(8 * 64, 64)), axis=1), ecol[...])
    w_hi, w_mid, w_lo = split3(wide)
    lane_head = iota((TP, GRP), 1) >> 5
    k32 = k.astype(F32)
    outs = []
    for h in range(8):
        km = jnp.where(lane_head == h, k32, 0.0).astype(BF) + spots[h]
        part = slice(h * 64, h * 64 + 64)
        table = jnp.concatenate([w_hi[part], w_mid[part], w_lo[part], jnp.zeros((32, TP), BF)], axis=0)
        own = [q_t[32 * h:32 * h + 32]]
        if h < 7:
            own = own + [table[:224 - 32 * h]]
        if h:
            own = [table[224 - 32 * h:]] + own
        s = dot(km, jnp.concatenate(own, axis=0)) * (32.0 ** -0.5) + mask[...]
        e = jnp.exp(s - jnp.max(s, axis=0, keepdims=True))
        p = (e * (1.0 / jnp.sum(e, axis=0, keepdims=True))).astype(BF)
        probs[pl.ds(pl.multiple_of((g * 8 + h) * TP, 16), TP), :] = p
        outs.append(dot(v_t[32 * h:32 * h + 32], p))
    mixed_t = jnp.concatenate(outs, axis=0).astype(BF)
    mixed[g] = mixed_t
    acc[...] += dot(mixed_t, wo[pl.ds(pl.multiple_of(g * GRP, GRP), GRP), :], 0, 0)


def attn_group_back(g, d_att, wqkv, wo, qkv, probs, mixed, acc):
    q, k, v = qkv[0, g], qkv[1, g], qkv[2, g]
    eye = unit_table()
    d_out = dot(d_att[...], wo[pl.ds(pl.multiple_of(g * GRP, GRP), GRP), :], 1, 1).astype(BF)
    d_out_t = turned(d_out, eye)
    weighed = d_out_t * mixed[g].astype(F32)
    d_out_t = d_out_t.astype(BF)
    k_t = turned(k, eye).astype(BF)
    v32 = v.astype(F32)
    lane_head = iota((TP, GRP), 1) >> 5
    dq_t = []
    dk = jnp.zeros((TP, GRP), F32)
    dv = jnp.zeros((TP, GRP), F32)
    for h in range(8):
        mine = lane_head == h
        vm = jnp.where(mine, v32, 0.0).astype(BF)
        p = probs[pl.ds(pl.multiple_of((g * 8 + h) * TP, 16), TP), :]
        shared = jnp.sum(weighed[32 * h:32 * h + 32], axis=0, keepdims=True)
        ds = (p.astype(F32) * (dot(vm, d_out_t) - shared)).astype(BF)
        dq_t.append(dot(k_t[32 * h:32 * h + 32], ds))
        dk = jnp.where(mine, dot(ds, q), dk)
        dv = jnp.where(mine, dot(p, d_out), dv)
    scale = 32.0 ** -0.5
    dq = jnp.transpose(jnp.concatenate(dq_t, axis=0) * scale)
    acc[...] += (
        dot(dq.astype(BF), wqkv[:, cols(g * GRP)], 1, 1)
        + dot((dk * scale).astype(BF), wqkv[:, cols(C + g * GRP)], 1, 1)
        + dot(dv.astype(BF), wqkv[:, cols(2 * C + g * GRP)], 1, 1)
    )


def route(r, x, att, halo, choice, after_out, slots, table_out):
    top = jnp.where(iota((HALO, C), 0) < 14 * r, halo[...].astype(F32), att[:HALO, :].astype(F32))
    after_out[:HALO, :] = (x[:HALO, :].astype(F32) + top).astype(BF)
    after_out[HALO:, :] = (x[HALO:, :].astype(F32) + att[HALO:, :].astype(F32)).astype(BF)
    after = after_out[...].astype(F32)
    n2 = norm_parts(after)[0].astype(BF)
    tok, other = iota((TP, TP), 0), iota((TP, TP), 1)
    col = jnp.where(iota((TP, 1), 0) < TOK, choice, -1000.0)
    line = jnp.sum(jnp.where(tok == other, col, 0.0), axis=0, keepdims=True)
    same = jnp.where(col == line, 1.0, 0.0)
    same = jnp.where(other < tok, same, 0.0)
    rank = jnp.sum(same, axis=1, keepdims=True).astype(jnp.int32)
    table = jnp.where(col.astype(jnp.int32) * 8 + rank == iota((TP, 256), 1), 1.0, 0.0).astype(BF)
    table_out[...] = table
    slots[...] = pack_rows(dot(table, n2[:, :HC], 0, 0), dot(table, n2[:, HC:], 0, 0), 32)


def quad_table():
    row = iota((256, TP), 0)
    tok = iota((256, TP), 1)
    q = row >> 6
    n = row & 63
    a = (n * 9363) >> 16
    b = n - 7 * a
    want = (2 * a + (q & 1)) * 14 + 2 * b + (q >> 1)
    hit = jnp.where(want == tok, 1.0, 0.0)
    return jnp.where(n < 49, hit, 0.0).astype(BF)


def gathered(ret, table):
    low, high = unpack_rows(ret[0].astype(F32) + ret[1].astype(F32), 32)
    return jnp.concatenate([dot(table, low.astype(BF)), dot(table, high.astype(BF))], axis=1)


def merge_mid(after, ret, table_in, gate, parts, tail, mn_out, mn_tail, d_block_out, slots, spread, t_wide):
    table = table_in[...]
    block = (after[...].astype(F32) + gate * gathered(ret, table)).astype(BF)
    perm = quad_table()
    quads = dot(perm, block)
    vals = [quads[64 * q:64 * q + 49, :] for q in range(4)]
    inv = 1.0 / (4 * C)
    centre = sum(jnp.sum(v, axis=-1, keepdims=True) for v in vals) * inv
    cent = [v - centre for v in vals]
    var = sum(jnp.sum(v * v, axis=-1, keepdims=True) for v in cent) * inv
    scale = lax.rsqrt(var + EPS)
    unit = [v * scale for v in cent]
    for q in range(4):
        mn_out[:, q * C:(q + 1) * C] = unit[q][:48].astype(BF)
        for i in range(4):
            t_wide[0, 4 * q + i:4 * q + i + 1, :] = unit[q][48:49, i * 256:(i + 1) * 256]
    mn_tail[...] = t_wide[0].astype(BF)
    tails = jnp.sum(tail[...].astype(F32), axis=0)
    cots = []
    for q in range(4):
        tot = sum(part[:, q * C:(q + 1) * C].astype(F32) for part in parts)
        last = jnp.concatenate([tails[4 * q + i:4 * q + i + 1, :] for i in range(4)], axis=1)
        cots.append(jnp.concatenate([tot, last], axis=0))
    mean_cot = sum(jnp.sum(v, axis=-1, keepdims=True) for v in cots) * inv
    mean_dot = sum(jnp.sum(v * u, axis=-1, keepdims=True) for v, u in zip(cots, unit)) * inv
    spread[...] = jnp.zeros_like(spread)
    for q in range(4):
        spread[64 * q:64 * q + 49, :] = scale * (cots[q] - mean_cot - unit[q] * mean_dot)
    high, mid, low = split3(spread[...])
    d_block = dot(perm, high, 0, 0) + dot(perm, mid, 0, 0) + dot(perm, low, 0, 0)
    d_block_out[...] = d_block
    scaled = (gate * d_block).astype(BF)
    slots[...] = pack_rows(dot(table, scaled[:, :HC], 0, 0), dot(table, scaled[:, HC:], 0, 0), 32)


def after_back(after, ret, table, d_block, d_after_out, d_att_out):
    d_second = gathered(ret, table[...])
    d_after = d_block[...] + norm_back(after[...].astype(F32), d_second)
    d_after_out[...] = d_after
    d_att_out[...] = d_after.astype(BF)


def token_column(grid):
    tok = iota((TP, 14), 0)
    rho = (tok * 4682) >> 16
    place = iota((TP, 14), 1)
    pick = jnp.where(rho == place, 1.0, 0.0).astype(BF)
    high, mid, low = split3(grid[...].reshape(14, 14))
    rows = dot(pick, high) + dot(pick, mid) + dot(pick, low)
    return jnp.sum(jnp.where(tok - 14 * rho == place, rows, 0.0), axis=1, keepdims=True)


def lay_rows(tokens, wide, x):
    wide[TOK - 4:, :] = jnp.zeros((TP - TOK + 4, C), F32)
    for i in range(14):
        wide[14 * i:14 * i + 14, :] = tokens[0, i].astype(F32)
    x[...] = wide[...].astype(BF)


def expert_chunk(j, recv, part, ups, downs, flat, act_out, slope_out, ready):
    here = pl.ds(8 * j, 8)
    rows_here = pl.ds(256 * j, 256)
    low, high = unpack_rows(recv[:, here].reshape(32, 16, HC), 32)
    rows = jnp.concatenate([low, high], axis=1).astype(BF)
    flat[rows_here, :] = rows
    total = jnp.zeros((256, C), F32)
    for k in (0, 1, 3, 2):
        ready(k)
        pre = dot(rows, ups[k])
        cdf = 0.5 * (1.0 + lax.erf(pre * np.float32(2.0 ** -0.5)))
        act = (pre * cdf).astype(BF)
        slope = cdf + pre * jnp.exp(-0.5 * pre * pre) * np.float32((2.0 * np.pi) ** -0.5)
        act_out[rows_here, k * 256:(k + 1) * 256] = act
        slope_out[rows_here, k * 256:(k + 1) * 256] = slope.astype(BF)
        total = total + dot(act, downs[k])
    part[:, here] = pack_rows(total[:, :HC], total[:, HC:], 32).reshape(4, 8, 16, HC)


def expert_chunk_back(j, recv, part, ups, downs, flat, slope):
    here = pl.ds(8 * j, 8)
    rows_here = pl.ds(256 * j, 256)
    low, high = unpack_rows(recv[:, here].reshape(32, 16, HC), 32)
    rows = jnp.concatenate([low, high], axis=1).astype(BF)
    flat[rows_here, :] = rows
    total = jnp.zeros((256, C), F32)
    for k in range(4):
        span = slice(k * 256, (k + 1) * 256)
        d_pre = (slope[rows_here, span].astype(F32) * dot(rows, downs[k], 1, 1)).astype(BF)
        slope[rows_here, span] = d_pre
        total = total + dot(d_pre, ups[k], 1, 1)
    part[:, here] = pack_rows(total[:, :HC], total[:, HC:], 32).reshape(4, 8, 16, HC)


def coords():
    s = lax.axis_index("scene")
    row = lax.axis_index("row")
    z, m = row // 4, row % 4
    return s, z, m // 2, m % 2


def at(s, z, y, c):
    return (s, z * 4 + y * 2 + c)


def greet(s, z, y, c, total=64):
    barrier = pltpu.get_barrier_semaphore()
    mine = s * 4 + z

    def hail(k, carry):
        peer = (mine + k) % 32
        pl.semaphore_signal(barrier, inc=1, device_id=at(peer // 4, peer % 4, y, c), device_id_type=MESH)
        pl.semaphore_signal(barrier, inc=1, device_id=at(peer // 4, peer % 4, 1 - y, c), device_id_type=MESH)
        return carry

    lax.fori_loop(1, 32, hail, 0)
    pl.semaphore_signal(barrier, inc=1, device_id=at(s, z, 1 - y, c), device_id_type=MESH)
    pl.semaphore_signal(barrier, inc=1, device_id=at(s, z, y, 1 - c), device_id_type=MESH)
    pl.semaphore_wait(barrier, total)


def greet_all(place):
    s, z, y, c = place
    barrier = pltpu.get_barrier_semaphore()
    row = z * 4 + y * 2 + c
    pl.semaphore_signal(barrier, inc=1, device_id=(s, (row + 1) % 16), device_id_type=MESH)
    pl.semaphore_signal(barrier, inc=1, device_id=(s, (row + 15) % 16), device_id_type=MESH)
    greet(s, z, y, c, 66)


def remote(src, dst, send, recv, device):
    return pltpu.make_async_remote_copy(
        src_ref=src, dst_ref=dst, send_sem=send, recv_sem=recv, device_id=device, device_id_type=MESH
    )


def await_bytes(ref, sem):
    pltpu.make_async_copy(ref, ref, sem).wait()


SLOT_SEMS = [
    pltpu.SemaphoreType.DMA,
    pltpu.SemaphoreType.DMA((2, 4)),
    pltpu.SemaphoreType.DMA((2, 4)),
    pltpu.SemaphoreType.DMA((2, 4)),
    pltpu.SemaphoreType.DMA((2, 4)),
    pltpu.SemaphoreType.DMA((2, 4)),
    pltpu.SemaphoreType.DMA,
    pltpu.SemaphoreType.DMA,
]


def slots_through(place, slots, recv, part, other, total, ret, sems, compute, meanwhile=None):
    s, z, y, c = place
    mine = s * 4 + z
    yh, xx = s // 4, s % 4

    def steps(k):
        dx = k % 4
        return (k % 8) // 4, dx, (k // 8 + 4 - dx) % 4

    def ahead(k):
        dy, dx, dz = steps(k)
        return ((yh + dy) % 2 * 4 + (xx + dx) % 4) * 4 + (z + dz) % 4

    def behind(k):
        dy, dx, dz = steps(k)
        return ((yh + dy) % 2 * 4 + (xx + 4 - dx) % 4) * 4 + (z + 4 - dz) % 4

    send, arrive, f_send, f_recv, p_send, p_recv, r_send, r_recv = sems
    pair = at(s, z, y, 1 - c)

    def to_peer(k, peer, yy):
        remote(slots.at[peer], recv.at[y * 2 + c, k], send, arrive.at[y, k // 8], at(peer // 4, peer % 4, yy, c)).start()

    def push(k, carry):
        peer = ahead(k)
        to_peer(k, peer, y)
        to_peer(k, peer, 1 - y)
        return carry

    pltpu.make_async_copy(slots.at[mine], recv.at[y * 2 + c, 0], arrive.at[y, 0]).start()
    to_peer(0, mine, 1 - y)
    lax.fori_loop(1, 32, push, 0)
    forwards, partials = {}, {}

    def forward(j):
        for yy in range(2):
            block = recv.at[yy * 2 + c, pl.ds(8 * j, 8)]
            await_bytes(block, arrive.at[yy, j])
            forwards[yy, j] = remote(block, block, f_send.at[yy, j], f_recv.at[yy, j], pair)
            forwards[yy, j].start()

    def work(j):
        for yy in range(2):
            forwards[yy, j].wait_recv()
        compute(j)
        for yy in range(2):
            here = pl.ds(8 * j, 8)
            partials[yy, j] = remote(
                part.at[yy * 2 + (1 - c), here], other.at[yy, here], p_send.at[yy, j], p_recv.at[yy, j], pair
            )
            partials[yy, j].start()

    def give(k, yy):
        peer = behind(k)
        remote(total.at[yy, k], ret.at[y, mine], r_send, r_recv, at(peer // 4, peer % 4, yy, c)).start()

    def give_both(k, carry):
        give(k, 1 - y)
        give(k, y)
        return carry

    def back(j):
        here = pl.ds(8 * j, 8)
        for yy in range(2):
            partials[yy, j].wait_recv()
            total[yy, here] = (part[yy * 2 + c, here].astype(F32) + other[yy, here].astype(F32)).astype(BF)
        if j == 0:
            give(0, 1 - y)
            pltpu.make_async_copy(total.at[y, 0], ret.at[y, mine], r_recv).start()
        lax.fori_loop(max(1, 8 * j), 8 * j + 8, give_both, 0)

    forward(0)
    forward(1)
    work(0)
    forward(2)
    work(1)
    back(0)
    forward(3)
    work(2)
    back(1)
    work(3)
    back(2)
    back(3)

    def finish_sends():
        for copy in list(forwards.values()) + list(partials.values()):
            copy.wait_send()
        for sem in (send, r_send):
            await_bytes(total.at[0], sem)
            await_bytes(total.at[0, pl.ds(0, 31)], sem)

    if meanwhile is not None:
        meanwhile()
    await_bytes(ret, r_recv)
    return finish_sends


def front(
    shift, tokens, choice_in, gate_in, position_bias, pairs, merged_grad, qkv_weight, out_weight, expert_up, expert_down, reduce_weight,
    after, table, merge_norm, mn_tail, d_block, d_slots, qkv_out, probs_out, mixed_out, flat_out, act_out, slope_out, up_out, down_out,
    x, x_wide, bias, table_of, grad_wide, halo, halo2, normed, mask, ecol, spots, acc, att, wqkv, wo, wred, qkv, probs, mixed,
    d_send, d_relay, d_direct, d_summed, d_across, t_wide, t_send, t_recv, ups, downs, relay_up, relay_down,
    slots, recv, part, other, total, ret, flat, act, slope, spread,
    io_sem, halo_sem, w_send, w_recv, d_sem, *slot_sems,
):
    place = coords()
    s, z, y, c = place
    row = z * 4 + y * 2 + c
    r, cc = shift[0], shift[1]
    last = jnp.where(row == 15, 1, 0)
    ins = [
        pltpu.make_async_copy(reduce_weight, wred, io_sem.at[0]),
        pltpu.make_async_copy(qkv_weight, wqkv, io_sem.at[1]),
        pltpu.make_async_copy(out_weight, wo, io_sem.at[2]),
        pltpu.make_async_copy(expert_up.at[z], ups.at[0], io_sem.at[3]),
        pltpu.make_async_copy(expert_down.at[z], downs.at[0], io_sem.at[4]),
        pltpu.make_async_copy(pairs, table_of, io_sem.at[14]),
    ]
    for copy in ins:
        copy.start()
    lay_rows(tokens, x_wide, x)
    greet_all(place)

    nxt = (s, (row + 1) % 16)
    prv = (s, (row + 15) % 16)
    z_up, z_down = at(s, (z + 1) % 4, y, c), at(s, (z + 3) % 4, y, c)
    halo_copy = remote(x.at[pl.ds(0, HALO)], halo, halo_sem.at[0], halo_sem.at[1], prv)
    halo_copy.start()
    weights = [
        remote(expert_up.at[(z + 2) % 4], relay_up, w_send.at[0], w_recv.at[0], z_up),
        remote(expert_down.at[(z + 2) % 4], relay_down, w_send.at[1], w_recv.at[1], z_down),
        remote(expert_up.at[(z + 1) % 4], ups.at[1], w_send.at[2], w_recv.at[2], z_up),
        remote(expert_up.at[(z + 3) % 4], ups.at[3], w_send.at[3], w_recv.at[3], z_down),
        remote(expert_down.at[(z + 1) % 4], downs.at[1], w_send.at[4], w_recv.at[4], z_up),
        remote(expert_down.at[(z + 3) % 4], downs.at[3], w_send.at[5], w_recv.at[5], z_down),
    ]
    for copy in weights[:4]:
        copy.start()
    relayed = [
        remote(relay_up, ups.at[2], w_send.at[6], w_recv.at[6], z_up),
        remote(relay_down, downs.at[2], w_send.at[7], w_recv.at[7], z_down),
    ]

    by_place = merged_grad[...].astype(F32).reshape(49, 8, 256)
    for n in range(8):
        grad_wide[n] = by_place[:, n, :]
    grad48 = grad_wide[:, :48, :].astype(BF).reshape(8 * 48, 256)
    grad_tail = jnp.concatenate([grad_wide[:, 48, :], jnp.zeros((8, 256), F32)], axis=0).astype(BF)
    ins[0].wait()
    for half in range(4):
        span = pl.ds(half * C, C)
        d_send[:, :, span] = dot(grad48, wred[span, :], 1, 1).astype(BF).reshape(8, 48, C)
        tail = dot(grad_tail, wred[span, :], 1, 1)
        for i in range(4):
            t_wide[:, 4 * half + i, :] = tail[:8, i * 256:(i + 1) * 256]
    t_send[...] = t_wide[...].astype(BF)
    yh, xx = s // 4, s % 4
    x_up, x_down, x_far = (xx + 1) % 4, (xx + 3) % 4, (xx + 2) % 4
    to_up, to_down = at(yh * 4 + x_up, z, y, c), at(yh * 4 + x_down, z, y, c)
    first = [
        remote(d_send.at[x_far], d_relay.at[0], d_sem.at[0, 0], d_sem.at[1, 0], to_up),
        remote(d_send.at[4 + x_far], d_relay.at[1], d_sem.at[0, 1], d_sem.at[1, 1], to_down),
        remote(d_send.at[4 + x_up], d_direct.at[1], d_sem.at[0, 2], d_sem.at[1, 2], to_up),
        remote(d_send.at[x_down], d_direct.at[0], d_sem.at[0, 3], d_sem.at[1, 3], to_down),
    ]
    second = [
        remote(d_send.at[x_up], d_summed.at[0], d_sem.at[0, 4], d_sem.at[1, 4], to_up),
        remote(d_send.at[4 + x_down], d_summed.at[1], d_sem.at[0, 5], d_sem.at[1, 5], to_down),
    ]
    other_yh = 1 - yh
    across = remote(
        d_send.at[other_yh * 4 + xx], d_across, d_sem.at[0, 6], d_sem.at[1, 6], at(other_yh * 4 + xx, z, y, c)
    )
    gifts = []
    for k in range(1, 8):
        peer = (s + k) % 8
        gifts.append(remote(t_send.at[peer], t_recv.at[s], d_sem.at[2, k], d_sem.at[3, k], at(peer, z, y, c)))
    for copy in first + gifts:
        copy.start()
    own = pltpu.make_async_copy(t_send.at[s], t_recv.at[s], io_sem.at[6])
    own.start()

    def pass_on():
        for i, mine_at in enumerate((x_up, 4 + x_down)):
            first[i].wait_recv()
            d_send[mine_at] = (d_send[mine_at].astype(F32) + d_relay[i].astype(F32)).astype(BF)
            second[i].start()

    def cross():
        for copy in first[2:] + second:
            copy.wait_recv()
        there = other_yh * 4 + xx
        d_send[there] = (
            d_send[there].astype(F32) + d_direct[other_yh].astype(F32) + d_summed[other_yh].astype(F32)
        ).astype(BF)
        across.start()

    attn_masks(r, cc, last, mask, ecol, spots)
    ins[5].wait()
    bias[...] = jnp.zeros_like(bias)
    parts3 = jnp.concatenate(split3(position_bias[...]), axis=0)
    for pair in range(25):
        wide = dot(parts3, table_of[:, pair * 256:(pair + 1) * 256])
        wide = wide[:32] + wide[32:64] + wide[64:]
        for i in range(2):
            if 2 * pair + i < 49:
                bias[:, 2 * pair + i, :] = wide[:, i * 128:(i + 1) * 128] * np.float32(32.0 ** 0.5)
    normed[HALO:, :] = norm_parts(x[HALO:, :].astype(F32))[0].astype(BF)
    acc[...] = jnp.zeros_like(acc)
    halo_copy.wait_recv()
    top = jnp.where(iota((HALO, C), 0) < 14 * r, halo[...].astype(F32), x[:HALO, :].astype(F32))
    normed[:HALO, :] = norm_parts(top)[0].astype(BF)
    ins[1].wait()
    ins[2].wait()

    def group(g, carry):
        attn_group(g, normed, wqkv, wo, bias, mask, ecol, spots, qkv, probs, mixed, acc)
        return carry

    lax.fori_loop(0, 1, group, 0)
    pass_on()
    lax.fori_loop(1, 2, group, 0)
    for arrived, onward in zip(weights, relayed):
        arrived.wait_recv()
        onward.start()
    for copy in weights[4:]:
        copy.start()
    lax.fori_loop(2, 4, group, 0)
    att[...] = acc[...].astype(BF)
    halo2_copy = remote(att.at[pl.ds(0, HALO)], halo2, halo_sem.at[2], halo_sem.at[3], nxt)
    halo2_copy.start()
    outs = [
        pltpu.make_async_copy(qkv, qkv_out, io_sem.at[7]),
        pltpu.make_async_copy(probs, probs_out, io_sem.at[8]),
        pltpu.make_async_copy(mixed, mixed_out, io_sem.at[15]),
    ]
    for copy in outs:
        copy.start()
    cross()
    halo2_copy.wait_recv()
    choice = token_column(choice_in[...].astype(F32))
    route(r, x, att, halo2, choice, after, slots, table)

    def ready(k):
        pieces = {0: (), 1: (weights[2], weights[4]), 3: (weights[3], weights[5]), 2: relayed}[k]
        for copy in pieces:
            copy.wait_recv()
        if k == 0:
            ins[3].wait()
            ins[4].wait()

    def compute(j):
        expert_chunk(j, recv, part, ups, downs, flat, act, slope, ready if j == 0 else lambda k: None)

    finish_sends = slots_through(place, slots, recv, part, other, total, ret, slot_sems, compute)
    more = [
        pltpu.make_async_copy(flat, flat_out, io_sem.at[9]),
        pltpu.make_async_copy(act, act_out, io_sem.at[10]),
        pltpu.make_async_copy(slope, slope_out, io_sem.at[11]),
        pltpu.make_async_copy(ups, up_out, io_sem.at[12]),
        pltpu.make_async_copy(downs, down_out, io_sem.at[13]),
    ]
    for copy in more:
        copy.start()
    for copy in gifts + [across]:
        copy.wait_recv()
    own.wait()
    parts = (d_send.at[s], d_direct.at[yh], d_summed.at[yh], d_across)
    merge_mid(after, ret, table, token_column(gate_in), parts, t_recv, merge_norm, mn_tail, d_block, d_slots, spread, t_wide)
    for copy in outs + more:
        copy.wait()
    finish_sends()
    for copy in weights + relayed + gifts + first + second + [across, halo_copy, halo2_copy]:
        copy.wait_send()


def back(
    shift, tokens, after, table, merge_norm, mn_tail, d_block, d_slots,
    qkv_weight, out_weight, reduce_weight, qkv_in, probs_in, mixed_in, flat_in, act_in, slope_in, up_in, down_in,
    tokens_grad, merged, up_grad, down_grad,
    x, x_wide, halo, halo2, d_att, acc, d_after, d_shift, wqkv, wo, wred, qkv, probs, mixed, flat, act, slope, ups, downs,
    recv, part, other, total, ret, flat_d, send_up, send_down, relay_up, relay_down,
    mn_all, mt_all, merged_wide, merged_rows,
    io_sem, halo_sem, g_send, g_recv, m_sem, *slot_sems,
):
    place = coords()
    s, z, y, c = place
    row = z * 4 + y * 2 + c
    r = shift[0]
    loads = [
        (down_in, downs), (slope_in, slope), (up_in, ups), (act_in, act), (flat_in, flat),
        (out_weight, wo), (qkv_in, qkv), (probs_in, probs), (qkv_weight, wqkv), (reduce_weight, wred), (mixed_in, mixed),
    ]
    ins = [pltpu.make_async_copy(a, b, io_sem.at[i]) for i, (a, b) in enumerate(loads)]
    for copy in ins:
        copy.start()
    greet_all(place)
    nxt = (s, (row + 1) % 16)
    prv = (s, (row + 15) % 16)
    z_up, z_down = at(s, (z + 1) % 4, y, c), at(s, (z + 3) % 4, y, c)

    def compute(j):
        if j == 0:
            for copy in ins[:3]:
                copy.wait()
        expert_chunk_back(j, recv, part, ups, downs, flat_d, slope)

    returns = [
        remote(send_up.at[1], relay_up, g_send.at[0], g_recv.at[0], z_up),
        remote(send_down.at[1], relay_down, g_send.at[1], g_recv.at[1], z_down),
        remote(send_up.at[0], up_grad.at[z], g_send.at[2], g_recv.at[2], z_down),
        remote(send_down.at[0], down_grad.at[z], g_send.at[3], g_recv.at[3], z_down),
        remote(send_up.at[2], up_grad.at[z], g_send.at[4], g_recv.at[4], z_up),
        remote(send_down.at[2], down_grad.at[z], g_send.at[5], g_recv.at[5], z_up),
    ]
    relayed = [
        remote(relay_up, up_grad.at[(z + 3) % 4], g_send.at[6], g_recv.at[6], z_up),
        remote(relay_down, down_grad.at[(z + 1) % 4], g_send.at[7], g_recv.at[7], z_down),
    ]
    yh, xx = s // 4, s % 4
    x_up, x_down = (xx + 1) % 4, (xx + 3) % 4
    to_up, to_down = at(yh * 4 + x_up, z, y, c), at(yh * 4 + x_down, z, y, c)
    across = (1 - yh) * 4 + xx
    half = (pl.ds(0, 2 * C), pl.ds(2 * C, 2 * C))

    def neighbours(source, slot, n):
        return [
            remote(source, mn_all.at[slot], m_sem.at[0, n], m_sem.at[1, n], to_up),
            remote(source, mn_all.at[slot], m_sem.at[0, n + 1], m_sem.at[1, n + 1], to_down),
        ]

    def halves(base, n):
        below, above = base * 4 + x_down, base * 4 + x_up
        low, high = mn_all.at[below, :, half[0]], mn_all.at[above, :, half[1]]
        return [
            remote(low, low, m_sem.at[0, n], m_sem.at[1, n], to_up),
            remote(high, high, m_sem.at[0, n + 1], m_sem.at[1, n + 1], to_down),
        ]

    spread_own = neighbours(merge_norm, s, 0)
    spread_across = neighbours(mn_all.at[across], across, 2)
    far_own = halves(yh, 4)
    far_across = halves(1 - yh, 6)
    partner = remote(merge_norm, mn_all.at[s], m_sem.at[0, 8], m_sem.at[1, 8], at(across, z, y, c))
    tail_copies = []
    for k in range(1, 8):
        peer = (s + k) % 8
        tail_copies.append(remote(mn_tail, mt_all.at[s], m_sem.at[2, k], m_sem.at[3, k], at(peer, z, y, c)))
    gifts = spread_own + spread_across + far_own + far_across + [partner] + tail_copies
    own = [
        pltpu.make_async_copy(merge_norm, mn_all.at[s], io_sem.at[14]),
        pltpu.make_async_copy(mn_tail, mt_all.at[s], io_sem.at[11]),
    ]
    own_out = [
        pltpu.make_async_copy(send_up.at[3], up_grad.at[z], io_sem.at[12]),
        pltpu.make_async_copy(send_down.at[3], down_grad.at[z], io_sem.at[13]),
    ]

    def grads():
        for copy in ins[3:5]:
            copy.wait()
        for k in (2, 1, 3, 0):
            span = slice(k * 256, (k + 1) * 256)
            up_part = dot(flat[...], slope[:, span], 0, 0)
            down_part = dot(act[:, span], flat_d[...], 0, 0)
            send_up[(k + 3) % 4] = up_part.astype(BF)
            send_down[(k + 3) % 4] = down_part.astype(BF)
            if k:
                first = {2: 0, 1: 2, 3: 4}[k]
                returns[first].start()
                returns[first + 1].start()
            else:
                for copy in own_out:
                    copy.start()

    finish_sends = slots_through(place, d_slots, recv, part, other, total, ret, slot_sems, compute, grads)
    for copy in spread_own + [partner] + tail_copies + own:
        copy.start()
    after_back(after, ret, table, d_block, d_after, d_att)
    halo_copy = remote(d_att.at[pl.ds(0, HALO)], halo, halo_sem.at[0], halo_sem.at[1], prv)
    halo_copy.start()
    lay_rows(tokens, x_wide, x)
    acc[...] = jnp.zeros_like(acc)
    for copy in ins[5:9] + ins[10:]:
        copy.wait()
    halo_copy.wait_recv()
    halo_copy.wait_send()
    top = jnp.where(iota((HALO, C), 0) < 14 * r, halo[...].astype(F32), d_att[:HALO, :].astype(F32))
    d_att[:HALO, :] = top.astype(BF)

    def group(g, carry):
        attn_group_back(g, d_att, wqkv, wo, qkv, probs, mixed, acc)
        return carry

    lax.fori_loop(0, 1, group, 0)
    for arrived, onward in zip(spread_own, far_own):
        arrived.wait_recv()
        onward.start()
    lax.fori_loop(1, 2, group, 0)
    partner.wait_recv()
    for onward in spread_across:
        onward.start()
    lax.fori_loop(2, 3, group, 0)
    for arrived, onward in zip(returns, relayed):
        arrived.wait_recv()
        onward.start()
    lax.fori_loop(3, 4, group, 0)
    d_shift[...] = acc[...].astype(BF)
    halo2_copy = remote(d_shift.at[pl.ds(0, HALO)], halo2, halo_sem.at[2], halo_sem.at[3], nxt)
    halo2_copy.start()

    for arrived, onward in zip(spread_across, far_across):
        arrived.wait_recv()
        onward.start()
    halo2_copy.wait_recv()
    top = jnp.where(iota((HALO, C), 0) < 14 * r, halo2[...].astype(F32), d_shift[:HALO, :].astype(F32))
    x_wide[:HALO, :] = d_after[:HALO, :] + norm_back(x[:HALO, :].astype(F32), top)
    x_wide[HALO:, :] = d_after[HALO:, :] + norm_back(x[HALO:, :].astype(F32), d_shift[HALO:, :].astype(F32))
    for i in range(14):
        tokens_grad[0, i] = x_wide[14 * i:14 * i + 14, :].astype(BF)

    for copy in far_own + far_across + tail_copies:
        copy.wait_recv()
    for copy in own + [ins[9]]:
        copy.wait()
    merged_wide[:, :48, :] = dot(mn_all[...].reshape(8 * 48, 4 * C), wred[...]).reshape(8, 48, 256)
    tails = mt_all[...].astype(F32)
    last = jnp.concatenate([tails[:, i, :] for i in range(16)], axis=1)
    last = jnp.concatenate([last, jnp.zeros_like(last)], axis=0).astype(BF)
    merged_wide[:, 48, :] = dot(last, wred[...])[:8]
    for n in range(8):
        merged_rows[:, n, :] = merged_wide[n]
    merged[...] = merged_rows[...].reshape(7, 7, 8, 256).astype(BF)

    for copy in returns[2:] + relayed:
        copy.wait_recv()
    for copy in own_out:
        copy.wait()
    finish_sends()
    for copy in returns + relayed + gifts + [halo2_copy]:
        copy.wait_send()


def widen(up_in, down_in, grad_in, merged_in, up_out, down_out, grad_out, merged_out):
    up_out[...] = up_in[...].astype(F32)
    down_out[...] = down_in[...].astype(F32)

    @pl.when(pl.program_id(0) == 0)
    def _():
        grad_out[...] = grad_in[...]
        merged_out[...] = merged_in[...]


def bias_pairs():
    spot = np.arange(49)
    py, px = spot // 7, spot % 7
    relative = (py[:, None] - py[None, :] + 6) * 13 + (px[:, None] - px[None, :] + 6)
    table = np.zeros((169, 50, 128), np.float32)
    a, b = np.meshgrid(spot, spot, indexing="ij")
    table[relative.reshape(-1), b.reshape(-1), a.reshape(-1)] = 1.0
    return table.reshape(169, 6400)


def local(
    tokens,
    qkv_weight,
    out_weight,
    position_bias,
    window_shift,
    expert_up,
    expert_down,
    expert_choice,
    combine_weight,
    reduce_weight,
    merged_grad,
):
    choice = jnp.transpose(expert_choice, (1, 0, 3, 2)).reshape(14, 1, 14)
    gate = jnp.transpose(combine_weight, (1, 0, 2))
    pairs = jnp.asarray(bias_pairs(), dtype=BF)
    V = pltpu.VMEM
    D = pltpu.SemaphoreType.DMA

    after, table, merge_norm, mn_tail, d_block, d_slots, qkv, probs, mixed, flat_in, act, slope, ups, downs = pl.pallas_call(
        front,
        out_shape=[
            sds((TP, C), BF), sds((TP, 256), BF), sds((48, 4 * C), BF), sds((16, 256), BF), sds((TP, C), F32),
            sds((32, 16, HC), BF), sds((3, 4, TP, GRP), BF), sds((32 * TP, TP), BF), sds((4, GRP, TP), BF), sds((C, C), BF), sds((C, C), BF),
            sds((C, C), BF), sds((4, C, 256), BF), sds((4, 256, C), BF),
        ],
        in_specs=[SM, VM, VM, VM, VM, HB, VM] + [HB] * 5,
        out_specs=[VM] * 6 + [HB] * 8,
        scratch_shapes=[
            V((TP, C), BF), V((TP, C), F32), V((32, 64, 128), F32), V((169, 6400), BF), V((8, 49, 256), F32),
            V((HALO, C), BF), V((HALO, C), BF), V((TP, C), BF), V((TP, TP), F32),
            V((192, TP), BF), V((8, TP, GRP), BF), V((TP, C), F32), V((TP, C), BF),
            V((C, 3 * C), BF), V((C, C), BF), V((4 * C, 256), BF),
            V((3, 4, TP, GRP), BF), V((32 * TP, TP), BF), V((4, GRP, TP), BF),
            V((8, 48, 4 * C), BF), V((2, 48, 4 * C), BF), V((2, 48, 4 * C), BF), V((2, 48, 4 * C), BF),
            V((48, 4 * C), BF), V((8, 16, 256), F32),
            V((8, 16, 256), BF), V((8, 16, 256), BF),
            V((4, C, 256), BF), V((4, 256, C), BF), V((C, 256), BF), V((256, C), BF),
            V((32, 16, HC), BF), V((4, 32, 16, HC), BF), V((4, 32, 16, HC), BF),
            V((2, 32, 16, HC), BF), V((2, 32, 16, HC), BF), V((2, 32, 16, HC), BF),
            V((C, C), BF), V((C, C), BF), V((C, C), BF), V((256, C), F32),
            D((16,)), D((4,)), D((8,)), D((8,)), D((4, 8)), *SLOT_SEMS,
        ],
        compiler_params=params(collective_id=0, has_side_effects=True),
        cost_estimate=cost(12 << 30, 60 << 20),
        name="front",
    )(window_shift, tokens, choice, gate, position_bias, pairs, jnp.transpose(merged_grad, (1, 2, 0, 3)), qkv_weight, out_weight,
      expert_up, expert_down, reduce_weight)

    tokens_grad, merged, up_grad, down_grad = pl.pallas_call(
        back,
        out_shape=[
            sds(tokens.shape, BF), sds((7, 7, 8, 256), BF), sds((4, C, 256), BF), sds((4, 256, C), BF),
        ],
        in_specs=[SM] + [VM] * 7 + [HB] * 11,
        out_specs=[VM] * 2 + [HB] * 2,
        scratch_shapes=[
            V((TP, C), BF), V((TP, C), F32), V((HALO, C), BF), V((HALO, C), BF), V((TP, C), BF), V((TP, C), F32),
            V((TP, C), F32), V((TP, C), BF), V((C, 3 * C), BF), V((C, C), BF), V((4 * C, 256), BF),
            V((3, 4, TP, GRP), BF), V((32 * TP, TP), BF), V((4, GRP, TP), BF), V((C, C), BF), V((C, C), BF), V((C, C), BF),
            V((4, C, 256), BF), V((4, 256, C), BF),
            V((4, 32, 16, HC), BF), V((4, 32, 16, HC), BF), V((2, 32, 16, HC), BF), V((2, 32, 16, HC), BF),
            V((2, 32, 16, HC), BF), V((C, C), BF), V((4, C, 256), BF), V((4, 256, C), BF), V((C, 256), BF), V((256, C), BF),
            V((8, 48, 4 * C), BF), V((8, 16, 256), BF), V((8, 49, 256), F32), V((49, 8, 256), F32),
            D((20,)), D((4,)), D((8,)), D((8,)), D((4, 9)), *SLOT_SEMS,
        ],
        compiler_params=pltpu.CompilerParams(
            vmem_limit_bytes=60 * 1024 * 1024, collective_id=1, has_side_effects=True
        ),
        cost_estimate=cost(16 << 30, 60 << 20),
        name="back",
    )(window_shift, tokens, after, table, merge_norm, mn_tail, d_block, d_slots, qkv_weight, out_weight, reduce_weight,
      qkv, probs, mixed, flat_in, act, slope, ups, downs)
    whole = lambda shape: pl.BlockSpec(shape, lambda e: (0,) * len(shape))
    blocks = [
        pl.BlockSpec((1, C, 256), lambda e: (e, 0, 0)), pl.BlockSpec((1, 256, C), lambda e: (e, 0, 0)),
        whole(tokens_grad.shape), whole(merged.shape),
    ]
    up_grad, down_grad, tokens_grad, merged = pl.pallas_call(
        widen,
        grid=(4,),
        out_shape=[
            sds((4, C, 256), F32), sds((4, 256, C), F32), sds(tokens_grad.shape, BF), sds(merged.shape, BF),
        ],
        in_specs=blocks,
        out_specs=blocks,
        compiler_params=params(),
        cost_estimate=cost(0, 14 << 20),
        name="widen",
    )(up_grad, down_grad, tokens_grad, merged)
    return (jnp.transpose(merged, (2, 0, 1, 3)), tokens_grad, up_grad, down_grad)


def solution(mesh):
    placed = (
        P("scene", "row", None, None),
        P(),
        P(),
        P(),
        P(),
        P("scene", None, "row"),
        P("scene", "row", None),
        P("scene", "row", None, None),
        P("scene", "row", None),
        P(None, "scene"),
        P(None, "row", None, "scene"),
    )
    return jax.shard_map(
        local,
        mesh=mesh,
        in_specs=placed,
        out_specs=(
            P(None, "row", None, "scene"),
            P("scene", "row", None, None),
            P("scene", None, "row"),
            P("scene", "row", None),
        ),
        check_vma=False,
    )
```
